32 devices in a mesh: dp: 8 (over z, core), seq: 4 (over y, x).
Axes of the slice: x: 2, y: 2, z: 4, core: 2. Of those that a mesh axis runs over, the one named last changes fastest.
Arguments:
- layer_input: bfloat16 [2, 8, 1024, 1024], P(None, 'dp', 'seq'), may hold values from -6 to 6
- memory: bfloat16 [2, 8, 512, 1024], P(None, 'dp', 'seq'), may hold values from -6 to 6
- target_lengths: int32 [2, 8], P(None, 'dp'), may hold values from 512 to 1024, as said below
- memory_lengths: int32 [2, 8], P(None, 'dp'), may hold values from 256 to 512, as said below
- buckets: int32 [1024], replicated, may hold values from 0 to 31, as said below
- norm_self: bfloat16 [1024], P('dp'), may hold values from 0.25 to 1.75
- self_q: bfloat16 [1024, 1024], P('dp'), may hold values from -0.046875 to 0.046875
- self_k: bfloat16 [1024, 512], P('dp'), may hold values from -0.1875 to 0.1875
- self_v: bfloat16 [1024, 512], P('dp'), may hold values from -0.1875 to 0.1875
- self_out: bfloat16 [1024, 1024], P('dp'), may hold values from -0.75 to 0.75
- rel_bias: bfloat16 [32, 16], P('dp', 'seq'), may hold values from -4 to 4
- norm_cross: bfloat16 [1024], P('dp'), may hold values from 0.25 to 1.75
- cross_q: bfloat16 [1024, 1024], P('dp'), may hold values from -0.046875 to 0.046875
- cross_k: bfloat16 [1024, 512], P('dp'), may hold values from -0.1875 to 0.1875
- cross_v: bfloat16 [1024, 512], P('dp'), may hold values from -0.1875 to 0.1875
- cross_out: bfloat16 [1024, 1024], P('dp'), may hold values from -0.75 to 0.75
- norm_ff: bfloat16 [1024], P('dp'), may hold values from 0.25 to 1.75
- ff_gate: bfloat16 [1024, 2816], P('dp'), may hold values from -0.1875 to 0.1875
- ff_up: bfloat16 [1024, 2816], P('dp'), may hold values from -0.1875 to 0.1875
- ff_down: bfloat16 [2816, 1024], P('dp'), may hold values from -0.21875 to 0.21875
- cotangent: bfloat16 [2, 8, 1024, 1024], P(None, 'dp', 'seq'), may hold values from -6 to 6
Outputs:
- output: bfloat16 [2, 8, 1024, 1024], P(None, 'dp', 'seq')
- input_grad: float32 [2, 8, 1024, 1024], P(None, 'dp', 'seq')
- memory_grad: float32 [2, 8, 512, 1024], P(None, 'dp', 'seq')
- norm_self_grad: float32 [1024], P(('dp', 'seq'))
- self_q_grad: float32 [1024, 1024], P(('dp', 'seq'))
- self_k_grad: float32 [1024, 512], P(('dp', 'seq'))
- self_v_grad: float32 [1024, 512], P(('dp', 'seq'))
- self_out_grad: float32 [1024, 1024], P(('dp', 'seq'))
- rel_bias_grad: float32 [32, 16], P('dp', 'seq')
- norm_cross_grad: float32 [1024], P(('dp', 'seq'))
- cross_q_grad: float32 [1024, 1024], P(('dp', 'seq'))
- cross_k_grad: float32 [1024, 512], P(('dp', 'seq'))
- cross_v_grad: float32 [1024, 512], P(('dp', 'seq'))
- cross_out_grad: float32 [1024, 1024], P(('dp', 'seq'))
- norm_ff_grad: float32 [1024], P(('dp', 'seq'))
- ff_gate_grad: float32 [1024, 2816], P(('dp', 'seq'))
- ff_up_grad: float32 [1024, 2816], P(('dp', 'seq'))
- ff_down_grad: float32 [2816, 1024], P(('dp', 'seq'))
The draws below stay inside these ranges and needn't reach their ends.
Inputs may be any that keep to these rules, and one draw needn't show every extreme that they name: `target_lengths`: in every row one of the 2 micro-batches has all 1024 positions valid. `memory_lengths`: in every row one of the 2 micro-batches has all 512 positions valid. `buckets`: 0 at distance 0, never falling, rising by at most one from one distance to the next.
All inputs are finite; a program needn't handle non-finite values.
Results may differ from the reference program's by a relative error of at most 0.028.
The reference program's roundings to bfloat16 on the way count: a program that leaves them out, or rounds other values in their place, can miss the bound.
Values may be sent and summed in bfloat16 or wider, within the bound.
A program may use at most 512 MiB of HBM per device.

```python
import jax
import jax.numpy as jnp
from jax import lax

D = 1024
FF = 2816
HEADS = 16
HEAD_DIM = 64
BUCKETS = 32
KV_HEADS = 8
TGT = 1024
MEM = 512
MICRO = 2
INNER = 1024
KVD = 512
ROWS = 8


def lengths_for(key, longest):
    key_drawn, key_pick = jax.random.split(key)
    drawn = jax.random.randint(key_drawn, (MICRO, ROWS), longest // 2, longest + 1)
    full_row = jax.random.randint(key_pick, (ROWS,), 0, MICRO)
    chosen = jnp.arange(MICRO)[:, None] == full_row[None, :]
    return jnp.where(chosen, longest, drawn).astype(jnp.int32)


def draw_target_lengths(key, part):
    key = jax.random.fold_in(key, 11)
    return lengths_for(key, TGT)


def draw_memory_lengths(key, part):
    key = jax.random.fold_in(key, 12)
    return lengths_for(key, MEM)


def draw_buckets(key, part):
    key = jax.random.fold_in(key, 13)
    order = jax.random.permutation(key, TGT - 1) + 1
    rises = jnp.zeros((TGT,), jnp.int32).at[order[:BUCKETS - 1]].set(1)
    return jnp.cumsum(rises).astype(jnp.int32)


def level_of(key, extent, pieces, least, top_value):
    def one(dim, parts):
        heights = jax.random.uniform(jax.random.fold_in(jax.random.fold_in(key, 6), dim), (parts,), jnp.float32, least / len(pieces), top_value / len(pieces))
        return jnp.repeat(jnp.exp(heights), extent[dim] // parts).reshape((-1,) + (1,) * (len(extent) - dim - 1))

    loudness = one(*pieces[0])
    for cut in pieces[1:]:
        loudness = loudness * one(*cut)
    return loudness


def noise(own_key, dims, deviation, most, pieces=(), held_as=jnp.bfloat16):
    array = deviation * jax.random.normal(own_key, dims, jnp.float32)
    if pieces:
        array = array * level_of(own_key, dims, pieces, -0.22, 0.18)
    return jnp.clip(array, -most, most).astype(held_as)


def setup_inputs(seed: int = 0) -> dict:
    streams_of = jax.random.split(jax.random.key(seed), 22)
    return {
        "layer_input": noise(streams_of[0], (MICRO, ROWS, TGT, D), 1.0, 6.0, ((1, 8), (2, 4))),
        "memory": noise(streams_of[1], (MICRO, ROWS, MEM, D), 1.0, 6.0, ((1, 8), (2, 4))),
        "target_lengths": draw_target_lengths(jax.random.fold_in(streams_of[21], 71), 0),
        "memory_lengths": draw_memory_lengths(jax.random.fold_in(streams_of[21], 71), 0),
        "buckets": draw_buckets(jax.random.fold_in(streams_of[21], 71), 0),
        "norm_self": jnp.clip(1.0 + 0.15 * jax.random.normal(streams_of[5], (D,), jnp.float32), 0.25, 1.75).astype(jnp.bfloat16),
        "self_q": noise(streams_of[6], (D, INNER), (16 * D) ** -0.5, 0.046875, ((0, 8),)),
        "self_k": noise(streams_of[7], (D, KVD), D ** -0.5, 0.1875, ((0, 8),)),
        "self_v": noise(streams_of[8], (D, KVD), D ** -0.5, 0.1875, ((0, 8),)),
        "self_out": noise(streams_of[9], (INNER, D), (INNER // 16) ** -0.5, 0.75, ((0, 8),)),
        "rel_bias": noise(streams_of[10], (BUCKETS, HEADS), 1.0, 4.0, ((0, 8), (1, 4))),
        "norm_cross": jnp.clip(1.0 + 0.15 * jax.random.normal(streams_of[11], (D,), jnp.float32), 0.25, 1.75).astype(jnp.bfloat16),
        "cross_q": noise(streams_of[12], (D, INNER), (16 * D) ** -0.5, 0.046875, ((0, 8),)),
        "cross_k": noise(streams_of[13], (D, KVD), D ** -0.5, 0.1875, ((0, 8),)),
        "cross_v": noise(streams_of[14], (D, KVD), D ** -0.5, 0.1875, ((0, 8),)),
        "cross_out": noise(streams_of[15], (INNER, D), (INNER // 16) ** -0.5, 0.75, ((0, 8),)),
        "norm_ff": jnp.clip(1.0 + 0.15 * jax.random.normal(streams_of[16], (D,), jnp.float32), 0.25, 1.75).astype(jnp.bfloat16),
        "ff_gate": noise(streams_of[17], (D, FF), D ** -0.5, 0.1875, ((0, 8),)),
        "ff_up": noise(streams_of[18], (D, FF), D ** -0.5, 0.1875, ((0, 8),)),
        "ff_down": noise(streams_of[19], (FF, D), (FF // 4) ** -0.5, 0.21875, ((0, 8),)),
        "cotangent": noise(streams_of[20], (MICRO, ROWS, TGT, D), 1.0, 6.0, ((1, 8), (2, 4))),
    }


EPS = 1e-06
NEG = -1e+30
HIGH = lax.Precision.HIGHEST

@jax.custom_vjp
def low(v):
    return lax.optimization_barrier(v.astype(jnp.bfloat16)).astype(jnp.float32)

@jax.custom_vjp
def low_back(v):
    return v

def low_keep(v):
    return (low(v), None)

def low_pass(kept, grad):
    return (grad,)

def back_keep(v):
    return (v, None)

def back_low(kept, grad):
    return (low(grad),)
low.defvjp(low_keep, low_pass)
low_back.defvjp(back_keep, back_low)

def matmul(left, right):
    return jnp.dot(left, right, precision=HIGH)

def rms_norm(value, gain):
    return value * lax.rsqrt(lax.optimization_barrier(jnp.mean(value * value, axis=-1, keepdims=True)) + EPS) * gain

def attend(queries, keys, values, extra, keep):
    scores = low_back(jnp.einsum('rkgd,skd->kgrs', queries, keys, precision=HIGH) + extra)
    masked = jnp.where(keep, scores, NEG)
    peak = lax.optimization_barrier(jnp.max(masked, axis=-1, keepdims=True))
    weights = jnp.where(keep, jnp.exp(masked - peak), 0.0)
    probs = weights / lax.optimization_barrier(jnp.sum(weights, axis=-1, keepdims=True))
    mixed = jnp.einsum('kgrs,skd->rkgd', low(probs), values, precision=HIGH)
    return low(low_back(mixed))

def decoder_layer(params, hidden, memory, length, memory_length, buckets):
    norm_self, self_q, self_k, self_v, self_out, rel_bias, norm_cross, cross_q, cross_k, cross_v, cross_out, norm_ff, ff_gate, ff_up, ff_down = params
    block = min(512, TGT)
    group = HEADS // KV_HEADS
    positions = jnp.arange(TGT, dtype=jnp.int32)
    slots = jnp.arange(MEM, dtype=jnp.int32)
    starts = jnp.arange(TGT // block, dtype=jnp.int32) * block
    normed = low(rms_norm(hidden, norm_self))
    queries = low(low_back(matmul(normed, self_q))).reshape(TGT, KV_HEADS, group, HEAD_DIM)
    keys = low(low_back(matmul(normed, self_k))).reshape(TGT, KV_HEADS, HEAD_DIM)
    values = low(low_back(matmul(normed, self_v))).reshape(TGT, KV_HEADS, HEAD_DIM)
    table = rel_bias[buckets]

    def self_rows(start):
        rows = start + jnp.arange(block, dtype=jnp.int32)
        distance = rows[:, None] - positions[None, :]
        keep = (distance >= 0) & (positions[None, :] < length)
        extra = jnp.moveaxis(table[jnp.maximum(distance, 0)], 2, 0).reshape(KV_HEADS, group, block, TGT)
        return attend(lax.dynamic_slice_in_dim(queries, start, block, 0), keys, values, extra, keep)
    context = lax.map(jax.checkpoint(self_rows), starts).reshape(TGT, HEADS * HEAD_DIM)
    first = hidden + low_back(matmul(context, self_out))
    normed_cross = low(rms_norm(first, norm_cross))
    cross_queries = low(low_back(matmul(normed_cross, cross_q))).reshape(TGT, KV_HEADS, group, HEAD_DIM)
    memory_keys = low(low_back(matmul(memory, cross_k))).reshape(MEM, KV_HEADS, HEAD_DIM)
    memory_values = low(low_back(matmul(memory, cross_v))).reshape(MEM, KV_HEADS, HEAD_DIM)
    memory_keep = jnp.broadcast_to(slots[None, :] < memory_length, (block, MEM))
    no_bias = jnp.zeros((KV_HEADS, group, block, MEM), jnp.float32)

    def cross_rows(start):
        return attend(lax.dynamic_slice_in_dim(cross_queries, start, block, 0), memory_keys, memory_values, no_bias, memory_keep)
    cross_context = lax.map(jax.checkpoint(cross_rows), starts).reshape(TGT, HEADS * HEAD_DIM)
    second = first + low_back(matmul(cross_context, cross_out))
    normed_ff = low(rms_norm(second, norm_ff))
    gate = low_back(matmul(normed_ff, ff_gate))
    upward = low_back(matmul(normed_ff, ff_up))
    middle = low(jax.nn.gelu(gate, approximate=True) * upward)
    third = second + low_back(matmul(middle, ff_down))
    return third * (positions < length)[:, None].astype(jnp.float32)

def reference(layer_input, memory, target_lengths, memory_lengths, buckets, norm_self, self_q, self_k, self_v, self_out, rel_bias, norm_cross, cross_q, cross_k, cross_v, cross_out, norm_ff, ff_gate, ff_up, ff_down, cotangent):
    params = tuple((piece.astype(jnp.float32) for piece in (norm_self, self_q, self_k, self_v, self_out, rel_bias, norm_cross, cross_q, cross_k, cross_v, cross_out, norm_ff, ff_gate, ff_up, ff_down)))
    count = MICRO * ROWS
    items = (layer_input.reshape(count, TGT, D), memory.reshape(count, MEM, D), target_lengths.reshape(count), memory_lengths.reshape(count), cotangent.reshape(count, TGT, D))

    def one_sequence(totals, item):
        hidden, encoded, length, memory_length, upstream = item

        def forward(weights, tokens, context_rows):
            return decoder_layer(weights, tokens, context_rows, length, memory_length, buckets)
        result, pullback = jax.vjp(forward, params, hidden.astype(jnp.float32), encoded.astype(jnp.float32))
        weight_grads, token_grad, encoded_grad = pullback(upstream.astype(jnp.float32))
        totals = jax.tree.map(jnp.add, totals, weight_grads)
        return (totals, (result.astype(jnp.bfloat16), token_grad, encoded_grad))
    start_totals = jax.tree.map(jnp.zeros_like, params)
    totals, (output, input_grad, memory_grad) = lax.scan(one_sequence, start_totals, items)
    return (output.reshape(layer_input.shape), input_grad.reshape(layer_input.shape), memory_grad.reshape(memory.shape), totals[0], totals[1], totals[2], totals[3], totals[4], totals[5], totals[6], totals[7], totals[8], totals[9], totals[10], totals[11], totals[12], totals[13], totals[14])
```

```python
import functools

import jax
import jax.numpy as jnp
from jax import lax
from jax.experimental import pallas as pl
from jax.experimental.pallas import tpu as pltpu
from jax.sharding import PartitionSpec as P

HEADS = 16
HEAD_DIM = 64
BUCKETS = 32
KV_HEADS = 8
TGT = 1024
MEM = 512
QB = 256


EPS = 1e-06
NEG = -1e30
HIGH = lax.Precision.HIGHEST


def shortened(shard):
    return jax.tree.map(lambda a: a.astype(jnp.bfloat16) if a.dtype == jnp.float32 else a, shard)


def rms_norm(value, gain):
    return value * lax.rsqrt(jnp.mean(value * value, axis=-1, keepdims=True) + EPS) * gain


def gated(gate, upward):
    return jax.nn.gelu(gate, approximate=True) * upward


def project(left, right):
    return jnp.dot(left, right, preferred_element_type=jnp.float32)


def project_back(grad, weight):
    return lax.dot_general(
        grad, weight, (((1,), (1,)), ((), ())), preferred_element_type=jnp.float32
    )


def weight_grad(left, right):
    return lax.dot_general(
        left, right, (((0,), (0,)), ((), ())), preferred_element_type=jnp.float32
    )


def split_heads(values, group):
    return values.reshape(values.shape[:2] + (-1, group, HEAD_DIM))


def split_shared(values):
    return values.reshape(values.shape[:2] + (-1, HEAD_DIM))


def causal_masks(table, length, group):

    def masks(start, block):
        stop = start + block
        rows = start + jnp.arange(block, dtype=jnp.int32)
        columns = jnp.arange(stop, dtype=jnp.int32)
        distance = rows[:, None] - columns[None, :]
        keep = (distance >= 0) & (columns[None, :] < length)
        extra = jnp.take(table, jnp.maximum(distance, 0), axis=1)
        return (extra.reshape((-1, group, block, stop)), keep, stop)

    return masks


def memory_masks(length, width):

    def masks(start, block):
        keep = jnp.broadcast_to(
            jnp.arange(width, dtype=jnp.int32)[None, :] < length, (block, width)
        )
        return (None, keep, width)

    return masks


def diagonal_sums(grads, block, stop):
    leading = grads.shape[:2]
    flipped = jnp.pad(grads[..., ::-1], ((0, 0), (0, 0), (0, 0), (0, block)))
    skewed = flipped.reshape(leading + (block * (stop + block),))[..., : block * (stop + block - 1)]
    skewed = skewed.reshape(leading + (block, stop + block - 1))
    return jnp.sum(skewed, axis=2)[..., block - 1 :]


def attend_forward(queries, keys, values, masks):
    block = min(512, queries.shape[0])
    outputs = []
    totals = []
    for index in range(queries.shape[0] // block):
        start = index * block
        extra, keep, stop = masks(start, block)
        rows = queries[start : start + block]
        scores = jnp.einsum("rkgd,skd->kgrs", rows, keys[:stop], preferred_element_type=jnp.float32)
        if extra is not None:
            scores = scores + extra
        scores = jnp.where(keep, scores, NEG)
        peak = jnp.max(scores, axis=-1, keepdims=True)
        weights = jnp.where(keep, jnp.exp(scores - peak), 0.0)
        total = jnp.sum(weights, axis=-1, keepdims=True)
        probs = (weights / total).astype(jnp.bfloat16)
        mixed = jnp.einsum(
            "kgrs,skd->rkgd", probs, values[:stop], preferred_element_type=jnp.float32
        )
        outputs.append(mixed.astype(jnp.bfloat16))
        totals.append(peak + jnp.log(total))
    return (jnp.concatenate(outputs, 0), jnp.concatenate(totals, 2))


def attend_backward(queries, keys, values, sums, grads, masks):
    block = min(512, queries.shape[0])
    key_grads = jnp.zeros(keys.shape, jnp.float32)
    value_grads = jnp.zeros(values.shape, jnp.float32)
    diagonal = jnp.zeros(sums.shape[:3], jnp.float32)
    query_grads = []
    for index in range(queries.shape[0] // block):
        start = index * block
        extra, keep, stop = masks(start, block)
        rows = queries[start : start + block]
        grad_rows = grads[start : start + block]
        scores = jnp.einsum("rkgd,skd->kgrs", rows, keys[:stop], preferred_element_type=jnp.float32)
        if extra is not None:
            scores = scores + extra
        scores = jnp.where(keep, scores, NEG)
        probs = jnp.where(keep, jnp.exp(scores - sums[:, :, start : start + block]), 0.0)
        value_grads = value_grads.at[:stop].add(
            jnp.einsum(
                "kgrs,rkgd->skd",
                probs.astype(jnp.bfloat16),
                grad_rows,
                preferred_element_type=jnp.float32,
            )
        )
        dprobs = jnp.einsum(
            "rkgd,skd->kgrs", grad_rows, values[:stop], preferred_element_type=jnp.float32
        )
        delta = jnp.sum(probs * dprobs, axis=-1, keepdims=True)
        dscores = (probs * (dprobs - delta)).astype(jnp.bfloat16)
        query_grads.append(
            jnp.einsum(
                "kgrs,skd->rkgd", dscores, keys[:stop], preferred_element_type=jnp.float32
            ).astype(jnp.bfloat16)
        )
        key_grads = key_grads.at[:stop].add(
            jnp.einsum("kgrs,rkgd->skd", dscores, rows, preferred_element_type=jnp.float32)
        )
        if extra is not None:
            diagonal = diagonal.at[:, :, :stop].add(
                diagonal_sums(dscores.astype(jnp.float32), block, stop)
            )
    return (
        jnp.concatenate(query_grads, 0),
        key_grads.astype(jnp.bfloat16),
        value_grads.astype(jnp.bfloat16),
        diagonal,
    )


def self_forward(queries, keys, values, length, table):
    return attend_forward(queries, keys, values, causal_masks(table, length, queries.shape[2]))


def self_backward(queries, keys, values, sums, grads, length, table):
    return attend_backward(
        queries, keys, values, sums, grads, causal_masks(table, length, queries.shape[2])
    )


def cross_forward(queries, keys, values, length):
    return attend_forward(queries, keys, values, memory_masks(length, keys.shape[0]))


def cross_backward(queries, keys, values, sums, grads, length):
    return attend_backward(queries, keys, values, sums, grads, memory_masks(length, keys.shape[0]))


def to_tokens(values):
    return lax.all_to_all(shortened(values), "seq", split_axis=1, concat_axis=2, tiled=True).astype(
        values.dtype
    )


def to_heads(grads):
    return lax.all_to_all(grads, "seq", split_axis=2, concat_axis=1, tiled=True)


def per_device(
    layer_input,
    memory,
    target_lengths,
    memory_lengths,
    buckets,
    norm_self,
    self_q,
    self_k,
    self_v,
    self_out,
    rel_bias,
    norm_cross,
    cross_q,
    cross_k,
    cross_v,
    cross_out,
    norm_ff,
    ff_gate,
    ff_up,
    ff_down,
    cotangent,
):
    micro_count, batch_rows, local_tokens, model_width = layer_input.shape
    memory_tokens = memory.shape[2]
    group = HEADS // KV_HEADS
    replicas = lax.axis_size("dp")
    shards = (
        norm_self,
        self_q,
        self_k,
        self_v,
        self_out,
        rel_bias,
        norm_cross,
        cross_q,
        cross_k,
        cross_v,
        cross_out,
        norm_ff,
        ff_gate,
        ff_up,
        ff_down,
    )
    totals = [
        jnp.zeros((piece.shape[0] * replicas,) + piece.shape[1:], jnp.float32) for piece in shards
    ]
    onehot = (buckets[:, None] == jnp.arange(BUCKETS, dtype=jnp.int32)[None, :]).astype(jnp.float32)
    places = lax.axis_index("seq") * local_tokens + jnp.arange(local_tokens, dtype=jnp.int32)
    diagonal = jnp.zeros((rel_bias.shape[1] // group, group, TGT), jnp.float32)
    outputs = []
    input_grads = []
    memory_grads = []
    for micro_step in range(micro_count):
        gathered = (
            lax.all_gather(norm_self, "dp", axis=0, tiled=True),
            lax.all_gather(self_q, "dp", axis=0, tiled=True),
            lax.all_gather(self_k, "dp", axis=0, tiled=True),
            lax.all_gather(self_v, "dp", axis=0, tiled=True),
            lax.all_gather(self_out, "dp", axis=0, tiled=True),
            lax.all_gather(rel_bias, "dp", axis=0, tiled=True),
            lax.all_gather(norm_cross, "dp", axis=0, tiled=True),
            lax.all_gather(cross_q, "dp", axis=0, tiled=True),
            lax.all_gather(cross_k, "dp", axis=0, tiled=True),
            lax.all_gather(cross_v, "dp", axis=0, tiled=True),
            lax.all_gather(cross_out, "dp", axis=0, tiled=True),
            lax.all_gather(norm_ff, "dp", axis=0, tiled=True),
            lax.all_gather(ff_gate, "dp", axis=0, tiled=True),
            lax.all_gather(ff_up, "dp", axis=0, tiled=True),
            lax.all_gather(ff_down, "dp", axis=0, tiled=True),
        )
        (
            gain_self,
            query_self,
            key_self,
            value_self,
            output_self,
            bias_whole,
            gain_cross,
            query_cross,
            key_cross,
            value_cross,
            output_cross,
            gain_ff,
            gate_weight,
            up_weight,
            down_weight,
        ) = gathered
        gain_self = gain_self.astype(jnp.float32)
        gain_cross = gain_cross.astype(jnp.float32)
        gain_ff = gain_ff.astype(jnp.float32)
        table = lax.dot_general(
            bias_whole.astype(jnp.float32), onehot, (((0,), (1,)), ((), ())), precision=HIGH
        )
        lengths = target_lengths[micro_step]
        spans = memory_lengths[micro_step]
        valid = (places[None, :] < lengths[:, None]).astype(jnp.float32).reshape(-1, 1)
        hidden = layer_input[micro_step].reshape(-1, model_width).astype(jnp.float32)
        normed_self = rms_norm(hidden, gain_self).astype(jnp.bfloat16)
        queries = (
            project(normed_self, query_self)
            .astype(jnp.bfloat16)
            .reshape(batch_rows, local_tokens, -1)
        )
        keys = (
            project(normed_self, key_self)
            .astype(jnp.bfloat16)
            .reshape(batch_rows, local_tokens, -1)
        )
        values = (
            project(normed_self, value_self)
            .astype(jnp.bfloat16)
            .reshape(batch_rows, local_tokens, -1)
        )
        encoded = memory[micro_step].reshape(-1, model_width)
        memory_keys = (
            project(encoded, key_cross).astype(jnp.bfloat16).reshape(batch_rows, memory_tokens, -1)
        )
        memory_values = (
            project(encoded, value_cross)
            .astype(jnp.bfloat16)
            .reshape(batch_rows, memory_tokens, -1)
        )
        head_queries, head_keys, head_values, far_keys, far_values = (
            lax.all_to_all(queries, "seq", split_axis=2, concat_axis=1, tiled=True),
            lax.all_to_all(keys, "seq", split_axis=2, concat_axis=1, tiled=True),
            lax.all_to_all(values, "seq", split_axis=2, concat_axis=1, tiled=True),
            lax.all_to_all(memory_keys, "seq", split_axis=2, concat_axis=1, tiled=True),
            lax.all_to_all(memory_values, "seq", split_axis=2, concat_axis=1, tiled=True),
        )
        self_queries = split_heads(head_queries, group)
        self_keys = split_shared(head_keys)
        self_values = split_shared(head_values)
        far_keys = split_shared(far_keys)
        far_values = split_shared(far_values)
        attended, self_sums = jax.vmap(self_forward, in_axes=(0, 0, 0, 0, None))(
            self_queries, self_keys, self_values, lengths, table
        )
        context = to_tokens(attended.reshape(batch_rows, TGT, -1)).reshape(
            batch_rows * local_tokens, -1
        )
        first = hidden + project(context, output_self)
        normed_cross = rms_norm(first, gain_cross).astype(jnp.bfloat16)
        cross_queries = (
            project(normed_cross, query_cross)
            .astype(jnp.bfloat16)
            .reshape(batch_rows, local_tokens, -1)
        )
        cross_heads = split_heads(
            lax.all_to_all(cross_queries, "seq", split_axis=2, concat_axis=1, tiled=True), group
        )
        cross_attended, cross_sums = jax.vmap(cross_forward)(
            cross_heads, far_keys, far_values, spans
        )
        cross_context = to_tokens(cross_attended.reshape(batch_rows, TGT, -1)).reshape(
            batch_rows * local_tokens, -1
        )
        second = first + project(cross_context, output_cross)
        normed_ff = rms_norm(second, gain_ff).astype(jnp.bfloat16)
        gate = project(normed_ff, gate_weight)
        upward = project(normed_ff, up_weight)
        middle = gated(gate, upward).astype(jnp.bfloat16)
        third = second + project(middle, down_weight)
        outputs.append(
            (third * valid).astype(jnp.bfloat16).reshape(batch_rows, local_tokens, model_width)
        )
        upstream = cotangent[micro_step].reshape(-1, model_width).astype(jnp.float32) * valid
        down_grad = upstream.astype(jnp.bfloat16)
        totals[14] = totals[14] + weight_grad(middle, down_grad)
        _, pullback = jax.vjp(gated, gate, upward)
        gate_grad, upward_grad = pullback(project_back(down_grad, down_weight))
        gate_grad = gate_grad.astype(jnp.bfloat16)
        upward_grad = upward_grad.astype(jnp.bfloat16)
        totals[12] = totals[12] + weight_grad(normed_ff, gate_grad)
        totals[13] = totals[13] + weight_grad(normed_ff, upward_grad)
        _, pullback = jax.vjp(rms_norm, second, gain_ff)
        second_grad, gain_grad = pullback(
            project_back(gate_grad, gate_weight) + project_back(upward_grad, up_weight)
        )
        totals[11] = totals[11] + gain_grad
        second_grad = second_grad + upstream
        cross_grad = second_grad.astype(jnp.bfloat16)
        totals[10] = totals[10] + weight_grad(cross_context, cross_grad)
        context_grad = (
            project_back(cross_grad, output_cross)
            .astype(jnp.bfloat16)
            .reshape(batch_rows, local_tokens, -1)
        )
        cross_query_grad, far_key_grad, far_value_grad, _ = jax.vmap(cross_backward)(
            cross_heads,
            far_keys,
            far_values,
            cross_sums,
            split_heads(to_heads(context_grad), group),
            spans,
        )
        query_back, key_back, value_back = (
            lax.all_to_all(
                shortened(cross_query_grad.reshape(batch_rows, TGT, -1)),
                "seq",
                split_axis=1,
                concat_axis=2,
                tiled=True,
            ),
            lax.all_to_all(
                shortened(far_key_grad.reshape(batch_rows, MEM, -1)),
                "seq",
                split_axis=1,
                concat_axis=2,
                tiled=True,
            ),
            lax.all_to_all(
                shortened(far_value_grad.reshape(batch_rows, MEM, -1)),
                "seq",
                split_axis=1,
                concat_axis=2,
                tiled=True,
            ),
        )
        query_back = query_back.reshape(batch_rows * local_tokens, -1)
        key_back = key_back.reshape(batch_rows * memory_tokens, -1)
        value_back = value_back.reshape(batch_rows * memory_tokens, -1)
        totals[7] = totals[7] + weight_grad(normed_cross, query_back)
        totals[8] = totals[8] + weight_grad(encoded, key_back)
        totals[9] = totals[9] + weight_grad(encoded, value_back)
        memory_grads.append(
            (project_back(key_back, key_cross) + project_back(value_back, value_cross)).reshape(
                batch_rows, memory_tokens, model_width
            )
        )
        _, pullback = jax.vjp(rms_norm, first, gain_cross)
        first_grad, gain_grad = pullback(project_back(query_back, query_cross))
        totals[6] = totals[6] + gain_grad
        first_grad = first_grad + second_grad
        self_grad = first_grad.astype(jnp.bfloat16)
        totals[4] = totals[4] + weight_grad(context, self_grad)
        context_grad = (
            project_back(self_grad, output_self)
            .astype(jnp.bfloat16)
            .reshape(batch_rows, local_tokens, -1)
        )
        query_grad, key_grad, value_grad, bias_grad = jax.vmap(
            self_backward, in_axes=(0, 0, 0, 0, 0, 0, None)
        )(
            self_queries,
            self_keys,
            self_values,
            self_sums,
            split_heads(to_heads(context_grad), group),
            lengths,
            table,
        )
        diagonal = diagonal + jnp.sum(bias_grad, axis=0)
        query_back, key_back, value_back = (
            lax.all_to_all(
                shortened(query_grad.reshape(batch_rows, TGT, -1)),
                "seq",
                split_axis=1,
                concat_axis=2,
                tiled=True,
            ),
            lax.all_to_all(
                shortened(key_grad.reshape(batch_rows, TGT, -1)),
                "seq",
                split_axis=1,
                concat_axis=2,
                tiled=True,
            ),
            lax.all_to_all(
                shortened(value_grad.reshape(batch_rows, TGT, -1)),
                "seq",
                split_axis=1,
                concat_axis=2,
                tiled=True,
            ),
        )
        query_back = query_back.reshape(batch_rows * local_tokens, -1)
        key_back = key_back.reshape(batch_rows * local_tokens, -1)
        value_back = value_back.reshape(batch_rows * local_tokens, -1)
        totals[1] = totals[1] + weight_grad(normed_self, query_back)
        totals[2] = totals[2] + weight_grad(normed_self, key_back)
        totals[3] = totals[3] + weight_grad(normed_self, value_back)
        _, pullback = jax.vjp(rms_norm, hidden, gain_self)
        hidden_grad, gain_grad = pullback(
            project_back(query_back, query_self)
            + project_back(key_back, key_self)
            + project_back(value_back, value_self)
        )
        totals[0] = totals[0] + gain_grad
        input_grads.append(
            (hidden_grad + first_grad).reshape(batch_rows, local_tokens, model_width)
        )
    totals[5] = lax.dot_general(
        onehot, diagonal.reshape(-1, TGT), (((0,), (1,)), ((), ())), precision=HIGH
    )
    reduced = (
        lax.psum_scatter(totals[0], ("dp", "seq"), scatter_dimension=0, tiled=True),
        lax.psum_scatter(totals[1], ("dp", "seq"), scatter_dimension=0, tiled=True),
        lax.psum_scatter(totals[2], ("dp", "seq"), scatter_dimension=0, tiled=True),
        lax.psum_scatter(totals[3], ("dp", "seq"), scatter_dimension=0, tiled=True),
        lax.psum_scatter(totals[4], ("dp", "seq"), scatter_dimension=0, tiled=True),
        lax.psum_scatter(totals[6], ("dp", "seq"), scatter_dimension=0, tiled=True),
        lax.psum_scatter(totals[7], ("dp", "seq"), scatter_dimension=0, tiled=True),
        lax.psum_scatter(totals[8], ("dp", "seq"), scatter_dimension=0, tiled=True),
        lax.psum_scatter(totals[9], ("dp", "seq"), scatter_dimension=0, tiled=True),
        lax.psum_scatter(totals[10], ("dp", "seq"), scatter_dimension=0, tiled=True),
        lax.psum_scatter(totals[11], ("dp", "seq"), scatter_dimension=0, tiled=True),
        lax.psum_scatter(totals[12], ("dp", "seq"), scatter_dimension=0, tiled=True),
        lax.psum_scatter(totals[13], ("dp", "seq"), scatter_dimension=0, tiled=True),
        lax.psum_scatter(totals[14], ("dp", "seq"), scatter_dimension=0, tiled=True),
    )
    bias_share = lax.psum_scatter(totals[5], "dp", scatter_dimension=0, tiled=True)
    return (
        jnp.stack(outputs),
        jnp.stack(input_grads),
        jnp.stack(memory_grads),
        reduced[0],
        reduced[1],
        reduced[2],
        reduced[3],
        reduced[4],
        bias_share,
        reduced[5],
        reduced[6],
        reduced[7],
        reduced[8],
        reduced[9],
        reduced[10],
        reduced[11],
        reduced[12],
        reduced[13],
    )


def row_pieces(full):
    blocks = full.reshape(full.shape[0], -1, QB)
    return jnp.concatenate([blocks[:, 1:], blocks[:, :-1]], axis=2)


def seed_rows(vectors):
    return jnp.stack([jnp.roll(vectors, r, axis=-1) for r in range(8)], axis=-2)


def spread(seed):
    rows = 8
    tile = seed
    while rows < QB:
        tile = jnp.concatenate([tile, pltpu.roll(tile, rows, 1)], axis=0)
        rows *= 2
    return tile[:, :QB]


def fold(tile):
    width = 2 * QB
    tile = jnp.concatenate([tile, jnp.zeros_like(tile)], axis=1)
    rows = QB
    while rows > 8:
        rows //= 2
        tile = tile[:rows] + pltpu.roll(tile[rows:], width - rows, 1)
    return tile


def nt(left, right):
    return lax.dot_general(left, right, (((1,), (1,)), ((), ())), preferred_element_type=jnp.float32)


def tn(left, right):
    return lax.dot_general(left, right, (((0,), (0,)), ((), ())), preferred_element_type=jnp.float32)


def nn(left, right):
    return lax.dot_general(left, right, (((1,), (0,)), ((), ())), preferred_element_type=jnp.float32)


def forward_kernel(causal, q_ref, k_ref, v_ref, keep_ref, *rest):
    if causal:
        seed_ref, o_ref, lse_ref, bias = rest
    else:
        o_ref, lse_ref = rest
    span = k_ref.shape[0]
    for kv in range(2):
        lanes = slice(kv * HEAD_DIM, (kv + 1) * HEAD_DIM)
        keys = k_ref[:, lanes]
        values = v_ref[:, lanes]
        if causal:
            for member in range(2):
                for offset in range(4):
                    bias[member * QB : (member + 1) * QB, (3 - offset) * QB : (4 - offset) * QB] = spread(
                        seed_ref[2 * kv + member, offset]
                    )
        for block in range(q_ref.shape[0] // QB):
            stop = (block + 1) * QB if causal else span
            rows = slice(block * QB, (block + 1) * QB)
            both = q_ref[rows, 2 * kv * HEAD_DIM : 2 * (kv + 1) * HEAD_DIM]
            query = jnp.concatenate([both[:, :HEAD_DIM], both[:, HEAD_DIM:]], axis=0)
            scores = nt(query, keys[:stop]) + keep_ref[:, :stop]
            if causal:
                scores = scores + bias[:, (3 - block) * QB : (3 - block) * QB + stop]
            peak = jnp.max(scores, axis=1, keepdims=True)
            weights = jnp.exp(scores - peak)
            total = jnp.sum(weights, axis=1, keepdims=True)
            mixed = nn(weights.astype(jnp.bfloat16), values[:stop]) / total
            o_ref[rows, 2 * kv * HEAD_DIM : 2 * (kv + 1) * HEAD_DIM] = jnp.concatenate(
                [mixed[:QB], mixed[QB:]], axis=1
            ).astype(jnp.bfloat16)
            sums = jnp.broadcast_to(peak + jnp.log(total), (2 * QB, 128)).T
            lse_ref[2 * kv : 2 * kv + 1, rows] = sums[:1, :QB]
            lse_ref[2 * kv + 1 : 2 * kv + 2, rows] = sums[:1, QB:]


def backward_kernel(causal, q_ref, k_ref, v_ref, o_ref, do_ref, lse_ref, keep_ref, *rest):
    if causal:
        seed_ref, dq_ref, dk_ref, dv_ref, diag_ref, bias, sums, dk_sum, dv_sum = rest
    else:
        dq_ref, dk_ref, dv_ref, dk_sum, dv_sum = rest
    span = k_ref.shape[0]
    blocks = q_ref.shape[0] // QB
    for kv in range(2):
        lanes = slice(kv * HEAD_DIM, (kv + 1) * HEAD_DIM)
        dk_sum[...] = jnp.zeros_like(dk_sum)
        dv_sum[...] = jnp.zeros_like(dv_sum)
        if causal:
            for member in range(2):
                for offset in range(4):
                    bias[offset, :, member * QB : (member + 1) * QB] = spread(
                        seed_ref[2 * kv + member, offset]
                    )
            sums[...] = jnp.zeros_like(sums)
        for block in range(blocks):
            rows = slice(block * QB, (block + 1) * QB)
            both = slice(2 * kv * HEAD_DIM, 2 * (kv + 1) * HEAD_DIM)
            pair = q_ref[rows, both]
            query = jnp.concatenate([pair[:, :HEAD_DIM], pair[:, HEAD_DIM:]], axis=0)
            upstream = do_ref[rows, both]
            grads = jnp.concatenate([upstream[:, :HEAD_DIM], upstream[:, HEAD_DIM:]], axis=0)
            inner = (upstream.astype(jnp.float32) * o_ref[rows, both].astype(jnp.float32)).T
            delta = jnp.concatenate(
                [
                    jnp.sum(inner[:HEAD_DIM], axis=0, keepdims=True),
                    jnp.sum(inner[HEAD_DIM:], axis=0, keepdims=True),
                ],
                axis=1,
            )
            level = jnp.concatenate(
                [lse_ref[2 * kv : 2 * kv + 1, rows], lse_ref[2 * kv + 1 : 2 * kv + 2, rows]], axis=1
            )
            dq = jnp.zeros((2 * QB, HEAD_DIM), jnp.float32)
            for part in range(block + 1 if causal else span // QB):
                columns = slice(part * QB, (part + 1) * QB)
                keys = k_ref[columns, lanes]
                values = v_ref[columns, lanes]
                scores = nt(keys, query) + keep_ref[columns]
                if causal:
                    scores = scores + bias[block - part]
                probs = jnp.exp(scores - level)
                dscores = probs * (nt(values, grads) - delta)
                if causal:
                    sums[block - part] += dscores
                dscores = dscores.astype(jnp.bfloat16)
                dv_sum[columns] += nn(probs.astype(jnp.bfloat16), grads)
                dk_sum[columns] += nn(dscores, query)
                dq += tn(dscores, keys)
            dq_ref[rows, both] = jnp.concatenate([dq[:QB], dq[QB:]], axis=1).astype(jnp.bfloat16)
        dk_ref[:, lanes] = dk_sum[...].astype(jnp.bfloat16)
        dv_ref[:, lanes] = dv_sum[...].astype(jnp.bfloat16)
        if causal:
            for member in range(2):
                for offset in range(4):
                    diag_ref[2 * kv + member, offset] = fold(
                        sums[offset, :, member * QB : (member + 1) * QB]
                    )


PARAMS = pltpu.CompilerParams(vmem_limit_bytes=56 * 2**20)


def attention_forward(queries, kv, keep, seeds=None):
    tokens, width = queries.shape
    span = kv.shape[0]
    heads = width // HEAD_DIM
    causal = seeds is not None
    in_specs = [
        pl.BlockSpec((tokens, 256), lambda i: (0, i)),
        pl.BlockSpec((span, 128), lambda i: (0, i)),
        pl.BlockSpec((span, 128), lambda i: (0, i + 2)),
        pl.BlockSpec((1, span), lambda i: (0, 0)),
    ]
    operands = [queries, kv, kv, keep.reshape(1, span)]
    scratch = []
    if causal:
        in_specs.append(pl.BlockSpec((4, 4, 8, 512), lambda i: (i, 0, 0, 0)))
        operands.append(seeds)
        scratch.append(pltpu.VMEM((2 * QB, 4 * QB), jnp.float32))
    work = heads * tokens * span // (2 if causal else 1)
    context, sums = pl.pallas_call(
        functools.partial(forward_kernel, causal),
        grid=(heads // 4,),
        in_specs=in_specs,
        out_specs=[
            pl.BlockSpec((tokens, 256), lambda i: (0, i)),
            pl.BlockSpec((None, 4, tokens), lambda i: (i, 0, 0)),
        ],
        out_shape=[
            jax.ShapeDtypeStruct((tokens, width), jnp.bfloat16),
            jax.ShapeDtypeStruct((heads // 4, 4, tokens), jnp.float32),
        ],
        scratch_shapes=scratch,
        compiler_params=PARAMS,
        cost_estimate=pl.CostEstimate(
            flops=work * 4 * 4 * HEAD_DIM, bytes_accessed=4 * 2**20, transcendentals=work
        ),
    )(*operands)
    return context, sums


def attention_backward(queries, kv, context, grads, sums, keep, seeds=None):
    tokens, width = queries.shape
    span = kv.shape[0]
    heads = width // HEAD_DIM
    causal = seeds is not None
    wide = pl.BlockSpec((tokens, 256), lambda i: (0, i))
    narrow = pl.BlockSpec((span, 128), lambda i: (0, i))
    in_specs = [
        wide,
        narrow,
        pl.BlockSpec((span, 128), lambda i: (0, i + 2)),
        wide,
        wide,
        pl.BlockSpec((None, 4, tokens), lambda i: (i, 0, 0)),
        pl.BlockSpec((span, 1), lambda i: (0, 0)),
    ]
    operands = [queries, kv, kv, context, grads, sums, keep.reshape(span, 1)]
    out_specs = [wide, narrow, narrow]
    out_shape = [
        jax.ShapeDtypeStruct((tokens, width), jnp.bfloat16),
        jax.ShapeDtypeStruct((span, width // 2), jnp.bfloat16),
        jax.ShapeDtypeStruct((span, width // 2), jnp.bfloat16),
    ]
    scratch = []
    if causal:
        quad = pl.BlockSpec((4, 4, 8, 512), lambda i: (i, 0, 0, 0))
        in_specs.append(quad)
        operands.append(seeds)
        out_specs.append(quad)
        out_shape.append(jax.ShapeDtypeStruct((heads, 4, 8, 512), jnp.float32))
        scratch = [pltpu.VMEM((4, QB, 2 * QB), jnp.float32), pltpu.VMEM((4, QB, 2 * QB), jnp.float32)]
    scratch += [pltpu.VMEM((span, HEAD_DIM), jnp.float32), pltpu.VMEM((span, HEAD_DIM), jnp.float32)]
    work = heads * tokens * span // (2 if causal else 1)
    return pl.pallas_call(
        functools.partial(backward_kernel, causal),
        grid=(heads // 4,),
        in_specs=in_specs,
        out_specs=out_specs,
        out_shape=out_shape,
        scratch_shapes=scratch,
        compiler_params=PARAMS,
        cost_estimate=pl.CostEstimate(
            flops=work * 10 * 4 * HEAD_DIM, bytes_accessed=8 * 2**20, transcendentals=work
        ),
    )(*operands)


def inverse_rms(value):
    return lax.rsqrt(jnp.mean(value * value, axis=-1, keepdims=True) + EPS)


def rms_back(value, gain, upstream):
    inverse = inverse_rms(value)
    scaled = upstream * gain
    mean = jnp.mean(value * scaled, axis=-1, keepdims=True)
    return inverse * scaled - value * (inverse * inverse * inverse) * mean, upstream * value * inverse


def pick(array, index, axis=0):
    return lax.dynamic_index_in_dim(array, index, axis, keepdims=False)


class Plane:
    def __init__(self, dp, seq):
        self.depth = dp // 2
        self.seq = seq
        place = lax.axis_index("dp")
        self.z, self.core = place // 2, place % 2
        self.corner = lax.axis_index("seq")
        self.y, self.x = self.corner // 2, self.corner % 2

    def move(self, array, where):
        pairs = []
        for z in range(self.depth):
            for core in range(2):
                for y in range(2):
                    for x in range(2):
                        z2, core2, y2, x2 = where(z, core, y, x)
                        source = (z * 2 + core) * self.seq + y * 2 + x
                        target = (z2 * 2 + core2) * self.seq + y2 * 2 + x2
                        pairs.append((source, target))
        return lax.ppermute(array, ("dp", "seq"), pairs)

    def swap_core(self, array):
        return self.move(array, lambda z, c, y, x: (z, 1 - c, y, x))

    def swap_x(self, array):
        return self.move(array, lambda z, c, y, x: (z, c, y, 1 - x))

    def swap_y(self, array):
        return self.move(array, lambda z, c, y, x: (z, c, 1 - y, x))

    def shift_z(self, array, step):
        return self.move(array, lambda z, c, y, x: ((z + step) % self.depth, c, y, x))

    def collect(self, parcel):
        received = []
        for up in range(2):
            for across in range(2):
                piece = parcel.reshape((4,) + parcel.shape[2:])
                piece = pick(piece, (self.x ^ across) * 2 + (self.y ^ up))
                received.append(
                    self.move(piece, lambda z, c, y, x, up=up, across=across: (z, y ^ up, x ^ across, c))
                )
        mine = jnp.stack(received)
        both = jnp.concatenate([mine, self.swap_core(mine)])
        pieces = []
        for block in range(4):
            for half in range(2):
                index = 2 * (half ^ (block >> 1)) + (self.y ^ (block & 1))
                pieces.append(pick(both, index + jnp.where(half == self.core, 0, 4)))
        return jnp.stack(pieces).reshape((4, 2) + parcel.shape[2:])

    def deliver(self, pieces):
        received = []
        for up in range(2):
            for across in range(2):
                piece = pick(pieces, 2 * (self.core ^ up) + (self.y ^ across))
                received.append(
                    self.move(piece, lambda z, k, Y, X, up=up, across=across: (z, X, k ^ up, Y ^ across))
                )
        stacked = jnp.stack(received)
        homes = []
        for micro in range(2):
            for half in range(2):
                homes.append(pick(stacked, 2 * (self.y ^ half) + (self.x ^ micro)))
        return jnp.stack(homes).reshape((2, 2) + pieces.shape[1:])

    def gather(self, shard):
        quarter = pick(shard, self.corner, 2)
        others = jnp.stack([self.shift_z(quarter, step) for step in range(1, self.depth)])
        beside = self.swap_x(others)
        below = self.swap_y(others)
        middle = shard.shape[0]
        near = self.swap_y(beside[..., : shard.shape[3] // 2, :])
        far = self.swap_x(below[..., shard.shape[3] // 2 :, :])
        diagonal = jnp.concatenate([near, far], axis=-2)
        pieces = jnp.stack([others, beside, below, diagonal])
        wholes = []
        for matrix in range(middle):
            blocks = []
            for z in range(self.depth):
                step = (self.z - z + self.depth) % self.depth
                for part in range(4):
                    away = pick(pick(pieces[:, :, matrix], self.corner ^ part), jnp.maximum(step - 1, 0))
                    blocks.append(jnp.where(step == 0, shard[matrix, :, part], away))
            whole = jnp.stack(blocks).reshape((self.depth, 4) + shard.shape[1:2] + shard.shape[3:])
            whole = jnp.swapaxes(whole, 1, 2)
            wholes.append(whole.reshape(-1, shard.shape[-1]))
        return wholes

    def scatter(self, wholes, lanes):
        shape = (self.depth, lanes, 2, 2, wholes[0].shape[0] // (self.depth * lanes * 4), wholes[0].shape[1])
        grads = jnp.stack([whole.reshape(shape) for whole in wholes])
        half = self.depth // 2
        low, high = grads[:, :half], grads[:, half:]
        wide = lambda a: a.astype(jnp.float32)
        low_got = self.swap_x(pick(low, 1 - self.x, 4))
        high_got = self.swap_y(pick(high, 1 - self.y, 3))
        low = (wide(pick(low, self.x, 4)) + wide(low_got)).astype(jnp.bfloat16)
        high = (wide(pick(high, self.y, 3)) + wide(high_got)).astype(jnp.bfloat16)
        low_got = self.swap_y(pick(low, 1 - self.y, 3))
        high_got = self.swap_x(pick(high, 1 - self.x, 3))
        low = (wide(pick(low, self.y, 3)) + wide(low_got)).astype(jnp.bfloat16)
        high = (wide(pick(high, self.x, 3)) + wide(high_got)).astype(jnp.bfloat16)
        column = jnp.concatenate([low, high], axis=1)
        total = wide(pick(column, self.z, 1))
        for step in range(1, self.depth):
            total = total + wide(self.shift_z(pick(column, (self.z + step) % self.depth, 1), step))
        return total


def parity_columns(weight, core):
    rows, columns = weight.shape
    return pick(weight.reshape(rows, 4, 2, columns // 8), core, 2).reshape(rows, columns // 2)


def per_chip(
    layer_input,
    memory,
    target_lengths,
    memory_lengths,
    buckets,
    norm_self,
    self_q,
    self_k,
    self_v,
    self_out,
    rel_bias,
    norm_cross,
    cross_q,
    cross_k,
    cross_v,
    cross_out,
    norm_ff,
    ff_gate,
    ff_up,
    ff_down,
    cotangent,
):
    bf16, f32 = jnp.bfloat16, jnp.float32
    plane = Plane(lax.axis_size("dp"), lax.axis_size("seq"))
    core = plane.core
    width = layer_input.shape[3]
    local = layer_input.shape[2]
    near = memory.shape[2]

    small = jnp.concatenate(
        [norm_self, norm_cross, norm_ff, rel_bias.reshape(-1), jnp.zeros((112,), bf16)]
    )
    small = lax.all_gather(small, ("dp", "seq"), axis=0, tiled=False)
    small = small.reshape(-1, 4, 512).astype(f32)
    shard = norm_self.shape[0]
    gain_self, gain_cross, gain_ff = (
        small[:, 0, i * shard : (i + 1) * shard].reshape(-1) for i in range(3)
    )
    bias = small[:, :, 3 * shard : 3 * shard + 16].reshape(-1, 4, 4, 4)
    bias = jnp.swapaxes(bias, 1, 2).reshape(BUCKETS, HEADS)
    bias = pick(bias.reshape(BUCKETS, 4, 2, 2), core, 2).reshape(BUCKETS, -1)
    onehot = (buckets[:, None] == jnp.arange(BUCKETS, dtype=jnp.int32)[None, :]).astype(f32)
    table = lax.dot_general(bias, onehot, (((0,), (1,)), ((), ())), precision=HIGH)
    full = jnp.concatenate([jnp.full((table.shape[0], QB), NEG, f32), table], axis=1)
    vectors = row_pieces(full)
    seeds_back = seed_rows(vectors)
    seeds_fore = seed_rows(jnp.roll(vectors[..., ::-1], 1, axis=-1))

    parcel = jnp.concatenate(
        [
            layer_input.reshape(2, 2, local // 2, width),
            cotangent.reshape(2, 2, local // 2, width),
            memory.reshape(2, 2, near // 2, width),
        ],
        axis=2,
    )
    everything = plane.collect(parcel)
    inputs = everything[:, :, : local // 2].reshape(-1, width)
    upstream = everything[:, :, local // 2 : local].reshape(-1, width)
    encoded = everything[:, :, local:].reshape(-1, width)
    both = jnp.concatenate([target_lengths, memory_lengths]).reshape(2, 2, 1)
    others = plane.swap_core(both.astype(f32)).astype(jnp.int32)
    both = jnp.where(plane.x == core, both, others)[:, :, 0]
    mine = pick(both, plane.y, 1)
    length, span = mine[0], mine[1]
    tokens = inputs.shape[0]
    positions = jnp.arange(tokens, dtype=jnp.int32)
    valid = (positions < length).astype(f32)[:, None]
    keep_self = jnp.where(positions < length, 0.0, NEG).astype(f32)
    keep_cross = jnp.where(jnp.arange(encoded.shape[0], dtype=jnp.int32) < span, 0.0, NEG).astype(f32)

    def column_shards(matrices):
        packed = [
            jnp.stack([jnp.concatenate([parity_columns(w, side) for w in group], axis=1) for group in matrices])
            for side in range(2)
        ]
        packed = jnp.stack(packed)
        got = plane.swap_core(pick(packed, 1 - core))
        own = pick(packed, core)
        ordered = jnp.stack([jnp.where(core == 0, own, got), jnp.where(core == 0, got, own)], axis=1)
        return ordered.reshape(ordered.shape[:2] + (4, -1) + ordered.shape[3:])

    def row_shards(matrices):
        packed = jnp.stack(matrices)[:, None]
        return packed.reshape(packed.shape[:2] + (4, -1) + packed.shape[3:])

    w_q, w_kv, w_ckv, w_cq = plane.gather(
        column_shards([[self_q], [self_k, self_v], [cross_k, cross_v], [cross_q]])
    )
    w_out, w_cout = plane.gather(row_shards([self_out, cross_out]))
    w_gate, w_up = plane.gather(column_shards([[ff_gate], [ff_up]]))
    (w_down,) = plane.gather(row_shards([ff_down]))

    def share(partial):
        partial = partial.astype(bf16)
        return partial.astype(f32) + plane.swap_core(partial).astype(f32)

    def share_half(partial):
        partial = partial.astype(bf16).reshape(4, 2, -1, partial.shape[-1])
        got = plane.swap_core(pick(partial, 1 - core, 1))
        return pick(partial, core, 1).astype(f32) + got.astype(f32)

    def own_half(value):
        return pick(value.reshape(4, 2, -1, value.shape[-1]), core, 1)

    hidden = inputs.astype(f32)
    normed_self = (hidden * inverse_rms(hidden) * gain_self).astype(bf16)
    queries = project(normed_self, w_q).astype(bf16)
    kv = project(normed_self, w_kv).astype(bf16)
    far_kv = project(encoded, w_ckv).astype(bf16)
    context, self_sums = attention_forward(queries, kv, keep_self, seeds_fore)
    first = hidden + share(project(context, w_out))
    normed_cross = (first * inverse_rms(first) * gain_cross).astype(bf16)
    cross_queries = project(normed_cross, w_cq).astype(bf16)
    cross_context, cross_sums = attention_forward(cross_queries, far_kv, keep_cross)
    second = first + share(project(cross_context, w_cout))
    normed_ff = (second * inverse_rms(second) * gain_ff).astype(bf16)
    gate = project(normed_ff, w_gate)
    upward = project(normed_ff, w_up)
    middle = gated(gate, upward).astype(bf16)
    third = own_half(second) + share_half(project(middle, w_down))
    output = plane.deliver((third * own_half(valid)).astype(bf16))

    top = upstream.astype(f32) * valid
    top_low = top.astype(bf16)
    _, pullback = jax.vjp(gated, gate, upward)
    gate_grad, upward_grad = pullback(project_back(top_low, w_down))
    gate_grad = gate_grad.astype(bf16)
    upward_grad = upward_grad.astype(bf16)
    g_down = weight_grad(middle, top_low).astype(bf16)
    g_gate = weight_grad(normed_ff, gate_grad).astype(bf16)
    g_up = weight_grad(normed_ff, upward_grad).astype(bf16)
    r_down = plane.scatter([g_down], 1)
    r_ff = plane.scatter([g_gate, g_up], 2)
    change, gain_ff_terms = rms_back(
        second, gain_ff, share(project_back(gate_grad, w_gate) + project_back(upward_grad, w_up))
    )
    second_grad = top + change
    cross_grad = second_grad.astype(bf16)
    g_cout = weight_grad(cross_context, cross_grad).astype(bf16)
    cross_up = project_back(cross_grad, w_cout).astype(bf16)
    dqc, dkc, dvc = attention_backward(
        cross_queries, far_kv, cross_context, cross_up, cross_sums, keep_cross
    )
    dkvc = jnp.concatenate([dkc, dvc], axis=1)
    g_cq = weight_grad(normed_cross, dqc).astype(bf16)
    g_ckv = weight_grad(encoded, dkvc).astype(bf16)
    memory_grad = plane.deliver(share_half(project_back(dkvc, w_ckv)).astype(bf16))
    change, gain_cross_terms = rms_back(first, gain_cross, share(project_back(dqc, w_cq)))
    first_grad = second_grad + change
    self_grad = first_grad.astype(bf16)
    g_out = weight_grad(context, self_grad).astype(bf16)
    self_up = project_back(self_grad, w_out).astype(bf16)
    dq, dk, dv, diagonal = attention_backward(
        queries, kv, context, self_up, self_sums, keep_self, seeds_back
    )
    dkv = jnp.concatenate([dk, dv], axis=1)
    g_q = weight_grad(normed_self, dq).astype(bf16)
    g_kv = weight_grad(normed_self, dkv).astype(bf16)
    r_rows = plane.scatter([g_out, g_cout], 1)
    r_columns = plane.scatter([g_q, g_kv, g_ckv, g_cq], 2)
    change, gain_self_terms = rms_back(
        own_half(hidden), gain_self, share_half(project_back(dq, w_q) + project_back(dkv, w_kv))
    )
    input_grad = plane.deliver((own_half(first_grad) + change).astype(bf16)).astype(f32)

    terms = [
        jnp.sum(own_half(gain_ff_terms), axis=(0, 1)),
        jnp.sum(own_half(gain_cross_terms), axis=(0, 1)),
        jnp.sum(gain_self_terms, axis=(0, 1)),
    ]
    diagonal = sum(jnp.roll(diagonal[:, :, r], -r, axis=-1) for r in range(8))
    blocks = jnp.zeros((diagonal.shape[0], 5, QB), f32)
    blocks = blocks.at[:, 1:].add(diagonal[:, :, :QB]).at[:, :4].add(diagonal[:, :, QB:])
    distances = blocks[:, 1:].reshape(-1, tokens)
    bias_terms = lax.dot_general(onehot, distances, (((0,), (1,)), ((), ())), precision=HIGH)
    bias_terms = bias_terms.reshape(BUCKETS, 4, 1, 2)
    bias_terms = jnp.concatenate(
        [jnp.where(core == 0, bias_terms, 0.0), jnp.where(core == 1, bias_terms, 0.0)], axis=2
    ).reshape(-1)
    packed = lax.psum(jnp.concatenate(terms + [bias_terms]), ("dp", "seq"))
    mine = lax.axis_index("dp") * 4 + plane.corner
    piece = width // (plane.depth * 8)
    n_ff, n_cross, n_self = (
        lax.dynamic_slice_in_dim(packed, i * width + mine * piece, piece) for i in range(3)
    )
    bias_grad = packed[3 * width :].reshape(BUCKETS, HEADS)
    bias_grad = lax.dynamic_slice(
        bias_grad, (lax.axis_index("dp") * rel_bias.shape[0], plane.corner * rel_bias.shape[1]), rel_bias.shape
    )

    def columns_home(sums):
        got = plane.swap_core(pick(sums, 1 - core, 1).astype(bf16)).astype(f32)
        own = pick(sums, core, 1)
        return jnp.where(core == 0, own, got), jnp.where(core == 0, got, own)

    def merge(even, odd):
        rows = even.shape[0]
        return jnp.stack([even.reshape(rows, 4, -1), odd.reshape(rows, 4, -1)], axis=2).reshape(rows, -1)

    even, odd = columns_home(r_columns)
    quarter = even.shape[-1] // 2
    d_q = merge(even[0], odd[0])
    d_k, d_v = (merge(even[1][:, s], odd[1][:, s]) for s in (slice(0, quarter), slice(quarter, None)))
    d_ck, d_cv = (merge(even[2][:, s], odd[2][:, s]) for s in (slice(0, quarter), slice(quarter, None)))
    d_cq = merge(even[3], odd[3])
    even, odd = columns_home(r_ff)
    d_gate, d_up = merge(even[0], odd[0]), merge(even[1], odd[1])
    return (
        output.reshape(layer_input.shape),
        input_grad.reshape(layer_input.shape),
        memory_grad.astype(f32).reshape(memory.shape),
        n_self,
        d_q,
        d_k,
        d_v,
        r_rows[0, 0],
        bias_grad,
        n_cross,
        d_cq,
        d_ck,
        d_cv,
        r_rows[1, 0],
        n_ff,
        d_gate,
        d_up,
        r_down[0, 0],
    )


def solution(mesh):
    placed = (
        P(None, "dp", "seq", None),
        P(None, "dp", "seq", None),
        P(None, "dp"),
        P(None, "dp"),
        P(),
        P("dp"),
        P("dp", None),
        P("dp", None),
        P("dp", None),
        P("dp", None),
        P("dp", "seq"),
        P("dp"),
        P("dp", None),
        P("dp", None),
        P("dp", None),
        P("dp", None),
        P("dp"),
        P("dp", None),
        P("dp", None),
        P("dp", None),
        P(None, "dp", "seq", None),
    )
    chips = mesh.shape["seq"] == 4 and mesh.shape["dp"] == HEADS // 2
    return jax.shard_map(
        per_chip if chips else per_device,
        mesh=mesh,
        in_specs=placed,
        out_specs=(
            P(None, "dp", "seq", None),
            P(None, "dp", "seq", None),
            P(None, "dp", "seq", None),
            P(("dp", "seq")),
            P(("dp", "seq"), None),
            P(("dp", "seq"), None),
            P(("dp", "seq"), None),
            P(("dp", "seq"), None),
            P("dp", "seq"),
            P(("dp", "seq")),
            P(("dp", "seq"), None),
            P(("dp", "seq"), None),
            P(("dp", "seq"), None),
            P(("dp", "seq"), None),
            P(("dp", "seq")),
            P(("dp", "seq"), None),
            P(("dp", "seq"), None),
            P(("dp", "seq"), None),
        ),
        check_vma=False,
    )
```

```python
import functools

import jax
import jax.numpy as jnp
from jax import lax
from jax.experimental import pallas as pl
from jax.experimental.pallas import tpu as pltpu
from jax.sharding import PartitionSpec as P

HEADS = 16
HEAD_DIM = 64
BUCKETS = 32
KV_HEADS = 8
TGT = 1024
MEM = 512
QB = 256


EPS = 1e-06
NEG = -1e30
HIGH = lax.Precision.HIGHEST


def shortened(shard):
    return jax.tree.map(lambda a: a.astype(jnp.bfloat16) if a.dtype == jnp.float32 else a, shard)


def rms_norm(value, gain):
    return value * lax.rsqrt(jnp.mean(value * value, axis=-1, keepdims=True) + EPS) * gain


def gated(gate, upward):
    return jax.nn.gelu(gate, approximate=True) * upward


def project(left, right):
    return jnp.dot(left, right, preferred_element_type=jnp.float32)


def project_back(grad, weight):
    return lax.dot_general(
        grad, weight, (((1,), (1,)), ((), ())), preferred_element_type=jnp.float32
    )


def weight_grad(left, right):
    return lax.dot_general(
        left, right, (((0,), (0,)), ((), ())), preferred_element_type=jnp.float32
    )


def split_heads(values, group):
    return values.reshape(values.shape[:2] + (-1, group, HEAD_DIM))


def split_shared(values):
    return values.reshape(values.shape[:2] + (-1, HEAD_DIM))


def causal_masks(table, length, group):

    def masks(start, block):
        stop = start + block
        rows = start + jnp.arange(block, dtype=jnp.int32)
        columns = jnp.arange(stop, dtype=jnp.int32)
        distance = rows[:, None] - columns[None, :]
        keep = (distance >= 0) & (columns[None, :] < length)
        extra = jnp.take(table, jnp.maximum(distance, 0), axis=1)
        return (extra.reshape((-1, group, block, stop)), keep, stop)

    return masks


def memory_masks(length, width):

    def masks(start, block):
        keep = jnp.broadcast_to(
            jnp.arange(width, dtype=jnp.int32)[None, :] < length, (block, width)
        )
        return (None, keep, width)

    return masks


def diagonal_sums(grads, block, stop):
    leading = grads.shape[:2]
    flipped = jnp.pad(grads[..., ::-1], ((0, 0), (0, 0), (0, 0), (0, block)))
    skewed = flipped.reshape(leading + (block * (stop + block),))[..., : block * (stop + block - 1)]
    skewed = skewed.reshape(leading + (block, stop + block - 1))
    return jnp.sum(skewed, axis=2)[..., block - 1 :]


def attend_forward(queries, keys, values, masks):
    block = min(512, queries.shape[0])
    outputs = []
    totals = []
    for index in range(queries.shape[0] // block):
        start = index * block
        extra, keep, stop = masks(start, block)
        rows = queries[start : start + block]
        scores = jnp.einsum("rkgd,skd->kgrs", rows, keys[:stop], preferred_element_type=jnp.float32)
        if extra is not None:
            scores = scores + extra
        scores = jnp.where(keep, scores, NEG)
        peak = jnp.max(scores, axis=-1, keepdims=True)
        weights = jnp.where(keep, jnp.exp(scores - peak), 0.0)
        total = jnp.sum(weights, axis=-1, keepdims=True)
        probs = (weights / total).astype(jnp.bfloat16)
        mixed = jnp.einsum(
            "kgrs,skd->rkgd", probs, values[:stop], preferred_element_type=jnp.float32
        )
        outputs.append(mixed.astype(jnp.bfloat16))
        totals.append(peak + jnp.log(total))
    return (jnp.concatenate(outputs, 0), jnp.concatenate(totals, 2))


def attend_backward(queries, keys, values, sums, grads, masks):
    block = min(512, queries.shape[0])
    key_grads = jnp.zeros(keys.shape, jnp.float32)
    value_grads = jnp.zeros(values.shape, jnp.float32)
    diagonal = jnp.zeros(sums.shape[:3], jnp.float32)
    query_grads = []
    for index in range(queries.shape[0] // block):
        start = index * block
        extra, keep, stop = masks(start, block)
        rows = queries[start : start + block]
        grad_rows = grads[start : start + block]
        scores = jnp.einsum("rkgd,skd->kgrs", rows, keys[:stop], preferred_element_type=jnp.float32)
        if extra is not None:
            scores = scores + extra
        scores = jnp.where(keep, scores, NEG)
        probs = jnp.where(keep, jnp.exp(scores - sums[:, :, start : start + block]), 0.0)
        value_grads = value_grads.at[:stop].add(
            jnp.einsum(
                "kgrs,rkgd->skd",
                probs.astype(jnp.bfloat16),
                grad_rows,
                preferred_element_type=jnp.float32,
            )
        )
        dprobs = jnp.einsum(
            "rkgd,skd->kgrs", grad_rows, values[:stop], preferred_element_type=jnp.float32
        )
        delta = jnp.sum(probs * dprobs, axis=-1, keepdims=True)
        dscores = (probs * (dprobs - delta)).astype(jnp.bfloat16)
        query_grads.append(
            jnp.einsum(
                "kgrs,skd->rkgd", dscores, keys[:stop], preferred_element_type=jnp.float32
            ).astype(jnp.bfloat16)
        )
        key_grads = key_grads.at[:stop].add(
            jnp.einsum("kgrs,rkgd->skd", dscores, rows, preferred_element_type=jnp.float32)
        )
        if extra is not None:
            diagonal = diagonal.at[:, :, :stop].add(
                diagonal_sums(dscores.astype(jnp.float32), block, stop)
            )
    return (
        jnp.concatenate(query_grads, 0),
        key_grads.astype(jnp.bfloat16),
        value_grads.astype(jnp.bfloat16),
        diagonal,
    )


def self_forward(queries, keys, values, length, table):
    return attend_forward(queries, keys, values, causal_masks(table, length, queries.shape[2]))


def self_backward(queries, keys, values, sums, grads, length, table):
    return attend_backward(
        queries, keys, values, sums, grads, causal_masks(table, length, queries.shape[2])
    )


def cross_forward(queries, keys, values, length):
    return attend_forward(queries, keys, values, memory_masks(length, keys.shape[0]))


def cross_backward(queries, keys, values, sums, grads, length):
    return attend_backward(queries, keys, values, sums, grads, memory_masks(length, keys.shape[0]))


def to_tokens(values):
    return lax.all_to_all(shortened(values), "seq", split_axis=1, concat_axis=2, tiled=True).astype(
        values.dtype
    )


def to_heads(grads):
    return lax.all_to_all(grads, "seq", split_axis=2, concat_axis=1, tiled=True)


def per_device(
    layer_input,
    memory,
    target_lengths,
    memory_lengths,
    buckets,
    norm_self,
    self_q,
    self_k,
    self_v,
    self_out,
    rel_bias,
    norm_cross,
    cross_q,
    cross_k,
    cross_v,
    cross_out,
    norm_ff,
    ff_gate,
    ff_up,
    ff_down,
    cotangent,
):
    micro_count, batch_rows, local_tokens, model_width = layer_input.shape
    memory_tokens = memory.shape[2]
    group = HEADS // KV_HEADS
    replicas = lax.axis_size("dp")
    shards = (
        norm_self,
        self_q,
        self_k,
        self_v,
        self_out,
        rel_bias,
        norm_cross,
        cross_q,
        cross_k,
        cross_v,
        cross_out,
        norm_ff,
        ff_gate,
        ff_up,
        ff_down,
    )
    totals = [
        jnp.zeros((piece.shape[0] * replicas,) + piece.shape[1:], jnp.float32) for piece in shards
    ]
    onehot = (buckets[:, None] == jnp.arange(BUCKETS, dtype=jnp.int32)[None, :]).astype(jnp.float32)
    places = lax.axis_index("seq") * local_tokens + jnp.arange(local_tokens, dtype=jnp.int32)
    diagonal = jnp.zeros((rel_bias.shape[1] // group, group, TGT), jnp.float32)
    outputs = []
    input_grads = []
    memory_grads = []
    for micro_step in range(micro_count):
        gathered = (
            lax.all_gather(norm_self, "dp", axis=0, tiled=True),
            lax.all_gather(self_q, "dp", axis=0, tiled=True),
            lax.all_gather(self_k, "dp", axis=0, tiled=True),
            lax.all_gather(self_v, "dp", axis=0, tiled=True),
            lax.all_gather(self_out, "dp", axis=0, tiled=True),
            lax.all_gather(rel_bias, "dp", axis=0, tiled=True),
            lax.all_gather(norm_cross, "dp", axis=0, tiled=True),
            lax.all_gather(cross_q, "dp", axis=0, tiled=True),
            lax.all_gather(cross_k, "dp", axis=0, tiled=True),
            lax.all_gather(cross_v, "dp", axis=0, tiled=True),
            lax.all_gather(cross_out, "dp", axis=0, tiled=True),
            lax.all_gather(norm_ff, "dp", axis=0, tiled=True),
            lax.all_gather(ff_gate, "dp", axis=0, tiled=True),
            lax.all_gather(ff_up, "dp", axis=0, tiled=True),
            lax.all_gather(ff_down, "dp", axis=0, tiled=True),
        )
        (
            gain_self,
            query_self,
            key_self,
            value_self,
            output_self,
            bias_whole,
            gain_cross,
            query_cross,
            key_cross,
            value_cross,
            output_cross,
            gain_ff,
            gate_weight,
            up_weight,
            down_weight,
        ) = gathered
        gain_self = gain_self.astype(jnp.float32)
        gain_cross = gain_cross.astype(jnp.float32)
        gain_ff = gain_ff.astype(jnp.float32)
        table = lax.dot_general(
            bias_whole.astype(jnp.float32), onehot, (((0,), (1,)), ((), ())), precision=HIGH
        )
        lengths = target_lengths[micro_step]
        spans = memory_lengths[micro_step]
        valid = (places[None, :] < lengths[:, None]).astype(jnp.float32).reshape(-1, 1)
        hidden = layer_input[micro_step].reshape(-1, model_width).astype(jnp.float32)
        normed_self = rms_norm(hidden, gain_self).astype(jnp.bfloat16)
        queries = (
            project(normed_self, query_self)
            .astype(jnp.bfloat16)
            .reshape(batch_rows, local_tokens, -1)
        )
        keys = (
            project(normed_self, key_self)
            .astype(jnp.bfloat16)
            .reshape(batch_rows, local_tokens, -1)
        )
        values = (
            project(normed_self, value_self)
            .astype(jnp.bfloat16)
            .reshape(batch_rows, local_tokens, -1)
        )
        encoded = memory[micro_step].reshape(-1, model_width)
        memory_keys = (
            project(encoded, key_cross).astype(jnp.bfloat16).reshape(batch_rows, memory_tokens, -1)
        )
        memory_values = (
            project(encoded, value_cross)
            .astype(jnp.bfloat16)
            .reshape(batch_rows, memory_tokens, -1)
        )
        head_queries, head_keys, head_values, far_keys, far_values = (
            lax.all_to_all(queries, "seq", split_axis=2, concat_axis=1, tiled=True),
            lax.all_to_all(keys, "seq", split_axis=2, concat_axis=1, tiled=True),
            lax.all_to_all(values, "seq", split_axis=2, concat_axis=1, tiled=True),
            lax.all_to_all(memory_keys, "seq", split_axis=2, concat_axis=1, tiled=True),
            lax.all_to_all(memory_values, "seq", split_axis=2, concat_axis=1, tiled=True),
        )
        self_queries = split_heads(head_queries, group)
        self_keys = split_shared(head_keys)
        self_values = split_shared(head_values)
        far_keys = split_shared(far_keys)
        far_values = split_shared(far_values)
        attended, self_sums = jax.vmap(self_forward, in_axes=(0, 0, 0, 0, None))(
            self_queries, self_keys, self_values, lengths, table
        )
        context = to_tokens(attended.reshape(batch_rows, TGT, -1)).reshape(
            batch_rows * local_tokens, -1
        )
        first = hidden + project(context, output_self)
        normed_cross = rms_norm(first, gain_cross).astype(jnp.bfloat16)
        cross_queries = (
            project(normed_cross, query_cross)
            .astype(jnp.bfloat16)
            .reshape(batch_rows, local_tokens, -1)
        )
        cross_heads = split_heads(
            lax.all_to_all(cross_queries, "seq", split_axis=2, concat_axis=1, tiled=True), group
        )
        cross_attended, cross_sums = jax.vmap(cross_forward)(
            cross_heads, far_keys, far_values, spans
        )
        cross_context = to_tokens(cross_attended.reshape(batch_rows, TGT, -1)).reshape(
            batch_rows * local_tokens, -1
        )
        second = first + project(cross_context, output_cross)
        normed_ff = rms_norm(second, gain_ff).astype(jnp.bfloat16)
        gate = project(normed_ff, gate_weight)
        upward = project(normed_ff, up_weight)
        middle = gated(gate, upward).astype(jnp.bfloat16)
        third = second + project(middle, down_weight)
        outputs.append(
            (third * valid).astype(jnp.bfloat16).reshape(batch_rows, local_tokens, model_width)
        )
        upstream = cotangent[micro_step].reshape(-1, model_width).astype(jnp.float32) * valid
        down_grad = upstream.astype(jnp.bfloat16)
        totals[14] = totals[14] + weight_grad(middle, down_grad)
        _, pullback = jax.vjp(gated, gate, upward)
        gate_grad, upward_grad = pullback(project_back(down_grad, down_weight))
        gate_grad = gate_grad.astype(jnp.bfloat16)
        upward_grad = upward_grad.astype(jnp.bfloat16)
        totals[12] = totals[12] + weight_grad(normed_ff, gate_grad)
        totals[13] = totals[13] + weight_grad(normed_ff, upward_grad)
        _, pullback = jax.vjp(rms_norm, second, gain_ff)
        second_grad, gain_grad = pullback(
            project_back(gate_grad, gate_weight) + project_back(upward_grad, up_weight)
        )
        totals[11] = totals[11] + gain_grad
        second_grad = second_grad + upstream
        cross_grad = second_grad.astype(jnp.bfloat16)
        totals[10] = totals[10] + weight_grad(cross_context, cross_grad)
        context_grad = (
            project_back(cross_grad, output_cross)
            .astype(jnp.bfloat16)
            .reshape(batch_rows, local_tokens, -1)
        )
        cross_query_grad, far_key_grad, far_value_grad, _ = jax.vmap(cross_backward)(
            cross_heads,
            far_keys,
            far_values,
            cross_sums,
            split_heads(to_heads(context_grad), group),
            spans,
        )
        query_back, key_back, value_back = (
            lax.all_to_all(
                shortened(cross_query_grad.reshape(batch_rows, TGT, -1)),
                "seq",
                split_axis=1,
                concat_axis=2,
                tiled=True,
            ),
            lax.all_to_all(
                shortened(far_key_grad.reshape(batch_rows, MEM, -1)),
                "seq",
                split_axis=1,
                concat_axis=2,
                tiled=True,
            ),
            lax.all_to_all(
                shortened(far_value_grad.reshape(batch_rows, MEM, -1)),
                "seq",
                split_axis=1,
                concat_axis=2,
                tiled=True,
            ),
        )
        query_back = query_back.reshape(batch_rows * local_tokens, -1)
        key_back = key_back.reshape(batch_rows * memory_tokens, -1)
        value_back = value_back.reshape(batch_rows * memory_tokens, -1)
        totals[7] = totals[7] + weight_grad(normed_cross, query_back)
        totals[8] = totals[8] + weight_grad(encoded, key_back)
        totals[9] = totals[9] + weight_grad(encoded, value_back)
        memory_grads.append(
            (project_back(key_back, key_cross) + project_back(value_back, value_cross)).reshape(
                batch_rows, memory_tokens, model_width
            )
        )
        _, pullback = jax.vjp(rms_norm, first, gain_cross)
        first_grad, gain_grad = pullback(project_back(query_back, query_cross))
        totals[6] = totals[6] + gain_grad
        first_grad = first_grad + second_grad
        self_grad = first_grad.astype(jnp.bfloat16)
        totals[4] = totals[4] + weight_grad(context, self_grad)
        context_grad = (
            project_back(self_grad, output_self)
            .astype(jnp.bfloat16)
            .reshape(batch_rows, local_tokens, -1)
        )
        query_grad, key_grad, value_grad, bias_grad = jax.vmap(
            self_backward, in_axes=(0, 0, 0, 0, 0, 0, None)
        )(
            self_queries,
            self_keys,
            self_values,
            self_sums,
            split_heads(to_heads(context_grad), group),
            lengths,
            table,
        )
        diagonal = diagonal + jnp.sum(bias_grad, axis=0)
        query_back, key_back, value_back = (
            lax.all_to_all(
                shortened(query_grad.reshape(batch_rows, TGT, -1)),
                "seq",
                split_axis=1,
                concat_axis=2,
                tiled=True,
            ),
            lax.all_to_all(
                shortened(key_grad.reshape(batch_rows, TGT, -1)),
                "seq",
                split_axis=1,
                concat_axis=2,
                tiled=True,
            ),
            lax.all_to_all(
                shortened(value_grad.reshape(batch_rows, TGT, -1)),
                "seq",
                split_axis=1,
                concat_axis=2,
                tiled=True,
            ),
        )
        query_back = query_back.reshape(batch_rows * local_tokens, -1)
        key_back = key_back.reshape(batch_rows * local_tokens, -1)
        value_back = value_back.reshape(batch_rows * local_tokens, -1)
        totals[1] = totals[1] + weight_grad(normed_self, query_back)
        totals[2] = totals[2] + weight_grad(normed_self, key_back)
        totals[3] = totals[3] + weight_grad(normed_self, value_back)
        _, pullback = jax.vjp(rms_norm, hidden, gain_self)
        hidden_grad, gain_grad = pullback(
            project_back(query_back, query_self)
            + project_back(key_back, key_self)
            + project_back(value_back, value_self)
        )
        totals[0] = totals[0] + gain_grad
        input_grads.append(
            (hidden_grad + first_grad).reshape(batch_rows, local_tokens, model_width)
        )
    totals[5] = lax.dot_general(
        onehot, diagonal.reshape(-1, TGT), (((0,), (1,)), ((), ())), precision=HIGH
    )
    reduced = (
        lax.psum_scatter(totals[0], ("dp", "seq"), scatter_dimension=0, tiled=True),
        lax.psum_scatter(totals[1], ("dp", "seq"), scatter_dimension=0, tiled=True),
        lax.psum_scatter(totals[2], ("dp", "seq"), scatter_dimension=0, tiled=True),
        lax.psum_scatter(totals[3], ("dp", "seq"), scatter_dimension=0, tiled=True),
        lax.psum_scatter(totals[4], ("dp", "seq"), scatter_dimension=0, tiled=True),
        lax.psum_scatter(totals[6], ("dp", "seq"), scatter_dimension=0, tiled=True),
        lax.psum_scatter(totals[7], ("dp", "seq"), scatter_dimension=0, tiled=True),
        lax.psum_scatter(totals[8], ("dp", "seq"), scatter_dimension=0, tiled=True),
        lax.psum_scatter(totals[9], ("dp", "seq"), scatter_dimension=0, tiled=True),
        lax.psum_scatter(totals[10], ("dp", "seq"), scatter_dimension=0, tiled=True),
        lax.psum_scatter(totals[11], ("dp", "seq"), scatter_dimension=0, tiled=True),
        lax.psum_scatter(totals[12], ("dp", "seq"), scatter_dimension=0, tiled=True),
        lax.psum_scatter(totals[13], ("dp", "seq"), scatter_dimension=0, tiled=True),
        lax.psum_scatter(totals[14], ("dp", "seq"), scatter_dimension=0, tiled=True),
    )
    bias_share = lax.psum_scatter(totals[5], "dp", scatter_dimension=0, tiled=True)
    return (
        jnp.stack(outputs),
        jnp.stack(input_grads),
        jnp.stack(memory_grads),
        reduced[0],
        reduced[1],
        reduced[2],
        reduced[3],
        reduced[4],
        bias_share,
        reduced[5],
        reduced[6],
        reduced[7],
        reduced[8],
        reduced[9],
        reduced[10],
        reduced[11],
        reduced[12],
        reduced[13],
    )


def row_pieces(full):
    blocks = full.reshape(full.shape[0], -1, QB)
    return jnp.concatenate([blocks[:, 1:], blocks[:, :-1]], axis=2)


def seed_rows(vectors):
    return jnp.stack([jnp.roll(vectors, r, axis=-1) for r in range(8)], axis=-2)


def spread(seed):
    rows = 8
    tile = seed
    while rows < QB:
        tile = jnp.concatenate([tile, pltpu.roll(tile, rows, 1)], axis=0)
        rows *= 2
    return tile[:, :QB]


def fold(tile):
    width = 2 * QB
    tile = jnp.concatenate([tile, jnp.zeros_like(tile)], axis=1)
    rows = QB
    while rows > 8:
        rows //= 2
        tile = tile[:rows] + pltpu.roll(tile[rows:], width - rows, 1)
    return tile


def nt(left, right):
    return lax.dot_general(left, right, (((1,), (1,)), ((), ())), preferred_element_type=jnp.float32)


def tn(left, right):
    return lax.dot_general(left, right, (((0,), (0,)), ((), ())), preferred_element_type=jnp.float32)


def nn(left, right):
    return lax.dot_general(left, right, (((1,), (0,)), ((), ())), preferred_element_type=jnp.float32)


def forward_kernel(causal, q_ref, k_ref, v_ref, keep_ref, *rest):
    if causal:
        seed_ref, o_ref, lse_ref, bias = rest
    else:
        o_ref, lse_ref = rest
    span = k_ref.shape[0]
    for kv in range(2):
        lanes = slice(kv * HEAD_DIM, (kv + 1) * HEAD_DIM)
        keys = k_ref[:, lanes]
        values = v_ref[:, lanes]
        if causal:
            for member in range(2):
                for offset in range(4):
                    bias[member * QB : (member + 1) * QB, (3 - offset) * QB : (4 - offset) * QB] = spread(
                        seed_ref[2 * kv + member, offset]
                    )
        for block in range(q_ref.shape[0] // QB):
            stop = (block + 1) * QB if causal else span
            rows = slice(block * QB, (block + 1) * QB)
            both = q_ref[rows, 2 * kv * HEAD_DIM : 2 * (kv + 1) * HEAD_DIM]
            query = jnp.concatenate([both[:, :HEAD_DIM], both[:, HEAD_DIM:]], axis=0)
            scores = nt(query, keys[:stop]) + keep_ref[:, :stop]
            if causal:
                scores = scores + bias[:, (3 - block) * QB : (3 - block) * QB + stop]
            peak = jnp.max(scores, axis=1, keepdims=True)
            weights = jnp.exp(scores - peak)
            total = jnp.sum(weights, axis=1, keepdims=True)
            mixed = nn(weights.astype(jnp.bfloat16), values[:stop]) / total
            o_ref[rows, 2 * kv * HEAD_DIM : 2 * (kv + 1) * HEAD_DIM] = jnp.concatenate(
                [mixed[:QB], mixed[QB:]], axis=1
            ).astype(jnp.bfloat16)
            sums = jnp.broadcast_to(peak + jnp.log(total), (2 * QB, 128)).T
            lse_ref[2 * kv : 2 * kv + 1, rows] = sums[:1, :QB]
            lse_ref[2 * kv + 1 : 2 * kv + 2, rows] = sums[:1, QB:]


def backward_kernel(causal, q_ref, k_ref, v_ref, o_ref, do_ref, lse_ref, keep_ref, *rest):
    if causal:
        seed_ref, dq_ref, dk_ref, dv_ref, diag_ref, bias, sums, dk_sum, dv_sum = rest
    else:
        dq_ref, dk_ref, dv_ref, dk_sum, dv_sum = rest
    span = k_ref.shape[0]
    blocks = q_ref.shape[0] // QB
    for kv in range(2):
        lanes = slice(kv * HEAD_DIM, (kv + 1) * HEAD_DIM)
        dk_sum[...] = jnp.zeros_like(dk_sum)
        dv_sum[...] = jnp.zeros_like(dv_sum)
        if causal:
            for member in range(2):
                for offset in range(4):
                    bias[offset, :, member * QB : (member + 1) * QB] = spread(
                        seed_ref[2 * kv + member, offset]
                    )
            sums[...] = jnp.zeros_like(sums)
        for block in range(blocks):
            rows = slice(block * QB, (block + 1) * QB)
            both = slice(2 * kv * HEAD_DIM, 2 * (kv + 1) * HEAD_DIM)
            pair = q_ref[rows, both]
            query = jnp.concatenate([pair[:, :HEAD_DIM], pair[:, HEAD_DIM:]], axis=0)
            upstream = do_ref[rows, both]
            grads = jnp.concatenate([upstream[:, :HEAD_DIM], upstream[:, HEAD_DIM:]], axis=0)
            inner = (upstream.astype(jnp.float32) * o_ref[rows, both].astype(jnp.float32)).T
            delta = jnp.concatenate(
                [
                    jnp.sum(inner[:HEAD_DIM], axis=0, keepdims=True),
                    jnp.sum(inner[HEAD_DIM:], axis=0, keepdims=True),
                ],
                axis=1,
            )
            level = jnp.concatenate(
                [lse_ref[2 * kv : 2 * kv + 1, rows], lse_ref[2 * kv + 1 : 2 * kv + 2, rows]], axis=1
            )
            dq = jnp.zeros((2 * QB, HEAD_DIM), jnp.float32)
            for part in range(block + 1 if causal else span // QB):
                columns = slice(part * QB, (part + 1) * QB)
                keys = k_ref[columns, lanes]
                values = v_ref[columns, lanes]
                scores = nt(keys, query) + keep_ref[columns]
                if causal:
                    scores = scores + bias[block - part]
                probs = jnp.exp(scores - level)
                dscores = probs * (nt(values, grads) - delta)
                if causal:
                    sums[block - part] += dscores
                dscores = dscores.astype(jnp.bfloat16)
                dv_sum[columns] += nn(probs.astype(jnp.bfloat16), grads)
                dk_sum[columns] += nn(dscores, query)
                dq += tn(dscores, keys)
            dq_ref[rows, both] = jnp.concatenate([dq[:QB], dq[QB:]], axis=1).astype(jnp.bfloat16)
        dk_ref[:, lanes] = dk_sum[...].astype(jnp.bfloat16)
        dv_ref[:, lanes] = dv_sum[...].astype(jnp.bfloat16)
        if causal:
            for member in range(2):
                for offset in range(4):
                    diag_ref[2 * kv + member, offset] = fold(
                        sums[offset, :, member * QB : (member + 1) * QB]
                    )


PARAMS = pltpu.CompilerParams(vmem_limit_bytes=56 * 2**20)


def attention_forward(queries, kv, keep, seeds=None):
    tokens, width = queries.shape
    span = kv.shape[0]
    heads = width // HEAD_DIM
    causal = seeds is not None
    in_specs = [
        pl.BlockSpec((tokens, 256), lambda i: (0, i)),
        pl.BlockSpec((span, 128), lambda i: (0, i)),
        pl.BlockSpec((span, 128), lambda i: (0, i + 2)),
        pl.BlockSpec((1, span), lambda i: (0, 0)),
    ]
    operands = [queries, kv, kv, keep.reshape(1, span)]
    scratch = []
    if causal:
        in_specs.append(pl.BlockSpec((4, 4, 8, 512), lambda i: (i, 0, 0, 0)))
        operands.append(seeds)
        scratch.append(pltpu.VMEM((2 * QB, 4 * QB), jnp.float32))
    work = heads * tokens * span // (2 if causal else 1)
    context, sums = pl.pallas_call(
        functools.partial(forward_kernel, causal),
        grid=(heads // 4,),
        in_specs=in_specs,
        out_specs=[
            pl.BlockSpec((tokens, 256), lambda i: (0, i)),
            pl.BlockSpec((None, 4, tokens), lambda i: (i, 0, 0)),
        ],
        out_shape=[
            jax.ShapeDtypeStruct((tokens, width), jnp.bfloat16),
            jax.ShapeDtypeStruct((heads // 4, 4, tokens), jnp.float32),
        ],
        scratch_shapes=scratch,
        compiler_params=PARAMS,
        cost_estimate=pl.CostEstimate(
            flops=work * 4 * 4 * HEAD_DIM, bytes_accessed=4 * 2**20, transcendentals=work
        ),
    )(*operands)
    return context, sums


def attention_backward(queries, kv, context, grads, sums, keep, seeds=None):
    tokens, width = queries.shape
    span = kv.shape[0]
    heads = width // HEAD_DIM
    causal = seeds is not None
    wide = pl.BlockSpec((tokens, 256), lambda i: (0, i))
    narrow = pl.BlockSpec((span, 128), lambda i: (0, i))
    in_specs = [
        wide,
        narrow,
        pl.BlockSpec((span, 128), lambda i: (0, i + 2)),
        wide,
        wide,
        pl.BlockSpec((None, 4, tokens), lambda i: (i, 0, 0)),
        pl.BlockSpec((span, 1), lambda i: (0, 0)),
    ]
    operands = [queries, kv, kv, context, grads, sums, keep.reshape(span, 1)]
    out_specs = [wide, narrow, narrow]
    out_shape = [
        jax.ShapeDtypeStruct((tokens, width), jnp.bfloat16),
        jax.ShapeDtypeStruct((span, width // 2), jnp.bfloat16),
        jax.ShapeDtypeStruct((span, width // 2), jnp.bfloat16),
    ]
    scratch = []
    if causal:
        quad = pl.BlockSpec((4, 4, 8, 512), lambda i: (i, 0, 0, 0))
        in_specs.append(quad)
        operands.append(seeds)
        out_specs.append(quad)
        out_shape.append(jax.ShapeDtypeStruct((heads, 4, 8, 512), jnp.float32))
        scratch = [pltpu.VMEM((4, QB, 2 * QB), jnp.float32), pltpu.VMEM((4, QB, 2 * QB), jnp.float32)]
    scratch += [pltpu.VMEM((span, HEAD_DIM), jnp.float32), pltpu.VMEM((span, HEAD_DIM), jnp.float32)]
    work = heads * tokens * span // (2 if causal else 1)
    return pl.pallas_call(
        functools.partial(backward_kernel, causal),
        grid=(heads // 4,),
        in_specs=in_specs,
        out_specs=out_specs,
        out_shape=out_shape,
        scratch_shapes=scratch,
        compiler_params=PARAMS,
        cost_estimate=pl.CostEstimate(
            flops=work * 10 * 4 * HEAD_DIM, bytes_accessed=8 * 2**20, transcendentals=work
        ),
    )(*operands)


def inverse_rms(value):
    return lax.rsqrt(jnp.mean(value * value, axis=-1, keepdims=True) + EPS)


def rms_back(value, gain, upstream):
    inverse = inverse_rms(value)
    scaled = upstream * gain
    mean = jnp.mean(value * scaled, axis=-1, keepdims=True)
    return inverse * scaled - value * (inverse * inverse * inverse) * mean, upstream * value * inverse


def pick(array, index, axis=0):
    return lax.dynamic_index_in_dim(array, index, axis, keepdims=False)


MESH = pl.DeviceIdType.MESH


class Spot:
    def __init__(self, depth):
        self.depth = depth
        place = lax.axis_index("dp")
        self.corner = lax.axis_index("seq")
        self.z, self.core = place // 2, place % 2
        self.y, self.x = self.corner // 2, self.corner % 2

    def at(self, z=None, core=None, y=None, x=None):
        z = self.z if z is None else z
        core = self.core if core is None else core
        y = self.y if y is None else y
        x = self.x if x is None else x
        return (z * 2 + core, y * 2 + x)

    def beside(self):
        return self.at(x=1 - self.x)

    def below(self):
        return self.at(y=1 - self.y)

    def sibling(self):
        return self.at(core=1 - self.core)

    def greet(self):
        barrier = pltpu.get_barrier_semaphore()
        others = [
            self.at(None, self.core ^ (i >> 2), self.y ^ (i >> 1 & 1), self.x ^ (i & 1)) for i in range(1, 8)
        ]
        for step in range(1, self.depth):
            for flip in range(2):
                others.append(self.at((self.z + step) % self.depth, self.core ^ flip))
        for other in others:
            pl.semaphore_signal(barrier, inc=1, device_id=other, device_id_type=MESH)
        pl.semaphore_wait(barrier, len(others))


class Wires:
    def __init__(self, sends, arrivals, moves):
        self.sends, self.arrivals, self.moves = sends, arrivals, moves
        self.count = 0
        self.moved = 0
        self.open = []

    def take(self, number):
        first = self.count
        self.count += number
        return first

    def send(self, source, target, device, index, landing=None):
        landing = index if landing is None else landing
        copy = pltpu.make_async_remote_copy(
            src_ref=source,
            dst_ref=target,
            send_sem=self.sends.at[index],
            recv_sem=self.arrivals.at[landing],
            device_id=device,
            device_id_type=MESH,
        )
        copy.start()
        self.open.append(copy)
        return copy

    def arrive(self, target, device, index):
        pltpu.make_async_remote_copy(
            src_ref=target,
            dst_ref=target,
            send_sem=self.sends.at[0],
            recv_sem=self.arrivals.at[index],
            device_id=device,
            device_id_type=MESH,
        ).wait_recv()

    def move(self, source, target):
        copy = pltpu.make_async_copy(source, target, self.moves.at[self.moved])
        self.moved += 1
        copy.start()
        return copy

    def close(self):
        for copy in self.open:
            copy.wait_send()
        self.open = []


def collect_tokens(spot, wires, parcel, whole):
    away = wires.take(4)
    over = wires.take(4)
    local = wires.moved
    wires.moved += 1
    for index in range(4):
        half, micro = spot.y ^ (index >> 1), spot.x ^ (index & 1)
        home = (half == spot.core) & (micro == spot.y) & (spot.core == spot.x)
        source = parcel.at[micro, half]
        target = whole.at[spot.corner, half]
        copy = pltpu.make_async_remote_copy(
            src_ref=source,
            dst_ref=target,
            send_sem=wires.sends.at[away + index],
            recv_sem=wires.arrivals.at[away + index],
            device_id=spot.at(core=half, y=micro, x=spot.core),
            device_id_type=MESH,
        )
        here = pltpu.make_async_copy(source, target, wires.moves.at[local])

        @pl.when(jnp.logical_not(home))
        def _():
            copy.start()

        @pl.when(home)
        def _():
            here.start()

    yield
    for index in range(4):
        block = 2 * (spot.core ^ (index >> 1)) + (spot.y ^ (index & 1))
        home = (spot.x == spot.core) & (block == spot.corner)
        piece = whole.at[block, spot.core]
        here = pltpu.make_async_copy(piece, piece, wires.moves.at[local])
        landed = pltpu.make_async_remote_copy(
            src_ref=piece,
            dst_ref=piece,
            send_sem=wires.sends.at[away + index],
            recv_sem=wires.arrivals.at[away + index],
            device_id=spot.sibling(),
            device_id_type=MESH,
        )

        @pl.when(jnp.logical_not(home))
        def _():
            landed.wait_recv()

        @pl.when(home)
        def _():
            here.wait()

        wires.send(piece, piece, spot.sibling(), over + index)
    yield
    for index in range(4):
        block = 2 * ((1 - spot.core) ^ (index >> 1)) + (spot.y ^ (index & 1))
        wires.arrive(whole.at[block, 1 - spot.core], spot.sibling(), over + index)
    for index in range(4):
        half, micro = spot.y ^ (index >> 1), spot.x ^ (index & 1)
        home = (half == spot.core) & (micro == spot.y) & (spot.core == spot.x)
        source = parcel.at[micro, half]

        @pl.when(jnp.logical_not(home))
        def _():
            pltpu.make_async_remote_copy(
                src_ref=source,
                dst_ref=source,
                send_sem=wires.sends.at[away + index],
                recv_sem=wires.arrivals.at[away + index],
                device_id=spot.sibling(),
                device_id_type=MESH,
            ).wait_send()

    yield


def deliver_tokens(spot, wires, pieces, homes):
    away = wires.take(4)
    local = wires.moved
    wires.moved += 1

    def parts():
        for index in range(4):
            block = 2 * (spot.core ^ (index >> 1)) + (spot.y ^ (index & 1))
            home = (spot.x == spot.core) & (block == spot.corner)
            source = pieces.at[block]
            target = homes.at[spot.y, spot.core]
            remote = pltpu.make_async_remote_copy(
                src_ref=source,
                dst_ref=target,
                send_sem=wires.sends.at[away + index],
                recv_sem=wires.arrivals.at[away + index],
                device_id=spot.at(core=spot.x, y=block // 2, x=block % 2),
                device_id_type=MESH,
            )
            yield home, remote, pltpu.make_async_copy(source, target, wires.moves.at[local])

    for home, remote, here in parts():
        pl.when(jnp.logical_not(home))(remote.start)
        pl.when(home)(here.start)
    yield
    for index in range(4):
        half, micro = spot.y ^ (index >> 1), spot.x ^ (index & 1)
        home = (half == spot.core) & (micro == spot.y) & (spot.core == spot.x)
        piece = homes.at[micro, half]
        landed = pltpu.make_async_remote_copy(
            src_ref=piece,
            dst_ref=piece,
            send_sem=wires.sends.at[away + index],
            recv_sem=wires.arrivals.at[away + index],
            device_id=spot.sibling(),
            device_id_type=MESH,
        )
        here = pltpu.make_async_copy(piece, piece, wires.moves.at[local])
        pl.when(jnp.logical_not(home))(landed.wait_recv)
        pl.when(home)(here.wait)
    for home, remote, here in parts():
        pl.when(jnp.logical_not(home))(remote.wait_send)
    yield


def gather_small(spot, wires, block, whole):
    own = wires.move(block, whole.at[spot.z, spot.core, spot.corner])
    first = wires.take(spot.depth + 3)
    for step in range(1, spot.depth):
        target = whole.at[spot.z, spot.core, spot.corner]
        wires.send(block, target, spot.at(z=(spot.z + step) % spot.depth), first + step)
    yield
    own.wait()
    for step in range(1, spot.depth):
        z = (spot.z - step + spot.depth) % spot.depth
        wires.arrive(whole.at[z, spot.core, spot.corner], spot.sibling(), first + step)
    column = whole.at[:, spot.core, spot.corner]
    wires.send(column, column, spot.beside(), first)
    wires.send(column, column, spot.below(), first + spot.depth)
    wires.send(column, column, spot.at(y=1 - spot.y, x=1 - spot.x), first + spot.depth + 1)
    yield
    for flip, index in ((1, first), (2, first + spot.depth), (3, first + spot.depth + 1)):
        wires.arrive(whole.at[:, spot.core, spot.corner ^ flip], spot.sibling(), index)
    plane = whole.at[:, spot.core]
    wires.send(plane, plane, spot.sibling(), first + spot.depth + 2)
    yield
    wires.arrive(whole.at[:, 1 - spot.core], spot.sibling(), first + spot.depth + 2)
    yield


def gather_columns(spot, wires, pack, whole):
    depth, me = spot.depth, spot.corner
    ahead = wires.take(2 * depth)
    flat = wires.take(4 * depth)
    own = wires.move(pack.at[spot.core], whole.at[spot.z, spot.core])
    for step in range(1, depth):
        for flip in range(2):
            wires.send(
                pack.at[spot.core ^ flip, me],
                whole.at[spot.z, spot.core, me],
                spot.at((spot.z + step) % depth, spot.core ^ flip),
                ahead + 2 * step + flip,
            )
    wires.send(pack.at[1 - spot.core], whole.at[spot.z, spot.core], spot.sibling(), ahead)
    yield
    for step in range(1, depth):
        z = (spot.z - step + depth) % depth
        for flip in range(2):
            wires.arrive(whole.at[z, spot.core ^ flip, me], spot.sibling(), ahead + 2 * step + flip)
        quarter = whole.at[z, :, me]
        wires.send(quarter, quarter, spot.beside(), flat + 4 * step)
        wires.send(quarter, quarter, spot.below(), flat + 4 * step + 1)
    yield
    for step in range(1, depth):
        z = (spot.z - step + depth) % depth
        wires.arrive(whole.at[z, :, me ^ 1], spot.sibling(), flat + 4 * step)
        piece = whole.at[z, 0, me ^ 1]
        wires.send(piece, piece, spot.below(), flat + 4 * step + 2)
        wires.arrive(whole.at[z, :, me ^ 2], spot.sibling(), flat + 4 * step + 1)
        piece = whole.at[z, 1, me ^ 2]
        wires.send(piece, piece, spot.beside(), flat + 4 * step + 3)
    yield
    own.wait()
    wires.arrive(whole.at[spot.z, 1 - spot.core], spot.sibling(), ahead)
    for step in range(1, depth):
        z = (spot.z - step + depth) % depth
        wires.arrive(whole.at[z, 0, me ^ 3], spot.sibling(), flat + 4 * step + 2)
        wires.arrive(whole.at[z, 1, me ^ 3], spot.sibling(), flat + 4 * step + 3)
    yield


def gather_rows(spot, wires, pack, whole):
    depth, me = spot.depth, spot.corner
    ahead = wires.take(depth)
    flat = wires.take(4 * depth)
    middle = pack.shape[-1] // 2

    def part(z, corner, side):
        if pack.shape[0] == 2:
            return whole.at[side, z, corner]
        return whole.at[0, z, corner, :, pl.ds(side * middle, middle)]

    own = wires.move(pack, whole.at[:, spot.z])
    for step in range(1, depth):
        wires.send(
            pack.at[:, me], whole.at[:, spot.z, me], spot.at((spot.z + step) % depth), ahead + step
        )
    yield
    for step in range(1, depth):
        z = (spot.z - step + depth) % depth
        quarter = whole.at[:, z, me]
        wires.arrive(quarter, spot.sibling(), ahead + step)
        wires.send(quarter, quarter, spot.beside(), flat + 4 * step)
        wires.send(quarter, quarter, spot.below(), flat + 4 * step + 1)
    yield
    for step in range(1, depth):
        z = (spot.z - step + depth) % depth
        wires.arrive(whole.at[:, z, me ^ 1], spot.sibling(), flat + 4 * step)
        piece = part(z, me ^ 1, 0)
        wires.send(piece, piece, spot.below(), flat + 4 * step + 2)
        wires.arrive(whole.at[:, z, me ^ 2], spot.sibling(), flat + 4 * step + 1)
        piece = part(z, me ^ 2, 1)
        wires.send(piece, piece, spot.beside(), flat + 4 * step + 3)
    yield
    own.wait()
    for step in range(1, depth):
        z = (spot.z - step + depth) % depth
        wires.arrive(part(z, me ^ 3, 0), spot.sibling(), flat + 4 * step + 2)
        wires.arrive(part(z, me ^ 3, 1), spot.sibling(), flat + 4 * step + 3)
    yield


def add_into(target, other, places):
    for place in places:
        target[place] = (
            target[place].astype(jnp.float32) + other[place].astype(jnp.float32)
        ).astype(jnp.bfloat16)


def scatter_buffers(depth, lanes, rows, width):
    half = depth // 2
    return [
        pltpu.VMEM((half, lanes, 2, rows, width), jnp.bfloat16),
        pltpu.VMEM((half, lanes, 2, rows, width), jnp.bfloat16),
        pltpu.VMEM((half, lanes, 2, rows, width), jnp.bfloat16),
        pltpu.VMEM((half, lanes, 2, rows, width), jnp.bfloat16),
        pltpu.VMEM((half, lanes, rows, width), jnp.bfloat16),
        pltpu.VMEM((half, lanes, rows, width), jnp.bfloat16),
        pltpu.VMEM((depth, lanes, rows, width), jnp.bfloat16),
        pltpu.VMEM((depth, lanes, rows, width), jnp.bfloat16),
        pltpu.VMEM((rows, width), jnp.bfloat16),
    ]


def scatter_sums(spot, wires, grads, buffers, total, got):
    depth, half = spot.depth, spot.depth // 2
    lanes = grads.shape[1]
    low, high, low_in, high_in, low_last, high_last, column, column_in, passing = buffers
    first = wires.take(4)
    away = wires.take(depth)
    mine = [
        wires.move(grads.at[pl.ds(0, half), :, :, spot.x], low),
        wires.move(grads.at[pl.ds(half, half), :, spot.y], high),
    ]
    wires.send(grads.at[pl.ds(0, half), :, :, 1 - spot.x], low_in, spot.beside(), first)
    wires.send(grads.at[pl.ds(half, half), :, 1 - spot.y], high_in, spot.below(), first + 1)
    yield
    for copy in mine:
        copy.wait()
    wires.arrive(low_in, spot.beside(), first)
    add_into(low, low_in, [(z, a, s) for z in range(half) for a in range(lanes) for s in range(2)])
    wires.send(low.at[:, :, 1 - spot.y], low_last, spot.below(), first + 2)
    wires.arrive(high_in, spot.below(), first + 1)
    add_into(high, high_in, [(z, a, s) for z in range(half) for a in range(lanes) for s in range(2)])
    wires.send(high.at[:, :, 1 - spot.x], high_last, spot.beside(), first + 3)
    yield
    wires.arrive(low_last, spot.below(), first + 2)
    wires.arrive(high_last, spot.beside(), first + 3)
    for z in range(half):
        for a in range(lanes):
            column[z, a] = (
                low[z, a, spot.y].astype(jnp.float32) + low_last[z, a].astype(jnp.float32)
            ).astype(jnp.bfloat16)
            column[half + z, a] = (
                high[z, a, spot.x].astype(jnp.float32) + high_last[z, a].astype(jnp.float32)
            ).astype(jnp.bfloat16)
    for step in range(1, depth):
        z = (spot.z + step) % depth
        wires.send(column.at[z], column_in.at[step], spot.at(z), away + step)
    yield
    for step in range(1, depth):
        wires.arrive(column_in.at[step], spot.sibling(), away + step)

    def added(lane):
        result = column[spot.z, lane].astype(jnp.float32)
        for step in range(1, depth):
            result = result + column_in[step, lane].astype(jnp.float32)
        return result

    if lanes == 1:
        total[...] = added(0)
    else:
        passing[...] = added(1 - spot.core).astype(jnp.bfloat16)
        wires.send(passing, got, spot.sibling(), away)
        total[...] = added(spot.core)
    yield
    if lanes == 2:
        wires.arrive(got, spot.sibling(), away)
    yield


def total_small(spot, wires, terms, work, total):
    first = wires.take(3 + spot.depth)
    work[0] = terms[...]
    wires.send(work.at[0], work.at[1], spot.sibling(), first)
    yield
    wires.arrive(work.at[1], spot.sibling(), first)
    work[2] = work[0] + work[1]
    wires.send(work.at[2], work.at[3], spot.beside(), first + 1)
    yield
    wires.arrive(work.at[3], spot.sibling(), first + 1)
    work[4] = work[2] + work[3]
    wires.send(work.at[4], work.at[5], spot.below(), first + 2)
    yield
    wires.arrive(work.at[5], spot.sibling(), first + 2)
    work[6] = work[4] + work[5]
    for step in range(1, spot.depth):
        target = work.at[6 + step]
        wires.send(work.at[6], target, spot.at((spot.z + step) % spot.depth), first + 2 + step)
    yield
    result = work[6]
    for step in range(1, spot.depth):
        wires.arrive(work.at[6 + step], spot.sibling(), first + 2 + step)
        result = result + work[6 + step]
    total[...] = result
    yield


def staggered(programs):
    live = list(enumerate(programs))
    step = 0
    while live:
        rest = []
        for start, program in reversed(live):
            if step < start or next(program, False) is not False:
                rest.append((start, program))
        live = rest[::-1]
        step += 1


def wire_scratch(number, moves):
    return [
        pltpu.SemaphoreType.DMA((number,)),
        pltpu.SemaphoreType.DMA((number,)),
        pltpu.SemaphoreType.DMA((moves,)),
    ]


def front_kernel(depth, x, t, m, s, p1, p2, p3, p4, p5, wx, wt, wm, ws, w1, w2, w3, w4, w5, *sems):
    spot = Spot(depth)
    wires = Wires(*sems)
    spot.greet()
    staggered(
        [
            collect_tokens(spot, wires, x, wx),
            gather_columns(spot, wires, p1, w1),
            gather_small(spot, wires, s, ws),
            collect_tokens(spot, wires, m, wm),
            gather_columns(spot, wires, p2, w2),
            gather_rows(spot, wires, p3, w3),
            gather_columns(spot, wires, p4, w4),
            gather_rows(spot, wires, p5, w5),
            collect_tokens(spot, wires, t, wt),
        ]
    )
    wires.close()


def front(depth, x, t, m, small, p1, p2, p3, p4, p5):
    bf16 = jnp.bfloat16

    def whole_columns(pack):
        return jax.ShapeDtypeStruct((depth, 2) + pack.shape[1:], bf16)

    def whole_rows(pack):
        return jax.ShapeDtypeStruct((pack.shape[0], depth) + pack.shape[1:], bf16)

    def whole_tokens(parcel):
        return jax.ShapeDtypeStruct((4, 2) + parcel.shape[2:], bf16)

    hbm = pl.BlockSpec(memory_space=pl.ANY)
    return pl.pallas_call(
        functools.partial(front_kernel, depth),
        in_specs=[hbm] * 9,
        out_specs=[hbm] * 9,
        out_shape=[
            whole_tokens(x),
            whole_tokens(t),
            whole_tokens(m),
            jax.ShapeDtypeStruct((depth, 2, 4, 8, 128), jnp.float32),
            whole_columns(p1),
            whole_columns(p2),
            whole_rows(p3),
            whole_columns(p4),
            whole_rows(p5),
        ],
        scratch_shapes=wire_scratch(24 + 8 * depth + 22 * depth, 12),
        compiler_params=pltpu.CompilerParams(
            collective_id=0, has_side_effects=True, vmem_limit_bytes=16 * 2**20
        ),
        cost_estimate=pl.CostEstimate(flops=0, bytes_accessed=256 * 2**20, transcendentals=0),
    )(x, t, m, small, p1, p2, p3, p4, p5)


def reduce_kernel(depth, lanes, tokens, small, *refs):
    spot = Spot(depth)
    refs = list(refs)
    take = lambda n: [refs.pop(0) for _ in range(n)]
    grads = take(len(lanes))
    pieces = take(tokens)
    terms = take(1 if small else 0)
    totals = take(len(lanes))
    gots = [take(1)[0] if count == 2 else None for count in lanes]
    homes = take(tokens)
    sums = take(1 if small else 0)
    buffers = [take(9) for _ in lanes]
    work = take(1 if small else 0)
    wires = Wires(*refs)
    spot.greet()
    programs = [deliver_tokens(spot, wires, *pair) for pair in zip(pieces, homes)]
    if small:
        programs.append(total_small(spot, wires, terms[0], work[0], sums[0]))
    programs += [
        scatter_sums(spot, wires, grad, scratch, total, got)
        for grad, scratch, total, got in zip(grads, buffers, totals, gots)
    ]
    staggered(programs)
    wires.close()


def reduce_over_chips(depth, identity, grads, pieces=(), terms=None):
    lanes = tuple(g.shape[1] for g in grads)
    hbm = pl.BlockSpec(memory_space=pl.ANY)
    vmem = pl.BlockSpec(memory_space=pltpu.VMEM)
    extra = 0 if terms is None else 1
    out_shape = [jax.ShapeDtypeStruct(g.shape[4:], jnp.float32) for g in grads]
    out_shape += [jax.ShapeDtypeStruct(g.shape[4:], jnp.bfloat16) for g in grads if g.shape[1] == 2]
    out_shape += [jax.ShapeDtypeStruct((2, 2) + p.shape[1:], p.dtype) for p in pieces]
    out_shape += [jax.ShapeDtypeStruct((32, 128), jnp.float32)] * extra
    out_specs = [vmem] * (len(grads) + sum(n == 2 for n in lanes)) + [hbm] * len(pieces) + [vmem] * extra
    scratch = []
    for grad in grads:
        scratch += scatter_buffers(depth, grad.shape[1], *grad.shape[4:])
    scratch += [pltpu.VMEM((6 + depth, 32, 128), jnp.float32)] * extra
    number = len(grads) * (4 + depth) + 4 * len(pieces) + extra * (3 + depth)
    results = pl.pallas_call(
        functools.partial(reduce_kernel, depth, lanes, len(pieces), extra == 1),
        in_specs=[hbm] * (len(grads) + len(pieces)) + [vmem] * extra,
        out_specs=out_specs,
        out_shape=out_shape,
        scratch_shapes=scratch + wire_scratch(number, 2 * len(grads) + len(pieces) + 1),
        compiler_params=pltpu.CompilerParams(
            collective_id=identity, has_side_effects=True, vmem_limit_bytes=56 * 2**20
        ),
        cost_estimate=pl.CostEstimate(flops=0, bytes_accessed=256 * 2**20, transcendentals=0),
    )(*grads, *pieces, *(() if terms is None else (terms,)))
    results = list(results)
    totals = [results.pop(0) for _ in grads]
    gots = [results.pop(0) if n == 2 else None for n in lanes]
    homes = [results.pop(0) for _ in pieces]
    return totals, gots, homes, results[0] if extra else None


def parity_columns(weight):
    rows, columns = weight.shape
    return jnp.moveaxis(weight.reshape(rows, 4, 2, columns // 8), 2, 0).reshape(2, rows, columns // 2)


def per_chip(
    layer_input,
    memory,
    target_lengths,
    memory_lengths,
    buckets,
    norm_self,
    self_q,
    self_k,
    self_v,
    self_out,
    rel_bias,
    norm_cross,
    cross_q,
    cross_k,
    cross_v,
    cross_out,
    norm_ff,
    ff_gate,
    ff_up,
    ff_down,
    cotangent,
):
    bf16, f32 = jnp.bfloat16, jnp.float32
    depth = lax.axis_size("dp") // 2
    spot = Spot(depth)
    core = spot.core
    width = layer_input.shape[3]
    local = layer_input.shape[2]
    near = memory.shape[2]
    shard = norm_self.shape[0]

    def column_pack(weights):
        pack = jnp.concatenate([parity_columns(w) for w in weights], axis=2)
        return pack.reshape(2, 4, -1, pack.shape[2])

    small = jnp.concatenate(
        [norm_self, norm_cross, norm_ff, rel_bias.reshape(-1)]
    ).astype(f32)
    lengths = jnp.concatenate([target_lengths, memory_lengths]).reshape(-1).astype(f32)
    small = jnp.concatenate([small, lengths, jnp.zeros((1024 - small.size - 4,), f32)]).reshape(8, 128)
    inputs, upstream, encoded, small, w_qkv, w_cross, w_outs, w_gu, w_down = front(
        depth,
        layer_input.reshape(2, 2, local // 2, width),
        cotangent.reshape(2, 2, local // 2, width),
        memory.reshape(2, 2, near // 2, width),
        small,
        column_pack([self_q, self_k, self_v]),
        column_pack([cross_k, cross_v, cross_q]),
        jnp.stack([self_out, cross_out]).reshape(2, 4, -1, width),
        column_pack([ff_gate, ff_up]),
        ff_down.reshape(1, 4, -1, width),
    )
    inputs, upstream, encoded = (a.reshape(-1, width) for a in (inputs, upstream, encoded))
    w_qkv, w_cross, w_gu, w_down = (a.reshape(-1, a.shape[-1]) for a in (w_qkv, w_cross, w_gu, w_down))
    w_out, w_cout = w_outs[0].reshape(-1, width), w_outs[1].reshape(-1, width)
    inner = self_q.shape[1] // 2
    w_ckv, w_cq = w_cross[:, :inner], w_cross[:, inner:]
    hidden_width = w_gu.shape[1] // 2
    w_gate, w_up = w_gu[:, :hidden_width], w_gu[:, hidden_width:]
    small = small.reshape(2 * depth, 4, 1024)
    gain_self, gain_cross, gain_ff = (
        small[:, 0, i * shard : (i + 1) * shard].reshape(-1) for i in range(3)
    )
    bias = small[:, :, 3 * shard : 3 * shard + 16].reshape(-1, 4, 4, 4)
    bias = jnp.swapaxes(bias, 1, 2).reshape(BUCKETS, HEADS)
    bias = pick(bias.reshape(BUCKETS, 4, 2, 2), core, 2).reshape(BUCKETS, -1)
    lengths = pick(small[:, 0], 2 * spot.z + spot.x)[3 * shard + 16 : 3 * shard + 20]
    lengths = pick(lengths.reshape(2, 2), spot.y, 1).astype(jnp.int32)
    length, span = lengths[0], lengths[1]

    onehot = (buckets[:, None] == jnp.arange(BUCKETS, dtype=jnp.int32)[None, :]).astype(f32)
    table = lax.dot_general(bias, onehot, (((0,), (1,)), ((), ())), precision=HIGH)
    full = jnp.concatenate([jnp.full((table.shape[0], QB), NEG, f32), table], axis=1)
    vectors = row_pieces(full)
    seeds_back = seed_rows(vectors)
    seeds_fore = seed_rows(jnp.roll(vectors[..., ::-1], 1, axis=-1))

    tokens = inputs.shape[0]
    positions = jnp.arange(tokens, dtype=jnp.int32)
    valid = (positions < length).astype(f32)[:, None]
    keep_self = jnp.where(positions < length, 0.0, NEG).astype(f32)
    keep_cross = jnp.where(jnp.arange(encoded.shape[0], dtype=jnp.int32) < span, 0.0, NEG).astype(f32)

    def swap_core(array):
        pairs = [
            (place * 4 + corner, (place ^ 1) * 4 + corner) for place in range(2 * depth) for corner in range(4)
        ]
        return lax.ppermute(array, ("dp", "seq"), pairs)

    def share(partial):
        partial = partial.astype(bf16)
        return partial.astype(f32) + swap_core(partial).astype(f32)

    def share_half(partial):
        partial = partial.astype(bf16).reshape(4, 2, -1, partial.shape[-1])
        got = swap_core(pick(partial, 1 - core, 1))
        return pick(partial, core, 1).astype(f32) + got.astype(f32)

    def own_half(value):
        return pick(value.reshape(4, 2, -1, value.shape[-1]), core, 1)

    def grad_pack(left, right, lanes):
        grad = weight_grad(left, right).astype(bf16)
        return grad.reshape(depth, lanes, 2, 2, -1, grad.shape[-1])

    hidden = inputs.astype(f32)
    normed_self = (hidden * inverse_rms(hidden) * gain_self).astype(bf16)
    qkv = project(normed_self, w_qkv).astype(bf16)
    queries, kv = qkv[:, :inner], qkv[:, inner:]
    far_kv = project(encoded, w_ckv).astype(bf16)
    context, self_sums = attention_forward(queries, kv, keep_self, seeds_fore)
    first = hidden + share(project(context, w_out))
    normed_cross = (first * inverse_rms(first) * gain_cross).astype(bf16)
    cross_queries = project(normed_cross, w_cq).astype(bf16)
    cross_context, cross_sums = attention_forward(cross_queries, far_kv, keep_cross)
    second = first + share(project(cross_context, w_cout))
    normed_ff = (second * inverse_rms(second) * gain_ff).astype(bf16)
    gate = project(normed_ff, w_gate)
    upward = project(normed_ff, w_up)
    middle = gated(gate, upward).astype(bf16)
    third = own_half(second) + share_half(project(middle, w_down))
    output = (third * own_half(valid)).astype(bf16)

    top = upstream.astype(f32) * valid
    top_low = top.astype(bf16)
    _, pullback = jax.vjp(gated, gate, upward)
    gate_grad, upward_grad = pullback(project_back(top_low, w_down))
    gate_grad = gate_grad.astype(bf16)
    upward_grad = upward_grad.astype(bf16)
    change, gain_ff_terms = rms_back(
        second, gain_ff, share(project_back(gate_grad, w_gate) + project_back(upward_grad, w_up))
    )
    g_down = grad_pack(middle, top_low, 1)
    g_gate = grad_pack(normed_ff, gate_grad, 2)
    g_up = grad_pack(normed_ff, upward_grad, 2)
    (r_gate, r_up, r_down), (q_gate, q_up, _), (output,), _ = reduce_over_chips(
        depth, 1, [g_gate, g_up, g_down], [output]
    )
    second_grad = top + change
    cross_grad = second_grad.astype(bf16)
    g_cout = grad_pack(cross_context, cross_grad, 1)
    cross_up = project_back(cross_grad, w_cout).astype(bf16)
    dqc, dkc, dvc = attention_backward(
        cross_queries, far_kv, cross_context, cross_up, cross_sums, keep_cross
    )
    dkvc = jnp.concatenate([dkc, dvc], axis=1)
    g_cq = grad_pack(normed_cross, dqc, 2)
    g_ckv = grad_pack(encoded, dkvc, 2)
    memory_grad = share_half(project_back(dkvc, w_ckv)).astype(bf16)
    change, gain_cross_terms = rms_back(first, gain_cross, share(project_back(dqc, w_cq)))
    first_grad = second_grad + change
    self_grad = first_grad.astype(bf16)
    g_out = grad_pack(context, self_grad, 1)
    self_up = project_back(self_grad, w_out).astype(bf16)
    dq, dk, dv, diagonal = attention_backward(
        queries, kv, context, self_up, self_sums, keep_self, seeds_back
    )
    dqkv = jnp.concatenate([dq, dk, dv], axis=1)
    g_qkv = grad_pack(normed_self, dqkv, 2)
    change, gain_self_terms = rms_back(
        own_half(hidden), gain_self, share_half(project_back(dqkv, w_qkv))
    )
    input_grad = (own_half(first_grad) + change).astype(bf16)

    terms = [
        jnp.sum(own_half(gain_ff_terms), axis=(0, 1)),
        jnp.sum(own_half(gain_cross_terms), axis=(0, 1)),
        jnp.sum(gain_self_terms, axis=(0, 1)),
    ]
    diagonal = sum(jnp.roll(diagonal[:, :, r], -r, axis=-1) for r in range(8))
    blocks = jnp.zeros((diagonal.shape[0], 5, QB), f32)
    blocks = blocks.at[:, 1:].add(diagonal[:, :, :QB]).at[:, :4].add(diagonal[:, :, QB:])
    distances = blocks[:, 1:].reshape(-1, tokens)
    bias_terms = lax.dot_general(onehot, distances, (((0,), (1,)), ((), ())), precision=HIGH)
    bias_terms = bias_terms.reshape(BUCKETS, 4, 1, 2)
    bias_terms = jnp.concatenate(
        [jnp.where(core == 0, bias_terms, 0.0), jnp.where(core == 1, bias_terms, 0.0)], axis=2
    ).reshape(-1)
    terms = jnp.concatenate(terms + [bias_terms, jnp.zeros((4096 - 3 * width - BUCKETS * HEADS,), f32)])
    (r_cout, r_cq, r_ckv, r_out, r_qkv), (_, q_cq, q_ckv, _, q_qkv), (memory_grad, input_grad), packed = (
        reduce_over_chips(
            depth,
            2,
            [g_cout, g_cq, g_ckv, g_out, g_qkv],
            [memory_grad, input_grad],
            terms.reshape(32, 128),
        )
    )
    packed = packed.reshape(-1)
    mine = lax.axis_index("dp") * 4 + spot.corner
    piece = width // (depth * 8)
    n_ff, n_cross, n_self = (
        lax.dynamic_slice_in_dim(packed, i * width + mine * piece, piece) for i in range(3)
    )
    bias_grad = packed[3 * width : 3 * width + BUCKETS * HEADS].reshape(BUCKETS, HEADS)
    bias_grad = lax.dynamic_slice(
        bias_grad, (lax.axis_index("dp") * rel_bias.shape[0], spot.corner * rel_bias.shape[1]), rel_bias.shape
    )

    def merge(own, got):
        rows = own.shape[0]
        got = got.astype(f32)
        even, odd = jnp.where(core == 0, own, got), jnp.where(core == 0, got, own)
        return jnp.stack([even.reshape(rows, 4, -1), odd.reshape(rows, 4, -1)], axis=2).reshape(rows, -1)

    half = inner // 2
    return (
        output.reshape(layer_input.shape),
        input_grad.astype(f32).reshape(layer_input.shape),
        memory_grad.astype(f32).reshape(memory.shape),
        n_self,
        merge(r_qkv[:, :inner], q_qkv[:, :inner]),
        merge(r_qkv[:, inner : inner + half], q_qkv[:, inner : inner + half]),
        merge(r_qkv[:, inner + half :], q_qkv[:, inner + half :]),
        r_out,
        bias_grad,
        n_cross,
        merge(r_cq, q_cq),
        merge(r_ckv[:, :half], q_ckv[:, :half]),
        merge(r_ckv[:, half:], q_ckv[:, half:]),
        r_cout,
        n_ff,
        merge(r_gate, q_gate),
        merge(r_up, q_up),
        r_down,
    )


def solution(mesh):
    placed = (
        P(None, "dp", "seq", None),
        P(None, "dp", "seq", None),
        P(None, "dp"),
        P(None, "dp"),
        P(),
        P("dp"),
        P("dp", None),
        P("dp", None),
        P("dp", None),
        P("dp", None),
        P("dp", "seq"),
        P("dp"),
        P("dp", None),
        P("dp", None),
        P("dp", None),
        P("dp", None),
        P("dp"),
        P("dp", None),
        P("dp", None),
        P("dp", None),
        P(None, "dp", "seq", None),
    )
    chips = mesh.shape["seq"] == 4 and mesh.shape["dp"] == HEADS // 2
    return jax.shard_map(
        per_chip if chips else per_device,
        mesh=mesh,
        in_specs=placed,
        out_specs=(
            P(None, "dp", "seq", None),
            P(None, "dp", "seq", None),
            P(None, "dp", "seq", None),
            P(("dp", "seq")),
            P(("dp", "seq"), None),
            P(("dp", "seq"), None),
            P(("dp", "seq"), None),
            P(("dp", "seq"), None),
            P("dp", "seq"),
            P(("dp", "seq")),
            P(("dp", "seq"), None),
            P(("dp", "seq"), None),
            P(("dp", "seq"), None),
            P(("dp", "seq"), None),
            P(("dp", "seq")),
            P(("dp", "seq"), None),
            P(("dp", "seq"), None),
            P(("dp", "seq"), None),
        ),
        check_vma=False,
    )
```

```python
import functools

import jax
import jax.numpy as jnp
from jax import lax
from jax.experimental import pallas as pl
from jax.experimental.pallas import tpu as pltpu
from jax.sharding import PartitionSpec as P

HEADS = 16
HEAD_DIM = 64
BUCKETS = 32
KV_HEADS = 8
TGT = 1024
MEM = 512
QB = 256


EPS = 1e-06
NEG = -1e30
HIGH = lax.Precision.HIGHEST


def shortened(shard):
    return jax.tree.map(lambda a: a.astype(jnp.bfloat16) if a.dtype == jnp.float32 else a, shard)


def rms_norm(value, gain):
    return value * lax.rsqrt(jnp.mean(value * value, axis=-1, keepdims=True) + EPS) * gain


def gated(gate, upward):
    return jax.nn.gelu(gate, approximate=True) * upward


def project(left, right):
    return jnp.dot(left, right, preferred_element_type=jnp.float32)


def project_back(grad, weight):
    return lax.dot_general(
        grad, weight, (((1,), (1,)), ((), ())), preferred_element_type=jnp.float32
    )


def weight_grad(left, right):
    return lax.dot_general(
        left, right, (((0,), (0,)), ((), ())), preferred_element_type=jnp.float32
    )


def split_heads(values, group):
    return values.reshape(values.shape[:2] + (-1, group, HEAD_DIM))


def split_shared(values):
    return values.reshape(values.shape[:2] + (-1, HEAD_DIM))


def causal_masks(table, length, group):

    def masks(start, block):
        stop = start + block
        rows = start + jnp.arange(block, dtype=jnp.int32)
        columns = jnp.arange(stop, dtype=jnp.int32)
        distance = rows[:, None] - columns[None, :]
        keep = (distance >= 0) & (columns[None, :] < length)
        extra = jnp.take(table, jnp.maximum(distance, 0), axis=1)
        return (extra.reshape((-1, group, block, stop)), keep, stop)

    return masks


def memory_masks(length, width):

    def masks(start, block):
        keep = jnp.broadcast_to(
            jnp.arange(width, dtype=jnp.int32)[None, :] < length, (block, width)
        )
        return (None, keep, width)

    return masks


def diagonal_sums(grads, block, stop):
    leading = grads.shape[:2]
    flipped = jnp.pad(grads[..., ::-1], ((0, 0), (0, 0), (0, 0), (0, block)))
    skewed = flipped.reshape(leading + (block * (stop + block),))[..., : block * (stop + block - 1)]
    skewed = skewed.reshape(leading + (block, stop + block - 1))
    return jnp.sum(skewed, axis=2)[..., block - 1 :]


def attend_forward(queries, keys, values, masks):
    block = min(512, queries.shape[0])
    outputs = []
    totals = []
    for index in range(queries.shape[0] // block):
        start = index * block
        extra, keep, stop = masks(start, block)
        rows = queries[start : start + block]
        scores = jnp.einsum("rkgd,skd->kgrs", rows, keys[:stop], preferred_element_type=jnp.float32)
        if extra is not None:
            scores = scores + extra
        scores = jnp.where(keep, scores, NEG)
        peak = jnp.max(scores, axis=-1, keepdims=True)
        weights = jnp.where(keep, jnp.exp(scores - peak), 0.0)
        total = jnp.sum(weights, axis=-1, keepdims=True)
        probs = (weights / total).astype(jnp.bfloat16)
        mixed = jnp.einsum(
            "kgrs,skd->rkgd", probs, values[:stop], preferred_element_type=jnp.float32
        )
        outputs.append(mixed.astype(jnp.bfloat16))
        totals.append(peak + jnp.log(total))
    return (jnp.concatenate(outputs, 0), jnp.concatenate(totals, 2))


def attend_backward(queries, keys, values, sums, grads, masks):
    block = min(512, queries.shape[0])
    key_grads = jnp.zeros(keys.shape, jnp.float32)
    value_grads = jnp.zeros(values.shape, jnp.float32)
    diagonal = jnp.zeros(sums.shape[:3], jnp.float32)
    query_grads = []
    for index in range(queries.shape[0] // block):
        start = index * block
        extra, keep, stop = masks(start, block)
        rows = queries[start : start + block]
        grad_rows = grads[start : start + block]
        scores = jnp.einsum("rkgd,skd->kgrs", rows, keys[:stop], preferred_element_type=jnp.float32)
        if extra is not None:
            scores = scores + extra
        scores = jnp.where(keep, scores, NEG)
        probs = jnp.where(keep, jnp.exp(scores - sums[:, :, start : start + block]), 0.0)
        value_grads = value_grads.at[:stop].add(
            jnp.einsum(
                "kgrs,rkgd->skd",
                probs.astype(jnp.bfloat16),
                grad_rows,
                preferred_element_type=jnp.float32,
            )
        )
        dprobs = jnp.einsum(
            "rkgd,skd->kgrs", grad_rows, values[:stop], preferred_element_type=jnp.float32
        )
        delta = jnp.sum(probs * dprobs, axis=-1, keepdims=True)
        dscores = (probs * (dprobs - delta)).astype(jnp.bfloat16)
        query_grads.append(
            jnp.einsum(
                "kgrs,skd->rkgd", dscores, keys[:stop], preferred_element_type=jnp.float32
            ).astype(jnp.bfloat16)
        )
        key_grads = key_grads.at[:stop].add(
            jnp.einsum("kgrs,rkgd->skd", dscores, rows, preferred_element_type=jnp.float32)
        )
        if extra is not None:
            diagonal = diagonal.at[:, :, :stop].add(
                diagonal_sums(dscores.astype(jnp.float32), block, stop)
            )
    return (
        jnp.concatenate(query_grads, 0),
        key_grads.astype(jnp.bfloat16),
        value_grads.astype(jnp.bfloat16),
        diagonal,
    )


def self_forward(queries, keys, values, length, table):
    return attend_forward(queries, keys, values, causal_masks(table, length, queries.shape[2]))


def self_backward(queries, keys, values, sums, grads, length, table):
    return attend_backward(
        queries, keys, values, sums, grads, causal_masks(table, length, queries.shape[2])
    )


def cross_forward(queries, keys, values, length):
    return attend_forward(queries, keys, values, memory_masks(length, keys.shape[0]))


def cross_backward(queries, keys, values, sums, grads, length):
    return attend_backward(queries, keys, values, sums, grads, memory_masks(length, keys.shape[0]))


def to_tokens(values):
    return lax.all_to_all(shortened(values), "seq", split_axis=1, concat_axis=2, tiled=True).astype(
        values.dtype
    )


def to_heads(grads):
    return lax.all_to_all(grads, "seq", split_axis=2, concat_axis=1, tiled=True)


def per_device(
    layer_input,
    memory,
    target_lengths,
    memory_lengths,
    buckets,
    norm_self,
    self_q,
    self_k,
    self_v,
    self_out,
    rel_bias,
    norm_cross,
    cross_q,
    cross_k,
    cross_v,
    cross_out,
    norm_ff,
    ff_gate,
    ff_up,
    ff_down,
    cotangent,
):
    micro_count, batch_rows, local_tokens, model_width = layer_input.shape
    memory_tokens = memory.shape[2]
    group = HEADS // KV_HEADS
    replicas = lax.axis_size("dp")
    shards = (
        norm_self,
        self_q,
        self_k,
        self_v,
        self_out,
        rel_bias,
        norm_cross,
        cross_q,
        cross_k,
        cross_v,
        cross_out,
        norm_ff,
        ff_gate,
        ff_up,
        ff_down,
    )
    totals = [
        jnp.zeros((piece.shape[0] * replicas,) + piece.shape[1:], jnp.float32) for piece in shards
    ]
    onehot = (buckets[:, None] == jnp.arange(BUCKETS, dtype=jnp.int32)[None, :]).astype(jnp.float32)
    places = lax.axis_index("seq") * local_tokens + jnp.arange(local_tokens, dtype=jnp.int32)
    diagonal = jnp.zeros((rel_bias.shape[1] // group, group, TGT), jnp.float32)
    outputs = []
    input_grads = []
    memory_grads = []
    for micro_step in range(micro_count):
        gathered = (
            lax.all_gather(norm_self, "dp", axis=0, tiled=True),
            lax.all_gather(self_q, "dp", axis=0, tiled=True),
            lax.all_gather(self_k, "dp", axis=0, tiled=True),
            lax.all_gather(self_v, "dp", axis=0, tiled=True),
            lax.all_gather(self_out, "dp", axis=0, tiled=True),
            lax.all_gather(rel_bias, "dp", axis=0, tiled=True),
            lax.all_gather(norm_cross, "dp", axis=0, tiled=True),
            lax.all_gather(cross_q, "dp", axis=0, tiled=True),
            lax.all_gather(cross_k, "dp", axis=0, tiled=True),
            lax.all_gather(cross_v, "dp", axis=0, tiled=True),
            lax.all_gather(cross_out, "dp", axis=0, tiled=True),
            lax.all_gather(norm_ff, "dp", axis=0, tiled=True),
            lax.all_gather(ff_gate, "dp", axis=0, tiled=True),
            lax.all_gather(ff_up, "dp", axis=0, tiled=True),
            lax.all_gather(ff_down, "dp", axis=0, tiled=True),
        )
        (
            gain_self,
            query_self,
            key_self,
            value_self,
            output_self,
            bias_whole,
            gain_cross,
            query_cross,
            key_cross,
            value_cross,
            output_cross,
            gain_ff,
            gate_weight,
            up_weight,
            down_weight,
        ) = gathered
        gain_self = gain_self.astype(jnp.float32)
        gain_cross = gain_cross.astype(jnp.float32)
        gain_ff = gain_ff.astype(jnp.float32)
        table = lax.dot_general(
            bias_whole.astype(jnp.float32), onehot, (((0,), (1,)), ((), ())), precision=HIGH
        )
        lengths = target_lengths[micro_step]
        spans = memory_lengths[micro_step]
        valid = (places[None, :] < lengths[:, None]).astype(jnp.float32).reshape(-1, 1)
        hidden = layer_input[micro_step].reshape(-1, model_width).astype(jnp.float32)
        normed_self = rms_norm(hidden, gain_self).astype(jnp.bfloat16)
        queries = (
            project(normed_self, query_self)
            .astype(jnp.bfloat16)
            .reshape(batch_rows, local_tokens, -1)
        )
        keys = (
            project(normed_self, key_self)
            .astype(jnp.bfloat16)
            .reshape(batch_rows, local_tokens, -1)
        )
        values = (
            project(normed_self, value_self)
            .astype(jnp.bfloat16)
            .reshape(batch_rows, local_tokens, -1)
        )
        encoded = memory[micro_step].reshape(-1, model_width)
        memory_keys = (
            project(encoded, key_cross).astype(jnp.bfloat16).reshape(batch_rows, memory_tokens, -1)
        )
        memory_values = (
            project(encoded, value_cross)
            .astype(jnp.bfloat16)
            .reshape(batch_rows, memory_tokens, -1)
        )
        head_queries, head_keys, head_values, far_keys, far_values = (
            lax.all_to_all(queries, "seq", split_axis=2, concat_axis=1, tiled=True),
            lax.all_to_all(keys, "seq", split_axis=2, concat_axis=1, tiled=True),
            lax.all_to_all(values, "seq", split_axis=2, concat_axis=1, tiled=True),
            lax.all_to_all(memory_keys, "seq", split_axis=2, concat_axis=1, tiled=True),
            lax.all_to_all(memory_values, "seq", split_axis=2, concat_axis=1, tiled=True),
        )
        self_queries = split_heads(head_queries, group)
        self_keys = split_shared(head_keys)
        self_values = split_shared(head_values)
        far_keys = split_shared(far_keys)
        far_values = split_shared(far_values)
        attended, self_sums = jax.vmap(self_forward, in_axes=(0, 0, 0, 0, None))(
            self_queries, self_keys, self_values, lengths, table
        )
        context = to_tokens(attended.reshape(batch_rows, TGT, -1)).reshape(
            batch_rows * local_tokens, -1
        )
        first = hidden + project(context, output_self)
        normed_cross = rms_norm(first, gain_cross).astype(jnp.bfloat16)
        cross_queries = (
            project(normed_cross, query_cross)
            .astype(jnp.bfloat16)
            .reshape(batch_rows, local_tokens, -1)
        )
        cross_heads = split_heads(
            lax.all_to_all(cross_queries, "seq", split_axis=2, concat_axis=1, tiled=True), group
        )
        cross_attended, cross_sums = jax.vmap(cross_forward)(
            cross_heads, far_keys, far_values, spans
        )
        cross_context = to_tokens(cross_attended.reshape(batch_rows, TGT, -1)).reshape(
            batch_rows * local_tokens, -1
        )
        second = first + project(cross_context, output_cross)
        normed_ff = rms_norm(second, gain_ff).astype(jnp.bfloat16)
        gate = project(normed_ff, gate_weight)
        upward = project(normed_ff, up_weight)
        middle = gated(gate, upward).astype(jnp.bfloat16)
        third = second + project(middle, down_weight)
        outputs.append(
            (third * valid).astype(jnp.bfloat16).reshape(batch_rows, local_tokens, model_width)
        )
        upstream = cotangent[micro_step].reshape(-1, model_width).astype(jnp.float32) * valid
        down_grad = upstream.astype(jnp.bfloat16)
        totals[14] = totals[14] + weight_grad(middle, down_grad)
        _, pullback = jax.vjp(gated, gate, upward)
        gate_grad, upward_grad = pullback(project_back(down_grad, down_weight))
        gate_grad = gate_grad.astype(jnp.bfloat16)
        upward_grad = upward_grad.astype(jnp.bfloat16)
        totals[12] = totals[12] + weight_grad(normed_ff, gate_grad)
        totals[13] = totals[13] + weight_grad(normed_ff, upward_grad)
        _, pullback = jax.vjp(rms_norm, second, gain_ff)
        second_grad, gain_grad = pullback(
            project_back(gate_grad, gate_weight) + project_back(upward_grad, up_weight)
        )
        totals[11] = totals[11] + gain_grad
        second_grad = second_grad + upstream
        cross_grad = second_grad.astype(jnp.bfloat16)
        totals[10] = totals[10] + weight_grad(cross_context, cross_grad)
        context_grad = (
            project_back(cross_grad, output_cross)
            .astype(jnp.bfloat16)
            .reshape(batch_rows, local_tokens, -1)
        )
        cross_query_grad, far_key_grad, far_value_grad, _ = jax.vmap(cross_backward)(
            cross_heads,
            far_keys,
            far_values,
            cross_sums,
            split_heads(to_heads(context_grad), group),
            spans,
        )
        query_back, key_back, value_back = (
            lax.all_to_all(
                shortened(cross_query_grad.reshape(batch_rows, TGT, -1)),
                "seq",
                split_axis=1,
                concat_axis=2,
                tiled=True,
            ),
            lax.all_to_all(
                shortened(far_key_grad.reshape(batch_rows, MEM, -1)),
                "seq",
                split_axis=1,
                concat_axis=2,
                tiled=True,
            ),
            lax.all_to_all(
                shortened(far_value_grad.reshape(batch_rows, MEM, -1)),
                "seq",
                split_axis=1,
                concat_axis=2,
                tiled=True,
            ),
        )
        query_back = query_back.reshape(batch_rows * local_tokens, -1)
        key_back = key_back.reshape(batch_rows * memory_tokens, -1)
        value_back = value_back.reshape(batch_rows * memory_tokens, -1)
        totals[7] = totals[7] + weight_grad(normed_cross, query_back)
        totals[8] = totals[8] + weight_grad(encoded, key_back)
        totals[9] = totals[9] + weight_grad(encoded, value_back)
        memory_grads.append(
            (project_back(key_back, key_cross) + project_back(value_back, value_cross)).reshape(
                batch_rows, memory_tokens, model_width
            )
        )
        _, pullback = jax.vjp(rms_norm, first, gain_cross)
        first_grad, gain_grad = pullback(project_back(query_back, query_cross))
        totals[6] = totals[6] + gain_grad
        first_grad = first_grad + second_grad
        self_grad = first_grad.astype(jnp.bfloat16)
        totals[4] = totals[4] + weight_grad(context, self_grad)
        context_grad = (
            project_back(self_grad, output_self)
            .astype(jnp.bfloat16)
            .reshape(batch_rows, local_tokens, -1)
        )
        query_grad, key_grad, value_grad, bias_grad = jax.vmap(
            self_backward, in_axes=(0, 0, 0, 0, 0, 0, None)
        )(
            self_queries,
            self_keys,
            self_values,
            self_sums,
            split_heads(to_heads(context_grad), group),
            lengths,
            table,
        )
        diagonal = diagonal + jnp.sum(bias_grad, axis=0)
        query_back, key_back, value_back = (
            lax.all_to_all(
                shortened(query_grad.reshape(batch_rows, TGT, -1)),
                "seq",
                split_axis=1,
                concat_axis=2,
                tiled=True,
            ),
            lax.all_to_all(
                shortened(key_grad.reshape(batch_rows, TGT, -1)),
                "seq",
                split_axis=1,
                concat_axis=2,
                tiled=True,
            ),
            lax.all_to_all(
                shortened(value_grad.reshape(batch_rows, TGT, -1)),
                "seq",
                split_axis=1,
                concat_axis=2,
                tiled=True,
            ),
        )
        query_back = query_back.reshape(batch_rows * local_tokens, -1)
        key_back = key_back.reshape(batch_rows * local_tokens, -1)
        value_back = value_back.reshape(batch_rows * local_tokens, -1)
        totals[1] = totals[1] + weight_grad(normed_self, query_back)
        totals[2] = totals[2] + weight_grad(normed_self, key_back)
        totals[3] = totals[3] + weight_grad(normed_self, value_back)
        _, pullback = jax.vjp(rms_norm, hidden, gain_self)
        hidden_grad, gain_grad = pullback(
            project_back(query_back, query_self)
            + project_back(key_back, key_self)
            + project_back(value_back, value_self)
        )
        totals[0] = totals[0] + gain_grad
        input_grads.append(
            (hidden_grad + first_grad).reshape(batch_rows, local_tokens, model_width)
        )
    totals[5] = lax.dot_general(
        onehot, diagonal.reshape(-1, TGT), (((0,), (1,)), ((), ())), precision=HIGH
    )
    reduced = (
        lax.psum_scatter(totals[0], ("dp", "seq"), scatter_dimension=0, tiled=True),
        lax.psum_scatter(totals[1], ("dp", "seq"), scatter_dimension=0, tiled=True),
        lax.psum_scatter(totals[2], ("dp", "seq"), scatter_dimension=0, tiled=True),
        lax.psum_scatter(totals[3], ("dp", "seq"), scatter_dimension=0, tiled=True),
        lax.psum_scatter(totals[4], ("dp", "seq"), scatter_dimension=0, tiled=True),
        lax.psum_scatter(totals[6], ("dp", "seq"), scatter_dimension=0, tiled=True),
        lax.psum_scatter(totals[7], ("dp", "seq"), scatter_dimension=0, tiled=True),
        lax.psum_scatter(totals[8], ("dp", "seq"), scatter_dimension=0, tiled=True),
        lax.psum_scatter(totals[9], ("dp", "seq"), scatter_dimension=0, tiled=True),
        lax.psum_scatter(totals[10], ("dp", "seq"), scatter_dimension=0, tiled=True),
        lax.psum_scatter(totals[11], ("dp", "seq"), scatter_dimension=0, tiled=True),
        lax.psum_scatter(totals[12], ("dp", "seq"), scatter_dimension=0, tiled=True),
        lax.psum_scatter(totals[13], ("dp", "seq"), scatter_dimension=0, tiled=True),
        lax.psum_scatter(totals[14], ("dp", "seq"), scatter_dimension=0, tiled=True),
    )
    bias_share = lax.psum_scatter(totals[5], "dp", scatter_dimension=0, tiled=True)
    return (
        jnp.stack(outputs),
        jnp.stack(input_grads),
        jnp.stack(memory_grads),
        reduced[0],
        reduced[1],
        reduced[2],
        reduced[3],
        reduced[4],
        bias_share,
        reduced[5],
        reduced[6],
        reduced[7],
        reduced[8],
        reduced[9],
        reduced[10],
        reduced[11],
        reduced[12],
        reduced[13],
    )


def row_pieces(full):
    blocks = full.reshape(full.shape[0], -1, QB)
    return jnp.concatenate([blocks[:, 1:], blocks[:, :-1]], axis=2)


def seed_rows(vectors):
    return jnp.stack([jnp.roll(vectors, r, axis=-1) for r in range(8)], axis=-2)


def spread(seed):
    rows = 8
    tile = seed
    while rows < QB:
        tile = jnp.concatenate([tile, pltpu.roll(tile, rows, 1)], axis=0)
        rows *= 2
    return tile[:, :QB]


def fold(tile):
    width = 2 * QB
    tile = jnp.concatenate([tile, jnp.zeros_like(tile)], axis=1)
    rows = QB
    while rows > 8:
        rows //= 2
        tile = tile[:rows] + pltpu.roll(tile[rows:], width - rows, 1)
    return tile


def nt(left, right):
    return lax.dot_general(left, right, (((1,), (1,)), ((), ())), preferred_element_type=jnp.float32)


def tn(left, right):
    return lax.dot_general(left, right, (((0,), (0,)), ((), ())), preferred_element_type=jnp.float32)


def nn(left, right):
    return lax.dot_general(left, right, (((1,), (0,)), ((), ())), preferred_element_type=jnp.float32)


def forward_kernel(causal, q_ref, k_ref, v_ref, keep_ref, *rest):
    if causal:
        seed_ref, o_ref, lse_ref, bias = rest
    else:
        o_ref, lse_ref = rest
    span = k_ref.shape[0]
    for kv in range(2):
        lanes = slice(kv * HEAD_DIM, (kv + 1) * HEAD_DIM)
        keys = k_ref[:, lanes]
        values = v_ref[:, lanes]
        if causal:
            for member in range(2):
                for offset in range(4):
                    bias[member * QB : (member + 1) * QB, (3 - offset) * QB : (4 - offset) * QB] = spread(
                        seed_ref[2 * kv + member, offset]
                    )
        for block in range(q_ref.shape[0] // QB):
            stop = (block + 1) * QB if causal else span
            rows = slice(block * QB, (block + 1) * QB)
            both = q_ref[rows, 2 * kv * HEAD_DIM : 2 * (kv + 1) * HEAD_DIM]
            query = jnp.concatenate([both[:, :HEAD_DIM], both[:, HEAD_DIM:]], axis=0)
            scores = nt(query, keys[:stop]) + keep_ref[:, :stop]
            if causal:
                scores = scores + bias[:, (3 - block) * QB : (3 - block) * QB + stop]
            peak = jnp.max(scores, axis=1, keepdims=True)
            weights = jnp.exp(scores - peak)
            total = jnp.sum(weights, axis=1, keepdims=True)
            mixed = nn(weights.astype(jnp.bfloat16), values[:stop]) / total
            o_ref[rows, 2 * kv * HEAD_DIM : 2 * (kv + 1) * HEAD_DIM] = jnp.concatenate(
                [mixed[:QB], mixed[QB:]], axis=1
            ).astype(jnp.bfloat16)
            sums = jnp.broadcast_to(peak + jnp.log(total), (2 * QB, 128)).T
            lse_ref[2 * kv : 2 * kv + 1, rows] = sums[:1, :QB]
            lse_ref[2 * kv + 1 : 2 * kv + 2, rows] = sums[:1, QB:]


def backward_kernel(causal, q_ref, k_ref, v_ref, o_ref, do_ref, lse_ref, keep_ref, *rest):
    if causal:
        seed_ref, dq_ref, dk_ref, dv_ref, diag_ref, bias, sums, dk_sum, dv_sum = rest
    else:
        dq_ref, dk_ref, dv_ref, dk_sum, dv_sum = rest
    span = k_ref.shape[0]
    blocks = q_ref.shape[0] // QB
    for kv in range(2):
        lanes = slice(kv * HEAD_DIM, (kv + 1) * HEAD_DIM)
        dk_sum[...] = jnp.zeros_like(dk_sum)
        dv_sum[...] = jnp.zeros_like(dv_sum)
        if causal:
            for member in range(2):
                for offset in range(4):
                    bias[offset, :, member * QB : (member + 1) * QB] = spread(
                        seed_ref[2 * kv + member, offset]
                    )
            sums[...] = jnp.zeros_like(sums)
        for block in range(blocks):
            rows = slice(block * QB, (block + 1) * QB)
            both = slice(2 * kv * HEAD_DIM, 2 * (kv + 1) * HEAD_DIM)
            pair = q_ref[rows, both]
            query = jnp.concatenate([pair[:, :HEAD_DIM], pair[:, HEAD_DIM:]], axis=0)
            upstream = do_ref[rows, both]
            grads = jnp.concatenate([upstream[:, :HEAD_DIM], upstream[:, HEAD_DIM:]], axis=0)
            inner = (upstream.astype(jnp.float32) * o_ref[rows, both].astype(jnp.float32)).T
            delta = jnp.concatenate(
                [
                    jnp.sum(inner[:HEAD_DIM], axis=0, keepdims=True),
                    jnp.sum(inner[HEAD_DIM:], axis=0, keepdims=True),
                ],
                axis=1,
            )
            level = jnp.concatenate(
                [lse_ref[2 * kv : 2 * kv + 1, rows], lse_ref[2 * kv + 1 : 2 * kv + 2, rows]], axis=1
            )
            dq = jnp.zeros((2 * QB, HEAD_DIM), jnp.float32)
            for part in range(block + 1 if causal else span // QB):
                columns = slice(part * QB, (part + 1) * QB)
                keys = k_ref[columns, lanes]
                values = v_ref[columns, lanes]
                scores = nt(keys, query) + keep_ref[columns]
                if causal:
                    scores = scores + bias[block - part]
                probs = jnp.exp(scores - level)
                dscores = probs * (nt(values, grads) - delta)
                if causal:
                    sums[block - part] += dscores
                dscores = dscores.astype(jnp.bfloat16)
                dv_sum[columns] += nn(probs.astype(jnp.bfloat16), grads)
                dk_sum[columns] += nn(dscores, query)
                dq += tn(dscores, keys)
            dq_ref[rows, both] = jnp.concatenate([dq[:QB], dq[QB:]], axis=1).astype(jnp.bfloat16)
        dk_ref[:, lanes] = dk_sum[...].astype(jnp.bfloat16)
        dv_ref[:, lanes] = dv_sum[...].astype(jnp.bfloat16)
        if causal:
            for member in range(2):
                for offset in range(4):
                    diag_ref[2 * kv + member, offset] = fold(
                        sums[offset, :, member * QB : (member + 1) * QB]
                    )


PARAMS = pltpu.CompilerParams(vmem_limit_bytes=56 * 2**20)


def attention_forward(queries, kv, keep, seeds=None):
    tokens, width = queries.shape
    span = kv.shape[0]
    heads = width // HEAD_DIM
    causal = seeds is not None
    in_specs = [
        pl.BlockSpec((tokens, 256), lambda i: (0, i)),
        pl.BlockSpec((span, 128), lambda i: (0, i)),
        pl.BlockSpec((span, 128), lambda i: (0, i + 2)),
        pl.BlockSpec((1, span), lambda i: (0, 0)),
    ]
    operands = [queries, kv, kv, keep.reshape(1, span)]
    scratch = []
    if causal:
        in_specs.append(pl.BlockSpec((4, 4, 8, 512), lambda i: (i, 0, 0, 0)))
        operands.append(seeds)
        scratch.append(pltpu.VMEM((2 * QB, 4 * QB), jnp.float32))
    work = heads * tokens * span // (2 if causal else 1)
    context, sums = pl.pallas_call(
        functools.partial(forward_kernel, causal),
        grid=(heads // 4,),
        in_specs=in_specs,
        out_specs=[
            pl.BlockSpec((tokens, 256), lambda i: (0, i)),
            pl.BlockSpec((None, 4, tokens), lambda i: (i, 0, 0)),
        ],
        out_shape=[
            jax.ShapeDtypeStruct((tokens, width), jnp.bfloat16),
            jax.ShapeDtypeStruct((heads // 4, 4, tokens), jnp.float32),
        ],
        scratch_shapes=scratch,
        compiler_params=PARAMS,
        cost_estimate=pl.CostEstimate(
            flops=work * 4 * 4 * HEAD_DIM, bytes_accessed=4 * 2**20, transcendentals=work
        ),
    )(*operands)
    return context, sums


def attention_backward(queries, kv, context, grads, sums, keep, seeds=None):
    tokens, width = queries.shape
    span = kv.shape[0]
    heads = width // HEAD_DIM
    causal = seeds is not None
    wide = pl.BlockSpec((tokens, 256), lambda i: (0, i))
    narrow = pl.BlockSpec((span, 128), lambda i: (0, i))
    in_specs = [
        wide,
        narrow,
        pl.BlockSpec((span, 128), lambda i: (0, i + 2)),
        wide,
        wide,
        pl.BlockSpec((None, 4, tokens), lambda i: (i, 0, 0)),
        pl.BlockSpec((span, 1), lambda i: (0, 0)),
    ]
    operands = [queries, kv, kv, context, grads, sums, keep.reshape(span, 1)]
    out_specs = [wide, narrow, narrow]
    out_shape = [
        jax.ShapeDtypeStruct((tokens, width), jnp.bfloat16),
        jax.ShapeDtypeStruct((span, width // 2), jnp.bfloat16),
        jax.ShapeDtypeStruct((span, width // 2), jnp.bfloat16),
    ]
    scratch = []
    if causal:
        quad = pl.BlockSpec((4, 4, 8, 512), lambda i: (i, 0, 0, 0))
        in_specs.append(quad)
        operands.append(seeds)
        out_specs.append(quad)
        out_shape.append(jax.ShapeDtypeStruct((heads, 4, 8, 512), jnp.float32))
        scratch = [pltpu.VMEM((4, QB, 2 * QB), jnp.float32), pltpu.VMEM((4, QB, 2 * QB), jnp.float32)]
    scratch += [pltpu.VMEM((span, HEAD_DIM), jnp.float32), pltpu.VMEM((span, HEAD_DIM), jnp.float32)]
    work = heads * tokens * span // (2 if causal else 1)
    return pl.pallas_call(
        functools.partial(backward_kernel, causal),
        grid=(heads // 4,),
        in_specs=in_specs,
        out_specs=out_specs,
        out_shape=out_shape,
        scratch_shapes=scratch,
        compiler_params=PARAMS,
        cost_estimate=pl.CostEstimate(
            flops=work * 10 * 4 * HEAD_DIM, bytes_accessed=8 * 2**20, transcendentals=work
        ),
    )(*operands)


def inverse_rms(value):
    return lax.rsqrt(jnp.mean(value * value, axis=-1, keepdims=True) + EPS)


def rms_back(value, gain, upstream):
    inverse = inverse_rms(value)
    scaled = upstream * gain
    mean = jnp.mean(value * scaled, axis=-1, keepdims=True)
    return inverse * scaled - value * (inverse * inverse * inverse) * mean, upstream * value * inverse


def pick(array, index, axis=0):
    return lax.dynamic_index_in_dim(array, index, axis, keepdims=False)


MESH = pl.DeviceIdType.MESH


class Spot:
    def __init__(self, depth):
        self.depth = depth
        place = lax.axis_index("dp")
        self.corner = lax.axis_index("seq")
        self.z, self.core = place // 2, place % 2
        self.y, self.x = self.corner // 2, self.corner % 2

    def at(self, z=None, core=None, y=None, x=None):
        z = self.z if z is None else z
        core = self.core if core is None else core
        y = self.y if y is None else y
        x = self.x if x is None else x
        return (z * 2 + core, y * 2 + x)

    def beside(self):
        return self.at(x=1 - self.x)

    def below(self):
        return self.at(y=1 - self.y)

    def sibling(self):
        return self.at(core=1 - self.core)

    def greet(self):
        barrier = pltpu.get_barrier_semaphore()
        others = [
            self.at(None, self.core ^ (i >> 2), self.y ^ (i >> 1 & 1), self.x ^ (i & 1)) for i in range(1, 8)
        ]
        for step in range(1, self.depth):
            for flip in range(2):
                others.append(self.at((self.z + step) % self.depth, self.core ^ flip))
        for other in others:
            pl.semaphore_signal(barrier, inc=1, device_id=other, device_id_type=MESH)
        pl.semaphore_wait(barrier, len(others))


class Wires:
    def __init__(self, sends, arrivals, moves):
        self.sends, self.arrivals, self.moves = sends, arrivals, moves
        self.count = 0
        self.moved = 0
        self.open = []

    def take(self, number):
        first = self.count
        self.count += number
        return first

    def send(self, source, target, device, index, landing=None):
        landing = index if landing is None else landing
        copy = pltpu.make_async_remote_copy(
            src_ref=source,
            dst_ref=target,
            send_sem=self.sends.at[index],
            recv_sem=self.arrivals.at[landing],
            device_id=device,
            device_id_type=MESH,
        )
        copy.start()
        self.open.append(copy)
        return copy

    def arrive(self, target, device, index):
        pltpu.make_async_remote_copy(
            src_ref=target,
            dst_ref=target,
            send_sem=self.sends.at[0],
            recv_sem=self.arrivals.at[index],
            device_id=device,
            device_id_type=MESH,
        ).wait_recv()

    def move(self, source, target):
        copy = pltpu.make_async_copy(source, target, self.moves.at[self.moved])
        self.moved += 1
        copy.start()
        return copy

    def close(self):
        for copy in self.open:
            copy.wait_send()
        self.open = []


def collect_tokens(spot, wires, parcel, whole):
    away = wires.take(4)
    over = wires.take(4)
    local = wires.moved
    wires.moved += 1
    for index in range(4):
        half, micro = spot.y ^ (index >> 1), spot.x ^ (index & 1)
        home = (half == spot.core) & (micro == spot.y) & (spot.core == spot.x)
        source = parcel.at[micro, half]
        target = whole.at[spot.corner, half]
        copy = pltpu.make_async_remote_copy(
            src_ref=source,
            dst_ref=target,
            send_sem=wires.sends.at[away + index],
            recv_sem=wires.arrivals.at[away + index],
            device_id=spot.at(core=half, y=micro, x=spot.core),
            device_id_type=MESH,
        )
        here = pltpu.make_async_copy(source, target, wires.moves.at[local])

        @pl.when(jnp.logical_not(home))
        def _():
            copy.start()

        @pl.when(home)
        def _():
            here.start()

    yield
    for index in range(4):
        block = 2 * (spot.core ^ (index >> 1)) + (spot.y ^ (index & 1))
        home = (spot.x == spot.core) & (block == spot.corner)
        piece = whole.at[block, spot.core]
        here = pltpu.make_async_copy(piece, piece, wires.moves.at[local])
        landed = pltpu.make_async_remote_copy(
            src_ref=piece,
            dst_ref=piece,
            send_sem=wires.sends.at[away + index],
            recv_sem=wires.arrivals.at[away + index],
            device_id=spot.sibling(),
            device_id_type=MESH,
        )

        @pl.when(jnp.logical_not(home))
        def _():
            landed.wait_recv()

        @pl.when(home)
        def _():
            here.wait()

        wires.send(piece, piece, spot.sibling(), over + index)
    yield
    for index in range(4):
        block = 2 * ((1 - spot.core) ^ (index >> 1)) + (spot.y ^ (index & 1))
        wires.arrive(whole.at[block, 1 - spot.core], spot.sibling(), over + index)
    for index in range(4):
        half, micro = spot.y ^ (index >> 1), spot.x ^ (index & 1)
        home = (half == spot.core) & (micro == spot.y) & (spot.core == spot.x)
        source = parcel.at[micro, half]

        @pl.when(jnp.logical_not(home))
        def _():
            pltpu.make_async_remote_copy(
                src_ref=source,
                dst_ref=source,
                send_sem=wires.sends.at[away + index],
                recv_sem=wires.arrivals.at[away + index],
                device_id=spot.sibling(),
                device_id_type=MESH,
            ).wait_send()

    yield


def deliver_tokens(spot, wires, pieces, homes):
    away = wires.take(4)
    local = wires.moved
    wires.moved += 1

    def parts():
        for index in range(4):
            block = 2 * (spot.core ^ (index >> 1)) + (spot.y ^ (index & 1))
            home = (spot.x == spot.core) & (block == spot.corner)
            source = pieces.at[block]
            target = homes.at[spot.y, spot.core]
            remote = pltpu.make_async_remote_copy(
                src_ref=source,
                dst_ref=target,
                send_sem=wires.sends.at[away + index],
                recv_sem=wires.arrivals.at[away + index],
                device_id=spot.at(core=spot.x, y=block // 2, x=block % 2),
                device_id_type=MESH,
            )
            yield home, remote, pltpu.make_async_copy(source, target, wires.moves.at[local])

    for home, remote, here in parts():
        pl.when(jnp.logical_not(home))(remote.start)
        pl.when(home)(here.start)
    yield
    for index in range(4):
        half, micro = spot.y ^ (index >> 1), spot.x ^ (index & 1)
        home = (half == spot.core) & (micro == spot.y) & (spot.core == spot.x)
        piece = homes.at[micro, half]
        landed = pltpu.make_async_remote_copy(
            src_ref=piece,
            dst_ref=piece,
            send_sem=wires.sends.at[away + index],
            recv_sem=wires.arrivals.at[away + index],
            device_id=spot.sibling(),
            device_id_type=MESH,
        )
        here = pltpu.make_async_copy(piece, piece, wires.moves.at[local])
        pl.when(jnp.logical_not(home))(landed.wait_recv)
        pl.when(home)(here.wait)
    for home, remote, here in parts():
        pl.when(jnp.logical_not(home))(remote.wait_send)
    yield


def gather_small(spot, wires, block, whole):
    own = wires.move(block, whole.at[spot.z, spot.core, spot.corner])
    first = wires.take(spot.depth + 3)
    for step in range(1, spot.depth):
        target = whole.at[spot.z, spot.core, spot.corner]
        wires.send(block, target, spot.at(z=(spot.z + step) % spot.depth), first + step)
    yield
    own.wait()
    for step in range(1, spot.depth):
        z = (spot.z - step + spot.depth) % spot.depth
        wires.arrive(whole.at[z, spot.core, spot.corner], spot.sibling(), first + step)
    column = whole.at[:, spot.core, spot.corner]
    wires.send(column, column, spot.beside(), first)
    wires.send(column, column, spot.below(), first + spot.depth)
    wires.send(column, column, spot.at(y=1 - spot.y, x=1 - spot.x), first + spot.depth + 1)
    yield
    for flip, index in ((1, first), (2, first + spot.depth), (3, first + spot.depth + 1)):
        wires.arrive(whole.at[:, spot.core, spot.corner ^ flip], spot.sibling(), index)
    plane = whole.at[:, spot.core]
    wires.send(plane, plane, spot.sibling(), first + spot.depth + 2)
    yield
    wires.arrive(whole.at[:, 1 - spot.core], spot.sibling(), first + spot.depth + 2)
    yield


def gather_columns(spot, wires, pack, whole):
    depth, me = spot.depth, spot.corner
    ahead = wires.take(2 * depth)
    flat = wires.take(4 * depth)
    own = wires.move(pack.at[spot.core], whole.at[spot.z, spot.core])
    for step in range(1, depth):
        for flip in range(2):
            wires.send(
                pack.at[spot.core ^ flip, me],
                whole.at[spot.z, spot.core, me],
                spot.at((spot.z + step) % depth, spot.core ^ flip),
                ahead + 2 * step + flip,
            )
    wires.send(pack.at[1 - spot.core], whole.at[spot.z, spot.core], spot.sibling(), ahead)
    yield
    for step in range(1, depth):
        z = (spot.z - step + depth) % depth
        for flip in range(2):
            wires.arrive(whole.at[z, spot.core ^ flip, me], spot.sibling(), ahead + 2 * step + flip)
        quarter = whole.at[z, :, me]
        wires.send(quarter, quarter, spot.beside(), flat + 4 * step)
        wires.send(quarter, quarter, spot.below(), flat + 4 * step + 1)
    yield
    for step in range(1, depth):
        z = (spot.z - step + depth) % depth
        wires.arrive(whole.at[z, :, me ^ 1], spot.sibling(), flat + 4 * step)
        piece = whole.at[z, 0, me ^ 1]
        wires.send(piece, piece, spot.below(), flat + 4 * step + 2)
        wires.arrive(whole.at[z, :, me ^ 2], spot.sibling(), flat + 4 * step + 1)
        piece = whole.at[z, 1, me ^ 2]
        wires.send(piece, piece, spot.beside(), flat + 4 * step + 3)
    yield
    own.wait()
    wires.arrive(whole.at[spot.z, 1 - spot.core], spot.sibling(), ahead)
    for step in range(1, depth):
        z = (spot.z - step + depth) % depth
        wires.arrive(whole.at[z, 0, me ^ 3], spot.sibling(), flat + 4 * step + 2)
        wires.arrive(whole.at[z, 1, me ^ 3], spot.sibling(), flat + 4 * step + 3)
    yield


def gather_rows(spot, wires, pack, whole):
    depth, me = spot.depth, spot.corner
    ahead = wires.take(depth)
    flat = wires.take(4 * depth)
    middle = pack.shape[-1] // 2

    def part(z, corner, side):
        if pack.shape[0] == 2:
            return whole.at[side, z, corner]
        return whole.at[0, z, corner, :, pl.ds(side * middle, middle)]

    own = wires.move(pack, whole.at[:, spot.z])
    for step in range(1, depth):
        wires.send(
            pack.at[:, me], whole.at[:, spot.z, me], spot.at((spot.z + step) % depth), ahead + step
        )
    yield
    for step in range(1, depth):
        z = (spot.z - step + depth) % depth
        quarter = whole.at[:, z, me]
        wires.arrive(quarter, spot.sibling(), ahead + step)
        wires.send(quarter, quarter, spot.beside(), flat + 4 * step)
        wires.send(quarter, quarter, spot.below(), flat + 4 * step + 1)
    yield
    for step in range(1, depth):
        z = (spot.z - step + depth) % depth
        wires.arrive(whole.at[:, z, me ^ 1], spot.sibling(), flat + 4 * step)
        piece = part(z, me ^ 1, 0)
        wires.send(piece, piece, spot.below(), flat + 4 * step + 2)
        wires.arrive(whole.at[:, z, me ^ 2], spot.sibling(), flat + 4 * step + 1)
        piece = part(z, me ^ 2, 1)
        wires.send(piece, piece, spot.beside(), flat + 4 * step + 3)
    yield
    own.wait()
    for step in range(1, depth):
        z = (spot.z - step + depth) % depth
        wires.arrive(part(z, me ^ 3, 0), spot.sibling(), flat + 4 * step + 2)
        wires.arrive(part(z, me ^ 3, 1), spot.sibling(), flat + 4 * step + 3)
    yield


def add_into(target, other, places):
    for place in places:
        target[place] = (
            target[place].astype(jnp.float32) + other[place].astype(jnp.float32)
        ).astype(jnp.bfloat16)


def scatter_buffers(depth, lanes, rows, width):
    half = depth // 2
    return [
        pltpu.VMEM((half, lanes, 2, rows, width), jnp.bfloat16),
        pltpu.VMEM((half, lanes, 2, rows, width), jnp.bfloat16),
        pltpu.VMEM((half, lanes, 2, rows, width), jnp.bfloat16),
        pltpu.VMEM((half, lanes, 2, rows, width), jnp.bfloat16),
        pltpu.VMEM((half, lanes, rows, width), jnp.bfloat16),
        pltpu.VMEM((half, lanes, rows, width), jnp.bfloat16),
        pltpu.VMEM((depth, lanes, rows, width), jnp.bfloat16),
        pltpu.VMEM((depth, lanes, rows, width), jnp.bfloat16),
        pltpu.VMEM((rows, width), jnp.bfloat16),
    ]


def scatter_sums(spot, wires, grads, buffers, total, got):
    depth, half = spot.depth, spot.depth // 2
    lanes = grads.shape[1]
    low, high, low_in, high_in, low_last, high_last, column, column_in, passing = buffers
    first = wires.take(4)
    away = wires.take(depth)
    mine = [
        wires.move(grads.at[pl.ds(0, half), :, :, spot.x], low),
        wires.move(grads.at[pl.ds(half, half), :, spot.y], high),
    ]
    wires.send(grads.at[pl.ds(0, half), :, :, 1 - spot.x], low_in, spot.beside(), first)
    wires.send(grads.at[pl.ds(half, half), :, 1 - spot.y], high_in, spot.below(), first + 1)
    yield
    for copy in mine:
        copy.wait()
    wires.arrive(low_in, spot.beside(), first)
    add_into(low, low_in, [(z, a, s) for z in range(half) for a in range(lanes) for s in range(2)])
    wires.send(low.at[:, :, 1 - spot.y], low_last, spot.below(), first + 2)
    wires.arrive(high_in, spot.below(), first + 1)
    add_into(high, high_in, [(z, a, s) for z in range(half) for a in range(lanes) for s in range(2)])
    wires.send(high.at[:, :, 1 - spot.x], high_last, spot.beside(), first + 3)
    yield
    wires.arrive(low_last, spot.below(), first + 2)
    wires.arrive(high_last, spot.beside(), first + 3)
    for z in range(half):
        for a in range(lanes):
            column[z, a] = (
                low[z, a, spot.y].astype(jnp.float32) + low_last[z, a].astype(jnp.float32)
            ).astype(jnp.bfloat16)
            column[half + z, a] = (
                high[z, a, spot.x].astype(jnp.float32) + high_last[z, a].astype(jnp.float32)
            ).astype(jnp.bfloat16)
    for step in range(1, depth):
        z = (spot.z + step) % depth
        wires.send(column.at[z], column_in.at[step], spot.at(z), away + step)
    yield
    for step in range(1, depth):
        wires.arrive(column_in.at[step], spot.sibling(), away + step)

    def added(lane):
        result = column[spot.z, lane].astype(jnp.float32)
        for step in range(1, depth):
            result = result + column_in[step, lane].astype(jnp.float32)
        return result

    if lanes == 1:
        total[...] = added(0)
    else:
        passing[...] = added(1 - spot.core).astype(jnp.bfloat16)
        wires.send(passing, got, spot.sibling(), away)
        total[...] = added(spot.core)
    yield
    if lanes == 2:
        wires.arrive(got, spot.sibling(), away)
    yield


def total_small(spot, wires, terms, work, total):
    first = wires.take(3 + spot.depth)
    work[0] = terms[...]
    wires.send(work.at[0], work.at[1], spot.sibling(), first)
    yield
    wires.arrive(work.at[1], spot.sibling(), first)
    work[2] = work[0] + work[1]
    wires.send(work.at[2], work.at[3], spot.beside(), first + 1)
    yield
    wires.arrive(work.at[3], spot.sibling(), first + 1)
    work[4] = work[2] + work[3]
    wires.send(work.at[4], work.at[5], spot.below(), first + 2)
    yield
    wires.arrive(work.at[5], spot.sibling(), first + 2)
    work[6] = work[4] + work[5]
    for step in range(1, spot.depth):
        target = work.at[6 + step]
        wires.send(work.at[6], target, spot.at((spot.z + step) % spot.depth), first + 2 + step)
    yield
    result = work[6]
    for step in range(1, spot.depth):
        wires.arrive(work.at[6 + step], spot.sibling(), first + 2 + step)
        result = result + work[6 + step]
    total[...] = result
    yield


def staggered(programs):
    live = list(enumerate(programs))
    step = 0
    while live:
        rest = []
        for start, program in reversed(live):
            if step < start or next(program, False) is not False:
                rest.append((start, program))
        live = rest[::-1]
        step += 1


def wire_scratch(number, moves):
    return [
        pltpu.SemaphoreType.DMA((number,)),
        pltpu.SemaphoreType.DMA((number,)),
        pltpu.SemaphoreType.DMA((moves,)),
    ]


def spread_row(vector):
    tile = pltpu.roll(jnp.broadcast_to(vector, (8, 2 * QB)), 0, 1, stride=1, stride_axis=0)
    return spread(tile)


def attend_block(query, keys, values, keep, bias):
    scores = nt(query, keys) + keep
    if bias is not None:
        scores = scores + bias
    peak = jnp.max(scores, axis=1, keepdims=True)
    weights = jnp.exp(scores - peak)
    total = jnp.sum(weights, axis=1, keepdims=True)
    return nn(weights.astype(jnp.bfloat16), values) / total, peak + jnp.log(total)


def pair_rows(block, kv):
    both = block[:, 2 * kv * HEAD_DIM : 2 * (kv + 1) * HEAD_DIM]
    return jnp.concatenate([both[:, :HEAD_DIM], both[:, HEAD_DIM:]], axis=0)


def normed(value, gain):
    return (value * inverse_rms(value) * gain).astype(jnp.bfloat16)


def forward_layer_kernel(depth, *refs):
    (
        x, t, m, s, p1, p2, p3, p4, p5, codes, holes,
        wx, wt, wm, ws, w1, w2, w3, w4, w5,
        a1, qkv, ctx, lse, x1, a2, qc, ckv, ctxc, lsec, x2, a3, gains, keeps, keepc, bent,
        bias, own, got, own2, got2, *sems
    ) = refs
    f32, bf16 = jnp.float32, jnp.bfloat16
    spot = Spot(depth)
    wires = Wires(*sems)
    blocks = 4
    kvs = 4
    inner = 2 * kvs * HEAD_DIM

    def rows(block):
        return slice(block * QB, (block + 1) * QB)

    spot.greet()
    tokens = collect_tokens(spot, wires, x, wx)
    small = gather_small(spot, wires, s, ws)
    first = gather_columns(spot, wires, p1, w1)
    memory = collect_tokens(spot, wires, m, wm)
    second = gather_columns(spot, wires, p2, w2)
    outs = gather_rows(spot, wires, p3, w3)
    wide = gather_columns(spot, wires, p4, w4)
    down = gather_rows(spot, wires, p5, w5)
    top = collect_tokens(spot, wires, t, wt)
    over = wires.take(2 * blocks)
    for program in (tokens, small, first, small, tokens, first):
        next(program)
    next(outs)
    next(second)
    next(memory)
    for program in (small, first, tokens, small, first):
        next(program)

    def line(row):
        return jnp.concatenate([ws[z, c, 0, row : row + 1, :] for z in range(depth) for c in range(2)], axis=1)

    for row in range(3):
        gains[row : row + 1, :] = line(row)
    counts = ws[spot.z, spot.x, 0, 3:4, :]
    length = jnp.where(spot.y == 0, counts[:, 0:1], counts[:, 1:2])
    span = jnp.where(spot.y == 0, counts[:, 2:3], counts[:, 3:4])
    places = lax.broadcasted_iota(jnp.int32, (1, blocks * QB), 1).astype(f32)
    keeps[...] = jnp.where(places < length, 0.0, NEG)
    keepc[...] = jnp.where(places[:, : keepc.shape[1]] < span, 0.0, NEG)
    table = jnp.concatenate(
        [
            ws[z, c, 0, 4:8, :] + ws[z, c, 1, 4:8, :] + ws[z, c, 2, 4:8, :] + ws[z, c, 3, 4:8, :]
            for z in range(depth)
            for c in range(2)
        ],
        axis=0,
    )
    table = jnp.where(spot.core == 0, table[:, :64], table[:, 64:]).astype(bf16)
    vectors = tn(table, codes[...])[:8] + holes[...]
    bent[...] = vectors[:, 4 * 2 * QB :]
    for kv in range(kvs):
        for member in range(2):
            for offset in range(4):
                head = 2 * kv + member
                bias[kv, member * QB : (member + 1) * QB, (3 - offset) * QB : (4 - offset) * QB] = spread_row(
                    vectors[head : head + 1, offset * 2 * QB : (offset + 1) * 2 * QB]
                )

    def attend_rows(block, queries, keys, stop, keep, mixed, sums, causal):
        for kv in range(kvs):
            lanes = slice(kv * HEAD_DIM, (kv + 1) * HEAD_DIM)
            upper = slice(inner // 2 + kv * HEAD_DIM, inner // 2 + (kv + 1) * HEAD_DIM)
            shape = None
            if causal:
                shape = bias[kv, :, (3 - block) * QB : (3 - block) * QB + stop]
            out, level = attend_block(
                pair_rows(queries[rows(block), :inner], kv),
                keys[:stop, lanes],
                keys[:stop, upper],
                keep[:, :stop],
                shape,
            )
            mixed[rows(block), 2 * kv * HEAD_DIM : 2 * (kv + 1) * HEAD_DIM] = jnp.concatenate(
                [out[:QB], out[QB:]], axis=1
            ).astype(bf16)
            level = jnp.broadcast_to(level, (2 * QB, 128)).T
            sums[2 * kv : 2 * kv + 1, rows(block)] = level[:1, :QB]
            sums[2 * kv + 1 : 2 * kv + 2, rows(block)] = level[:1, QB:]

    weight = w1[...].reshape(-1, w1.shape[-1])
    for block in range(blocks):
        value = wx[block].reshape(QB, -1).astype(f32)
        a1[rows(block), :] = normed(value, gains[0:1, :])
        qkv[rows(block), :] = nn(a1[rows(block), :], weight).astype(bf16)
        if block == 0:
            next(outs)
            next(second)
            next(wide)
        if block == 1:
            next(outs)
            next(second)
            next(memory)
        if block == 2:
            next(outs)
            next(second)
            next(memory)
            next(wide)
            next(down)
        attend_rows(block, qkv, qkv.at[:, inner:], (block + 1) * QB, keeps, ctx, lse, True)

    def pass_on(block, mine, theirs, value, weight, index):
        mine[rows(block), :] = nn(value[rows(block), :], weight).astype(bf16)
        wires.send(mine.at[rows(block)], theirs.at[rows(block)], spot.sibling(), over + index + block)

    def joined(block, mine, theirs, index):
        wires.arrive(theirs.at[rows(block)], spot.sibling(), over + index + block)
        return mine[rows(block), :].astype(f32) + theirs[rows(block), :].astype(f32)

    weight = w3[0].reshape(-1, w3.shape[-1])
    for block in range(blocks):
        pass_on(block, own, got, ctx, weight, 0)
    next(wide)
    next(down)
    next(top)
    weight = w2[...].reshape(-1, w2.shape[-1])
    ckv[...] = nn(wm[...].reshape(-1, wm.shape[-1]), weight[:, :inner]).astype(bf16)
    for block in range(blocks):
        value = wx[block].reshape(QB, -1).astype(f32) + joined(block, own, got, 0)
        x1[rows(block), :] = value
        a2[rows(block), :] = normed(value, gains[1:2, :])
        qc[rows(block), :] = nn(a2[rows(block), :], weight[:, inner:]).astype(bf16)
    weight = w3[1].reshape(-1, w3.shape[-1])
    for block in range(blocks):
        attend_rows(block, qc, ckv, ckv.shape[0], keepc, ctxc, lsec, False)
        pass_on(block, own2, got2, ctxc, weight, blocks)
        if block == 1:
            next(down)
            next(top)
    for block in range(blocks):
        value = x1[rows(block), :] + joined(block, own2, got2, blocks)
        x2[rows(block), :] = value
        a3[rows(block), :] = normed(value, gains[2:3, :])
    for program in (wide, down, top):
        next(program)
    for program in (tokens, small, first, memory, second, outs, wide, down, top):
        assert next(program, None) is None
    wires.close()


def forward_layer(depth, x, t, m, small, p1, p2, p3, p4, p5, codes, holes):
    bf16, f32 = jnp.bfloat16, jnp.float32
    shape = jax.ShapeDtypeStruct

    def whole_columns(pack):
        return shape((depth, 2) + pack.shape[1:], bf16)

    def whole_rows(pack):
        return shape((pack.shape[0], depth) + pack.shape[1:], bf16)

    def whole_tokens(parcel):
        return shape((4, 2) + parcel.shape[2:], bf16)

    width = x.shape[-1]
    tokens = 8 * x.shape[2]
    span = 8 * m.shape[2]
    inner = p3.shape[0] * p3.shape[1] * p3.shape[2] * depth // 2
    heads = inner // HEAD_DIM
    hbm = pl.BlockSpec(memory_space=pl.ANY)
    vmem = pl.BlockSpec(memory_space=pltpu.VMEM)
    outs = [
        (whole_tokens(x), vmem),
        (whole_tokens(t), hbm),
        (whole_tokens(m), vmem),
        (shape((depth, 2, 4, 8, 128), f32), vmem),
        (whole_columns(p1), vmem),
        (whole_columns(p2), vmem),
        (whole_rows(p3), vmem),
        (whole_columns(p4), hbm),
        (whole_rows(p5), hbm),
        (shape((tokens, width), bf16), vmem),
        (shape((tokens, 2 * inner), bf16), vmem),
        (shape((tokens, inner), bf16), vmem),
        (shape((heads, tokens), f32), vmem),
        (shape((tokens, width), f32), vmem),
        (shape((tokens, width), bf16), vmem),
        (shape((tokens, inner), bf16), vmem),
        (shape((span, inner), bf16), vmem),
        (shape((tokens, inner), bf16), vmem),
        (shape((heads, tokens), f32), vmem),
        (shape((tokens, width), f32), vmem),
        (shape((tokens, width), bf16), vmem),
        (shape((8, width), f32), vmem),
        (shape((1, tokens), f32), vmem),
        (shape((1, span), f32), vmem),
        (shape((heads, 8 * QB), f32), vmem),
    ]
    swap = pltpu.VMEM((tokens, width), bf16)
    return pl.pallas_call(
        functools.partial(forward_layer_kernel, depth),
        in_specs=[hbm] * 9 + [vmem] * 2,
        out_specs=[spec for _, spec in outs],
        out_shape=[kind for kind, _ in outs],
        scratch_shapes=[pltpu.VMEM((heads // 2, 2 * QB, 4 * QB), f32), swap, swap, swap, swap]
        + wire_scratch(35 + 30 * depth, 12),
        compiler_params=pltpu.CompilerParams(
            collective_id=0, has_side_effects=True, vmem_limit_bytes=60 * 2**20
        ),
        cost_estimate=pl.CostEstimate(
            flops=16 * 10**9, bytes_accessed=128 * 2**20, transcendentals=10**7
        ),
    )(x, t, m, small, p1, p2, p3, p4, p5, codes, holes)


def reduce_kernel(depth, lanes, tokens, small, *refs):
    spot = Spot(depth)
    refs = list(refs)
    take = lambda n: [refs.pop(0) for _ in range(n)]
    grads = take(len(lanes))
    pieces = take(tokens)
    terms = take(1 if small else 0)
    totals = take(len(lanes))
    gots = [take(1)[0] if count == 2 else None for count in lanes]
    homes = take(tokens)
    sums = take(1 if small else 0)
    buffers = [take(9) for _ in lanes]
    work = take(1 if small else 0)
    wires = Wires(*refs)
    spot.greet()
    programs = [deliver_tokens(spot, wires, *pair) for pair in zip(pieces, homes)]
    if small:
        programs.append(total_small(spot, wires, terms[0], work[0], sums[0]))
    programs += [
        scatter_sums(spot, wires, grad, scratch, total, got)
        for grad, scratch, total, got in zip(grads, buffers, totals, gots)
    ]
    staggered(programs)
    wires.close()


def reduce_over_chips(depth, identity, grads, pieces=(), terms=None):
    lanes = tuple(g.shape[1] for g in grads)
    hbm = pl.BlockSpec(memory_space=pl.ANY)
    vmem = pl.BlockSpec(memory_space=pltpu.VMEM)
    extra = 0 if terms is None else 1
    out_shape = [jax.ShapeDtypeStruct(g.shape[4:], jnp.float32) for g in grads]
    out_shape += [jax.ShapeDtypeStruct(g.shape[4:], jnp.bfloat16) for g in grads if g.shape[1] == 2]
    out_shape += [jax.ShapeDtypeStruct((2, 2) + p.shape[1:], p.dtype) for p in pieces]
    out_shape += [jax.ShapeDtypeStruct((32, 128), jnp.float32)] * extra
    out_specs = [vmem] * (len(grads) + sum(n == 2 for n in lanes)) + [hbm] * len(pieces) + [vmem] * extra
    scratch = []
    for grad in grads:
        scratch += scatter_buffers(depth, grad.shape[1], *grad.shape[4:])
    scratch += [pltpu.VMEM((6 + depth, 32, 128), jnp.float32)] * extra
    number = len(grads) * (4 + depth) + 4 * len(pieces) + extra * (3 + depth)
    results = pl.pallas_call(
        functools.partial(reduce_kernel, depth, lanes, len(pieces), extra == 1),
        in_specs=[hbm] * (len(grads) + len(pieces)) + [vmem] * extra,
        out_specs=out_specs,
        out_shape=out_shape,
        scratch_shapes=scratch + wire_scratch(number, 2 * len(grads) + len(pieces) + 1),
        compiler_params=pltpu.CompilerParams(
            collective_id=identity, has_side_effects=True, vmem_limit_bytes=56 * 2**20
        ),
        cost_estimate=pl.CostEstimate(flops=0, bytes_accessed=256 * 2**20, transcendentals=0),
    )(*grads, *pieces, *(() if terms is None else (terms,)))
    results = list(results)
    totals = [results.pop(0) for _ in grads]
    gots = [results.pop(0) if n == 2 else None for n in lanes]
    homes = [results.pop(0) for _ in pieces]
    return totals, gots, homes, results[0] if extra else None


def parity_columns(weight):
    rows, columns = weight.shape
    return jnp.moveaxis(weight.reshape(rows, 4, 2, columns // 8), 2, 0).reshape(2, rows, columns // 2)


def per_chip(
    layer_input,
    memory,
    target_lengths,
    memory_lengths,
    buckets,
    norm_self,
    self_q,
    self_k,
    self_v,
    self_out,
    rel_bias,
    norm_cross,
    cross_q,
    cross_k,
    cross_v,
    cross_out,
    norm_ff,
    ff_gate,
    ff_up,
    ff_down,
    cotangent,
):
    bf16, f32 = jnp.bfloat16, jnp.float32
    depth = lax.axis_size("dp") // 2
    spot = Spot(depth)
    core = spot.core
    width = layer_input.shape[3]
    local = layer_input.shape[2]
    near = memory.shape[2]
    shard = norm_self.shape[0]

    def column_pack(weights):
        pack = jnp.concatenate([parity_columns(w) for w in weights], axis=2)
        return pack.reshape(2, 4, -1, pack.shape[2])

    heads = jnp.arange(4)
    spots = (heads // 2) * 64 + 2 * spot.corner + heads % 2
    placed = jnp.sum(
        jnp.where(jnp.arange(128)[None, None, :] == spots[None, :, None], rel_bias[:, :, None].astype(f32), 0.0),
        axis=1,
    )
    lengths = jnp.concatenate([target_lengths, memory_lengths]).reshape(1, 4).astype(f32)
    small = jnp.concatenate(
        [
            jnp.stack([norm_self, norm_cross, norm_ff]).astype(f32),
            jnp.pad(lengths, ((0, 0), (0, 124))),
            placed,
        ]
    )
    padded = jnp.concatenate([jnp.full((1, QB), -1, jnp.int32), buckets[None, :]], axis=1)
    vectors = row_pieces(padded)
    vectors = jnp.concatenate([jnp.roll(vectors[..., ::-1], 1, axis=-1), vectors], axis=1).reshape(1, -1)
    codes = (vectors == jnp.arange(BUCKETS, dtype=jnp.int32)[:, None]).astype(bf16)
    holes = jnp.where(vectors < 0, NEG, 0.0).astype(f32)
    onehot = (buckets[:, None] == jnp.arange(BUCKETS, dtype=jnp.int32)[None, :]).astype(f32)
    (
        inputs, upstream, encoded, _, w_qkv, w_cross, w_outs, w_gu, w_down,
        normed_self, qkv, context, self_sums, first, normed_cross, cross_queries, far_kv, cross_context,
        cross_sums, second, normed_ff, gains, keep_self, keep_cross, bent,
    ) = forward_layer(
        depth,
        layer_input.reshape(2, 2, local // 2, width),
        cotangent.reshape(2, 2, local // 2, width),
        memory.reshape(2, 2, near // 2, width),
        small,
        column_pack([self_q, self_k, self_v]),
        column_pack([cross_k, cross_v, cross_q]),
        jnp.stack([self_out, cross_out]).reshape(2, 4, -1, width),
        column_pack([ff_gate, ff_up]),
        ff_down.reshape(1, 4, -1, width),
        codes,
        holes,
    )
    inputs, upstream, encoded = (a.reshape(-1, width) for a in (inputs, upstream, encoded))
    w_qkv, w_cross, w_gu, w_down = (a.reshape(-1, a.shape[-1]) for a in (w_qkv, w_cross, w_gu, w_down))
    w_out, w_cout = w_outs[0].reshape(-1, width), w_outs[1].reshape(-1, width)
    inner = self_q.shape[1] // 2
    w_ckv, w_cq = w_cross[:, :inner], w_cross[:, inner:]
    hidden_width = w_gu.shape[1] // 2
    w_gate, w_up = w_gu[:, :hidden_width], w_gu[:, hidden_width:]
    gain_self, gain_cross, gain_ff = gains[0], gains[1], gains[2]
    queries, kv = qkv[:, :inner], qkv[:, inner:]
    self_sums, cross_sums = self_sums.reshape(2, 4, -1), cross_sums.reshape(2, 4, -1)
    seeds_back = seed_rows(bent.reshape(-1, 4, 2 * QB))
    tokens = inputs.shape[0]
    hidden = inputs.astype(f32)
    valid = (keep_self[0] == 0).astype(f32)[:, None]

    def swap_core(array):
        pairs = [
            (place * 4 + corner, (place ^ 1) * 4 + corner) for place in range(2 * depth) for corner in range(4)
        ]
        return lax.ppermute(array, ("dp", "seq"), pairs)

    def share(partial):
        partial = partial.astype(bf16)
        return partial.astype(f32) + swap_core(partial).astype(f32)

    def share_half(partial):
        partial = partial.astype(bf16).reshape(4, 2, -1, partial.shape[-1])
        got = swap_core(pick(partial, 1 - core, 1))
        return pick(partial, core, 1).astype(f32) + got.astype(f32)

    def own_half(value):
        return pick(value.reshape(4, 2, -1, value.shape[-1]), core, 1)

    def grad_pack(left, right, lanes):
        grad = weight_grad(left, right).astype(bf16)
        return grad.reshape(depth, lanes, 2, 2, -1, grad.shape[-1])

    gate = project(normed_ff, w_gate)
    upward = project(normed_ff, w_up)
    middle = gated(gate, upward).astype(bf16)
    third = own_half(second) + share_half(project(middle, w_down))
    output = (third * own_half(valid)).astype(bf16)

    top = upstream.astype(f32) * valid
    top_low = top.astype(bf16)
    _, pullback = jax.vjp(gated, gate, upward)
    gate_grad, upward_grad = pullback(project_back(top_low, w_down))
    gate_grad = gate_grad.astype(bf16)
    upward_grad = upward_grad.astype(bf16)
    change, gain_ff_terms = rms_back(
        second, gain_ff, share(project_back(gate_grad, w_gate) + project_back(upward_grad, w_up))
    )
    g_down = grad_pack(middle, top_low, 1)
    g_gate = grad_pack(normed_ff, gate_grad, 2)
    g_up = grad_pack(normed_ff, upward_grad, 2)
    (r_gate, r_up, r_down), (q_gate, q_up, _), (output,), _ = reduce_over_chips(
        depth, 1, [g_gate, g_up, g_down], [output]
    )
    second_grad = top + change
    cross_grad = second_grad.astype(bf16)
    g_cout = grad_pack(cross_context, cross_grad, 1)
    cross_up = project_back(cross_grad, w_cout).astype(bf16)
    dqc, dkc, dvc = attention_backward(
        cross_queries, far_kv, cross_context, cross_up, cross_sums, keep_cross
    )
    dkvc = jnp.concatenate([dkc, dvc], axis=1)
    g_cq = grad_pack(normed_cross, dqc, 2)
    g_ckv = grad_pack(encoded, dkvc, 2)
    memory_grad = share_half(project_back(dkvc, w_ckv)).astype(bf16)
    change, gain_cross_terms = rms_back(first, gain_cross, share(project_back(dqc, w_cq)))
    first_grad = second_grad + change
    self_grad = first_grad.astype(bf16)
    g_out = grad_pack(context, self_grad, 1)
    self_up = project_back(self_grad, w_out).astype(bf16)
    dq, dk, dv, diagonal = attention_backward(
        queries, kv, context, self_up, self_sums, keep_self, seeds_back
    )
    dqkv = jnp.concatenate([dq, dk, dv], axis=1)
    g_qkv = grad_pack(normed_self, dqkv, 2)
    change, gain_self_terms = rms_back(
        own_half(hidden), gain_self, share_half(project_back(dqkv, w_qkv))
    )
    input_grad = (own_half(first_grad) + change).astype(bf16)

    terms = [
        jnp.sum(own_half(gain_ff_terms), axis=(0, 1)),
        jnp.sum(own_half(gain_cross_terms), axis=(0, 1)),
        jnp.sum(gain_self_terms, axis=(0, 1)),
    ]
    diagonal = sum(jnp.roll(diagonal[:, :, r], -r, axis=-1) for r in range(8))
    blocks = jnp.zeros((diagonal.shape[0], 5, QB), f32)
    blocks = blocks.at[:, 1:].add(diagonal[:, :, :QB]).at[:, :4].add(diagonal[:, :, QB:])
    distances = blocks[:, 1:].reshape(-1, tokens)
    bias_terms = lax.dot_general(onehot, distances, (((0,), (1,)), ((), ())), precision=HIGH)
    bias_terms = bias_terms.reshape(BUCKETS, 4, 1, 2)
    bias_terms = jnp.concatenate(
        [jnp.where(core == 0, bias_terms, 0.0), jnp.where(core == 1, bias_terms, 0.0)], axis=2
    ).reshape(-1)
    terms = jnp.concatenate(terms + [bias_terms, jnp.zeros((4096 - 3 * width - BUCKETS * HEADS,), f32)])
    (r_cout, r_cq, r_ckv, r_out, r_qkv), (_, q_cq, q_ckv, _, q_qkv), (memory_grad, input_grad), packed = (
        reduce_over_chips(
            depth,
            2,
            [g_cout, g_cq, g_ckv, g_out, g_qkv],
            [memory_grad, input_grad],
            terms.reshape(32, 128),
        )
    )
    packed = packed.reshape(-1)
    mine = lax.axis_index("dp") * 4 + spot.corner
    piece = width // (depth * 8)
    n_ff, n_cross, n_self = (
        lax.dynamic_slice_in_dim(packed, i * width + mine * piece, piece) for i in range(3)
    )
    bias_grad = packed[3 * width : 3 * width + BUCKETS * HEADS].reshape(BUCKETS, HEADS)
    bias_grad = lax.dynamic_slice(
        bias_grad, (lax.axis_index("dp") * rel_bias.shape[0], spot.corner * rel_bias.shape[1]), rel_bias.shape
    )

    def merge(own, got):
        rows = own.shape[0]
        got = got.astype(f32)
        even, odd = jnp.where(core == 0, own, got), jnp.where(core == 0, got, own)
        return jnp.stack([even.reshape(rows, 4, -1), odd.reshape(rows, 4, -1)], axis=2).reshape(rows, -1)

    half = inner // 2
    return (
        output.reshape(layer_input.shape),
        input_grad.astype(f32).reshape(layer_input.shape),
        memory_grad.astype(f32).reshape(memory.shape),
        n_self,
        merge(r_qkv[:, :inner], q_qkv[:, :inner]),
        merge(r_qkv[:, inner : inner + half], q_qkv[:, inner : inner + half]),
        merge(r_qkv[:, inner + half :], q_qkv[:, inner + half :]),
        r_out,
        bias_grad,
        n_cross,
        merge(r_cq, q_cq),
        merge(r_ckv[:, :half], q_ckv[:, :half]),
        merge(r_ckv[:, half:], q_ckv[:, half:]),
        r_cout,
        n_ff,
        merge(r_gate, q_gate),
        merge(r_up, q_up),
        r_down,
    )


def solution(mesh):
    placed = (
        P(None, "dp", "seq", None),
        P(None, "dp", "seq", None),
        P(None, "dp"),
        P(None, "dp"),
        P(),
        P("dp"),
        P("dp", None),
        P("dp", None),
        P("dp", None),
        P("dp", None),
        P("dp", "seq"),
        P("dp"),
        P("dp", None),
        P("dp", None),
        P("dp", None),
        P("dp", None),
        P("dp"),
        P("dp", None),
        P("dp", None),
        P("dp", None),
        P(None, "dp", "seq", None),
    )
    chips = mesh.shape["seq"] == 4 and mesh.shape["dp"] == HEADS // 2
    return jax.shard_map(
        per_chip if chips else per_device,
        mesh=mesh,
        in_specs=placed,
        out_specs=(
            P(None, "dp", "seq", None),
            P(None, "dp", "seq", None),
            P(None, "dp", "seq", None),
            P(("dp", "seq")),
            P(("dp", "seq"), None),
            P(("dp", "seq"), None),
            P(("dp", "seq"), None),
            P(("dp", "seq"), None),
            P("dp", "seq"),
            P(("dp", "seq")),
            P(("dp", "seq"), None),
            P(("dp", "seq"), None),
            P(("dp", "seq"), None),
            P(("dp", "seq"), None),
            P(("dp", "seq")),
            P(("dp", "seq"), None),
            P(("dp", "seq"), None),
            P(("dp", "seq"), None),
        ),
        check_vma=False,
    )
```

```python
import functools

import jax
import jax.numpy as jnp
from jax import lax
from jax.experimental import pallas as pl
from jax.experimental.pallas import tpu as pltpu
from jax.sharding import PartitionSpec as P

HEADS = 16
HEAD_DIM = 64
BUCKETS = 32
KV_HEADS = 8
TGT = 1024
MEM = 512
QB = 256


EPS = 1e-06
NEG = -1e30
HIGH = lax.Precision.HIGHEST


def shortened(shard):
    return jax.tree.map(lambda a: a.astype(jnp.bfloat16) if a.dtype == jnp.float32 else a, shard)


def rms_norm(value, gain):
    return value * lax.rsqrt(jnp.mean(value * value, axis=-1, keepdims=True) + EPS) * gain


def gated(gate, upward):
    return jax.nn.gelu(gate, approximate=True) * upward


def project(left, right):
    return jnp.dot(left, right, preferred_element_type=jnp.float32)


def project_back(grad, weight):
    return lax.dot_general(
        grad, weight, (((1,), (1,)), ((), ())), preferred_element_type=jnp.float32
    )


def weight_grad(left, right):
    return lax.dot_general(
        left, right, (((0,), (0,)), ((), ())), preferred_element_type=jnp.float32
    )


def split_heads(values, group):
    return values.reshape(values.shape[:2] + (-1, group, HEAD_DIM))


def split_shared(values):
    return values.reshape(values.shape[:2] + (-1, HEAD_DIM))


def causal_masks(table, length, group):

    def masks(start, block):
        stop = start + block
        rows = start + jnp.arange(block, dtype=jnp.int32)
        columns = jnp.arange(stop, dtype=jnp.int32)
        distance = rows[:, None] - columns[None, :]
        keep = (distance >= 0) & (columns[None, :] < length)
        extra = jnp.take(table, jnp.maximum(distance, 0), axis=1)
        return (extra.reshape((-1, group, block, stop)), keep, stop)

    return masks


def memory_masks(length, width):

    def masks(start, block):
        keep = jnp.broadcast_to(
            jnp.arange(width, dtype=jnp.int32)[None, :] < length, (block, width)
        )
        return (None, keep, width)

    return masks


def diagonal_sums(grads, block, stop):
    leading = grads.shape[:2]
    flipped = jnp.pad(grads[..., ::-1], ((0, 0), (0, 0), (0, 0), (0, block)))
    skewed = flipped.reshape(leading + (block * (stop + block),))[..., : block * (stop + block - 1)]
    skewed = skewed.reshape(leading + (block, stop + block - 1))
    return jnp.sum(skewed, axis=2)[..., block - 1 :]


def attend_forward(queries, keys, values, masks):
    block = min(512, queries.shape[0])
    outputs = []
    totals = []
    for index in range(queries.shape[0] // block):
        start = index * block
        extra, keep, stop = masks(start, block)
        rows = queries[start : start + block]
        scores = jnp.einsum("rkgd,skd->kgrs", rows, keys[:stop], preferred_element_type=jnp.float32)
        if extra is not None:
            scores = scores + extra
        scores = jnp.where(keep, scores, NEG)
        peak = jnp.max(scores, axis=-1, keepdims=True)
        weights = jnp.where(keep, jnp.exp(scores - peak), 0.0)
        total = jnp.sum(weights, axis=-1, keepdims=True)
        probs = (weights / total).astype(jnp.bfloat16)
        mixed = jnp.einsum(
            "kgrs,skd->rkgd", probs, values[:stop], preferred_element_type=jnp.float32
        )
        outputs.append(mixed.astype(jnp.bfloat16))
        totals.append(peak + jnp.log(total))
    return (jnp.concatenate(outputs, 0), jnp.concatenate(totals, 2))


def attend_backward(queries, keys, values, sums, grads, masks):
    block = min(512, queries.shape[0])
    key_grads = jnp.zeros(keys.shape, jnp.float32)
    value_grads = jnp.zeros(values.shape, jnp.float32)
    diagonal = jnp.zeros(sums.shape[:3], jnp.float32)
    query_grads = []
    for index in range(queries.shape[0] // block):
        start = index * block
        extra, keep, stop = masks(start, block)
        rows = queries[start : start + block]
        grad_rows = grads[start : start + block]
        scores = jnp.einsum("rkgd,skd->kgrs", rows, keys[:stop], preferred_element_type=jnp.float32)
        if extra is not None:
            scores = scores + extra
        scores = jnp.where(keep, scores, NEG)
        probs = jnp.where(keep, jnp.exp(scores - sums[:, :, start : start + block]), 0.0)
        value_grads = value_grads.at[:stop].add(
            jnp.einsum(
                "kgrs,rkgd->skd",
                probs.astype(jnp.bfloat16),
                grad_rows,
                preferred_element_type=jnp.float32,
            )
        )
        dprobs = jnp.einsum(
            "rkgd,skd->kgrs", grad_rows, values[:stop], preferred_element_type=jnp.float32
        )
        delta = jnp.sum(probs * dprobs, axis=-1, keepdims=True)
        dscores = (probs * (dprobs - delta)).astype(jnp.bfloat16)
        query_grads.append(
            jnp.einsum(
                "kgrs,skd->rkgd", dscores, keys[:stop], preferred_element_type=jnp.float32
            ).astype(jnp.bfloat16)
        )
        key_grads = key_grads.at[:stop].add(
            jnp.einsum("kgrs,rkgd->skd", dscores, rows, preferred_element_type=jnp.float32)
        )
        if extra is not None:
            diagonal = diagonal.at[:, :, :stop].add(
                diagonal_sums(dscores.astype(jnp.float32), block, stop)
            )
    return (
        jnp.concatenate(query_grads, 0),
        key_grads.astype(jnp.bfloat16),
        value_grads.astype(jnp.bfloat16),
        diagonal,
    )


def self_forward(queries, keys, values, length, table):
    return attend_forward(queries, keys, values, causal_masks(table, length, queries.shape[2]))


def self_backward(queries, keys, values, sums, grads, length, table):
    return attend_backward(
        queries, keys, values, sums, grads, causal_masks(table, length, queries.shape[2])
    )


def cross_forward(queries, keys, values, length):
    return attend_forward(queries, keys, values, memory_masks(length, keys.shape[0]))


def cross_backward(queries, keys, values, sums, grads, length):
    return attend_backward(queries, keys, values, sums, grads, memory_masks(length, keys.shape[0]))


def to_tokens(values):
    return lax.all_to_all(shortened(values), "seq", split_axis=1, concat_axis=2, tiled=True).astype(
        values.dtype
    )


def to_heads(grads):
    return lax.all_to_all(grads, "seq", split_axis=2, concat_axis=1, tiled=True)


def per_device(
    layer_input,
    memory,
    target_lengths,
    memory_lengths,
    buckets,
    norm_self,
    self_q,
    self_k,
    self_v,
    self_out,
    rel_bias,
    norm_cross,
    cross_q,
    cross_k,
    cross_v,
    cross_out,
    norm_ff,
    ff_gate,
    ff_up,
    ff_down,
    cotangent,
):
    micro_count, batch_rows, local_tokens, model_width = layer_input.shape
    memory_tokens = memory.shape[2]
    group = HEADS // KV_HEADS
    replicas = lax.axis_size("dp")
    shards = (
        norm_self,
        self_q,
        self_k,
        self_v,
        self_out,
        rel_bias,
        norm_cross,
        cross_q,
        cross_k,
        cross_v,
        cross_out,
        norm_ff,
        ff_gate,
        ff_up,
        ff_down,
    )
    totals = [
        jnp.zeros((piece.shape[0] * replicas,) + piece.shape[1:], jnp.float32) for piece in shards
    ]
    onehot = (buckets[:, None] == jnp.arange(BUCKETS, dtype=jnp.int32)[None, :]).astype(jnp.float32)
    places = lax.axis_index("seq") * local_tokens + jnp.arange(local_tokens, dtype=jnp.int32)
    diagonal = jnp.zeros((rel_bias.shape[1] // group, group, TGT), jnp.float32)
    outputs = []
    input_grads = []
    memory_grads = []
    for micro_step in range(micro_count):
        gathered = (
            lax.all_gather(norm_self, "dp", axis=0, tiled=True),
            lax.all_gather(self_q, "dp", axis=0, tiled=True),
            lax.all_gather(self_k, "dp", axis=0, tiled=True),
            lax.all_gather(self_v, "dp", axis=0, tiled=True),
            lax.all_gather(self_out, "dp", axis=0, tiled=True),
            lax.all_gather(rel_bias, "dp", axis=0, tiled=True),
            lax.all_gather(norm_cross, "dp", axis=0, tiled=True),
            lax.all_gather(cross_q, "dp", axis=0, tiled=True),
            lax.all_gather(cross_k, "dp", axis=0, tiled=True),
            lax.all_gather(cross_v, "dp", axis=0, tiled=True),
            lax.all_gather(cross_out, "dp", axis=0, tiled=True),
            lax.all_gather(norm_ff, "dp", axis=0, tiled=True),
            lax.all_gather(ff_gate, "dp", axis=0, tiled=True),
            lax.all_gather(ff_up, "dp", axis=0, tiled=True),
            lax.all_gather(ff_down, "dp", axis=0, tiled=True),
        )
        (
            gain_self,
            query_self,
            key_self,
            value_self,
            output_self,
            bias_whole,
            gain_cross,
            query_cross,
            key_cross,
            value_cross,
            output_cross,
            gain_ff,
            gate_weight,
            up_weight,
            down_weight,
        ) = gathered
        gain_self = gain_self.astype(jnp.float32)
        gain_cross = gain_cross.astype(jnp.float32)
        gain_ff = gain_ff.astype(jnp.float32)
        table = lax.dot_general(
            bias_whole.astype(jnp.float32), onehot, (((0,), (1,)), ((), ())), precision=HIGH
        )
        lengths = target_lengths[micro_step]
        spans = memory_lengths[micro_step]
        valid = (places[None, :] < lengths[:, None]).astype(jnp.float32).reshape(-1, 1)
        hidden = layer_input[micro_step].reshape(-1, model_width).astype(jnp.float32)
        normed_self = rms_norm(hidden, gain_self).astype(jnp.bfloat16)
        queries = (
            project(normed_self, query_self)
            .astype(jnp.bfloat16)
            .reshape(batch_rows, local_tokens, -1)
        )
        keys = (
            project(normed_self, key_self)
            .astype(jnp.bfloat16)
            .reshape(batch_rows, local_tokens, -1)
        )
        values = (
            project(normed_self, value_self)
            .astype(jnp.bfloat16)
            .reshape(batch_rows, local_tokens, -1)
        )
        encoded = memory[micro_step].reshape(-1, model_width)
        memory_keys = (
            project(encoded, key_cross).astype(jnp.bfloat16).reshape(batch_rows, memory_tokens, -1)
        )
        memory_values = (
            project(encoded, value_cross)
            .astype(jnp.bfloat16)
            .reshape(batch_rows, memory_tokens, -1)
        )
        head_queries, head_keys, head_values, far_keys, far_values = (
            lax.all_to_all(queries, "seq", split_axis=2, concat_axis=1, tiled=True),
            lax.all_to_all(keys, "seq", split_axis=2, concat_axis=1, tiled=True),
            lax.all_to_all(values, "seq", split_axis=2, concat_axis=1, tiled=True),
            lax.all_to_all(memory_keys, "seq", split_axis=2, concat_axis=1, tiled=True),
            lax.all_to_all(memory_values, "seq", split_axis=2, concat_axis=1, tiled=True),
        )
        self_queries = split_heads(head_queries, group)
        self_keys = split_shared(head_keys)
        self_values = split_shared(head_values)
        far_keys = split_shared(far_keys)
        far_values = split_shared(far_values)
        attended, self_sums = jax.vmap(self_forward, in_axes=(0, 0, 0, 0, None))(
            self_queries, self_keys, self_values, lengths, table
        )
        context = to_tokens(attended.reshape(batch_rows, TGT, -1)).reshape(
            batch_rows * local_tokens, -1
        )
        first = hidden + project(context, output_self)
        normed_cross = rms_norm(first, gain_cross).astype(jnp.bfloat16)
        cross_queries = (
            project(normed_cross, query_cross)
            .astype(jnp.bfloat16)
            .reshape(batch_rows, local_tokens, -1)
        )
        cross_heads = split_heads(
            lax.all_to_all(cross_queries, "seq", split_axis=2, concat_axis=1, tiled=True), group
        )
        cross_attended, cross_sums = jax.vmap(cross_forward)(
            cross_heads, far_keys, far_values, spans
        )
        cross_context = to_tokens(cross_attended.reshape(batch_rows, TGT, -1)).reshape(
            batch_rows * local_tokens, -1
        )
        second = first + project(cross_context, output_cross)
        normed_ff = rms_norm(second, gain_ff).astype(jnp.bfloat16)
        gate = project(normed_ff, gate_weight)
        upward = project(normed_ff, up_weight)
        middle = gated(gate, upward).astype(jnp.bfloat16)
        third = second + project(middle, down_weight)
        outputs.append(
            (third * valid).astype(jnp.bfloat16).reshape(batch_rows, local_tokens, model_width)
        )
        upstream = cotangent[micro_step].reshape(-1, model_width).astype(jnp.float32) * valid
        down_grad = upstream.astype(jnp.bfloat16)
        totals[14] = totals[14] + weight_grad(middle, down_grad)
        _, pullback = jax.vjp(gated, gate, upward)
        gate_grad, upward_grad = pullback(project_back(down_grad, down_weight))
        gate_grad = gate_grad.astype(jnp.bfloat16)
        upward_grad = upward_grad.astype(jnp.bfloat16)
        totals[12] = totals[12] + weight_grad(normed_ff, gate_grad)
        totals[13] = totals[13] + weight_grad(normed_ff, upward_grad)
        _, pullback = jax.vjp(rms_norm, second, gain_ff)
        second_grad, gain_grad = pullback(
            project_back(gate_grad, gate_weight) + project_back(upward_grad, up_weight)
        )
        totals[11] = totals[11] + gain_grad
        second_grad = second_grad + upstream
        cross_grad = second_grad.astype(jnp.bfloat16)
        totals[10] = totals[10] + weight_grad(cross_context, cross_grad)
        context_grad = (
            project_back(cross_grad, output_cross)
            .astype(jnp.bfloat16)
            .reshape(batch_rows, local_tokens, -1)
        )
        cross_query_grad, far_key_grad, far_value_grad, _ = jax.vmap(cross_backward)(
            cross_heads,
            far_keys,
            far_values,
            cross_sums,
            split_heads(to_heads(context_grad), group),
            spans,
        )
        query_back, key_back, value_back = (
            lax.all_to_all(
                shortened(cross_query_grad.reshape(batch_rows, TGT, -1)),
                "seq",
                split_axis=1,
                concat_axis=2,
                tiled=True,
            ),
            lax.all_to_all(
                shortened(far_key_grad.reshape(batch_rows, MEM, -1)),
                "seq",
                split_axis=1,
                concat_axis=2,
                tiled=True,
            ),
            lax.all_to_all(
                shortened(far_value_grad.reshape(batch_rows, MEM, -1)),
                "seq",
                split_axis=1,
                concat_axis=2,
                tiled=True,
            ),
        )
        query_back = query_back.reshape(batch_rows * local_tokens, -1)
        key_back = key_back.reshape(batch_rows * memory_tokens, -1)
        value_back = value_back.reshape(batch_rows * memory_tokens, -1)
        totals[7] = totals[7] + weight_grad(normed_cross, query_back)
        totals[8] = totals[8] + weight_grad(encoded, key_back)
        totals[9] = totals[9] + weight_grad(encoded, value_back)
        memory_grads.append(
            (project_back(key_back, key_cross) + project_back(value_back, value_cross)).reshape(
                batch_rows, memory_tokens, model_width
            )
        )
        _, pullback = jax.vjp(rms_norm, first, gain_cross)
        first_grad, gain_grad = pullback(project_back(query_back, query_cross))
        totals[6] = totals[6] + gain_grad
        first_grad = first_grad + second_grad
        self_grad = first_grad.astype(jnp.bfloat16)
        totals[4] = totals[4] + weight_grad(context, self_grad)
        context_grad = (
            project_back(self_grad, output_self)
            .astype(jnp.bfloat16)
            .reshape(batch_rows, local_tokens, -1)
        )
        query_grad, key_grad, value_grad, bias_grad = jax.vmap(
            self_backward, in_axes=(0, 0, 0, 0, 0, 0, None)
        )(
            self_queries,
            self_keys,
            self_values,
            self_sums,
            split_heads(to_heads(context_grad), group),
            lengths,
            table,
        )
        diagonal = diagonal + jnp.sum(bias_grad, axis=0)
        query_back, key_back, value_back = (
            lax.all_to_all(
                shortened(query_grad.reshape(batch_rows, TGT, -1)),
                "seq",
                split_axis=1,
                concat_axis=2,
                tiled=True,
            ),
            lax.all_to_all(
                shortened(key_grad.reshape(batch_rows, TGT, -1)),
                "seq",
                split_axis=1,
                concat_axis=2,
                tiled=True,
            ),
            lax.all_to_all(
                shortened(value_grad.reshape(batch_rows, TGT, -1)),
                "seq",
                split_axis=1,
                concat_axis=2,
                tiled=True,
            ),
        )
        query_back = query_back.reshape(batch_rows * local_tokens, -1)
        key_back = key_back.reshape(batch_rows * local_tokens, -1)
        value_back = value_back.reshape(batch_rows * local_tokens, -1)
        totals[1] = totals[1] + weight_grad(normed_self, query_back)
        totals[2] = totals[2] + weight_grad(normed_self, key_back)
        totals[3] = totals[3] + weight_grad(normed_self, value_back)
        _, pullback = jax.vjp(rms_norm, hidden, gain_self)
        hidden_grad, gain_grad = pullback(
            project_back(query_back, query_self)
            + project_back(key_back, key_self)
            + project_back(value_back, value_self)
        )
        totals[0] = totals[0] + gain_grad
        input_grads.append(
            (hidden_grad + first_grad).reshape(batch_rows, local_tokens, model_width)
        )
    totals[5] = lax.dot_general(
        onehot, diagonal.reshape(-1, TGT), (((0,), (1,)), ((), ())), precision=HIGH
    )
    reduced = (
        lax.psum_scatter(totals[0], ("dp", "seq"), scatter_dimension=0, tiled=True),
        lax.psum_scatter(totals[1], ("dp", "seq"), scatter_dimension=0, tiled=True),
        lax.psum_scatter(totals[2], ("dp", "seq"), scatter_dimension=0, tiled=True),
        lax.psum_scatter(totals[3], ("dp", "seq"), scatter_dimension=0, tiled=True),
        lax.psum_scatter(totals[4], ("dp", "seq"), scatter_dimension=0, tiled=True),
        lax.psum_scatter(totals[6], ("dp", "seq"), scatter_dimension=0, tiled=True),
        lax.psum_scatter(totals[7], ("dp", "seq"), scatter_dimension=0, tiled=True),
        lax.psum_scatter(totals[8], ("dp", "seq"), scatter_dimension=0, tiled=True),
        lax.psum_scatter(totals[9], ("dp", "seq"), scatter_dimension=0, tiled=True),
        lax.psum_scatter(totals[10], ("dp", "seq"), scatter_dimension=0, tiled=True),
        lax.psum_scatter(totals[11], ("dp", "seq"), scatter_dimension=0, tiled=True),
        lax.psum_scatter(totals[12], ("dp", "seq"), scatter_dimension=0, tiled=True),
        lax.psum_scatter(totals[13], ("dp", "seq"), scatter_dimension=0, tiled=True),
        lax.psum_scatter(totals[14], ("dp", "seq"), scatter_dimension=0, tiled=True),
    )
    bias_share = lax.psum_scatter(totals[5], "dp", scatter_dimension=0, tiled=True)
    return (
        jnp.stack(outputs),
        jnp.stack(input_grads),
        jnp.stack(memory_grads),
        reduced[0],
        reduced[1],
        reduced[2],
        reduced[3],
        reduced[4],
        bias_share,
        reduced[5],
        reduced[6],
        reduced[7],
        reduced[8],
        reduced[9],
        reduced[10],
        reduced[11],
        reduced[12],
        reduced[13],
    )


def row_pieces(full):
    blocks = full.reshape(full.shape[0], -1, QB)
    return jnp.concatenate([blocks[:, 1:], blocks[:, :-1]], axis=2)


def seed_rows(vectors):
    return jnp.stack([jnp.roll(vectors, r, axis=-1) for r in range(8)], axis=-2)


def spread(seed):
    rows = 8
    tile = seed
    while rows < QB:
        tile = jnp.concatenate([tile, pltpu.roll(tile, rows, 1)], axis=0)
        rows *= 2
    return tile[:, :QB]


def fold(tile):
    width = 2 * QB
    tile = jnp.concatenate([tile, jnp.zeros_like(tile)], axis=1)
    rows = QB
    while rows > 8:
        rows //= 2
        tile = tile[:rows] + pltpu.roll(tile[rows:], width - rows, 1)
    return tile


def nt(left, right):
    return lax.dot_general(left, right, (((1,), (1,)), ((), ())), preferred_element_type=jnp.float32)


def tn(left, right):
    return lax.dot_general(left, right, (((0,), (0,)), ((), ())), preferred_element_type=jnp.float32)


def nn(left, right):
    return lax.dot_general(left, right, (((1,), (0,)), ((), ())), preferred_element_type=jnp.float32)


def inverse_rms(value):
    return lax.rsqrt(jnp.mean(value * value, axis=-1, keepdims=True) + EPS)


def pick(array, index, axis=0):
    return lax.dynamic_index_in_dim(array, index, axis, keepdims=False)


MESH = pl.DeviceIdType.MESH


class Spot:
    def __init__(self, depth):
        self.depth = depth
        place = lax.axis_index("dp")
        self.corner = lax.axis_index("seq")
        self.z, self.core = place // 2, place % 2
        self.y, self.x = self.corner // 2, self.corner % 2

    def at(self, z=None, core=None, y=None, x=None):
        z = self.z if z is None else z
        core = self.core if core is None else core
        y = self.y if y is None else y
        x = self.x if x is None else x
        return (z * 2 + core, y * 2 + x)

    def beside(self):
        return self.at(x=1 - self.x)

    def below(self):
        return self.at(y=1 - self.y)

    def sibling(self):
        return self.at(core=1 - self.core)

    def greet(self):
        barrier = pltpu.get_barrier_semaphore()
        others = [
            self.at(None, self.core ^ (i >> 2), self.y ^ (i >> 1 & 1), self.x ^ (i & 1)) for i in range(1, 8)
        ]
        for step in range(1, self.depth):
            for flip in range(2):
                others.append(self.at((self.z + step) % self.depth, self.core ^ flip))
        for other in others:
            pl.semaphore_signal(barrier, inc=1, device_id=other, device_id_type=MESH)
        pl.semaphore_wait(barrier, len(others))


class Wires:
    def __init__(self, sends, arrivals, moves):
        self.sends, self.arrivals, self.moves = sends, arrivals, moves
        self.count = 0
        self.moved = 0
        self.open = []

    def take(self, number):
        first = self.count
        self.count += number
        return first

    def send(self, source, target, device, index, landing=None):
        landing = index if landing is None else landing
        copy = pltpu.make_async_remote_copy(
            src_ref=source,
            dst_ref=target,
            send_sem=self.sends.at[index],
            recv_sem=self.arrivals.at[landing],
            device_id=device,
            device_id_type=MESH,
        )
        copy.start()
        self.open.append(copy)
        return copy

    def arrive(self, target, device, index):
        pltpu.make_async_remote_copy(
            src_ref=target,
            dst_ref=target,
            send_sem=self.sends.at[0],
            recv_sem=self.arrivals.at[index],
            device_id=device,
            device_id_type=MESH,
        ).wait_recv()

    def move(self, source, target):
        copy = pltpu.make_async_copy(source, target, self.moves.at[self.moved])
        self.moved += 1
        copy.start()
        return copy

    def close(self):
        for copy in self.open:
            copy.wait_send()
        self.open = []


def collect_tokens(spot, wires, parcel, whole):
    away = wires.take(4)
    over = wires.take(4)
    local = wires.moved
    wires.moved += 1
    for index in range(4):
        half, micro = spot.y ^ (index >> 1), spot.x ^ (index & 1)
        home = (half == spot.core) & (micro == spot.y) & (spot.core == spot.x)
        source = parcel.at[micro, half]
        target = whole.at[spot.corner, half]
        copy = pltpu.make_async_remote_copy(
            src_ref=source,
            dst_ref=target,
            send_sem=wires.sends.at[away + index],
            recv_sem=wires.arrivals.at[away + index],
            device_id=spot.at(core=half, y=micro, x=spot.core),
            device_id_type=MESH,
        )
        here = pltpu.make_async_copy(source, target, wires.moves.at[local])

        @pl.when(jnp.logical_not(home))
        def _():
            copy.start()

        @pl.when(home)
        def _():
            here.start()

    yield
    for index in range(4):
        block = 2 * (spot.core ^ (index >> 1)) + (spot.y ^ (index & 1))
        home = (spot.x == spot.core) & (block == spot.corner)
        piece = whole.at[block, spot.core]
        here = pltpu.make_async_copy(piece, piece, wires.moves.at[local])
        landed = pltpu.make_async_remote_copy(
            src_ref=piece,
            dst_ref=piece,
            send_sem=wires.sends.at[away + index],
            recv_sem=wires.arrivals.at[away + index],
            device_id=spot.sibling(),
            device_id_type=MESH,
        )

        @pl.when(jnp.logical_not(home))
        def _():
            landed.wait_recv()

        @pl.when(home)
        def _():
            here.wait()

        wires.send(piece, piece, spot.sibling(), over + index)
    yield
    for index in range(4):
        block = 2 * ((1 - spot.core) ^ (index >> 1)) + (spot.y ^ (index & 1))
        wires.arrive(whole.at[block, 1 - spot.core], spot.sibling(), over + index)
    for index in range(4):
        half, micro = spot.y ^ (index >> 1), spot.x ^ (index & 1)
        home = (half == spot.core) & (micro == spot.y) & (spot.core == spot.x)
        source = parcel.at[micro, half]

        @pl.when(jnp.logical_not(home))
        def _():
            pltpu.make_async_remote_copy(
                src_ref=source,
                dst_ref=source,
                send_sem=wires.sends.at[away + index],
                recv_sem=wires.arrivals.at[away + index],
                device_id=spot.sibling(),
                device_id_type=MESH,
            ).wait_send()

    yield


def deliver_tokens(spot, wires, pieces, homes):
    away = wires.take(4)
    local = wires.moved
    wires.moved += 1

    def parts():
        for index in range(4):
            block = 2 * (spot.core ^ (index >> 1)) + (spot.y ^ (index & 1))
            home = (spot.x == spot.core) & (block == spot.corner)
            source = pieces.at[block]
            target = homes.at[spot.y, spot.core]
            remote = pltpu.make_async_remote_copy(
                src_ref=source,
                dst_ref=target,
                send_sem=wires.sends.at[away + index],
                recv_sem=wires.arrivals.at[away + index],
                device_id=spot.at(core=spot.x, y=block // 2, x=block % 2),
                device_id_type=MESH,
            )
            yield home, remote, pltpu.make_async_copy(source, target, wires.moves.at[local])

    for home, remote, here in parts():
        pl.when(jnp.logical_not(home))(remote.start)
        pl.when(home)(here.start)
    yield
    for index in range(4):
        half, micro = spot.y ^ (index >> 1), spot.x ^ (index & 1)
        home = (half == spot.core) & (micro == spot.y) & (spot.core == spot.x)
        piece = homes.at[micro, half]
        landed = pltpu.make_async_remote_copy(
            src_ref=piece,
            dst_ref=piece,
            send_sem=wires.sends.at[away + index],
            recv_sem=wires.arrivals.at[away + index],
            device_id=spot.sibling(),
            device_id_type=MESH,
        )
        here = pltpu.make_async_copy(piece, piece, wires.moves.at[local])
        pl.when(jnp.logical_not(home))(landed.wait_recv)
        pl.when(home)(here.wait)
    for home, remote, here in parts():
        pl.when(jnp.logical_not(home))(remote.wait_send)
    yield


def gather_small(spot, wires, block, whole):
    own = wires.move(block, whole.at[spot.z, spot.core, spot.corner])
    first = wires.take(spot.depth + 3)
    for step in range(1, spot.depth):
        target = whole.at[spot.z, spot.core, spot.corner]
        wires.send(block, target, spot.at(z=(spot.z + step) % spot.depth), first + step)
    yield
    own.wait()
    for step in range(1, spot.depth):
        z = (spot.z - step + spot.depth) % spot.depth
        wires.arrive(whole.at[z, spot.core, spot.corner], spot.sibling(), first + step)
    column = whole.at[:, spot.core, spot.corner]
    wires.send(column, column, spot.beside(), first)
    wires.send(column, column, spot.below(), first + spot.depth)
    wires.send(column, column, spot.at(y=1 - spot.y, x=1 - spot.x), first + spot.depth + 1)
    yield
    for flip, index in ((1, first), (2, first + spot.depth), (3, first + spot.depth + 1)):
        wires.arrive(whole.at[:, spot.core, spot.corner ^ flip], spot.sibling(), index)
    plane = whole.at[:, spot.core]
    wires.send(plane, plane, spot.sibling(), first + spot.depth + 2)
    yield
    wires.arrive(whole.at[:, 1 - spot.core], spot.sibling(), first + spot.depth + 2)
    yield


def gather_columns(spot, wires, pack, whole):
    depth, me = spot.depth, spot.corner
    ahead = wires.take(2 * depth)
    flat = wires.take(4 * depth)
    own = wires.move(pack.at[spot.core], whole.at[spot.z, spot.core])
    for step in range(1, depth):
        for flip in range(2):
            wires.send(
                pack.at[spot.core ^ flip, me],
                whole.at[spot.z, spot.core, me],
                spot.at((spot.z + step) % depth, spot.core ^ flip),
                ahead + 2 * step + flip,
            )
    wires.send(pack.at[1 - spot.core], whole.at[spot.z, spot.core], spot.sibling(), ahead)
    yield
    for step in range(1, depth):
        z = (spot.z - step + depth) % depth
        for flip in range(2):
            wires.arrive(whole.at[z, spot.core ^ flip, me], spot.sibling(), ahead + 2 * step + flip)
        quarter = whole.at[z, :, me]
        wires.send(quarter, quarter, spot.beside(), flat + 4 * step)
        wires.send(quarter, quarter, spot.below(), flat + 4 * step + 1)
    yield
    for step in range(1, depth):
        z = (spot.z - step + depth) % depth
        wires.arrive(whole.at[z, :, me ^ 1], spot.sibling(), flat + 4 * step)
        piece = whole.at[z, 0, me ^ 1]
        wires.send(piece, piece, spot.below(), flat + 4 * step + 2)
        wires.arrive(whole.at[z, :, me ^ 2], spot.sibling(), flat + 4 * step + 1)
        piece = whole.at[z, 1, me ^ 2]
        wires.send(piece, piece, spot.beside(), flat + 4 * step + 3)
    yield
    own.wait()
    wires.arrive(whole.at[spot.z, 1 - spot.core], spot.sibling(), ahead)
    for step in range(1, depth):
        z = (spot.z - step + depth) % depth
        wires.arrive(whole.at[z, 0, me ^ 3], spot.sibling(), flat + 4 * step + 2)
        wires.arrive(whole.at[z, 1, me ^ 3], spot.sibling(), flat + 4 * step + 3)
    yield


def gather_rows(spot, wires, pack, whole):
    depth, me = spot.depth, spot.corner
    ahead = wires.take(depth)
    flat = wires.take(4 * depth)
    middle = pack.shape[-1] // 2

    def part(z, corner, side):
        if pack.shape[0] == 2:
            return whole.at[side, z, corner]
        return whole.at[0, z, corner, :, pl.ds(side * middle, middle)]

    own = wires.move(pack, whole.at[:, spot.z])
    for step in range(1, depth):
        wires.send(
            pack.at[:, me], whole.at[:, spot.z, me], spot.at((spot.z + step) % depth), ahead + step
        )
    yield
    for step in range(1, depth):
        z = (spot.z - step + depth) % depth
        quarter = whole.at[:, z, me]
        wires.arrive(quarter, spot.sibling(), ahead + step)
        wires.send(quarter, quarter, spot.beside(), flat + 4 * step)
        wires.send(quarter, quarter, spot.below(), flat + 4 * step + 1)
    yield
    for step in range(1, depth):
        z = (spot.z - step + depth) % depth
        wires.arrive(whole.at[:, z, me ^ 1], spot.sibling(), flat + 4 * step)
        piece = part(z, me ^ 1, 0)
        wires.send(piece, piece, spot.below(), flat + 4 * step + 2)
        wires.arrive(whole.at[:, z, me ^ 2], spot.sibling(), flat + 4 * step + 1)
        piece = part(z, me ^ 2, 1)
        wires.send(piece, piece, spot.beside(), flat + 4 * step + 3)
    yield
    own.wait()
    for step in range(1, depth):
        z = (spot.z - step + depth) % depth
        wires.arrive(part(z, me ^ 3, 0), spot.sibling(), flat + 4 * step + 2)
        wires.arrive(part(z, me ^ 3, 1), spot.sibling(), flat + 4 * step + 3)
    yield


def add_into(target, other, places):
    for place in places:
        target[place] = (
            target[place].astype(jnp.float32) + other[place].astype(jnp.float32)
        ).astype(jnp.bfloat16)


def scatter_buffers(depth, lanes, rows, width):
    half = depth // 2
    return [
        pltpu.VMEM((half, lanes, 2, rows, width), jnp.bfloat16),
        pltpu.VMEM((half, lanes, 2, rows, width), jnp.bfloat16),
        pltpu.VMEM((half, lanes, 2, rows, width), jnp.bfloat16),
        pltpu.VMEM((half, lanes, 2, rows, width), jnp.bfloat16),
        pltpu.VMEM((half, lanes, rows, width), jnp.bfloat16),
        pltpu.VMEM((half, lanes, rows, width), jnp.bfloat16),
        pltpu.VMEM((depth, lanes, rows, width), jnp.bfloat16),
        pltpu.VMEM((depth, lanes, rows, width), jnp.bfloat16),
        pltpu.VMEM((rows, width), jnp.bfloat16),
    ]


def scatter_sums(spot, wires, grads, buffers, total, got):
    depth, half = spot.depth, spot.depth // 2
    lanes = grads.shape[1]
    low, high, low_in, high_in, low_last, high_last, column, column_in, passing = buffers
    first = wires.take(4)
    away = wires.take(depth)
    mine = [
        wires.move(grads.at[pl.ds(0, half), :, :, spot.x], low),
        wires.move(grads.at[pl.ds(half, half), :, spot.y], high),
    ]
    wires.send(grads.at[pl.ds(0, half), :, :, 1 - spot.x], low_in, spot.beside(), first)
    wires.send(grads.at[pl.ds(half, half), :, 1 - spot.y], high_in, spot.below(), first + 1)
    yield
    for copy in mine:
        copy.wait()
    wires.arrive(low_in, spot.beside(), first)
    add_into(low, low_in, [(z, a, s) for z in range(half) for a in range(lanes) for s in range(2)])
    wires.send(low.at[:, :, 1 - spot.y], low_last, spot.below(), first + 2)
    wires.arrive(high_in, spot.below(), first + 1)
    add_into(high, high_in, [(z, a, s) for z in range(half) for a in range(lanes) for s in range(2)])
    wires.send(high.at[:, :, 1 - spot.x], high_last, spot.beside(), first + 3)
    yield
    wires.arrive(low_last, spot.below(), first + 2)
    wires.arrive(high_last, spot.beside(), first + 3)
    for z in range(half):
        for a in range(lanes):
            column[z, a] = (
                low[z, a, spot.y].astype(jnp.float32) + low_last[z, a].astype(jnp.float32)
            ).astype(jnp.bfloat16)
            column[half + z, a] = (
                high[z, a, spot.x].astype(jnp.float32) + high_last[z, a].astype(jnp.float32)
            ).astype(jnp.bfloat16)
    for step in range(1, depth):
        z = (spot.z + step) % depth
        wires.send(column.at[z], column_in.at[step], spot.at(z), away + step)
    yield
    for step in range(1, depth):
        wires.arrive(column_in.at[step], spot.sibling(), away + step)

    def added(lane):
        result = column[spot.z, lane].astype(jnp.float32)
        for step in range(1, depth):
            result = result + column_in[step, lane].astype(jnp.float32)
        return result

    if lanes == 1:
        total[...] = added(0)
    else:
        passing[...] = added(1 - spot.core).astype(jnp.bfloat16)
        wires.send(passing, got, spot.sibling(), away)
        total[...] = added(spot.core)
    yield
    if lanes == 2:
        wires.arrive(got, spot.sibling(), away)
    yield


def total_small(spot, wires, terms, work, total):
    first = wires.take(3 + spot.depth)
    work[0] = terms[...]
    wires.send(work.at[0], work.at[1], spot.sibling(), first)
    yield
    wires.arrive(work.at[1], spot.sibling(), first)
    work[2] = work[0] + work[1]
    wires.send(work.at[2], work.at[3], spot.beside(), first + 1)
    yield
    wires.arrive(work.at[3], spot.sibling(), first + 1)
    work[4] = work[2] + work[3]
    wires.send(work.at[4], work.at[5], spot.below(), first + 2)
    yield
    wires.arrive(work.at[5], spot.sibling(), first + 2)
    work[6] = work[4] + work[5]
    for step in range(1, spot.depth):
        target = work.at[6 + step]
        wires.send(work.at[6], target, spot.at((spot.z + step) % spot.depth), first + 2 + step)
    yield
    result = work[6]
    for step in range(1, spot.depth):
        wires.arrive(work.at[6 + step], spot.sibling(), first + 2 + step)
        result = result + work[6 + step]
    total[...] = result
    yield


def wire_scratch(number, moves):
    return [
        pltpu.SemaphoreType.DMA((number,)),
        pltpu.SemaphoreType.DMA((number,)),
        pltpu.SemaphoreType.DMA((moves,)),
    ]


def spread_row(vector):
    tile = pltpu.roll(jnp.broadcast_to(vector, (8, 2 * QB)), 0, 1, stride=1, stride_axis=0)
    return spread(tile)


def attend_block(query, keys, values, keep, bias):
    scores = nt(query, keys) + keep
    if bias is not None:
        scores = scores + bias
    peak = jnp.max(scores, axis=1, keepdims=True)
    weights = jnp.exp(scores - peak)
    total = jnp.sum(weights, axis=1, keepdims=True)
    return nn(weights.astype(jnp.bfloat16), values) / total, peak + jnp.log(total)


def pair_rows(block, kv):
    both = block[:, 2 * kv * HEAD_DIM : 2 * (kv + 1) * HEAD_DIM]
    return jnp.concatenate([both[:, :HEAD_DIM], both[:, HEAD_DIM:]], axis=0)


def normed(value, gain):
    return (value * inverse_rms(value) * gain).astype(jnp.bfloat16)


def forward_layer_kernel(depth, *refs):
    (
        x, t, m, s, p1, p2, p3, p4, p5, codes, holes,
        wx, wt, wm, ws, w1, w2, w3, w4, w5,
        a1, qkv, ctx, lse, x1, a2, qc, ckv, ctxc, lsec, x2, a3, gains, keeps, keepc, bent,
        bias, own, got, own2, got2, *sems
    ) = refs
    f32, bf16 = jnp.float32, jnp.bfloat16
    spot = Spot(depth)
    wires = Wires(*sems)
    blocks = 4
    kvs = 4
    inner = 2 * kvs * HEAD_DIM

    def rows(block):
        return slice(block * QB, (block + 1) * QB)

    spot.greet()
    tokens = collect_tokens(spot, wires, x, wx)
    small = gather_small(spot, wires, s, ws)
    first = gather_columns(spot, wires, p1, w1)
    memory = collect_tokens(spot, wires, m, wm)
    second = gather_columns(spot, wires, p2, w2)
    outs = gather_rows(spot, wires, p3, w3)
    wide = gather_columns(spot, wires, p4, w4)
    down = gather_rows(spot, wires, p5, w5)
    top = collect_tokens(spot, wires, t, wt)
    over = wires.take(2 * blocks)
    for program in (tokens, small, first, small, tokens, first):
        next(program)
    next(outs)
    next(second)
    next(memory)
    for program in (small, first, tokens, small, first):
        next(program)

    def line(row):
        return jnp.concatenate([ws[z, c, 0, row : row + 1, :] for z in range(depth) for c in range(2)], axis=1)

    for row in range(3):
        gains[row : row + 1, :] = line(row)
    counts = ws[spot.z, spot.x, 0, 3:4, :]
    length = jnp.where(spot.y == 0, counts[:, 0:1], counts[:, 1:2])
    span = jnp.where(spot.y == 0, counts[:, 2:3], counts[:, 3:4])
    places = lax.broadcasted_iota(jnp.int32, (1, blocks * QB), 1).astype(f32)
    keeps[...] = jnp.where(places < length, 0.0, NEG)
    keepc[...] = jnp.where(places[:, : keepc.shape[1]] < span, 0.0, NEG)
    table = jnp.concatenate(
        [
            ws[z, c, 0, 4:8, :] + ws[z, c, 1, 4:8, :] + ws[z, c, 2, 4:8, :] + ws[z, c, 3, 4:8, :]
            for z in range(depth)
            for c in range(2)
        ],
        axis=0,
    )
    table = jnp.where(spot.core == 0, table[:, :64], table[:, 64:]).astype(bf16)
    vectors = tn(table, codes[...])[:8] + holes[...]
    bent[...] = vectors[:, 4 * 2 * QB :]
    for kv in range(kvs):
        for member in range(2):
            for offset in range(4):
                head = 2 * kv + member
                bias[kv, member * QB : (member + 1) * QB, (3 - offset) * QB : (4 - offset) * QB] = spread_row(
                    vectors[head : head + 1, offset * 2 * QB : (offset + 1) * 2 * QB]
                )

    def attend_rows(block, queries, keys, stop, keep, mixed, sums, causal):
        for kv in range(kvs):
            base = 2 * kv * HEAD_DIM
            query = queries[rows(block), base : base + 2 * HEAD_DIM]
            shape = None
            if causal:
                base = 4 * kv * HEAD_DIM
                query = queries[rows(block), base : base + 2 * HEAD_DIM]
                base += 2 * HEAD_DIM
                shape = bias[kv, :, (3 - block) * QB : (3 - block) * QB + stop]
            out, level = attend_block(
                pair_rows(query, 0),
                keys[:stop, base : base + HEAD_DIM],
                keys[:stop, base + HEAD_DIM : base + 2 * HEAD_DIM],
                keep[:, :stop],
                shape,
            )
            mixed[rows(block), 2 * kv * HEAD_DIM : 2 * (kv + 1) * HEAD_DIM] = jnp.concatenate(
                [out[:QB], out[QB:]], axis=1
            ).astype(bf16)
            level = jnp.broadcast_to(level, (2 * QB, 128)).T
            sums[2 * kv : 2 * kv + 1, rows(block)] = level[:1, :QB]
            sums[2 * kv + 1 : 2 * kv + 2, rows(block)] = level[:1, QB:]

    weight = w1[...].reshape(-1, w1.shape[-1])
    for block in range(blocks):
        value = wx[block].reshape(QB, -1).astype(f32)
        a1[rows(block), :] = normed(value, gains[0:1, :])
        qkv[rows(block), :] = nn(a1[rows(block), :], weight).astype(bf16)
        if block == 0:
            next(outs)
            next(second)
            next(wide)
        if block == 1:
            next(outs)
            next(second)
            next(memory)
        if block == 2:
            next(outs)
            next(second)
            next(memory)
            next(wide)
            next(down)
        attend_rows(block, qkv, qkv, (block + 1) * QB, keeps, ctx, lse, True)

    def pass_on(block, mine, theirs, value, weight, index):
        mine[rows(block), :] = nn(value[rows(block), :], weight).astype(bf16)
        wires.send(mine.at[rows(block)], theirs.at[rows(block)], spot.sibling(), over + index + block)

    def joined(block, mine, theirs, index):
        wires.arrive(theirs.at[rows(block)], spot.sibling(), over + index + block)
        return mine[rows(block), :].astype(f32) + theirs[rows(block), :].astype(f32)

    weight = w3[0].reshape(-1, w3.shape[-1])
    for block in range(blocks):
        pass_on(block, own, got, ctx, weight, 0)
    next(wide)
    next(down)
    next(top)
    weight = w2[...].reshape(-1, w2.shape[-1])
    ckv[...] = nn(wm[...].reshape(-1, wm.shape[-1]), weight[:, :inner]).astype(bf16)
    for block in range(blocks):
        value = wx[block].reshape(QB, -1).astype(f32) + joined(block, own, got, 0)
        x1[rows(block), :] = value
        a2[rows(block), :] = normed(value, gains[1:2, :])
        qc[rows(block), :] = nn(a2[rows(block), :], weight[:, inner:]).astype(bf16)
    weight = w3[1].reshape(-1, w3.shape[-1])
    for block in range(blocks):
        attend_rows(block, qc, ckv, ckv.shape[0], keepc, ctxc, lsec, False)
        pass_on(block, own2, got2, ctxc, weight, blocks)
        if block == 1:
            next(down)
            next(top)
    for block in range(blocks):
        value = x1[rows(block), :] + joined(block, own2, got2, blocks)
        x2[rows(block), :] = value
        a3[rows(block), :] = normed(value, gains[2:3, :])
    for program in (wide, down, top):
        next(program)
    for program in (tokens, small, first, memory, second, outs, wide, down, top):
        assert next(program, None) is None
    wires.close()


def forward_layer(depth, x, t, m, small, p1, p2, p3, p4, p5, codes, holes):
    bf16, f32 = jnp.bfloat16, jnp.float32
    shape = jax.ShapeDtypeStruct

    def whole_columns(pack):
        return shape((depth, 2) + pack.shape[1:], bf16)

    def whole_rows(pack):
        return shape((pack.shape[0], depth) + pack.shape[1:], bf16)

    def whole_tokens(parcel):
        return shape((4, 2) + parcel.shape[2:], bf16)

    width = x.shape[-1]
    tokens = 8 * x.shape[2]
    span = 8 * m.shape[2]
    inner = p3.shape[0] * p3.shape[1] * p3.shape[2] * depth // 2
    heads = inner // HEAD_DIM
    hbm = pl.BlockSpec(memory_space=pl.ANY)
    vmem = pl.BlockSpec(memory_space=pltpu.VMEM)
    outs = [
        (whole_tokens(x), vmem),
        (whole_tokens(t), hbm),
        (whole_tokens(m), vmem),
        (shape((depth, 2, 4, 8, 128), f32), vmem),
        (whole_columns(p1), vmem),
        (whole_columns(p2), vmem),
        (whole_rows(p3), vmem),
        (whole_columns(p4), hbm),
        (whole_rows(p5), hbm),
        (shape((tokens, width), bf16), vmem),
        (shape((tokens, 2 * inner), bf16), vmem),
        (shape((tokens, inner), bf16), vmem),
        (shape((heads, tokens), f32), vmem),
        (shape((tokens, width), f32), vmem),
        (shape((tokens, width), bf16), vmem),
        (shape((tokens, inner), bf16), vmem),
        (shape((span, inner), bf16), vmem),
        (shape((tokens, inner), bf16), vmem),
        (shape((heads, tokens), f32), vmem),
        (shape((tokens, width), f32), vmem),
        (shape((tokens, width), bf16), vmem),
        (shape((8, width), f32), vmem),
        (shape((1, tokens), f32), vmem),
        (shape((1, span), f32), vmem),
        (shape((heads, 8 * QB), f32), vmem),
    ]
    swap = pltpu.VMEM((tokens, width), bf16)
    return pl.pallas_call(
        functools.partial(forward_layer_kernel, depth),
        in_specs=[hbm] * 9 + [vmem] * 2,
        out_specs=[spec for _, spec in outs],
        out_shape=[kind for kind, _ in outs],
        scratch_shapes=[pltpu.VMEM((heads // 2, 2 * QB, 4 * QB), f32), swap, swap, swap, swap]
        + wire_scratch(35 + 30 * depth, 12),
        compiler_params=pltpu.CompilerParams(
            collective_id=0, has_side_effects=True, vmem_limit_bytes=60 * 2**20
        ),
        cost_estimate=pl.CostEstimate(
            flops=16 * 10**9, bytes_accessed=128 * 2**20, transcendentals=10**7
        ),
    )(x, t, m, small, p1, p2, p3, p4, p5, codes, holes)


def parts_of(width, pieces):
    step = -(-width // (128 * pieces)) * 128
    return [(start, min(step, width - start)) for start in range(0, width, step)]


class Reduction:
    def __init__(self, spot, wires, grads, buffers, total, got, pieces):
        self.programs = []
        for (start, size), scratch in zip(pieces, buffers):
            lanes = pl.ds(start, size)
            self.programs.append(
                scatter_sums(
                    spot,
                    wires,
                    grads.at[:, :, :, :, :, lanes],
                    scratch,
                    total.at[:, lanes],
                    None if got is None else got.at[:, lanes],
                )
            )


def pipeline(programs, ahead=2, stages=5):
    count = len(programs)
    for turn in range(count + stages):
        if turn == 0:
            for program in programs[:ahead]:
                next(program)
            yield
        for stage in range(stages - 1, 0, -1):
            index = turn - (stage - 1)
            if 0 <= index < count:
                next(programs[index])
        if turn + ahead < count:
            next(programs[turn + ahead])
        yield


def backward_tile(keys, values, query, grads, keep, bias, level, delta):
    scores = nt(keys, query) + keep
    if bias is not None:
        scores = scores + bias
    probs = jnp.exp(scores - level)
    return probs, probs * (nt(values, grads) - delta)


def row_sums(upstream, mixed):
    inner = (upstream.astype(jnp.float32) * mixed.astype(jnp.float32)).T
    return jnp.concatenate(
        [
            jnp.sum(inner[:HEAD_DIM], axis=0, keepdims=True),
            jnp.sum(inner[HEAD_DIM:], axis=0, keepdims=True),
        ],
        axis=1,
    )


def cross_backward_kernel(depth, *refs):
    (
        g_down, g_gate, g_up, x2, x1, u, top, qc, ckv, ctxc, lsec, keep, a2, mem, w2, w3, ctx, gains,
        r_down, r_gate, r_up, q_gate, q_up, half, do_s, o_cout, o_cq, o_ckv, o_out, o_mem, terms,
        *rest
    ) = refs
    take = lambda n: [rest.pop(0) for _ in range(n)]
    stage, e2, eb, do_c, dqc, dkv, dk_sum, dv_sum, got, own_c, got_c, own_m, got_m, grad = take(14)
    buffers = [[take(9) for _ in range(2)] for _ in range(3)]
    f32, bf16 = jnp.float32, jnp.bfloat16
    spot = Spot(depth)
    wires = Wires(*rest)
    blocks = kvs = 4
    inner = 2 * kvs * HEAD_DIM

    def rows(block):
        return slice(block * QB, (block + 1) * QB)

    spot.greet()
    over = wires.take(2 * blocks + 4)
    for block in range(blocks):
        wires.send(u.at[rows(block)], got.at[rows(block)], spot.sibling(), over + block)
    programs = []
    for grads, scratch, total, other in (
        (g_down, buffers[0], r_down, None),
        (g_gate, buffers[1], r_gate, q_gate),
        (g_up, buffers[2], r_up, q_up),
    ):
        programs += Reduction(
            spot, wires, grads, scratch, total, other, parts_of(grads.shape[-1], 2)
        ).programs
    links = pipeline(programs)
    next(links)

    loads = {}

    def fetch(source, block, slot):
        loads[slot] = wires.move(source.at[rows(block)], stage.at[slot])

    def norm_back(block, slot, gain, upstream):
        loads[slot].wait()
        value = stage[slot]
        inverse = inverse_rms(value)
        scaled = upstream * gain
        mean = jnp.mean(value * scaled, axis=-1, keepdims=True)
        change = inverse * scaled - value * (inverse * inverse * inverse) * mean
        return change, jnp.sum(upstream * value * inverse, axis=0, keepdims=True)

    fetch(x2, 0, 0)
    gain_terms = jnp.zeros((1, e2.shape[1]), f32)
    for block in range(blocks):
        if block + 1 < blocks:
            fetch(x2, block + 1, (block + 1) % 2)
        else:
            fetch(x1, 0, 0)
        wires.arrive(got.at[rows(block)], spot.sibling(), over + block)
        change, term = norm_back(
            block, block % 2, gains[2:3, :], u[rows(block), :].astype(f32) + got[rows(block), :].astype(f32)
        )
        gain_terms = gain_terms + term
        value = top[rows(block), :].astype(f32) + change
        e2[rows(block), :] = value
        eb[rows(block), :] = value.astype(bf16)
        do_c[rows(block), :] = nt(value.astype(bf16), w3[1].reshape(inner, -1)).astype(bf16)
    terms[0:1, :] = 0.5 * gain_terms
    next(links)

    span = ckv.shape[0]
    for kv in range(kvs):
        both = slice(2 * kv * HEAD_DIM, 2 * (kv + 1) * HEAD_DIM)
        base = 2 * kv * HEAD_DIM
        dk_sum[...] = jnp.zeros_like(dk_sum)
        dv_sum[...] = jnp.zeros_like(dv_sum)
        for block in range(blocks):
            query = pair_rows(qc[rows(block), :], kv)
            grads = pair_rows(do_c[rows(block), :], kv)
            delta = row_sums(do_c[rows(block), both], ctxc[rows(block), both])
            level = jnp.concatenate(
                [lsec[2 * kv : 2 * kv + 1, rows(block)], lsec[2 * kv + 1 : 2 * kv + 2, rows(block)]], axis=1
            )
            dq = jnp.zeros((2 * QB, HEAD_DIM), f32)
            for part in range(span // QB):
                keys = ckv[rows(part), base : base + HEAD_DIM]
                values = ckv[rows(part), base + HEAD_DIM : base + 2 * HEAD_DIM]
                probs, dscores = backward_tile(keys, values, query, grads, keep[rows(part)], None, level, delta)
                dscores = dscores.astype(bf16)
                dv_sum[rows(part)] += nn(probs.astype(bf16), grads)
                dk_sum[rows(part)] += nn(dscores, query)
                dq += tn(dscores, keys)
            dqc[rows(block), both] = jnp.concatenate([dq[:QB], dq[QB:]], axis=1).astype(bf16)
        dkv[:, base : base + HEAD_DIM] = dk_sum[...].astype(bf16)
        dkv[:, base + HEAD_DIM : base + 2 * HEAD_DIM] = dv_sum[...].astype(bf16)
        if kv % 2 == 1:
            next(links)

    writes = {}

    def put(slot, value, target):
        if slot in writes:
            writes[slot].wait()
        view = grad.at[slot, pl.ds(0, value.shape[0]), pl.ds(0, value.shape[1])]
        view[...] = value.astype(bf16)
        writes[slot] = wires.move(view, target)

    weight = w2[...].reshape(-1, w2.shape[-1])
    for block in range(blocks):
        own_c[rows(block), :] = nt(dqc[rows(block), :], weight[:, inner:]).astype(bf16)
        wires.send(own_c.at[rows(block)], got_c.at[rows(block)], spot.sibling(), over + blocks + block)
    own_m[...] = nt(dkv[...], weight[:, :inner]).astype(bf16).reshape(own_m.shape)
    wires.send(own_m.at[:, 1 - spot.core], got_m, spot.sibling(), over + 2 * blocks)
    slot = 0
    for block in range(blocks):
        put(slot, tn(a2[:, rows(block)], dqc[...]), o_cq.at[rows(block)])
        slot = 1 - slot
    next(links)
    for block in range(blocks):
        put(slot, tn(mem[:, rows(block)], dkv[...]), o_ckv.at[rows(block)])
        slot = 1 - slot
    for block in range(inner // QB):
        put(slot, tn(ctxc[:, rows(block)], eb[...]), o_cout.at[rows(block)])
        slot = 1 - slot
    next(links)

    gain_terms = jnp.zeros((1, e2.shape[1]), f32)
    for block in range(blocks):
        if block + 1 < blocks:
            fetch(x1, block + 1, (block + 1) % 2)
        wires.arrive(got_c.at[rows(block)], spot.sibling(), over + blocks + block)
        change, term = norm_back(
            block,
            block % 2,
            gains[1:2, :],
            own_c[rows(block), :].astype(f32) + got_c[rows(block), :].astype(f32),
        )
        gain_terms = gain_terms + term
        value = e2[rows(block), :] + change
        e2[rows(block), :] = value
        half[block] = e2[pl.ds(pl.multiple_of(block * QB + spot.core * (QB // 2), QB // 2), QB // 2), :]
        eb[rows(block), :] = value.astype(bf16)
        do_s[rows(block), :] = nt(value.astype(bf16), w3[0].reshape(inner, -1)).astype(bf16)
    terms[1:2, :] = 0.5 * gain_terms
    next(links)
    for block in range(inner // QB):
        put(slot, tn(ctx[:, rows(block)], eb[...]), o_out.at[rows(block)])
        slot = 1 - slot
    wires.arrive(got_m, spot.sibling(), over + 2 * blocks)
    o_mem[...] = (own_m[:, spot.core].astype(f32) + got_m[...].astype(f32)).astype(bf16)
    for _ in links:
        pass
    for copy in writes.values():
        copy.wait()
    wires.close()


def cross_part(depth, g_down, g_gate, g_up, x2, x1, u, top, qc, ckv, ctxc, lsec, keep, a2, mem, w2, w3, ctx, gains):
    bf16, f32 = jnp.bfloat16, jnp.float32
    shape = jax.ShapeDtypeStruct
    hbm = pl.BlockSpec(memory_space=pl.ANY)
    vmem = pl.BlockSpec(memory_space=pltpu.VMEM)
    tokens, width = x2.shape
    span, inner = ckv.shape
    own = tokens // 8
    outs = [
        (shape(g_down.shape[4:], f32), vmem),
        (shape(g_gate.shape[4:], f32), vmem),
        (shape(g_up.shape[4:], f32), vmem),
        (shape(g_gate.shape[4:], bf16), vmem),
        (shape(g_up.shape[4:], bf16), vmem),
        (shape((4, own, width), f32), vmem),
        (shape((tokens, inner), bf16), vmem),
        (shape((inner, width), bf16), hbm),
        (shape((width, inner), bf16), hbm),
        (shape((width, inner), bf16), hbm),
        (shape((inner, width), bf16), hbm),
        (shape((4, span // 8, width), bf16), vmem),
        (shape((8, width), f32), vmem),
    ]
    scratch = [
        pltpu.VMEM((2, QB, width), f32),
        pltpu.VMEM((tokens, width), f32),
        pltpu.VMEM((tokens, width), bf16),
        pltpu.VMEM((tokens, inner), bf16),
        pltpu.VMEM((tokens, inner), bf16),
        pltpu.VMEM((span, inner), bf16),
        pltpu.VMEM((span, HEAD_DIM), f32),
        pltpu.VMEM((span, HEAD_DIM), f32),
        pltpu.VMEM((tokens, width), bf16),
        pltpu.VMEM((tokens, width), bf16),
        pltpu.VMEM((tokens, width), bf16),
        pltpu.VMEM((4, 2, span // 8, width), bf16),
        pltpu.VMEM((4, span // 8, width), bf16),
        pltpu.VMEM((2, QB, width), bf16),
    ]
    number = 12
    for grads in (g_down, g_gate, g_up):
        for _, size in parts_of(grads.shape[-1], 2):
            scratch += scatter_buffers(depth, grads.shape[1], grads.shape[4], size)
            number += 4 + depth
    return pl.pallas_call(
        functools.partial(cross_backward_kernel, depth),
        in_specs=[hbm] * 5 + [vmem] * 13,
        out_specs=[spec for _, spec in outs],
        out_shape=[kind for kind, _ in outs],
        scratch_shapes=scratch + wire_scratch(number, 48),
        compiler_params=pltpu.CompilerParams(
            collective_id=1, has_side_effects=True, vmem_limit_bytes=60 * 2**20
        ),
        cost_estimate=pl.CostEstimate(
            flops=16 * 10**9, bytes_accessed=128 * 2**20, transcendentals=10**7
        ),
    )(g_down, g_gate, g_up, x2, x1, u, top, qc, ckv, ctxc, lsec, keep, a2, mem, w2, w3, ctx, gains)


def self_backward_kernel(depth, *refs):
    (
        g_cout, g_cq, g_ckv, g_out, t_out, t_mem, do_s, qkv, ctx, lse, keep, bent, a1, x, gains, half, w1,
        terms, codes,
        r_cout, r_cq, r_ckv, r_out, r_qkv, q_cq, q_ckv, q_qkv, h_out, h_mem, h_in, packed,
        *rest
    ) = refs
    take = lambda n: [rest.pop(0) for _ in range(n)]
    bias, sums, dk_sum, dv_sum, dqkv, grad, mine, theirs, pieces, line, small, work = take(12)
    buffers = [take(9) for _ in range(8)]
    f32, bf16 = jnp.float32, jnp.bfloat16
    spot = Spot(depth)
    wires = Wires(*rest)
    blocks = kvs = 4
    inner = 2 * kvs * HEAD_DIM

    def rows(block):
        return slice(block * QB, (block + 1) * QB)

    spot.greet()
    over = wires.take(blocks)
    homes = [deliver_tokens(spot, wires, t_out, h_out), deliver_tokens(spot, wires, t_mem, h_mem)]
    programs = [
        scatter_sums(spot, wires, g_cout, buffers[0], r_cout, None),
        scatter_sums(spot, wires, g_out, buffers[1], r_out, None),
        scatter_sums(spot, wires, g_cq, buffers[2], r_cq, q_cq),
        scatter_sums(spot, wires, g_ckv, buffers[3], r_ckv, q_ckv),
    ]
    for kv in range(kvs):
        lanes = pl.ds(kv * QB, QB)
        programs.append(
            scatter_sums(spot, wires, grad.at[kv], buffers[4 + kv], r_qkv.at[:, lanes], q_qkv.at[:, lanes])
        )
    early = pipeline(programs[:4], ahead=2)
    late = programs[4:]
    next(early)
    for program in homes:
        next(program)
    for kv in range(kvs):
        base = kv * 4 * HEAD_DIM
        both = slice(2 * kv * HEAD_DIM, 2 * (kv + 1) * HEAD_DIM)
        dk_sum[...] = jnp.zeros_like(dk_sum)
        dv_sum[...] = jnp.zeros_like(dv_sum)
        sums[...] = jnp.zeros_like(sums)
        for member in range(2):
            for offset in range(4):
                head = 2 * kv + member
                bias[offset, :, member * QB : (member + 1) * QB] = spread_row(
                    bent[head : head + 1, offset * 2 * QB : (offset + 1) * 2 * QB]
                )
        for block in range(blocks):
            query = pair_rows(qkv[rows(block), base : base + 2 * HEAD_DIM], 0)
            grads = pair_rows(do_s[rows(block), :], kv)
            delta = row_sums(do_s[rows(block), both], ctx[rows(block), both])
            level = jnp.concatenate(
                [lse[2 * kv : 2 * kv + 1, rows(block)], lse[2 * kv + 1 : 2 * kv + 2, rows(block)]], axis=1
            )
            dq = jnp.zeros((2 * QB, HEAD_DIM), f32)
            for part in range(block + 1):
                keys = qkv[rows(part), base + 2 * HEAD_DIM : base + 3 * HEAD_DIM]
                values = qkv[rows(part), base + 3 * HEAD_DIM : base + 4 * HEAD_DIM]
                probs, dscores = backward_tile(
                    keys, values, query, grads, keep[rows(part)], bias[block - part], level, delta
                )
                sums[block - part] += dscores
                dscores = dscores.astype(bf16)
                dv_sum[rows(part)] += nn(probs.astype(bf16), grads)
                dk_sum[rows(part)] += nn(dscores, query)
                dq += tn(dscores, keys)
            dqkv[rows(block), base : base + 2 * HEAD_DIM] = jnp.concatenate(
                [dq[:QB], dq[QB:]], axis=1
            ).astype(bf16)
            if block == 2:
                next(early, None)
        dqkv[:, base + 2 * HEAD_DIM : base + 3 * HEAD_DIM] = dk_sum[...].astype(bf16)
        dqkv[:, base + 3 * HEAD_DIM : base + 4 * HEAD_DIM] = dv_sum[...].astype(bf16)
        for member in range(2):
            for offset in range(4):
                tile = fold(sums[offset, :, member * QB : (member + 1) * QB])
                row = tile[0:1]
                for r in range(1, 8):
                    row = row + pltpu.roll(tile[r : r + 1], 2 * QB - r, 1)
                head = 2 * kv + member
                line[head : head + 1, (offset + 1) * QB : (offset + 2) * QB] = row[:, :QB]
                if offset > 0:
                    line[head : head + 1, offset * QB : (offset + 1) * QB] += row[:, QB:]
        chunk = dqkv[:, base : base + 4 * HEAD_DIM]
        for block in range(blocks):
            grad[kv, block] = tn(a1[:, rows(block)], chunk).astype(bf16).reshape(grad.shape[2:])
        next(late[kv])
        for earlier in range(kv):
            next(late[earlier])
        next(early, None)
        if kv == 1:
            for program in homes:
                next(program)
    weight = w1[...].reshape(-1, w1.shape[-1])
    size = QB // 2

    def half_rows(block, core):
        return pl.ds(pl.multiple_of(block * QB + core * size, size), size)

    for block in range(blocks):
        mine[block] = nt(dqkv[half_rows(block, 1 - spot.core), :], weight).astype(bf16)
        wires.send(mine.at[block], theirs.at[block], spot.sibling(), over + block)
    for program in late:
        next(program, None)
    gain_terms = jnp.zeros((1, x.shape[-1]), f32)
    for block in range(blocks):
        upstream = nt(dqkv[half_rows(block, spot.core), :], weight).astype(bf16).astype(f32)
        wires.arrive(theirs.at[block], spot.sibling(), over + block)
        upstream = upstream + theirs[block].astype(f32)
        value = x[block, spot.core].astype(f32)
        inverse = inverse_rms(value)
        scaled = upstream * gains[0:1, :]
        mean = jnp.mean(value * scaled, axis=-1, keepdims=True)
        change = inverse * scaled - value * (inverse * inverse * inverse) * mean
        gain_terms = gain_terms + jnp.sum(upstream * value * inverse, axis=0, keepdims=True)
        pieces[block] = (half[block] + change).astype(bf16)
    homing = deliver_tokens(spot, wires, pieces, h_in)
    next(homing)
    shares = nt_exact(line[:, QB:], codes[...])
    small[...] = jnp.zeros_like(small)
    for r in range(8):
        lanes = slice(r * 128, (r + 1) * 128)
        small[r : r + 1, :] = terms[0:1, lanes]
        small[8 + r : 9 + r, :] = terms[1:2, lanes]
        small[16 + r : 17 + r, :] = gain_terms[:, lanes]
    zero = jnp.zeros_like(shares)
    small[24:32, :BUCKETS] = jnp.where(spot.core == 0, shares, zero)
    small[24:32, BUCKETS : 2 * BUCKETS] = jnp.where(spot.core == 1, shares, zero)
    summing = total_small(spot, wires, small, work, packed)
    next(summing)
    for _ in range(4):
        next(summing, None)
        for program in late:
            next(program, None)
    for program in late + homes + [homing, summing]:
        for _ in program:
            pass
    for _ in early:
        pass
    wires.close()


def nt_exact(left, right):
    return lax.dot_general(
        left, right, (((1,), (1,)), ((), ())), precision=HIGH, preferred_element_type=jnp.float32
    )


def self_part(depth, *operands):
    bf16, f32 = jnp.bfloat16, jnp.float32
    shape = jax.ShapeDtypeStruct
    hbm = pl.BlockSpec(memory_space=pl.ANY)
    vmem = pl.BlockSpec(memory_space=pltpu.VMEM)
    g_cout, g_cq, g_ckv, g_out, t_out, t_mem, do_s, qkv = operands[:8]
    tokens, inner = do_s.shape
    width = g_cout.shape[-1]
    rows = g_cout.shape[4]
    own = tokens // 8
    outs = [
        (shape((rows, width), f32), vmem),
        (shape((rows, inner), f32), vmem),
        (shape((rows, inner), f32), vmem),
        (shape((rows, width), f32), vmem),
        (shape((rows, 2 * inner), f32), vmem),
        (shape((rows, inner), bf16), vmem),
        (shape((rows, inner), bf16), vmem),
        (shape((rows, 2 * inner), bf16), vmem),
        (shape((2, 2) + t_out.shape[1:], bf16), hbm),
        (shape((2, 2) + t_mem.shape[1:], bf16), hbm),
        (shape((2, 2, own, width), bf16), hbm),
        (shape((32, 128), f32), vmem),
    ]
    scratch = [
        pltpu.VMEM((4, QB, 2 * QB), f32),
        pltpu.VMEM((4, QB, 2 * QB), f32),
        pltpu.VMEM((tokens, HEAD_DIM), f32),
        pltpu.VMEM((tokens, HEAD_DIM), f32),
        pltpu.VMEM((tokens, 2 * inner), bf16),
        pltpu.VMEM((4, depth, 2, 2, 2, rows, QB), bf16),
        pltpu.VMEM((4, own, width), bf16),
        pltpu.VMEM((4, own, width), bf16),
        pltpu.VMEM((4, own, width), bf16),
        pltpu.VMEM((8, 5 * QB), f32),
        pltpu.VMEM((32, 128), f32),
        pltpu.VMEM((6 + depth, 32, 128), f32),
    ]
    scratch += scatter_buffers(depth, 1, rows, width) + scatter_buffers(depth, 1, rows, width)
    scratch += scatter_buffers(depth, 2, rows, inner) + scatter_buffers(depth, 2, rows, inner)
    for _ in range(4):
        scratch += scatter_buffers(depth, 2, rows, QB)
    return pl.pallas_call(
        functools.partial(self_backward_kernel, depth),
        in_specs=[hbm] * 6 + [vmem] * 13,
        out_specs=[spec for _, spec in outs],
        out_shape=[kind for kind, _ in outs],
        scratch_shapes=scratch + wire_scratch(4 + 12 + 3 + depth + 8 * (4 + depth), 24),
        compiler_params=pltpu.CompilerParams(
            collective_id=2, has_side_effects=True, vmem_limit_bytes=60 * 2**20
        ),
        cost_estimate=pl.CostEstimate(
            flops=16 * 10**9, bytes_accessed=128 * 2**20, transcendentals=10**7
        ),
    )(*operands)


def parity_columns(weights):
    rows = weights[0].shape[0]
    pack = jnp.concatenate([w.reshape(rows, 4, 2, -1) for w in weights], axis=3)
    return jnp.moveaxis(pack, 2, 0).reshape(2, rows, -1)


def per_chip(
    layer_input,
    memory,
    target_lengths,
    memory_lengths,
    buckets,
    norm_self,
    self_q,
    self_k,
    self_v,
    self_out,
    rel_bias,
    norm_cross,
    cross_q,
    cross_k,
    cross_v,
    cross_out,
    norm_ff,
    ff_gate,
    ff_up,
    ff_down,
    cotangent,
):
    bf16, f32 = jnp.bfloat16, jnp.float32
    depth = lax.axis_size("dp") // 2
    spot = Spot(depth)
    core = spot.core
    width = layer_input.shape[3]
    local = layer_input.shape[2]
    near = memory.shape[2]
    shard = norm_self.shape[0]

    def column_pack(*groups):
        pack = jnp.concatenate([parity_columns(weights) for weights in groups], axis=2)
        return pack.reshape(2, 4, -1, pack.shape[2])

    heads = jnp.arange(4)
    spots = (heads // 2) * 64 + 2 * spot.corner + heads % 2
    placed = jnp.sum(
        jnp.where(jnp.arange(128)[None, None, :] == spots[None, :, None], rel_bias[:, :, None].astype(f32), 0.0),
        axis=1,
    )
    lengths = jnp.concatenate([target_lengths, memory_lengths]).reshape(1, 4).astype(f32)
    small = jnp.concatenate(
        [
            jnp.stack([norm_self, norm_cross, norm_ff]).astype(f32),
            jnp.pad(lengths, ((0, 0), (0, 124))),
            placed,
        ]
    )
    padded = jnp.concatenate([jnp.full((1, QB), -1, jnp.int32), buckets[None, :]], axis=1)
    vectors = row_pieces(padded)
    vectors = jnp.concatenate([jnp.roll(vectors[..., ::-1], 1, axis=-1), vectors], axis=1).reshape(1, -1)
    codes = (vectors == jnp.arange(BUCKETS, dtype=jnp.int32)[:, None]).astype(bf16)
    holes = jnp.where(vectors < 0, NEG, 0.0).astype(f32)
    onehot = (buckets[:, None] == jnp.arange(BUCKETS, dtype=jnp.int32)[None, :]).astype(f32)
    (
        inputs, upstream, encoded, _, w_qkv, w_cross, w_outs, w_gu, w_down,
        normed_self, qkv, context, self_sums, first, normed_cross, cross_queries, far_kv, cross_context,
        cross_sums, second, normed_ff, gains, keep_self, keep_cross, bent,
    ) = forward_layer(
        depth,
        layer_input.reshape(2, 2, local // 2, width),
        cotangent.reshape(2, 2, local // 2, width),
        memory.reshape(2, 2, near // 2, width),
        small,
        column_pack([self_q, self_k, self_v]),
        column_pack([cross_k, cross_v], [cross_q]),
        jnp.stack([self_out, cross_out]).reshape(2, 4, -1, width),
        column_pack([ff_gate], [ff_up]),
        ff_down.reshape(1, 4, -1, width),
        codes,
        holes,
    )
    upstream, encoded = upstream.reshape(-1, width), encoded.reshape(-1, width)
    w_gu, w_down = w_gu.reshape(-1, w_gu.shape[-1]), w_down.reshape(-1, width)
    hidden_width = w_gu.shape[1] // 2
    w_gate, w_up = w_gu[:, :hidden_width], w_gu[:, hidden_width:]
    valid = (keep_self[0] == 0).astype(f32)[:, None]

    def swap_core(array):
        pairs = [
            (place * 4 + corner, (place ^ 1) * 4 + corner) for place in range(2 * depth) for corner in range(4)
        ]
        return lax.ppermute(array, ("dp", "seq"), pairs)

    def share_half(partial):
        partial = partial.astype(bf16).reshape(4, 2, -1, partial.shape[-1])
        got = swap_core(pick(partial, 1 - core, 1))
        return pick(partial, core, 1).astype(f32) + got.astype(f32)

    def own_half(value):
        return pick(value.reshape(4, 2, -1, value.shape[-1]), core, 1)

    def grad_pack(left, right, lanes):
        grad = weight_grad(left, right).astype(bf16)
        return grad.reshape(depth, lanes, 2, 2, -1, grad.shape[-1])

    gate = project(normed_ff, w_gate)
    upward = project(normed_ff, w_up)
    middle = gated(gate, upward).astype(bf16)
    third = own_half(second) + share_half(project(middle, w_down))
    output = (third * own_half(valid)).astype(bf16)

    top = upstream.astype(f32) * valid
    top_low = top.astype(bf16)
    _, pullback = jax.vjp(gated, gate, upward)
    gate_grad, upward_grad = pullback(project_back(top_low, w_down))
    gate_grad = gate_grad.astype(bf16)
    upward_grad = upward_grad.astype(bf16)
    changed = (project_back(gate_grad, w_gate) + project_back(upward_grad, w_up)).astype(bf16)
    g_down = grad_pack(middle, top_low, 1)
    g_gate = grad_pack(normed_ff, gate_grad, 2)
    g_up = grad_pack(normed_ff, upward_grad, 2)
    (
        r_down, r_gate, r_up, q_gate, q_up, half, self_up, g_cout, g_cq, g_ckv, g_out, memory_grad, terms,
    ) = cross_part(
        depth, g_down, g_gate, g_up, second, first, changed, top_low, cross_queries, far_kv, cross_context,
        cross_sums, keep_cross.reshape(-1, 1), normed_cross, encoded, w_cross, w_outs, context, gains,
    )

    def pack(grad, lanes):
        return grad.reshape(depth, lanes, 2, 2, -1, grad.shape[-1])

    (
        r_cout, r_cq, r_ckv, r_out, r_qkv, q_cq, q_ckv, q_qkv, output, memory_grad, input_grad, packed,
    ) = self_part(
        depth, pack(g_cout, 1), pack(g_cq, 2), pack(g_ckv, 2), pack(g_out, 1), output, memory_grad, self_up,
        qkv, context, self_sums, keep_self.reshape(-1, 1), bent, normed_self, inputs, gains, half, w_qkv,
        terms, onehot.T,
    )
    bias_grad = packed[24:, :64].reshape(4, 2, 2, BUCKETS)
    bias_grad = jnp.transpose(bias_grad, (3, 0, 2, 1)).reshape(BUCKETS, HEADS)
    packed = packed[:24].reshape(3, width)
    mine = lax.axis_index("dp") * 4 + spot.corner
    piece = width // (depth * 8)
    n_ff, n_cross, n_self = (lax.dynamic_slice_in_dim(packed[i], mine * piece, piece) for i in range(3))
    bias_grad = lax.dynamic_slice(
        bias_grad, (lax.axis_index("dp") * rel_bias.shape[0], spot.corner * rel_bias.shape[1]), rel_bias.shape
    )

    def merge(own, got, *sizes):
        rows = own.shape[0]
        got = got.astype(f32)
        even, odd = jnp.where(core == 0, own, got), jnp.where(core == 0, got, own)
        both = jnp.stack([even.reshape(rows, 4, -1), odd.reshape(rows, 4, -1)], axis=2)
        results, start = [], 0
        for size in sizes or both.shape[3:]:
            results.append(both[..., start : start + size].reshape(rows, -1))
            start += size
        return results

    d_q, d_k, d_v = merge(r_qkv, q_qkv, 2 * HEAD_DIM, HEAD_DIM, HEAD_DIM)
    d_ck, d_cv = merge(r_ckv, q_ckv, HEAD_DIM, HEAD_DIM)
    (d_cq,), (d_gate,), (d_up,) = merge(r_cq, q_cq), merge(r_gate, q_gate), merge(r_up, q_up)
    return (
        output.reshape(layer_input.shape),
        input_grad.astype(f32).reshape(layer_input.shape),
        memory_grad.astype(f32).reshape(memory.shape),
        n_self,
        d_q,
        d_k,
        d_v,
        r_out,
        bias_grad,
        n_cross,
        d_cq,
        d_ck,
        d_cv,
        r_cout,
        n_ff,
        d_gate,
        d_up,
        r_down,
    )


def solution(mesh):
    placed = (
        P(None, "dp", "seq", None),
        P(None, "dp", "seq", None),
        P(None, "dp"),
        P(None, "dp"),
        P(),
        P("dp"),
        P("dp", None),
        P("dp", None),
        P("dp", None),
        P("dp", None),
        P("dp", "seq"),
        P("dp"),
        P("dp", None),
        P("dp", None),
        P("dp", None),
        P("dp", None),
        P("dp"),
        P("dp", None),
        P("dp", None),
        P("dp", None),
        P(None, "dp", "seq", None),
    )
    chips = mesh.shape["seq"] == 4 and mesh.shape["dp"] == HEADS // 2
    return jax.shard_map(
        per_chip if chips else per_device,
        mesh=mesh,
        in_specs=placed,
        out_specs=(
            P(None, "dp", "seq", None),
            P(None, "dp", "seq", None),
            P(None, "dp", "seq", None),
            P(("dp", "seq")),
            P(("dp", "seq"), None),
            P(("dp", "seq"), None),
            P(("dp", "seq"), None),
            P(("dp", "seq"), None),
            P("dp", "seq"),
            P(("dp", "seq")),
            P(("dp", "seq"), None),
            P(("dp", "seq"), None),
            P(("dp", "seq"), None),
            P(("dp", "seq"), None),
            P(("dp", "seq")),
            P(("dp", "seq"), None),
            P(("dp", "seq"), None),
            P(("dp", "seq"), None),
        ),
        check_vma=False,
    )
```

```python
import functools

import jax
import jax.numpy as jnp
from jax import lax
from jax.experimental import pallas as pl
from jax.experimental.pallas import tpu as pltpu
from jax.sharding import PartitionSpec as P

HEADS = 16
HEAD_DIM = 64
BUCKETS = 32
KV_HEADS = 8
TGT = 1024
MEM = 512
QB = 256
GELU_SCALE = 0.7978845608
GELU_CUBE = 0.044715


EPS = 1e-06
NEG = -1e30
HIGH = lax.Precision.HIGHEST


def shortened(shard):
    return jax.tree.map(lambda a: a.astype(jnp.bfloat16) if a.dtype == jnp.float32 else a, shard)


def rms_norm(value, gain):
    return value * lax.rsqrt(jnp.mean(value * value, axis=-1, keepdims=True) + EPS) * gain


def gated(gate, upward):
    return jax.nn.gelu(gate, approximate=True) * upward


def project(left, right):
    return jnp.dot(left, right, preferred_element_type=jnp.float32)


def project_back(grad, weight):
    return lax.dot_general(
        grad, weight, (((1,), (1,)), ((), ())), preferred_element_type=jnp.float32
    )


def weight_grad(left, right):
    return lax.dot_general(
        left, right, (((0,), (0,)), ((), ())), preferred_element_type=jnp.float32
    )


def split_heads(values, group):
    return values.reshape(values.shape[:2] + (-1, group, HEAD_DIM))


def split_shared(values):
    return values.reshape(values.shape[:2] + (-1, HEAD_DIM))


def causal_masks(table, length, group):

    def masks(start, block):
        stop = start + block
        rows = start + jnp.arange(block, dtype=jnp.int32)
        columns = jnp.arange(stop, dtype=jnp.int32)
        distance = rows[:, None] - columns[None, :]
        keep = (distance >= 0) & (columns[None, :] < length)
        extra = jnp.take(table, jnp.maximum(distance, 0), axis=1)
        return (extra.reshape((-1, group, block, stop)), keep, stop)

    return masks


def memory_masks(length, width):

    def masks(start, block):
        keep = jnp.broadcast_to(
            jnp.arange(width, dtype=jnp.int32)[None, :] < length, (block, width)
        )
        return (None, keep, width)

    return masks


def diagonal_sums(grads, block, stop):
    leading = grads.shape[:2]
    flipped = jnp.pad(grads[..., ::-1], ((0, 0), (0, 0), (0, 0), (0, block)))
    skewed = flipped.reshape(leading + (block * (stop + block),))[..., : block * (stop + block - 1)]
    skewed = skewed.reshape(leading + (block, stop + block - 1))
    return jnp.sum(skewed, axis=2)[..., block - 1 :]


def attend_forward(queries, keys, values, masks):
    block = min(512, queries.shape[0])
    outputs = []
    totals = []
    for index in range(queries.shape[0] // block):
        start = index * block
        extra, keep, stop = masks(start, block)
        rows = queries[start : start + block]
        scores = jnp.einsum("rkgd,skd->kgrs", rows, keys[:stop], preferred_element_type=jnp.float32)
        if extra is not None:
            scores = scores + extra
        scores = jnp.where(keep, scores, NEG)
        peak = jnp.max(scores, axis=-1, keepdims=True)
        weights = jnp.where(keep, jnp.exp(scores - peak), 0.0)
        total = jnp.sum(weights, axis=-1, keepdims=True)
        probs = (weights / total).astype(jnp.bfloat16)
        mixed = jnp.einsum(
            "kgrs,skd->rkgd", probs, values[:stop], preferred_element_type=jnp.float32
        )
        outputs.append(mixed.astype(jnp.bfloat16))
        totals.append(peak + jnp.log(total))
    return (jnp.concatenate(outputs, 0), jnp.concatenate(totals, 2))


def attend_backward(queries, keys, values, sums, grads, masks):
    block = min(512, queries.shape[0])
    key_grads = jnp.zeros(keys.shape, jnp.float32)
    value_grads = jnp.zeros(values.shape, jnp.float32)
    diagonal = jnp.zeros(sums.shape[:3], jnp.float32)
    query_grads = []
    for index in range(queries.shape[0] // block):
        start = index * block
        extra, keep, stop = masks(start, block)
        rows = queries[start : start + block]
        grad_rows = grads[start : start + block]
        scores = jnp.einsum("rkgd,skd->kgrs", rows, keys[:stop], preferred_element_type=jnp.float32)
        if extra is not None:
            scores = scores + extra
        scores = jnp.where(keep, scores, NEG)
        probs = jnp.where(keep, jnp.exp(scores - sums[:, :, start : start + block]), 0.0)
        value_grads = value_grads.at[:stop].add(
            jnp.einsum(
                "kgrs,rkgd->skd",
                probs.astype(jnp.bfloat16),
                grad_rows,
                preferred_element_type=jnp.float32,
            )
        )
        dprobs = jnp.einsum(
            "rkgd,skd->kgrs", grad_rows, values[:stop], preferred_element_type=jnp.float32
        )
        delta = jnp.sum(probs * dprobs, axis=-1, keepdims=True)
        dscores = (probs * (dprobs - delta)).astype(jnp.bfloat16)
        query_grads.append(
            jnp.einsum(
                "kgrs,skd->rkgd", dscores, keys[:stop], preferred_element_type=jnp.float32
            ).astype(jnp.bfloat16)
        )
        key_grads = key_grads.at[:stop].add(
            jnp.einsum("kgrs,rkgd->skd", dscores, rows, preferred_element_type=jnp.float32)
        )
        if extra is not None:
            diagonal = diagonal.at[:, :, :stop].add(
                diagonal_sums(dscores.astype(jnp.float32), block, stop)
            )
    return (
        jnp.concatenate(query_grads, 0),
        key_grads.astype(jnp.bfloat16),
        value_grads.astype(jnp.bfloat16),
        diagonal,
    )


def self_forward(queries, keys, values, length, table):
    return attend_forward(queries, keys, values, causal_masks(table, length, queries.shape[2]))


def self_backward(queries, keys, values, sums, grads, length, table):
    return attend_backward(
        queries, keys, values, sums, grads, causal_masks(table, length, queries.shape[2])
    )


def cross_forward(queries, keys, values, length):
    return attend_forward(queries, keys, values, memory_masks(length, keys.shape[0]))


def cross_backward(queries, keys, values, sums, grads, length):
    return attend_backward(queries, keys, values, sums, grads, memory_masks(length, keys.shape[0]))


def to_tokens(values):
    return lax.all_to_all(shortened(values), "seq", split_axis=1, concat_axis=2, tiled=True).astype(
        values.dtype
    )


def to_heads(grads):
    return lax.all_to_all(grads, "seq", split_axis=2, concat_axis=1, tiled=True)


def per_device(
    layer_input,
    memory,
    target_lengths,
    memory_lengths,
    buckets,
    norm_self,
    self_q,
    self_k,
    self_v,
    self_out,
    rel_bias,
    norm_cross,
    cross_q,
    cross_k,
    cross_v,
    cross_out,
    norm_ff,
    ff_gate,
    ff_up,
    ff_down,
    cotangent,
):
    micro_count, batch_rows, local_tokens, model_width = layer_input.shape
    memory_tokens = memory.shape[2]
    group = HEADS // KV_HEADS
    replicas = lax.axis_size("dp")
    shards = (
        norm_self,
        self_q,
        self_k,
        self_v,
        self_out,
        rel_bias,
        norm_cross,
        cross_q,
        cross_k,
        cross_v,
        cross_out,
        norm_ff,
        ff_gate,
        ff_up,
        ff_down,
    )
    totals = [
        jnp.zeros((piece.shape[0] * replicas,) + piece.shape[1:], jnp.float32) for piece in shards
    ]
    onehot = (buckets[:, None] == jnp.arange(BUCKETS, dtype=jnp.int32)[None, :]).astype(jnp.float32)
    places = lax.axis_index("seq") * local_tokens + jnp.arange(local_tokens, dtype=jnp.int32)
    diagonal = jnp.zeros((rel_bias.shape[1] // group, group, TGT), jnp.float32)
    outputs = []
    input_grads = []
    memory_grads = []
    for micro_step in range(micro_count):
        gathered = (
            lax.all_gather(norm_self, "dp", axis=0, tiled=True),
            lax.all_gather(self_q, "dp", axis=0, tiled=True),
            lax.all_gather(self_k, "dp", axis=0, tiled=True),
            lax.all_gather(self_v, "dp", axis=0, tiled=True),
            lax.all_gather(self_out, "dp", axis=0, tiled=True),
            lax.all_gather(rel_bias, "dp", axis=0, tiled=True),
            lax.all_gather(norm_cross, "dp", axis=0, tiled=True),
            lax.all_gather(cross_q, "dp", axis=0, tiled=True),
            lax.all_gather(cross_k, "dp", axis=0, tiled=True),
            lax.all_gather(cross_v, "dp", axis=0, tiled=True),
            lax.all_gather(cross_out, "dp", axis=0, tiled=True),
            lax.all_gather(norm_ff, "dp", axis=0, tiled=True),
            lax.all_gather(ff_gate, "dp", axis=0, tiled=True),
            lax.all_gather(ff_up, "dp", axis=0, tiled=True),
            lax.all_gather(ff_down, "dp", axis=0, tiled=True),
        )
        (
            gain_self,
            query_self,
            key_self,
            value_self,
            output_self,
            bias_whole,
            gain_cross,
            query_cross,
            key_cross,
            value_cross,
            output_cross,
            gain_ff,
            gate_weight,
            up_weight,
            down_weight,
        ) = gathered
        gain_self = gain_self.astype(jnp.float32)
        gain_cross = gain_cross.astype(jnp.float32)
        gain_ff = gain_ff.astype(jnp.float32)
        table = lax.dot_general(
            bias_whole.astype(jnp.float32), onehot, (((0,), (1,)), ((), ())), precision=HIGH
        )
        lengths = target_lengths[micro_step]
        spans = memory_lengths[micro_step]
        valid = (places[None, :] < lengths[:, None]).astype(jnp.float32).reshape(-1, 1)
        hidden = layer_input[micro_step].reshape(-1, model_width).astype(jnp.float32)
        normed_self = rms_norm(hidden, gain_self).astype(jnp.bfloat16)
        queries = (
            project(normed_self, query_self)
            .astype(jnp.bfloat16)
            .reshape(batch_rows, local_tokens, -1)
        )
        keys = (
            project(normed_self, key_self)
            .astype(jnp.bfloat16)
            .reshape(batch_rows, local_tokens, -1)
        )
        values = (
            project(normed_self, value_self)
            .astype(jnp.bfloat16)
            .reshape(batch_rows, local_tokens, -1)
        )
        encoded = memory[micro_step].reshape(-1, model_width)
        memory_keys = (
            project(encoded, key_cross).astype(jnp.bfloat16).reshape(batch_rows, memory_tokens, -1)
        )
        memory_values = (
            project(encoded, value_cross)
            .astype(jnp.bfloat16)
            .reshape(batch_rows, memory_tokens, -1)
        )
        head_queries, head_keys, head_values, far_keys, far_values = (
            lax.all_to_all(queries, "seq", split_axis=2, concat_axis=1, tiled=True),
            lax.all_to_all(keys, "seq", split_axis=2, concat_axis=1, tiled=True),
            lax.all_to_all(values, "seq", split_axis=2, concat_axis=1, tiled=True),
            lax.all_to_all(memory_keys, "seq", split_axis=2, concat_axis=1, tiled=True),
            lax.all_to_all(memory_values, "seq", split_axis=2, concat_axis=1, tiled=True),
        )
        self_queries = split_heads(head_queries, group)
        self_keys = split_shared(head_keys)
        self_values = split_shared(head_values)
        far_keys = split_shared(far_keys)
        far_values = split_shared(far_values)
        attended, self_sums = jax.vmap(self_forward, in_axes=(0, 0, 0, 0, None))(
            self_queries, self_keys, self_values, lengths, table
        )
        context = to_tokens(attended.reshape(batch_rows, TGT, -1)).reshape(
            batch_rows * local_tokens, -1
        )
        first = hidden + project(context, output_self)
        normed_cross = rms_norm(first, gain_cross).astype(jnp.bfloat16)
        cross_queries = (
            project(normed_cross, query_cross)
            .astype(jnp.bfloat16)
            .reshape(batch_rows, local_tokens, -1)
        )
        cross_heads = split_heads(
            lax.all_to_all(cross_queries, "seq", split_axis=2, concat_axis=1, tiled=True), group
        )
        cross_attended, cross_sums = jax.vmap(cross_forward)(
            cross_heads, far_keys, far_values, spans
        )
        cross_context = to_tokens(cross_attended.reshape(batch_rows, TGT, -1)).reshape(
            batch_rows * local_tokens, -1
        )
        second = first + project(cross_context, output_cross)
        normed_ff = rms_norm(second, gain_ff).astype(jnp.bfloat16)
        gate = project(normed_ff, gate_weight)
        upward = project(normed_ff, up_weight)
        middle = gated(gate, upward).astype(jnp.bfloat16)
        third = second + project(middle, down_weight)
        outputs.append(
            (third * valid).astype(jnp.bfloat16).reshape(batch_rows, local_tokens, model_width)
        )
        upstream = cotangent[micro_step].reshape(-1, model_width).astype(jnp.float32) * valid
        down_grad = upstream.astype(jnp.bfloat16)
        totals[14] = totals[14] + weight_grad(middle, down_grad)
        _, pullback = jax.vjp(gated, gate, upward)
        gate_grad, upward_grad = pullback(project_back(down_grad, down_weight))
        gate_grad = gate_grad.astype(jnp.bfloat16)
        upward_grad = upward_grad.astype(jnp.bfloat16)
        totals[12] = totals[12] + weight_grad(normed_ff, gate_grad)
        totals[13] = totals[13] + weight_grad(normed_ff, upward_grad)
        _, pullback = jax.vjp(rms_norm, second, gain_ff)
        second_grad, gain_grad = pullback(
            project_back(gate_grad, gate_weight) + project_back(upward_grad, up_weight)
        )
        totals[11] = totals[11] + gain_grad
        second_grad = second_grad + upstream
        cross_grad = second_grad.astype(jnp.bfloat16)
        totals[10] = totals[10] + weight_grad(cross_context, cross_grad)
        context_grad = (
            project_back(cross_grad, output_cross)
            .astype(jnp.bfloat16)
            .reshape(batch_rows, local_tokens, -1)
        )
        cross_query_grad, far_key_grad, far_value_grad, _ = jax.vmap(cross_backward)(
            cross_heads,
            far_keys,
            far_values,
            cross_sums,
            split_heads(to_heads(context_grad), group),
            spans,
        )
        query_back, key_back, value_back = (
            lax.all_to_all(
                shortened(cross_query_grad.reshape(batch_rows, TGT, -1)),
                "seq",
                split_axis=1,
                concat_axis=2,
                tiled=True,
            ),
            lax.all_to_all(
                shortened(far_key_grad.reshape(batch_rows, MEM, -1)),
                "seq",
                split_axis=1,
                concat_axis=2,
                tiled=True,
            ),
            lax.all_to_all(
                shortened(far_value_grad.reshape(batch_rows, MEM, -1)),
                "seq",
                split_axis=1,
                concat_axis=2,
                tiled=True,
            ),
        )
        query_back = query_back.reshape(batch_rows * local_tokens, -1)
        key_back = key_back.reshape(batch_rows * memory_tokens, -1)
        value_back = value_back.reshape(batch_rows * memory_tokens, -1)
        totals[7] = totals[7] + weight_grad(normed_cross, query_back)
        totals[8] = totals[8] + weight_grad(encoded, key_back)
        totals[9] = totals[9] + weight_grad(encoded, value_back)
        memory_grads.append(
            (project_back(key_back, key_cross) + project_back(value_back, value_cross)).reshape(
                batch_rows, memory_tokens, model_width
            )
        )
        _, pullback = jax.vjp(rms_norm, first, gain_cross)
        first_grad, gain_grad = pullback(project_back(query_back, query_cross))
        totals[6] = totals[6] + gain_grad
        first_grad = first_grad + second_grad
        self_grad = first_grad.astype(jnp.bfloat16)
        totals[4] = totals[4] + weight_grad(context, self_grad)
        context_grad = (
            project_back(self_grad, output_self)
            .astype(jnp.bfloat16)
            .reshape(batch_rows, local_tokens, -1)
        )
        query_grad, key_grad, value_grad, bias_grad = jax.vmap(
            self_backward, in_axes=(0, 0, 0, 0, 0, 0, None)
        )(
            self_queries,
            self_keys,
            self_values,
            self_sums,
            split_heads(to_heads(context_grad), group),
            lengths,
            table,
        )
        diagonal = diagonal + jnp.sum(bias_grad, axis=0)
        query_back, key_back, value_back = (
            lax.all_to_all(
                shortened(query_grad.reshape(batch_rows, TGT, -1)),
                "seq",
                split_axis=1,
                concat_axis=2,
                tiled=True,
            ),
            lax.all_to_all(
                shortened(key_grad.reshape(batch_rows, TGT, -1)),
                "seq",
                split_axis=1,
                concat_axis=2,
                tiled=True,
            ),
            lax.all_to_all(
                shortened(value_grad.reshape(batch_rows, TGT, -1)),
                "seq",
                split_axis=1,
                concat_axis=2,
                tiled=True,
            ),
        )
        query_back = query_back.reshape(batch_rows * local_tokens, -1)
        key_back = key_back.reshape(batch_rows * local_tokens, -1)
        value_back = value_back.reshape(batch_rows * local_tokens, -1)
        totals[1] = totals[1] + weight_grad(normed_self, query_back)
        totals[2] = totals[2] + weight_grad(normed_self, key_back)
        totals[3] = totals[3] + weight_grad(normed_self, value_back)
        _, pullback = jax.vjp(rms_norm, hidden, gain_self)
        hidden_grad, gain_grad = pullback(
            project_back(query_back, query_self)
            + project_back(key_back, key_self)
            + project_back(value_back, value_self)
        )
        totals[0] = totals[0] + gain_grad
        input_grads.append(
            (hidden_grad + first_grad).reshape(batch_rows, local_tokens, model_width)
        )
    totals[5] = lax.dot_general(
        onehot, diagonal.reshape(-1, TGT), (((0,), (1,)), ((), ())), precision=HIGH
    )
    reduced = (
        lax.psum_scatter(totals[0], ("dp", "seq"), scatter_dimension=0, tiled=True),
        lax.psum_scatter(totals[1], ("dp", "seq"), scatter_dimension=0, tiled=True),
        lax.psum_scatter(totals[2], ("dp", "seq"), scatter_dimension=0, tiled=True),
        lax.psum_scatter(totals[3], ("dp", "seq"), scatter_dimension=0, tiled=True),
        lax.psum_scatter(totals[4], ("dp", "seq"), scatter_dimension=0, tiled=True),
        lax.psum_scatter(totals[6], ("dp", "seq"), scatter_dimension=0, tiled=True),
        lax.psum_scatter(totals[7], ("dp", "seq"), scatter_dimension=0, tiled=True),
        lax.psum_scatter(totals[8], ("dp", "seq"), scatter_dimension=0, tiled=True),
        lax.psum_scatter(totals[9], ("dp", "seq"), scatter_dimension=0, tiled=True),
        lax.psum_scatter(totals[10], ("dp", "seq"), scatter_dimension=0, tiled=True),
        lax.psum_scatter(totals[11], ("dp", "seq"), scatter_dimension=0, tiled=True),
        lax.psum_scatter(totals[12], ("dp", "seq"), scatter_dimension=0, tiled=True),
        lax.psum_scatter(totals[13], ("dp", "seq"), scatter_dimension=0, tiled=True),
        lax.psum_scatter(totals[14], ("dp", "seq"), scatter_dimension=0, tiled=True),
    )
    bias_share = lax.psum_scatter(totals[5], "dp", scatter_dimension=0, tiled=True)
    return (
        jnp.stack(outputs),
        jnp.stack(input_grads),
        jnp.stack(memory_grads),
        reduced[0],
        reduced[1],
        reduced[2],
        reduced[3],
        reduced[4],
        bias_share,
        reduced[5],
        reduced[6],
        reduced[7],
        reduced[8],
        reduced[9],
        reduced[10],
        reduced[11],
        reduced[12],
        reduced[13],
    )


def row_pieces(full):
    blocks = full.reshape(full.shape[0], -1, QB)
    return jnp.concatenate([blocks[:, 1:], blocks[:, :-1]], axis=2)


def seed_rows(vectors):
    return jnp.stack([jnp.roll(vectors, r, axis=-1) for r in range(8)], axis=-2)


def spread(seed):
    rows = 8
    tile = seed
    while rows < QB:
        tile = jnp.concatenate([tile, pltpu.roll(tile, rows, 1)], axis=0)
        rows *= 2
    return tile[:, :QB]


def fold(tile):
    width = 2 * QB
    tile = jnp.concatenate([tile, jnp.zeros_like(tile)], axis=1)
    rows = QB
    while rows > 8:
        rows //= 2
        tile = tile[:rows] + pltpu.roll(tile[rows:], width - rows, 1)
    return tile


def nt(left, right):
    return lax.dot_general(left, right, (((1,), (1,)), ((), ())), preferred_element_type=jnp.float32)


def tn(left, right):
    return lax.dot_general(left, right, (((0,), (0,)), ((), ())), preferred_element_type=jnp.float32)


def nn(left, right):
    return lax.dot_general(left, right, (((1,), (0,)), ((), ())), preferred_element_type=jnp.float32)


def inverse_rms(value):
    return lax.rsqrt(jnp.mean(value * value, axis=-1, keepdims=True) + EPS)


def pick(array, index, axis=0):
    return lax.dynamic_index_in_dim(array, index, axis, keepdims=False)


MESH = pl.DeviceIdType.MESH


class Spot:
    def __init__(self, depth):
        self.depth = depth
        place = lax.axis_index("dp")
        self.corner = lax.axis_index("seq")
        self.z, self.core = place // 2, place % 2
        self.y, self.x = self.corner // 2, self.corner % 2

    def at(self, z=None, core=None, y=None, x=None):
        z = self.z if z is None else z
        core = self.core if core is None else core
        y = self.y if y is None else y
        x = self.x if x is None else x
        return (z * 2 + core, y * 2 + x)

    def beside(self):
        return self.at(x=1 - self.x)

    def below(self):
        return self.at(y=1 - self.y)

    def sibling(self):
        return self.at(core=1 - self.core)

    def greet(self):
        barrier = pltpu.get_barrier_semaphore()
        others = [
            self.at(None, self.core ^ (i >> 2), self.y ^ (i >> 1 & 1), self.x ^ (i & 1)) for i in range(1, 8)
        ]
        for step in range(1, self.depth):
            for flip in range(2):
                others.append(self.at((self.z + step) % self.depth, self.core ^ flip))
        for other in others:
            pl.semaphore_signal(barrier, inc=1, device_id=other, device_id_type=MESH)
        pl.semaphore_wait(barrier, len(others))


class Wires:
    def __init__(self, sends, arrivals, moves):
        self.sends, self.arrivals, self.moves = sends, arrivals, moves
        self.count = 0
        self.moved = 0
        self.open = []

    def take(self, number):
        first = self.count
        self.count += number
        return first

    def send(self, source, target, device, index, landing=None):
        landing = index if landing is None else landing
        copy = pltpu.make_async_remote_copy(
            src_ref=source,
            dst_ref=target,
            send_sem=self.sends.at[index],
            recv_sem=self.arrivals.at[landing],
            device_id=device,
            device_id_type=MESH,
        )
        copy.start()
        self.open.append(copy)
        return copy

    def arrive(self, target, device, index):
        pltpu.make_async_remote_copy(
            src_ref=target,
            dst_ref=target,
            send_sem=self.sends.at[0],
            recv_sem=self.arrivals.at[index],
            device_id=device,
            device_id_type=MESH,
        ).wait_recv()

    def move(self, source, target):
        copy = pltpu.make_async_copy(source, target, self.moves.at[self.moved])
        self.moved += 1
        copy.start()
        return copy

    def close(self):
        for copy in self.open:
            copy.wait_send()
        self.open = []


def collect_tokens(spot, wires, parcel, whole):
    away = wires.take(4)
    over = wires.take(4)
    local = wires.moved
    wires.moved += 1
    for index in range(4):
        half, micro = spot.y ^ (index >> 1), spot.x ^ (index & 1)
        home = (half == spot.core) & (micro == spot.y) & (spot.core == spot.x)
        source = parcel.at[micro, half]
        target = whole.at[spot.corner, half]
        copy = pltpu.make_async_remote_copy(
            src_ref=source,
            dst_ref=target,
            send_sem=wires.sends.at[away + index],
            recv_sem=wires.arrivals.at[away + index],
            device_id=spot.at(core=half, y=micro, x=spot.core),
            device_id_type=MESH,
        )
        here = pltpu.make_async_copy(source, target, wires.moves.at[local])

        @pl.when(jnp.logical_not(home))
        def _():
            copy.start()

        @pl.when(home)
        def _():
            here.start()

    yield
    for index in range(4):
        block = 2 * (spot.core ^ (index >> 1)) + (spot.y ^ (index & 1))
        home = (spot.x == spot.core) & (block == spot.corner)
        piece = whole.at[block, spot.core]
        here = pltpu.make_async_copy(piece, piece, wires.moves.at[local])
        landed = pltpu.make_async_remote_copy(
            src_ref=piece,
            dst_ref=piece,
            send_sem=wires.sends.at[away + index],
            recv_sem=wires.arrivals.at[away + index],
            device_id=spot.sibling(),
            device_id_type=MESH,
        )

        @pl.when(jnp.logical_not(home))
        def _():
            landed.wait_recv()

        @pl.when(home)
        def _():
            here.wait()

        wires.send(piece, piece, spot.sibling(), over + index)
    yield
    for index in range(4):
        block = 2 * ((1 - spot.core) ^ (index >> 1)) + (spot.y ^ (index & 1))
        wires.arrive(whole.at[block, 1 - spot.core], spot.sibling(), over + index)
    for index in range(4):
        half, micro = spot.y ^ (index >> 1), spot.x ^ (index & 1)
        home = (half == spot.core) & (micro == spot.y) & (spot.core == spot.x)
        source = parcel.at[micro, half]

        @pl.when(jnp.logical_not(home))
        def _():
            pltpu.make_async_remote_copy(
                src_ref=source,
                dst_ref=source,
                send_sem=wires.sends.at[away + index],
                recv_sem=wires.arrivals.at[away + index],
                device_id=spot.sibling(),
                device_id_type=MESH,
            ).wait_send()

    yield


def deliver_tokens(spot, wires, pieces, homes):
    away = wires.take(4)
    local = wires.moved
    wires.moved += 1

    def parts():
        for index in range(4):
            block = 2 * (spot.core ^ (index >> 1)) + (spot.y ^ (index & 1))
            home = (spot.x == spot.core) & (block == spot.corner)
            source = pieces.at[block]
            target = homes.at[spot.y, spot.core]
            remote = pltpu.make_async_remote_copy(
                src_ref=source,
                dst_ref=target,
                send_sem=wires.sends.at[away + index],
                recv_sem=wires.arrivals.at[away + index],
                device_id=spot.at(core=spot.x, y=block // 2, x=block % 2),
                device_id_type=MESH,
            )
            yield home, remote, pltpu.make_async_copy(source, target, wires.moves.at[local])

    for home, remote, here in parts():
        pl.when(jnp.logical_not(home))(remote.start)
        pl.when(home)(here.start)
    yield
    for index in range(4):
        half, micro = spot.y ^ (index >> 1), spot.x ^ (index & 1)
        home = (half == spot.core) & (micro == spot.y) & (spot.core == spot.x)
        piece = homes.at[micro, half]
        landed = pltpu.make_async_remote_copy(
            src_ref=piece,
            dst_ref=piece,
            send_sem=wires.sends.at[away + index],
            recv_sem=wires.arrivals.at[away + index],
            device_id=spot.sibling(),
            device_id_type=MESH,
        )
        here = pltpu.make_async_copy(piece, piece, wires.moves.at[local])
        pl.when(jnp.logical_not(home))(landed.wait_recv)
        pl.when(home)(here.wait)
    for home, remote, here in parts():
        pl.when(jnp.logical_not(home))(remote.wait_send)
    yield


def gather_small(spot, wires, block, whole):
    own = wires.move(block, whole.at[spot.z, spot.core, spot.corner])
    first = wires.take(spot.depth + 3)
    for step in range(1, spot.depth):
        target = whole.at[spot.z, spot.core, spot.corner]
        wires.send(block, target, spot.at(z=(spot.z + step) % spot.depth), first + step)
    yield
    own.wait()
    for step in range(1, spot.depth):
        z = (spot.z - step + spot.depth) % spot.depth
        wires.arrive(whole.at[z, spot.core, spot.corner], spot.sibling(), first + step)
    column = whole.at[:, spot.core, spot.corner]
    wires.send(column, column, spot.beside(), first)
    wires.send(column, column, spot.below(), first + spot.depth)
    wires.send(column, column, spot.at(y=1 - spot.y, x=1 - spot.x), first + spot.depth + 1)
    yield
    for flip, index in ((1, first), (2, first + spot.depth), (3, first + spot.depth + 1)):
        wires.arrive(whole.at[:, spot.core, spot.corner ^ flip], spot.sibling(), index)
    plane = whole.at[:, spot.core]
    wires.send(plane, plane, spot.sibling(), first + spot.depth + 2)
    yield
    wires.arrive(whole.at[:, 1 - spot.core], spot.sibling(), first + spot.depth + 2)
    yield


def gather_columns(spot, wires, pack, whole):
    depth, me = spot.depth, spot.corner
    ahead = wires.take(2 * depth)
    flat = wires.take(4 * depth)
    own = wires.move(pack.at[spot.core], whole.at[spot.z, spot.core])
    for step in range(1, depth):
        for flip in range(2):
            wires.send(
                pack.at[spot.core ^ flip, me],
                whole.at[spot.z, spot.core, me],
                spot.at((spot.z + step) % depth, spot.core ^ flip),
                ahead + 2 * step + flip,
            )
    wires.send(pack.at[1 - spot.core], whole.at[spot.z, spot.core], spot.sibling(), ahead)
    yield
    for step in range(1, depth):
        z = (spot.z - step + depth) % depth
        for flip in range(2):
            wires.arrive(whole.at[z, spot.core ^ flip, me], spot.sibling(), ahead + 2 * step + flip)
        quarter = whole.at[z, :, me]
        wires.send(quarter, quarter, spot.beside(), flat + 4 * step)
        wires.send(quarter, quarter, spot.below(), flat + 4 * step + 1)
    yield
    for step in range(1, depth):
        z = (spot.z - step + depth) % depth
        wires.arrive(whole.at[z, :, me ^ 1], spot.sibling(), flat + 4 * step)
        piece = whole.at[z, 0, me ^ 1]
        wires.send(piece, piece, spot.below(), flat + 4 * step + 2)
        wires.arrive(whole.at[z, :, me ^ 2], spot.sibling(), flat + 4 * step + 1)
        piece = whole.at[z, 1, me ^ 2]
        wires.send(piece, piece, spot.beside(), flat + 4 * step + 3)
    yield
    own.wait()
    wires.arrive(whole.at[spot.z, 1 - spot.core], spot.sibling(), ahead)
    for step in range(1, depth):
        z = (spot.z - step + depth) % depth
        wires.arrive(whole.at[z, 0, me ^ 3], spot.sibling(), flat + 4 * step + 2)
        wires.arrive(whole.at[z, 1, me ^ 3], spot.sibling(), flat + 4 * step + 3)
    yield


def gather_rows(spot, wires, pack, whole):
    depth, me = spot.depth, spot.corner
    ahead = wires.take(depth)
    flat = wires.take(4 * depth)
    middle = pack.shape[-1] // 2

    def part(z, corner, side):
        if pack.shape[0] == 2:
            return whole.at[side, z, corner]
        return whole.at[0, z, corner, :, pl.ds(side * middle, middle)]

    own = wires.move(pack, whole.at[:, spot.z])
    for step in range(1, depth):
        wires.send(
            pack.at[:, me], whole.at[:, spot.z, me], spot.at((spot.z + step) % depth), ahead + step
        )
    yield
    for step in range(1, depth):
        z = (spot.z - step + depth) % depth
        quarter = whole.at[:, z, me]
        wires.arrive(quarter, spot.sibling(), ahead + step)
        wires.send(quarter, quarter, spot.beside(), flat + 4 * step)
        wires.send(quarter, quarter, spot.below(), flat + 4 * step + 1)
    yield
    for step in range(1, depth):
        z = (spot.z - step + depth) % depth
        wires.arrive(whole.at[:, z, me ^ 1], spot.sibling(), flat + 4 * step)
        piece = part(z, me ^ 1, 0)
        wires.send(piece, piece, spot.below(), flat + 4 * step + 2)
        wires.arrive(whole.at[:, z, me ^ 2], spot.sibling(), flat + 4 * step + 1)
        piece = part(z, me ^ 2, 1)
        wires.send(piece, piece, spot.beside(), flat + 4 * step + 3)
    yield
    own.wait()
    for step in range(1, depth):
        z = (spot.z - step + depth) % depth
        wires.arrive(part(z, me ^ 3, 0), spot.sibling(), flat + 4 * step + 2)
        wires.arrive(part(z, me ^ 3, 1), spot.sibling(), flat + 4 * step + 3)
    yield


def reach_columns(spot, wires, pack, near):
    depth, me = spot.depth, spot.corner
    ahead = wires.take(2 * depth)
    own = wires.move(pack.at[spot.core, me], near.at[spot.z, spot.core])
    for step in range(depth):
        for flip in range(2):
            if step or flip:
                wires.send(
                    pack.at[spot.core ^ flip, me],
                    near.at[spot.z, spot.core],
                    spot.at((spot.z + step) % depth, spot.core ^ flip),
                    ahead + 2 * step + flip,
                )
    yield
    own.wait()
    for step in range(depth):
        z = (spot.z - step + depth) % depth
        for flip in range(2):
            if step or flip:
                wires.arrive(near.at[z, spot.core ^ flip], spot.sibling(), ahead + 2 * step + flip)
    yield


def reach_rows(spot, wires, pack, near):
    depth, me = spot.depth, spot.corner
    ahead = wires.take(depth)
    own = wires.move(pack.at[0, me], near.at[spot.z])
    for step in range(1, depth):
        wires.send(pack.at[0, me], near.at[spot.z], spot.at((spot.z + step) % depth), ahead + step)
    yield
    own.wait()
    for step in range(1, depth):
        z = (spot.z - step + depth) % depth
        wires.arrive(near.at[z], spot.sibling(), ahead + step)
    yield


def share_plane(spot, wires, near, whole, parts):
    me = spot.corner
    flat = wires.take(4)
    own = wires.move(near, whole(me))
    wires.send(near, whole(me), spot.beside(), flat)
    wires.send(near, whole(me), spot.below(), flat + 1)
    yield
    wires.arrive(whole(me ^ 1), spot.sibling(), flat)
    piece = parts(whole(me ^ 1), 0)
    wires.send(piece, piece, spot.below(), flat + 2)
    wires.arrive(whole(me ^ 2), spot.sibling(), flat + 1)
    piece = parts(whole(me ^ 2), 1)
    wires.send(piece, piece, spot.beside(), flat + 3)
    yield
    own.wait()
    wires.arrive(parts(whole(me ^ 3), 0), spot.sibling(), flat + 2)
    wires.arrive(parts(whole(me ^ 3), 1), spot.sibling(), flat + 3)
    yield


def scatter_buffers(depth, lanes, rows, width):
    half = depth // 2
    return [
        pltpu.VMEM((half, lanes, 2, rows, width), jnp.bfloat16),
        pltpu.VMEM((half, lanes, 2, rows, width), jnp.bfloat16),
        pltpu.VMEM((half, lanes, 2, rows, width), jnp.bfloat16),
        pltpu.VMEM((half, lanes, 2, rows, width), jnp.bfloat16),
        pltpu.VMEM((half, lanes, rows, width), jnp.bfloat16),
        pltpu.VMEM((half, lanes, rows, width), jnp.bfloat16),
        pltpu.VMEM((depth, lanes, rows, width), jnp.bfloat16),
        pltpu.VMEM((depth, lanes, rows, width), jnp.bfloat16),
        pltpu.VMEM((rows, width), jnp.bfloat16),
    ]


def scatter_sums(spot, wires, grads, buffers, total, got, resident=False):
    depth, half = spot.depth, spot.depth // 2
    lanes = grads.shape[1]
    places = [(z, a, s) for z in range(half) for a in range(lanes) for s in range(2)]
    if resident:
        low_in, high_in, low_last, high_last, column, column_in, passing = buffers
        low, high = low_in, high_in
    else:
        low, high, low_in, high_in, low_last, high_last, column, column_in, passing = buffers
    first = wires.take(4)
    away = wires.take(depth)
    mine = []
    if not resident:
        mine = [
            wires.move(grads.at[pl.ds(0, half), :, :, spot.x], low),
            wires.move(grads.at[pl.ds(half, half), :, spot.y], high),
        ]
    wires.send(grads.at[pl.ds(0, half), :, :, 1 - spot.x], low_in, spot.beside(), first)
    wires.send(grads.at[pl.ds(half, half), :, 1 - spot.y], high_in, spot.below(), first + 1)
    yield
    for copy in mine:
        copy.wait()

    def join(target, other, index):
        target[index] = (target[index].astype(jnp.float32) + other.astype(jnp.float32)).astype(jnp.bfloat16)

    wires.arrive(low_in, spot.beside(), first)
    for z, a, s in places:
        join(low, grads[z, a, s, spot.x] if resident else low_in[z, a, s], (z, a, s))
    wires.send(low.at[:, :, 1 - spot.y], low_last, spot.below(), first + 2)
    wires.arrive(high_in, spot.below(), first + 1)
    for z, a, s in places:
        join(high, grads[half + z, a, spot.y, s] if resident else high_in[z, a, s], (z, a, s))
    wires.send(high.at[:, :, 1 - spot.x], high_last, spot.beside(), first + 3)
    yield
    wires.arrive(low_last, spot.below(), first + 2)
    wires.arrive(high_last, spot.beside(), first + 3)
    for z in range(half):
        for a in range(lanes):
            column[z, a] = (
                low[z, a, spot.y].astype(jnp.float32) + low_last[z, a].astype(jnp.float32)
            ).astype(jnp.bfloat16)
            column[half + z, a] = (
                high[z, a, spot.x].astype(jnp.float32) + high_last[z, a].astype(jnp.float32)
            ).astype(jnp.bfloat16)
    for step in range(1, depth):
        z = (spot.z + step) % depth
        wires.send(column.at[z], column_in.at[step], spot.at(z), away + step)
    yield
    for step in range(1, depth):
        wires.arrive(column_in.at[step], spot.sibling(), away + step)

    def added(lane):
        result = column[spot.z, lane].astype(jnp.float32)
        for step in range(1, depth):
            result = result + column_in[step, lane].astype(jnp.float32)
        return result

    if lanes == 1:
        total[...] = added(0)
    else:
        passing[...] = added(1 - spot.core).astype(jnp.bfloat16)
        wires.send(passing, got, spot.sibling(), away)
        total[...] = added(spot.core)
    yield
    if lanes == 2:
        wires.arrive(got, spot.sibling(), away)
    yield


def total_small(spot, wires, terms, work, total):
    first = wires.take(3 + spot.depth)
    work[0] = terms[...]
    wires.send(work.at[0], work.at[1], spot.sibling(), first)
    yield
    wires.arrive(work.at[1], spot.sibling(), first)
    work[2] = work[0] + work[1]
    wires.send(work.at[2], work.at[3], spot.beside(), first + 1)
    yield
    wires.arrive(work.at[3], spot.sibling(), first + 1)
    work[4] = work[2] + work[3]
    wires.send(work.at[4], work.at[5], spot.below(), first + 2)
    yield
    wires.arrive(work.at[5], spot.sibling(), first + 2)
    work[6] = work[4] + work[5]
    for step in range(1, spot.depth):
        target = work.at[6 + step]
        wires.send(work.at[6], target, spot.at((spot.z + step) % spot.depth), first + 2 + step)
    yield
    result = work[6]
    for step in range(1, spot.depth):
        wires.arrive(work.at[6 + step], spot.sibling(), first + 2 + step)
        result = result + work[6 + step]
    total[...] = result
    yield


def wire_scratch(number, moves):
    return [
        pltpu.SemaphoreType.DMA((number,)),
        pltpu.SemaphoreType.DMA((number,)),
        pltpu.SemaphoreType.DMA((moves,)),
    ]


def spread_row(vector):
    tile = pltpu.roll(jnp.broadcast_to(vector, (8, 2 * QB)), 0, 1, stride=1, stride_axis=0)
    return spread(tile)


def attend_block(query, keys, values, keep, bias):
    scores = nt(query, keys) + keep
    if bias is not None:
        scores = scores + bias
    peak = jnp.max(scores, axis=1, keepdims=True)
    weights = jnp.exp(scores - peak)
    total = jnp.sum(weights, axis=1, keepdims=True)
    return nn(weights.astype(jnp.bfloat16), values) / total, peak + jnp.log(total)


def pair_rows(block, kv):
    both = block[:, 2 * kv * HEAD_DIM : 2 * (kv + 1) * HEAD_DIM]
    return jnp.concatenate([both[:, :HEAD_DIM], both[:, HEAD_DIM:]], axis=0)


def normed(value, gain):
    return (value * inverse_rms(value) * gain).astype(jnp.bfloat16)


def forward_layer_kernel(depth, *refs):
    (
        x, t, m, s, p1, p2, p3, p4, p5, p6, p7, codes, holes,
        o_wx, wt, o_wm, ws, o_w1, o_w2, o_w3, w4, w5,
        o_a1, o_qkv, o_ctx, lse, o_x1, o_a2, o_qc, o_ckv, o_ctxc, lsec, o_x2, o_a3, gains, keeps, keepc, bent,
        down_s, down_c, n6, n7,
        bias, own, got, own2, got2, wx, wm, w1, w2, w3, a1, qkv, ctx, x1, a2, qc, ckv, ctxc, x2, a3, *sems
    ) = refs
    leaving = []

    def leave(*pairs):
        leaving.extend(wires.move(source, target) for source, target in pairs)

    f32, bf16 = jnp.float32, jnp.bfloat16
    spot = Spot(depth)
    wires = Wires(*sems)
    blocks = 4
    kvs = 4
    inner = 2 * kvs * HEAD_DIM

    def rows(block):
        return slice(block * QB, (block + 1) * QB)

    spot.greet()
    tokens = collect_tokens(spot, wires, x, wx)
    small = gather_small(spot, wires, s, ws)
    first = gather_columns(spot, wires, p1, w1)
    memory = collect_tokens(spot, wires, m, wm)
    second = gather_columns(spot, wires, p2, w2)
    outs = gather_rows(spot, wires, p3, w3)
    wide = gather_columns(spot, wires, p4, w4)
    down = gather_rows(spot, wires, p5, w5)
    top = collect_tokens(spot, wires, t, wt)
    wide_next = reach_columns(spot, wires, p6, n6)
    down_next = reach_rows(spot, wires, p7, n7)
    over = wires.take(2 * blocks)

    def advance(*programs):
        for program in programs:
            next(program)

    advance(small, first, small, tokens, small, small)

    def line(row):
        return jnp.concatenate([ws[z, c, 0, row : row + 1, :] for z in range(depth) for c in range(2)], axis=1)

    for row in range(3):
        gains[row : row + 1, :] = line(row)
    counts = ws[spot.z, spot.x, 0, 3:4, :]
    length = jnp.where(spot.y == 0, counts[:, 0:1], counts[:, 1:2])
    span = jnp.where(spot.y == 0, counts[:, 2:3], counts[:, 3:4])
    places = lax.broadcasted_iota(jnp.int32, (1, blocks * QB), 1).astype(f32)
    keeps[...] = jnp.where(places < length, 0.0, NEG)
    keepc[...] = jnp.where(places[:, : keepc.shape[1]] < span, 0.0, NEG)
    places = lax.broadcasted_iota(jnp.int32, (blocks * QB, 1), 0).astype(f32)
    down_s[...] = jnp.where(places < length, 0.0, NEG)
    down_c[...] = jnp.where(places[: down_c.shape[0]] < span, 0.0, NEG)
    table = jnp.concatenate(
        [
            ws[z, c, 0, 4:8, :] + ws[z, c, 1, 4:8, :] + ws[z, c, 2, 4:8, :] + ws[z, c, 3, 4:8, :]
            for z in range(depth)
            for c in range(2)
        ],
        axis=0,
    )
    table = jnp.where(spot.core == 0, table[:, :64], table[:, 64:]).astype(bf16)
    vectors = tn(table, codes[...])[:8] + holes[...]
    bent[...] = vectors[:, 4 * 2 * QB :]
    for kv in range(kvs):
        for member in range(2):
            for offset in range(4):
                head = 2 * kv + member
                bias[kv, member * QB : (member + 1) * QB, (3 - offset) * QB : (4 - offset) * QB] = spread_row(
                    vectors[head : head + 1, offset * 2 * QB : (offset + 1) * 2 * QB]
                )

    advance(first, outs, second, tokens, tokens)
    for block in range(blocks):
        a1[rows(block), :] = normed(wx[block].reshape(QB, -1).astype(f32), gains[0:1, :])
    advance(first, memory, first)
    leave((wx, o_wx), (w1, o_w1), (a1, o_a1))

    def attend_rows(block, queries, keys, stop, keep, mixed, sums, causal):
        for kv in range(kvs):
            base = 2 * kv * HEAD_DIM
            query = queries[rows(block), base : base + 2 * HEAD_DIM]
            shape = None
            if causal:
                base = 4 * kv * HEAD_DIM
                query = queries[rows(block), base : base + 2 * HEAD_DIM]
                base += 2 * HEAD_DIM
                shape = bias[kv, :, (3 - block) * QB : (3 - block) * QB + stop]
            out, level = attend_block(
                pair_rows(query, 0),
                keys[:stop, base : base + HEAD_DIM],
                keys[:stop, base + HEAD_DIM : base + 2 * HEAD_DIM],
                keep[:, :stop],
                shape,
            )
            mixed[rows(block), 2 * kv * HEAD_DIM : 2 * (kv + 1) * HEAD_DIM] = jnp.concatenate(
                [out[:QB], out[QB:]], axis=1
            ).astype(bf16)
            level = jnp.broadcast_to(level, (2 * QB, 128)).T
            sums[2 * kv : 2 * kv + 1, rows(block)] = level[:1, :QB]
            sums[2 * kv + 1 : 2 * kv + 2, rows(block)] = level[:1, QB:]

    weight = w1[...].reshape(-1, w1.shape[-1])
    for block in range(blocks):
        qkv[rows(block), :] = nn(a1[rows(block), :], weight).astype(bf16)
        attend_rows(block, qkv, qkv, (block + 1) * QB, keeps, ctx, lse, True)
        if block == 1:
            advance(outs, wide, down, second, memory)
        if block == 2:
            advance(outs)
    advance(outs, second, wide, down, wide_next, down_next)

    def pass_on(block, mine, theirs, value, weight, index):
        mine[rows(block), :] = nn(value[rows(block), :], weight).astype(bf16)
        wires.send(mine.at[rows(block)], theirs.at[rows(block)], spot.sibling(), over + index + block)

    def joined(block, mine, theirs, index):
        wires.arrive(theirs.at[rows(block)], spot.sibling(), over + index + block)
        return mine[rows(block), :].astype(f32) + theirs[rows(block), :].astype(f32)

    weight = w3[0].reshape(-1, w3.shape[-1])
    for block in range(blocks):
        pass_on(block, own, got, ctx, weight, 0)
    advance(memory, second, wide, down, top)
    leave((wm, o_wm), (w2, o_w2), (w3, o_w3), (qkv, o_qkv), (ctx, o_ctx))
    weight = w2[...].reshape(-1, w2.shape[-1])
    ckv[...] = nn(wm[...].reshape(-1, wm.shape[-1]), weight[:, :inner]).astype(bf16)
    for block in range(blocks):
        value = wx[block].reshape(QB, -1).astype(f32) + joined(block, own, got, 0)
        x1[rows(block), :] = value
        a2[rows(block), :] = normed(value, gains[1:2, :])
        qc[rows(block), :] = nn(a2[rows(block), :], weight[:, inner:]).astype(bf16)
    leave((x1, o_x1), (a2, o_a2), (qc, o_qc), (ckv, o_ckv))
    weight = w3[1].reshape(-1, w3.shape[-1])
    for block in range(blocks):
        attend_rows(block, qc, ckv, ckv.shape[0], keepc, ctxc, lsec, False)
        pass_on(block, own2, got2, ctxc, weight, blocks)
        if block == 0:
            advance(wide, down)
        if block == 2:
            advance(top)
    for block in range(blocks):
        value = x1[rows(block), :] + joined(block, own2, got2, blocks)
        x2[rows(block), :] = value
        a3[rows(block), :] = normed(value, gains[2:3, :])
        leave(
            (x2.at[rows(block)], o_x2.at[rows(block)]),
            (a3.at[rows(block)], o_a3.at[rows(block)]),
            (ctxc.at[rows(block)], o_ctxc.at[rows(block)]),
        )
    advance(wide_next, down_next, top)
    for program in (tokens, small, first, memory, second, outs, wide, down, top, wide_next, down_next):
        assert next(program, None) is None
    for copy in leaving:
        copy.wait()
    wires.close()


def forward_layer(depth, x, t, m, small, p1, p2, p3, p4, p5, p6, p7, codes, holes):
    bf16, f32 = jnp.bfloat16, jnp.float32
    shape = jax.ShapeDtypeStruct

    def whole_columns(pack):
        return shape((depth, 2) + pack.shape[1:], bf16)

    def whole_rows(pack):
        return shape((pack.shape[0], depth) + pack.shape[1:], bf16)

    def whole_tokens(parcel):
        return shape((4, 2) + parcel.shape[2:], bf16)

    width = x.shape[-1]
    tokens = 8 * x.shape[2]
    span = 8 * m.shape[2]
    inner = p3.shape[0] * p3.shape[1] * p3.shape[2] * depth // 2
    heads = inner // HEAD_DIM
    hbm = pl.BlockSpec(memory_space=pl.ANY)
    vmem = pl.BlockSpec(memory_space=pltpu.VMEM)
    outs = [
        (whole_tokens(x), hbm),
        (whole_tokens(t), hbm),
        (whole_tokens(m), hbm),
        (shape((depth, 2, 4, 8, 128), f32), vmem),
        (whole_columns(p1), hbm),
        (whole_columns(p2), hbm),
        (whole_rows(p3), hbm),
        (whole_columns(p4), hbm),
        (whole_rows(p5), hbm),
        (shape((tokens, width), bf16), hbm),
        (shape((tokens, 2 * inner), bf16), hbm),
        (shape((tokens, inner), bf16), hbm),
        (shape((heads, tokens), f32), vmem),
        (shape((tokens, width), f32), hbm),
        (shape((tokens, width), bf16), hbm),
        (shape((tokens, inner), bf16), hbm),
        (shape((span, inner), bf16), hbm),
        (shape((tokens, inner), bf16), hbm),
        (shape((heads, tokens), f32), vmem),
        (shape((tokens, width), f32), hbm),
        (shape((tokens, width), bf16), hbm),
        (shape((8, width), f32), vmem),
        (shape((1, tokens), f32), vmem),
        (shape((1, span), f32), vmem),
        (shape((heads, 8 * QB), f32), vmem),
        (shape((tokens, 1), f32), vmem),
        (shape((span, 1), f32), vmem),
        (shape((depth, 2) + p6.shape[2:], bf16), hbm),
        (shape((depth,) + p7.shape[2:], bf16), hbm),
    ]
    swap = pltpu.VMEM((tokens, width), bf16)
    return pl.pallas_call(
        functools.partial(forward_layer_kernel, depth),
        in_specs=[hbm] * 11 + [vmem] * 2,
        out_specs=[spec for _, spec in outs],
        out_shape=[kind for kind, _ in outs],
        scratch_shapes=[pltpu.VMEM((heads // 2, 2 * QB, 4 * QB), f32), swap, swap, swap, swap]
        + [pltpu.VMEM(outs[i][0].shape, outs[i][0].dtype) for i in (0, 2, 4, 5, 6, 9, 10, 11, 13, 14, 15, 16, 17, 19, 20)]
        + wire_scratch(35 + 33 * depth, 40),
        compiler_params=pltpu.CompilerParams(
            collective_id=0, has_side_effects=True, vmem_limit_bytes=60 * 2**20
        ),
        cost_estimate=pl.CostEstimate(
            flops=16 * 10**9, bytes_accessed=128 * 2**20, transcendentals=10**7
        ),
    )(x, t, m, small, p1, p2, p3, p4, p5, p6, p7, codes, holes)


def pipeline(programs, ahead=2, stages=5):
    count = len(programs)
    for turn in range(count + stages):
        if turn == 0:
            for program in programs[:ahead]:
                next(program)
            yield
        for stage in range(stages - 1, 0, -1):
            index = turn - (stage - 1)
            if 0 <= index < count:
                next(programs[index])
        if turn + ahead < count:
            next(programs[turn + ahead])
        yield


def backward_tile(keys, values, query, grads, keep, bias, level, delta):
    scores = nt(keys, query) + keep
    if bias is not None:
        scores = scores + bias
    probs = jnp.exp(scores - level)
    return probs, probs * (nt(values, grads) - delta)


def row_sums(upstream, mixed):
    inner = (upstream.astype(jnp.float32) * mixed.astype(jnp.float32)).T
    return jnp.concatenate(
        [
            jnp.sum(inner[:HEAD_DIM], axis=0, keepdims=True),
            jnp.sum(inner[HEAD_DIM:], axis=0, keepdims=True),
        ],
        axis=1,
    )


def cross_backward_kernel(depth, *refs):
    g_down, g_gate, g_up, x2, x1, t_out, *far = refs[:16]
    (
        lsec, keep, gains,
        r_down, r_gate, r_up, q_gate, q_up, o_cout, o_cq, o_ckv, half, do_s, g_out, o_mem, terms, h_out,
        *rest
    ) = refs[16:]
    take = lambda n: [rest.pop(0) for _ in range(n)]
    near = take(10)
    u, top, qc, ckv, ctxc, a2, mem, w2, w3, ctx = near
    g_cout, g_cq, g_ckv = take(3)
    stage, e2, eb, do_c, dqc, dkv, dk_sum, dv_sum, got, own_c, got_c, own_m, got_m = take(13)
    buffers = [take(9) for _ in range(3)]
    f32, bf16 = jnp.float32, jnp.bfloat16
    spot = Spot(depth)
    wires = Wires(*rest)
    blocks = kvs = 4
    inner = 2 * kvs * HEAD_DIM

    def rows(block):
        return slice(block * QB, (block + 1) * QB)

    coming = [wires.move(source, target) for source, target in zip(far, near)]
    spot.greet()
    over = wires.take(2 * blocks + 4)
    for block in range(blocks):
        wires.send(far[0].at[rows(block)], got.at[rows(block)], spot.sibling(), over + block)
    home = deliver_tokens(spot, wires, t_out, h_out)
    programs = [
        scatter_sums(spot, wires, g_down, buffers[0], r_down, None),
        scatter_sums(spot, wires, g_gate, buffers[1], r_gate, q_gate),
        scatter_sums(spot, wires, g_up, buffers[2], r_up, q_up),
    ]
    links = pipeline(programs)
    next(links)
    next(home)

    loads = {}

    def fetch(source, block, slot):
        loads[slot] = wires.move(source.at[rows(block)], stage.at[slot])

    def norm_back(block, slot, gain, upstream):
        loads[slot].wait()
        value = stage[slot]
        inverse = inverse_rms(value)
        scaled = upstream * gain
        mean = jnp.mean(value * scaled, axis=-1, keepdims=True)
        change = inverse * scaled - value * (inverse * inverse * inverse) * mean
        return change, jnp.sum(upstream * value * inverse, axis=0, keepdims=True)

    fetch(x2, 0, 0)
    for copy in coming:
        copy.wait()
    gain_terms = jnp.zeros((1, e2.shape[1]), f32)
    for block in range(blocks):
        if block + 1 < blocks:
            fetch(x2, block + 1, (block + 1) % 2)
        else:
            fetch(x1, 0, 0)
        wires.arrive(got.at[rows(block)], spot.sibling(), over + block)
        change, term = norm_back(
            block, block % 2, gains[2:3, :], u[rows(block), :].astype(f32) + got[rows(block), :].astype(f32)
        )
        gain_terms = gain_terms + term
        value = top[rows(block), :].astype(f32) + change
        e2[rows(block), :] = value
        eb[rows(block), :] = value.astype(bf16)
        do_c[rows(block), :] = nt(value.astype(bf16), w3[1].reshape(inner, -1)).astype(bf16)
    terms[0:1, :] = 0.5 * gain_terms
    next(links)

    span = ckv.shape[0]
    for kv in range(kvs):
        both = slice(2 * kv * HEAD_DIM, 2 * (kv + 1) * HEAD_DIM)
        base = 2 * kv * HEAD_DIM
        dk_sum[...] = jnp.zeros_like(dk_sum)
        dv_sum[...] = jnp.zeros_like(dv_sum)
        for block in range(blocks):
            query = pair_rows(qc[rows(block), :], kv)
            grads = pair_rows(do_c[rows(block), :], kv)
            delta = row_sums(do_c[rows(block), both], ctxc[rows(block), both])
            level = jnp.concatenate(
                [lsec[2 * kv : 2 * kv + 1, rows(block)], lsec[2 * kv + 1 : 2 * kv + 2, rows(block)]], axis=1
            )
            dq = jnp.zeros((2 * QB, HEAD_DIM), f32)
            for part in range(span // QB):
                keys = ckv[rows(part), base : base + HEAD_DIM]
                values = ckv[rows(part), base + HEAD_DIM : base + 2 * HEAD_DIM]
                probs, dscores = backward_tile(keys, values, query, grads, keep[rows(part)], None, level, delta)
                dscores = dscores.astype(bf16)
                dv_sum[rows(part)] += nn(probs.astype(bf16), grads)
                dk_sum[rows(part)] += nn(dscores, query)
                dq += tn(dscores, keys)
            dqc[rows(block), both] = jnp.concatenate([dq[:QB], dq[QB:]], axis=1).astype(bf16)
        dkv[:, base : base + HEAD_DIM] = dk_sum[...].astype(bf16)
        dkv[:, base + HEAD_DIM : base + 2 * HEAD_DIM] = dv_sum[...].astype(bf16)
        if kv:
            next(links)
        if kv == 3:
            next(home)

    weight = w2[...].reshape(-1, w2.shape[-1])
    for block in range(blocks):
        own_c[rows(block), :] = nt(dqc[rows(block), :], weight[:, inner:]).astype(bf16)
        wires.send(own_c.at[rows(block)], got_c.at[rows(block)], spot.sibling(), over + blocks + block)
    own_m[...] = nt(dkv[...], weight[:, :inner]).astype(bf16).reshape(own_m.shape)
    wires.send(own_m.at[:, 1 - spot.core], got_m, spot.sibling(), over + 2 * blocks)
    for block in range(blocks):
        g_cq[block] = tn(a2[:, rows(block)], dqc[...]).reshape(g_cq.shape[1:]).astype(bf16)
    next(links)
    for block in range(blocks):
        g_ckv[block] = tn(mem[:, rows(block)], dkv[...]).reshape(g_ckv.shape[1:]).astype(bf16)
    next(links)
    for block in range(2):
        g_cout[2 * block : 2 * block + 2] = (
            tn(ctxc[:, rows(block)], eb[...]).reshape((2,) + g_cout.shape[1:]).astype(bf16)
        )
    leaving = [wires.move(*pair) for pair in ((g_cq, o_cq), (g_ckv, o_ckv), (g_cout, o_cout))]
    gain_terms = jnp.zeros((1, e2.shape[1]), f32)
    for block in range(blocks):
        if block + 1 < blocks:
            fetch(x1, block + 1, (block + 1) % 2)
        wires.arrive(got_c.at[rows(block)], spot.sibling(), over + blocks + block)
        change, term = norm_back(
            block,
            block % 2,
            gains[1:2, :],
            own_c[rows(block), :].astype(f32) + got_c[rows(block), :].astype(f32),
        )
        gain_terms = gain_terms + term
        value = e2[rows(block), :] + change
        e2[rows(block), :] = value
        half[block] = e2[pl.ds(pl.multiple_of(block * QB + spot.core * (QB // 2), QB // 2), QB // 2), :]
        eb[rows(block), :] = value.astype(bf16)
        do_s[rows(block), :] = nt(value.astype(bf16), w3[0].reshape(inner, -1)).astype(bf16)
    terms[1:2, :] = 0.5 * gain_terms
    next(links)
    for block in range(inner // QB):
        g_out[rows(block), :] = tn(ctx[:, rows(block)], eb[...]).astype(bf16)
    wires.arrive(got_m, spot.sibling(), over + 2 * blocks)
    o_mem[...] = (own_m[:, spot.core].astype(f32) + got_m[...].astype(f32)).astype(bf16)
    for _ in links:
        pass
    for program in [home]:
        for _ in program:
            pass
    for copy in leaving:
        copy.wait()
    wires.close()


def cross_part(depth, *operands):
    bf16, f32 = jnp.bfloat16, jnp.float32
    shape = jax.ShapeDtypeStruct
    hbm = pl.BlockSpec(memory_space=pl.ANY)
    vmem = pl.BlockSpec(memory_space=pltpu.VMEM)
    g_down, g_gate, g_up, x2, _, t_out, _, _, _, ckv = operands[:10]
    far = operands[6:16]
    tokens, width = x2.shape
    span, inner = ckv.shape
    own = tokens // 8
    rows = g_gate.shape[4]
    outs = [
        (shape(g_down.shape[4:], f32), vmem),
        (shape(g_gate.shape[4:], f32), vmem),
        (shape(g_up.shape[4:], f32), vmem),
        (shape(g_gate.shape[4:], bf16), vmem),
        (shape(g_up.shape[4:], bf16), vmem),
        (shape((depth, 1, 2, 2, rows, width), bf16), hbm),
        (shape((depth, 2, 2, 2, rows, inner), bf16), hbm),
        (shape((depth, 2, 2, 2, rows, inner), bf16), hbm),
        (shape((4, own, width), f32), vmem),
        (shape((tokens, inner), bf16), vmem),
        (shape((inner, width), bf16), vmem),
        (shape((4, span // 8, width), bf16), vmem),
        (shape((8, width), f32), vmem),
        (shape((2, 2) + t_out.shape[1:], bf16), hbm),
    ]
    scratch = [pltpu.VMEM(array.shape, bf16) for array in far]
    scratch += [pltpu.VMEM(outs[i][0].shape, bf16) for i in (5, 6, 7)]
    scratch += [
        pltpu.VMEM((2, QB, width), f32),
        pltpu.VMEM((tokens, width), f32),
        pltpu.VMEM((tokens, width), bf16),
        pltpu.VMEM((tokens, inner), bf16),
        pltpu.VMEM((tokens, inner), bf16),
        pltpu.VMEM((span, inner), bf16),
        pltpu.VMEM((span, HEAD_DIM), f32),
        pltpu.VMEM((span, HEAD_DIM), f32),
        pltpu.VMEM((tokens, width), bf16),
        pltpu.VMEM((tokens, width), bf16),
        pltpu.VMEM((tokens, width), bf16),
        pltpu.VMEM((4, 2, span // 8, width), bf16),
        pltpu.VMEM((4, span // 8, width), bf16),
    ]
    for grads in (g_down, g_gate, g_up):
        scratch += scatter_buffers(depth, grads.shape[1], *grads.shape[4:])
    number = 16 + 3 * (4 + depth)
    return pl.pallas_call(
        functools.partial(cross_backward_kernel, depth),
        in_specs=[hbm] * 16 + [vmem] * 3,
        out_specs=[spec for _, spec in outs],
        out_shape=[kind for kind, _ in outs],
        scratch_shapes=scratch + wire_scratch(number, 48),
        compiler_params=pltpu.CompilerParams(
            collective_id=1, has_side_effects=True, vmem_limit_bytes=60 * 2**20
        ),
        cost_estimate=pl.CostEstimate(
            flops=16 * 10**9, bytes_accessed=128 * 2**20, transcendentals=10**7
        ),
    )(*operands)


def self_backward_kernel(depth, *refs):
    (
        g_cout, g_cq, g_ckv, g_out, t_mem, f_do, f_qkv, f_ctx, f_a1, f_x, f_half, f_w1, lse, keep, bent, gains,
        terms, codes,
        r_cout, r_cq, r_ckv, r_out, r_qkv, q_cq, q_ckv, q_qkv, h_mem, h_in, packed,
        *rest
    ) = refs
    take = lambda n: [rest.pop(0) for _ in range(n)]
    bias, sums, dk_sum, dv_sum, dqkv, grad, mine, theirs, pieces, line, small, work = take(12)
    near = take(7)
    do_s, qkv, ctx, a1, x, half, w1 = near
    buffers = [take(9) for _ in range(4)]
    resident = [take(7) for _ in range(4)]
    f32, bf16 = jnp.float32, jnp.bfloat16
    spot = Spot(depth)
    wires = Wires(*rest)
    blocks = kvs = 4
    inner = 2 * kvs * HEAD_DIM

    def rows(block):
        return slice(block * QB, (block + 1) * QB)

    far = (f_do, f_qkv, f_ctx, f_a1, f_x, f_half, f_w1)
    coming = [wires.move(source, target) for source, target in zip(far, near)]
    spot.greet()
    over = wires.take(blocks)
    homes = [deliver_tokens(spot, wires, t_mem, h_mem)]
    early = pipeline(
        [
            scatter_sums(spot, wires, g_cout, buffers[0], r_cout, None),
            scatter_sums(spot, wires, g_cq, buffers[1], r_cq, q_cq),
            scatter_sums(spot, wires, g_ckv, buffers[2], r_ckv, q_ckv),
            scatter_sums(spot, wires, g_out, buffers[3], r_out, None),
        ]
    )
    late = []
    for kv in range(kvs):
        lanes = pl.ds(kv * QB, QB)
        late.append(
            scatter_sums(
                spot, wires, grad.at[kv], resident[kv], r_qkv.at[:, lanes], q_qkv.at[:, lanes], True
            )
        )
    next(early)
    for program in homes:
        next(program)
    for copy in coming:
        copy.wait()
    for kv in range(kvs):
        base = kv * 4 * HEAD_DIM
        both = slice(2 * kv * HEAD_DIM, 2 * (kv + 1) * HEAD_DIM)
        dk_sum[...] = jnp.zeros_like(dk_sum)
        dv_sum[...] = jnp.zeros_like(dv_sum)
        sums[...] = jnp.zeros_like(sums)
        for member in range(2):
            for offset in range(4):
                head = 2 * kv + member
                bias[offset, :, member * QB : (member + 1) * QB] = spread_row(
                    bent[head : head + 1, offset * 2 * QB : (offset + 1) * 2 * QB]
                )
        for block in range(blocks):
            query = pair_rows(qkv[rows(block), base : base + 2 * HEAD_DIM], 0)
            grads = pair_rows(do_s[rows(block), :], kv)
            delta = row_sums(do_s[rows(block), both], ctx[rows(block), both])
            level = jnp.concatenate(
                [lse[2 * kv : 2 * kv + 1, rows(block)], lse[2 * kv + 1 : 2 * kv + 2, rows(block)]], axis=1
            )
            dq = jnp.zeros((2 * QB, HEAD_DIM), f32)
            for part in range(block + 1):
                keys = qkv[rows(part), base + 2 * HEAD_DIM : base + 3 * HEAD_DIM]
                values = qkv[rows(part), base + 3 * HEAD_DIM : base + 4 * HEAD_DIM]
                probs, dscores = backward_tile(
                    keys, values, query, grads, keep[rows(part)], bias[block - part], level, delta
                )
                sums[block - part] += dscores
                dscores = dscores.astype(bf16)
                dv_sum[rows(part)] += nn(probs.astype(bf16), grads)
                dk_sum[rows(part)] += nn(dscores, query)
                dq += tn(dscores, keys)
            dqkv[rows(block), base : base + 2 * HEAD_DIM] = jnp.concatenate(
                [dq[:QB], dq[QB:]], axis=1
            ).astype(bf16)
            if block % 2 or kv == 0 and block:
                next(early, None)
            for earlier in range(kv):
                if block == 2:
                    next(late[earlier], None)
        dqkv[:, base + 2 * HEAD_DIM : base + 3 * HEAD_DIM] = dk_sum[...].astype(bf16)
        dqkv[:, base + 3 * HEAD_DIM : base + 4 * HEAD_DIM] = dv_sum[...].astype(bf16)
        for member in range(2):
            for offset in range(4):
                tile = fold(sums[offset, :, member * QB : (member + 1) * QB])
                row = tile[0:1]
                for r in range(1, 8):
                    row = row + pltpu.roll(tile[r : r + 1], 2 * QB - r, 1)
                head = 2 * kv + member
                line[head : head + 1, (offset + 1) * QB : (offset + 2) * QB] = row[:, :QB]
                if offset > 0:
                    line[head : head + 1, offset * QB : (offset + 1) * QB] += row[:, QB:]
        chunk = dqkv[:, base : base + 4 * HEAD_DIM]
        for block in range(blocks):
            grad[kv, block] = tn(a1[:, rows(block)], chunk).astype(bf16).reshape(grad.shape[2:])
        next(late[kv])
        if kv == 1:
            for program in homes:
                next(program)
    weight = w1[...].reshape(-1, w1.shape[-1])
    size = QB // 2

    def half_rows(block, core):
        return pl.ds(pl.multiple_of(block * QB + core * size, size), size)

    for block in range(blocks):
        mine[block] = nt(dqkv[half_rows(block, 1 - spot.core), :], weight).astype(bf16)
        wires.send(mine.at[block], theirs.at[block], spot.sibling(), over + block)
    for program in late:
        next(program, None)
    gain_terms = jnp.zeros((1, x.shape[-1]), f32)
    for block in range(blocks):
        upstream = nt(dqkv[half_rows(block, spot.core), :], weight).astype(bf16).astype(f32)
        wires.arrive(theirs.at[block], spot.sibling(), over + block)
        upstream = upstream + theirs[block].astype(f32)
        value = x[block, spot.core].astype(f32)
        inverse = inverse_rms(value)
        scaled = upstream * gains[0:1, :]
        mean = jnp.mean(value * scaled, axis=-1, keepdims=True)
        change = inverse * scaled - value * (inverse * inverse * inverse) * mean
        gain_terms = gain_terms + jnp.sum(upstream * value * inverse, axis=0, keepdims=True)
        pieces[block] = (half[block] + change).astype(bf16)
    homing = deliver_tokens(spot, wires, pieces, h_in)
    next(homing)
    shares = nt_exact(line[:, QB:], codes[...])
    small[...] = jnp.zeros_like(small)
    for r in range(8):
        lanes = slice(r * 128, (r + 1) * 128)
        small[r : r + 1, :] = terms[0:1, lanes]
        small[8 + r : 9 + r, :] = terms[1:2, lanes]
        small[16 + r : 17 + r, :] = gain_terms[:, lanes]
    zero = jnp.zeros_like(shares)
    small[24:32, :BUCKETS] = jnp.where(spot.core == 0, shares, zero)
    small[24:32, BUCKETS : 2 * BUCKETS] = jnp.where(spot.core == 1, shares, zero)
    summing = total_small(spot, wires, small, work, packed)
    next(summing)
    for _ in range(4):
        next(summing, None)
        for program in late:
            next(program, None)
    for program in late + homes + [homing, summing]:
        for _ in program:
            pass
    for _ in early:
        pass
    wires.close()


def nt_exact(left, right):
    return lax.dot_general(
        left, right, (((1,), (1,)), ((), ())), precision=HIGH, preferred_element_type=jnp.float32
    )


def self_part(depth, *operands):
    bf16, f32 = jnp.bfloat16, jnp.float32
    shape = jax.ShapeDtypeStruct
    hbm = pl.BlockSpec(memory_space=pl.ANY)
    vmem = pl.BlockSpec(memory_space=pltpu.VMEM)
    _, g_cq, _, g_out, t_mem, do_s = operands[:6]
    tokens, inner = do_s.shape
    width = g_out.shape[-1]
    rows = g_out.shape[4]
    own = tokens // 8
    outs = [
        (shape((rows, width), f32), vmem),
        (shape((rows, inner), f32), vmem),
        (shape((rows, inner), f32), vmem),
        (shape((rows, width), f32), vmem),
        (shape((rows, 2 * inner), f32), vmem),
        (shape((rows, inner), bf16), vmem),
        (shape((rows, inner), bf16), vmem),
        (shape((rows, 2 * inner), bf16), vmem),
        (shape((2, 2) + t_mem.shape[1:], bf16), hbm),
        (shape((2, 2, own, width), bf16), hbm),
        (shape((32, 128), f32), vmem),
    ]
    scratch = [
        pltpu.VMEM((4, QB, 2 * QB), f32),
        pltpu.VMEM((4, QB, 2 * QB), f32),
        pltpu.VMEM((tokens, HEAD_DIM), f32),
        pltpu.VMEM((tokens, HEAD_DIM), f32),
        pltpu.VMEM((tokens, 2 * inner), bf16),
        pltpu.VMEM((4, depth, 2, 2, 2, rows, QB), bf16),
        pltpu.VMEM((4, own, width), bf16),
        pltpu.VMEM((4, own, width), bf16),
        pltpu.VMEM((4, own, width), bf16),
        pltpu.VMEM((8, 5 * QB), f32),
        pltpu.VMEM((32, 128), f32),
        pltpu.VMEM((6 + depth, 32, 128), f32),
    ]
    scratch += [pltpu.VMEM(array.shape, array.dtype) for array in operands[5:12]]
    for lanes, size in ((1, width), (2, inner), (2, inner), (1, width)):
        scratch += scatter_buffers(depth, lanes, rows, size)
    for _ in range(4):
        scratch += scatter_buffers(depth, 2, rows, QB)[2:]
    return pl.pallas_call(
        functools.partial(self_backward_kernel, depth),
        in_specs=[hbm] * 12 + [vmem] * 6,
        out_specs=[spec for _, spec in outs],
        out_shape=[kind for kind, _ in outs],
        scratch_shapes=scratch + wire_scratch(4 + 8 + 3 + depth + 8 * (4 + depth), 20),
        compiler_params=pltpu.CompilerParams(
            collective_id=2, has_side_effects=True, vmem_limit_bytes=60 * 2**20
        ),
        cost_estimate=pl.CostEstimate(
            flops=16 * 10**9, bytes_accessed=128 * 2**20, transcendentals=10**7
        ),
    )(*operands)


def feed_forward_kernel(depth, tiles, *refs):
    (
        a3_far, wt_far, valid, x2, gu0_far, d0_far, gu1p, d1p, gu2p, d2p,
        o_top, o_u, pieces, g_gate2, g_up2, g_down2,
        r_gate0, r_up0, r_down0, r_gate1, r_up1, r_down1, q_gate0, q_up0, q_gate1, q_up1,
        *rest
    ) = refs
    take = lambda n: [rest.pop(0) for _ in range(n)]
    gu1, d1, gu2, d2, mid, dgate, dup, g0, g1, g2, g3, g4, g5, mine, theirs, second = take(16)
    a3, wt, gu0, d0, low_top, u = take(6)
    buffers = [take(7) for _ in range(6)]
    f32, bf16 = jnp.float32, jnp.bfloat16
    spot = Spot(depth)
    wires = Wires(*rest)
    blocks = 4
    starts = [sum(tiles[:i]) for i in range(3)]
    coming = [
        wires.move(source, target)
        for source, target in ((wt_far, wt), (a3_far, a3), (gu0_far, gu0), (d0_far, d0))
    ]

    def rows(block):
        return slice(block * QB, (block + 1) * QB)

    spot.greet()
    over = wires.take(blocks)
    middle = d1.shape[-1] // 2
    wide1 = share_plane(
        spot, wires, gu1p, lambda corner: gu1.at[:, :, corner], lambda view, side: view.at[:, side]
    )
    down1 = share_plane(
        spot,
        wires,
        d1p,
        lambda corner: d1.at[0, :, corner],
        lambda view, side: view.at[:, :, pl.ds(side * middle, middle)],
    )
    wide2 = gather_columns(spot, wires, gu2p, gu2)
    down2 = gather_rows(spot, wires, d2p, d2)
    sums = [
        scatter_sums(spot, wires, grads, scratch, total, got, True)
        for grads, scratch, total, got in (
            (g0, buffers[0], r_gate0, q_gate0),
            (g1, buffers[1], r_up0, q_up0),
            (g2, buffers[2], r_down0, None),
            (g3, buffers[3], r_gate1, q_gate1),
            (g4, buffers[4], r_up1, q_up1),
            (g5, buffers[5], r_down1, None),
        )
    ]

    def advance(*programs):
        for program in programs:
            next(program, None)

    advance(wide1, down1, wide2, down2)
    halves = [
        wires.move(
            x2.at[pl.ds(pl.multiple_of(block * QB + spot.core * (QB // 2), QB // 2), QB // 2)], second.at[block]
        )
        for block in range(blocks)
    ]
    for copy in coming:
        copy.wait()
    for block in range(blocks):
        value = wt[block].reshape(QB, -1).astype(f32) * valid[rows(block)]
        low_top[rows(block), :] = value.astype(bf16)
    coming = [wires.move(low_top, o_top)]
    wides = [gu0, gu1, gu2]
    downs = [d0, d1, d2]

    def wide_weight(tile, part):
        both = wides[tile]
        lanes = pl.ds(part * tiles[tile], tiles[tile])
        return both[:, :, :, :, lanes].reshape(-1, tiles[tile])

    def down_weight(tile):
        weight = downs[tile][0]
        if weight.shape[2] % 16:
            return weight.astype(f32).reshape(tiles[tile], -1).astype(bf16)
        return weight.reshape(tiles[tile], -1)

    def hidden(tile, block):
        lanes = slice(starts[tile], starts[tile] + tiles[tile])
        left = a3[rows(block), :]
        gate = nn(left, wide_weight(tile, 0))
        upward = nn(left, wide_weight(tile, 1))
        back = nt(low_top[rows(block), :], down_weight(tile))
        bend = jnp.tanh(GELU_SCALE * (gate + GELU_CUBE * gate * gate * gate))
        share = 0.5 * (1.0 + bend)
        active = gate * share
        slope = share + 0.5 * gate * (1.0 - bend * bend) * (
            GELU_SCALE * (1.0 + 3.0 * GELU_CUBE * gate * gate)
        )
        mid[rows(block), lanes] = (active * upward).astype(bf16)
        dgate[rows(block), lanes] = (back * upward * slope).astype(bf16)
        dup[rows(block), lanes] = (back * active).astype(bf16)

    def wide_grads(tile, source, target):
        lanes = slice(starts[tile], starts[tile] + tiles[tile])
        right = source[:, lanes]
        for block in range(blocks):
            target[block] = tn(a3[:, rows(block)], right).reshape(target.shape[1:]).astype(bf16)

    def down_grads(tile, target):
        lanes = slice(starts[tile], starts[tile] + tiles[tile])
        target[...] = tn(mid[:, lanes], low_top[...]).reshape(target.shape).astype(bf16)

    hidden(0, 0)
    hidden(0, 1)
    hidden(0, 2)
    hidden(0, 3)
    wide_grads(0, dgate, g0)
    advance(sums[0])
    wide_grads(0, dup, g1)
    advance(wide1, down1, wide2, down2)
    down_grads(0, g2)
    advance(wide1, down1, sums[1])
    for block in range(blocks):
        hidden(1, block)
        if block == 1:
            advance(sums[0], wide2, down2, sums[2])
    advance(sums[1])
    wide_grads(1, dgate, g3)
    advance(sums[0], wide2, down2, sums[3])
    wide_grads(1, dup, g4)
    advance(sums[2], sums[1])
    down_grads(1, g5)
    advance(sums[0], sums[4])
    for block in range(blocks):
        hidden(2, block)
        if block == 1:
            advance(sums[3], sums[2], sums[5])
        if block == 3:
            advance(sums[1], sums[0])
    wide_grads(2, dgate, g_gate2)
    wide_grads(2, dup, g_up2)
    advance(sums[4], sums[3], sums[2])
    down_grads(2, g_down2)

    def half_rows(block, core):
        return pl.ds(pl.multiple_of(block * QB + core * (QB // 2), QB // 2), QB // 2)

    def contribution(block, core):
        total = None
        for tile in range(3):
            lanes = slice(starts[tile], starts[tile] + tiles[tile])
            term = nn(mid[half_rows(block, core), lanes], down_weight(tile))
            total = term if total is None else total + term
        return total.astype(bf16)

    for block in range(blocks):
        mine[block] = contribution(block, 1 - spot.core)
        wires.send(mine.at[block], theirs.at[block], spot.sibling(), over + block)
    for block in range(blocks):
        total = None
        for tile in range(3):
            lanes = slice(starts[tile], starts[tile] + tiles[tile])
            term = nt(dgate[rows(block), lanes], wide_weight(tile, 0))
            term = term + nt(dup[rows(block), lanes], wide_weight(tile, 1))
            total = term if total is None else total + term
        u[rows(block), :] = total.astype(bf16)
        coming.append(wires.move(u.at[rows(block)], o_u.at[rows(block)]))
        if block == 1:
            advance(sums[5], sums[4], sums[3])
    advance(sums[5], sums[4])
    for block in range(blocks):
        value = contribution(block, spot.core).astype(f32)
        wires.arrive(theirs.at[block], spot.sibling(), over + block)
        value = value + theirs[block].astype(f32)
        halves[block].wait()
        pieces[block] = ((second[block] + value) * valid[half_rows(block, spot.core), :]).astype(bf16)
    for program in sums + [wide1, down1, wide2, down2]:
        for _ in program:
            pass
    for copy in coming:
        copy.wait()
    wires.close()


def feed_forward(depth, tiles, *operands):
    bf16, f32 = jnp.bfloat16, jnp.float32
    shape = jax.ShapeDtypeStruct
    hbm = pl.BlockSpec(memory_space=pl.ANY)
    vmem = pl.BlockSpec(memory_space=pltpu.VMEM)
    a3, _, _, _, gu0, d0, gu1p, d1p, gu2p, d2p = operands
    tokens, width = a3.shape
    hidden_width = sum(tiles)
    rows = [d1p.shape[1], d1p.shape[1], d2p.shape[2]]
    own = tokens // 8
    wide = gu2p.shape[2]

    def wide_grad(tile):
        return (depth, 2, 2, 2, wide, tiles[tile])

    def down_grad(tile):
        return (depth, 1, 2, 2, rows[tile], width)

    outs = [
        (shape((tokens, width), bf16), hbm),
        (shape((tokens, width), bf16), hbm),
        (shape((4, own, width), bf16), vmem),
        (shape(wide_grad(2), bf16), vmem),
        (shape(wide_grad(2), bf16), vmem),
        (shape(down_grad(2), bf16), vmem),
    ]
    for tile in range(2):
        outs += [(shape((wide, tiles[tile]), f32), vmem)] * 2 + [(shape((rows[tile], width), f32), vmem)]
    for tile in range(2):
        outs += [(shape((wide, tiles[tile]), bf16), vmem)] * 2
    scratch = [
        pltpu.VMEM(gu0.shape, bf16),
        pltpu.VMEM(d0.shape, bf16),
        pltpu.VMEM((depth, 2) + gu2p.shape[1:], bf16),
        pltpu.VMEM((1, depth) + d2p.shape[1:], bf16),
    ]
    scratch += [pltpu.VMEM((tokens, hidden_width), bf16)] * 3
    for tile in range(2):
        scratch += [pltpu.VMEM(wide_grad(tile), bf16)] * 2 + [pltpu.VMEM(down_grad(tile), bf16)]
    scratch += [
        pltpu.VMEM((4, own, width), bf16),
        pltpu.VMEM((4, own, width), bf16),
        pltpu.VMEM((4, own, width), f32),
        pltpu.VMEM((tokens, width), bf16),
        pltpu.VMEM((4, 2, own, width), bf16),
        pltpu.VMEM(gu0.shape, bf16),
        pltpu.VMEM(d0.shape, bf16),
        pltpu.VMEM((tokens, width), bf16),
        pltpu.VMEM((tokens, width), bf16),
    ]
    for tile in range(2):
        for _ in range(2):
            scratch += scatter_buffers(depth, 2, wide, tiles[tile])[2:]
        scratch += scatter_buffers(depth, 1, rows[tile], width)[2:]
    return pl.pallas_call(
        functools.partial(feed_forward_kernel, depth, tiles),
        in_specs=[hbm, hbm, vmem] + [hbm] * 7,
        out_specs=[spec for _, spec in outs],
        out_shape=[kind for kind, _ in outs],
        scratch_shapes=scratch + wire_scratch(4 + 22 * depth + 6 * (4 + depth), 24),
        compiler_params=pltpu.CompilerParams(
            collective_id=3, has_side_effects=True, vmem_limit_bytes=60 * 2**20
        ),
        cost_estimate=pl.CostEstimate(
            flops=27 * 10**9, bytes_accessed=64 * 2**20, transcendentals=10**7
        ),
    )(*operands)


def parity_columns(weights):
    rows = weights[0].shape[0]
    pack = jnp.concatenate([w.reshape(rows, 4, 2, -1) for w in weights], axis=3)
    return jnp.moveaxis(pack, 2, 0).reshape(2, rows, -1)


def per_chip(
    layer_input,
    memory,
    target_lengths,
    memory_lengths,
    buckets,
    norm_self,
    self_q,
    self_k,
    self_v,
    self_out,
    rel_bias,
    norm_cross,
    cross_q,
    cross_k,
    cross_v,
    cross_out,
    norm_ff,
    ff_gate,
    ff_up,
    ff_down,
    cotangent,
):
    bf16, f32 = jnp.bfloat16, jnp.float32
    depth = lax.axis_size("dp") // 2
    spot = Spot(depth)
    core = spot.core
    width = layer_input.shape[3]
    local = layer_input.shape[2]
    near = memory.shape[2]
    shard = norm_self.shape[0]

    def column_pack(*groups):
        pack = jnp.concatenate([parity_columns(weights) for weights in groups], axis=2)
        return pack.reshape(2, 4, -1, pack.shape[2])

    cuts = [(0, 32), (32, 64), (64, ff_down.shape[0] // 4)]
    tiles = tuple(16 * (stop - start) for start, stop in cuts)
    down_packs = [ff_down.reshape(4, -1, width)[None, :, start:stop] for start, stop in cuts]

    def wide_pack(weights, start, stop):
        sides = [
            jnp.moveaxis(w.reshape(-1, 4, 2, 4, w.shape[1] // 32)[..., start:stop], 2, 0).reshape(
                2, 4, -1, 16 * (stop - start)
            )
            for w in weights
        ]
        return jnp.concatenate(sides, axis=3)

    wide_packs = [wide_pack([ff_gate, ff_up], start, stop) for start, stop in cuts]
    heads = jnp.arange(4)
    spots = (heads // 2) * 64 + 2 * spot.corner + heads % 2
    placed = jnp.sum(
        jnp.where(jnp.arange(128)[None, None, :] == spots[None, :, None], rel_bias[:, :, None].astype(f32), 0.0),
        axis=1,
    )
    lengths = jnp.concatenate([target_lengths, memory_lengths]).reshape(1, 4).astype(f32)
    small = jnp.concatenate(
        [
            jnp.stack([norm_self, norm_cross, norm_ff]).astype(f32),
            jnp.pad(lengths, ((0, 0), (0, 124))),
            placed,
        ]
    )
    padded = jnp.concatenate([jnp.full((1, QB), -1, jnp.int32), buckets[None, :]], axis=1)
    vectors = row_pieces(padded)
    vectors = jnp.concatenate([jnp.roll(vectors[..., ::-1], 1, axis=-1), vectors], axis=1).reshape(1, -1)
    codes = (vectors == jnp.arange(BUCKETS, dtype=jnp.int32)[:, None]).astype(bf16)
    holes = jnp.where(vectors < 0, NEG, 0.0).astype(f32)
    onehot = (buckets[:, None] == jnp.arange(BUCKETS, dtype=jnp.int32)[None, :]).astype(f32)
    (
        inputs, upstream, encoded, _, w_qkv, w_cross, w_outs, w_gu, w_down,
        normed_self, qkv, context, self_sums, first, normed_cross, cross_queries, far_kv, cross_context,
        cross_sums, second, normed_ff, gains, _, _, bent, keep_self, keep_cross, near_wide, near_down,
    ) = forward_layer(
        depth,
        layer_input.reshape(2, 2, local // 2, width),
        cotangent.reshape(2, 2, local // 2, width),
        memory.reshape(2, 2, near // 2, width),
        small,
        column_pack([self_q, self_k, self_v]),
        column_pack([cross_k, cross_v], [cross_q]),
        jnp.stack([self_out, cross_out]).reshape(2, 4, -1, width),
        wide_packs[0],
        down_packs[0],
        wide_packs[1],
        down_packs[1],
        codes,
        holes,
    )
    encoded = encoded.reshape(-1, width)
    valid = (keep_self == 0).astype(f32)
    (
        top_low, changed, output, g_gate, g_up, g_down,
        r_gate0, r_up0, r_down0, r_gate1, r_up1, r_down1, q_gate0, q_up0, q_gate1, q_up1,
    ) = feed_forward(
        depth, tiles, normed_ff, upstream, valid, second, w_gu, w_down,
        near_wide, near_down, wide_packs[2], down_packs[2],
    )

    (
        r_down2, r_gate2, r_up2, q_gate2, q_up2, g_cout, g_cq, g_ckv, half, self_up, g_out, memory_grad, terms,
        output,
    ) = cross_part(
        depth, g_down, g_gate, g_up, second, first, output, changed, top_low, cross_queries, far_kv, cross_context,
        normed_cross, encoded, w_cross, w_outs, context, cross_sums, keep_cross, gains,
    )
    r_cout, r_cq, r_ckv, r_out, r_qkv, q_cq, q_ckv, q_qkv, memory_grad, input_grad, packed = self_part(
        depth, g_cout, g_cq, g_ckv, g_out.reshape(depth, 1, 2, 2, -1, width), memory_grad, self_up, qkv, context,
        normed_self, inputs, half, w_qkv, self_sums, keep_self, bent, gains, terms, onehot.T,
    )
    bias_grad = packed[24:, :64].reshape(4, 2, 2, BUCKETS)
    bias_grad = jnp.transpose(bias_grad, (3, 0, 2, 1)).reshape(BUCKETS, HEADS)
    packed = packed[:24].reshape(3, width)
    mine = lax.axis_index("dp") * 4 + spot.corner
    piece = width // (depth * 8)
    n_ff, n_cross, n_self = (lax.dynamic_slice_in_dim(packed[i], mine * piece, piece) for i in range(3))
    bias_grad = lax.dynamic_slice(
        bias_grad, (lax.axis_index("dp") * rel_bias.shape[0], spot.corner * rel_bias.shape[1]), rel_bias.shape
    )

    def merge(own, got, *sizes):
        rows = own.shape[0]
        got = got.astype(f32)
        even, odd = jnp.where(core == 0, own, got), jnp.where(core == 0, got, own)
        both = jnp.stack([even.reshape(rows, 4, -1), odd.reshape(rows, 4, -1)], axis=2)
        results, start = [], 0
        for size in sizes or both.shape[3:]:
            results.append(both[..., start : start + size].reshape(rows, -1))
            start += size
        return results

    d_q, d_k, d_v = merge(r_qkv, q_qkv, 2 * HEAD_DIM, HEAD_DIM, HEAD_DIM)
    d_ck, d_cv = merge(r_ckv, q_ckv, HEAD_DIM, HEAD_DIM)
    (d_cq,) = merge(r_cq, q_cq)

    def join(owns, gots):
        sides = []
        for own, got in zip(owns, gots):
            got = got.astype(f32)
            sides.append(
                jnp.stack([jnp.where(core == 0, own, got), jnp.where(core == 0, got, own)]).reshape(
                    2, own.shape[0], 4, 4, -1
                )
            )
        whole = jnp.concatenate(sides, axis=4)
        return jnp.transpose(whole, (1, 2, 0, 3, 4)).reshape(whole.shape[1], -1)

    d_gate = join((r_gate0, r_gate1, r_gate2), (q_gate0, q_gate1, q_gate2))
    d_up = join((r_up0, r_up1, r_up2), (q_up0, q_up1, q_up2))
    r_down = jnp.concatenate([r_down0, r_down1, r_down2], axis=0)
    return (
        output.reshape(layer_input.shape),
        input_grad.astype(f32).reshape(layer_input.shape),
        memory_grad.astype(f32).reshape(memory.shape),
        n_self,
        d_q,
        d_k,
        d_v,
        r_out,
        bias_grad,
        n_cross,
        d_cq,
        d_ck,
        d_cv,
        r_cout,
        n_ff,
        d_gate,
        d_up,
        r_down,
    )


def solution(mesh):
    placed = (
        P(None, "dp", "seq", None),
        P(None, "dp", "seq", None),
        P(None, "dp"),
        P(None, "dp"),
        P(),
        P("dp"),
        P("dp", None),
        P("dp", None),
        P("dp", None),
        P("dp", None),
        P("dp", "seq"),
        P("dp"),
        P("dp", None),
        P("dp", None),
        P("dp", None),
        P("dp", None),
        P("dp"),
        P("dp", None),
        P("dp", None),
        P("dp", None),
        P(None, "dp", "seq", None),
    )
    chips = mesh.shape["seq"] == 4 and mesh.shape["dp"] == HEADS // 2
    return jax.shard_map(
        per_chip if chips else per_device,
        mesh=mesh,
        in_specs=placed,
        out_specs=(
            P(None, "dp", "seq", None),
            P(None, "dp", "seq", None),
            P(None, "dp", "seq", None),
            P(("dp", "seq")),
            P(("dp", "seq"), None),
            P(("dp", "seq"), None),
            P(("dp", "seq"), None),
            P(("dp", "seq"), None),
            P("dp", "seq"),
            P(("dp", "seq")),
            P(("dp", "seq"), None),
            P(("dp", "seq"), None),
            P(("dp", "seq"), None),
            P(("dp", "seq"), None),
            P(("dp", "seq")),
            P(("dp", "seq"), None),
            P(("dp", "seq"), None),
            P(("dp", "seq"), None),
        ),
        check_vma=False,
    )
```

```python
import functools

import jax
import jax.numpy as jnp
from jax import lax
from jax.experimental import pallas as pl
from jax.experimental.pallas import tpu as pltpu
from jax.sharding import PartitionSpec as P

HEADS = 16
HEAD_DIM = 64
BUCKETS = 32
KV_HEADS = 8
TGT = 1024
MEM = 512
QB = 256
GELU_SCALE = 0.7978845608
GELU_CUBE = 0.044715


EPS = 1e-06
NEG = -1e30
HIGH = lax.Precision.HIGHEST


def shortened(shard):
    return jax.tree.map(lambda a: a.astype(jnp.bfloat16) if a.dtype == jnp.float32 else a, shard)


def rms_norm(value, gain):
    return value * lax.rsqrt(jnp.mean(value * value, axis=-1, keepdims=True) + EPS) * gain


def gated(gate, upward):
    return jax.nn.gelu(gate, approximate=True) * upward


def project(left, right):
    return jnp.dot(left, right, preferred_element_type=jnp.float32)


def project_back(grad, weight):
    return lax.dot_general(
        grad, weight, (((1,), (1,)), ((), ())), preferred_element_type=jnp.float32
    )


def weight_grad(left, right):
    return lax.dot_general(
        left, right, (((0,), (0,)), ((), ())), preferred_element_type=jnp.float32
    )


def split_heads(values, group):
    return values.reshape(values.shape[:2] + (-1, group, HEAD_DIM))


def split_shared(values):
    return values.reshape(values.shape[:2] + (-1, HEAD_DIM))


def causal_masks(table, length, group):

    def masks(start, block):
        stop = start + block
        rows = start + jnp.arange(block, dtype=jnp.int32)
        columns = jnp.arange(stop, dtype=jnp.int32)
        distance = rows[:, None] - columns[None, :]
        keep = (distance >= 0) & (columns[None, :] < length)
        extra = jnp.take(table, jnp.maximum(distance, 0), axis=1)
        return (extra.reshape((-1, group, block, stop)), keep, stop)

    return masks


def memory_masks(length, width):

    def masks(start, block):
        keep = jnp.broadcast_to(
            jnp.arange(width, dtype=jnp.int32)[None, :] < length, (block, width)
        )
        return (None, keep, width)

    return masks


def diagonal_sums(grads, block, stop):
    leading = grads.shape[:2]
    flipped = jnp.pad(grads[..., ::-1], ((0, 0), (0, 0), (0, 0), (0, block)))
    skewed = flipped.reshape(leading + (block * (stop + block),))[..., : block * (stop + block - 1)]
    skewed = skewed.reshape(leading + (block, stop + block - 1))
    return jnp.sum(skewed, axis=2)[..., block - 1 :]


def attend_forward(queries, keys, values, masks):
    block = min(512, queries.shape[0])
    outputs = []
    totals = []
    for index in range(queries.shape[0] // block):
        start = index * block
        extra, keep, stop = masks(start, block)
        rows = queries[start : start + block]
        scores = jnp.einsum("rkgd,skd->kgrs", rows, keys[:stop], preferred_element_type=jnp.float32)
        if extra is not None:
            scores = scores + extra
        scores = jnp.where(keep, scores, NEG)
        peak = jnp.max(scores, axis=-1, keepdims=True)
        weights = jnp.where(keep, jnp.exp(scores - peak), 0.0)
        total = jnp.sum(weights, axis=-1, keepdims=True)
        probs = (weights / total).astype(jnp.bfloat16)
        mixed = jnp.einsum(
            "kgrs,skd->rkgd", probs, values[:stop], preferred_element_type=jnp.float32
        )
        outputs.append(mixed.astype(jnp.bfloat16))
        totals.append(peak + jnp.log(total))
    return (jnp.concatenate(outputs, 0), jnp.concatenate(totals, 2))


def attend_backward(queries, keys, values, sums, grads, masks):
    block = min(512, queries.shape[0])
    key_grads = jnp.zeros(keys.shape, jnp.float32)
    value_grads = jnp.zeros(values.shape, jnp.float32)
    diagonal = jnp.zeros(sums.shape[:3], jnp.float32)
    query_grads = []
    for index in range(queries.shape[0] // block):
        start = index * block
        extra, keep, stop = masks(start, block)
        rows = queries[start : start + block]
        grad_rows = grads[start : start + block]
        scores = jnp.einsum("rkgd,skd->kgrs", rows, keys[:stop], preferred_element_type=jnp.float32)
        if extra is not None:
            scores = scores + extra
        scores = jnp.where(keep, scores, NEG)
        probs = jnp.where(keep, jnp.exp(scores - sums[:, :, start : start + block]), 0.0)
        value_grads = value_grads.at[:stop].add(
            jnp.einsum(
                "kgrs,rkgd->skd",
                probs.astype(jnp.bfloat16),
                grad_rows,
                preferred_element_type=jnp.float32,
            )
        )
        dprobs = jnp.einsum(
            "rkgd,skd->kgrs", grad_rows, values[:stop], preferred_element_type=jnp.float32
        )
        delta = jnp.sum(probs * dprobs, axis=-1, keepdims=True)
        dscores = (probs * (dprobs - delta)).astype(jnp.bfloat16)
        query_grads.append(
            jnp.einsum(
                "kgrs,skd->rkgd", dscores, keys[:stop], preferred_element_type=jnp.float32
            ).astype(jnp.bfloat16)
        )
        key_grads = key_grads.at[:stop].add(
            jnp.einsum("kgrs,rkgd->skd", dscores, rows, preferred_element_type=jnp.float32)
        )
        if extra is not None:
            diagonal = diagonal.at[:, :, :stop].add(
                diagonal_sums(dscores.astype(jnp.float32), block, stop)
            )
    return (
        jnp.concatenate(query_grads, 0),
        key_grads.astype(jnp.bfloat16),
        value_grads.astype(jnp.bfloat16),
        diagonal,
    )


def self_forward(queries, keys, values, length, table):
    return attend_forward(queries, keys, values, causal_masks(table, length, queries.shape[2]))


def self_backward(queries, keys, values, sums, grads, length, table):
    return attend_backward(
        queries, keys, values, sums, grads, causal_masks(table, length, queries.shape[2])
    )


def cross_forward(queries, keys, values, length):
    return attend_forward(queries, keys, values, memory_masks(length, keys.shape[0]))


def cross_backward(queries, keys, values, sums, grads, length):
    return attend_backward(queries, keys, values, sums, grads, memory_masks(length, keys.shape[0]))


def to_tokens(values):
    return lax.all_to_all(shortened(values), "seq", split_axis=1, concat_axis=2, tiled=True).astype(
        values.dtype
    )


def to_heads(grads):
    return lax.all_to_all(grads, "seq", split_axis=2, concat_axis=1, tiled=True)


def per_device(
    layer_input,
    memory,
    target_lengths,
    memory_lengths,
    buckets,
    norm_self,
    self_q,
    self_k,
    self_v,
    self_out,
    rel_bias,
    norm_cross,
    cross_q,
    cross_k,
    cross_v,
    cross_out,
    norm_ff,
    ff_gate,
    ff_up,
    ff_down,
    cotangent,
):
    micro_count, batch_rows, local_tokens, model_width = layer_input.shape
    memory_tokens = memory.shape[2]
    group = HEADS // KV_HEADS
    replicas = lax.axis_size("dp")
    shards = (
        norm_self,
        self_q,
        self_k,
        self_v,
        self_out,
        rel_bias,
        norm_cross,
        cross_q,
        cross_k,
        cross_v,
        cross_out,
        norm_ff,
        ff_gate,
        ff_up,
        ff_down,
    )
    totals = [
        jnp.zeros((piece.shape[0] * replicas,) + piece.shape[1:], jnp.float32) for piece in shards
    ]
    onehot = (buckets[:, None] == jnp.arange(BUCKETS, dtype=jnp.int32)[None, :]).astype(jnp.float32)
    places = lax.axis_index("seq") * local_tokens + jnp.arange(local_tokens, dtype=jnp.int32)
    diagonal = jnp.zeros((rel_bias.shape[1] // group, group, TGT), jnp.float32)
    outputs = []
    input_grads = []
    memory_grads = []
    for micro_step in range(micro_count):
        gathered = (
            lax.all_gather(norm_self, "dp", axis=0, tiled=True),
            lax.all_gather(self_q, "dp", axis=0, tiled=True),
            lax.all_gather(self_k, "dp", axis=0, tiled=True),
            lax.all_gather(self_v, "dp", axis=0, tiled=True),
            lax.all_gather(self_out, "dp", axis=0, tiled=True),
            lax.all_gather(rel_bias, "dp", axis=0, tiled=True),
            lax.all_gather(norm_cross, "dp", axis=0, tiled=True),
            lax.all_gather(cross_q, "dp", axis=0, tiled=True),
            lax.all_gather(cross_k, "dp", axis=0, tiled=True),
            lax.all_gather(cross_v, "dp", axis=0, tiled=True),
            lax.all_gather(cross_out, "dp", axis=0, tiled=True),
            lax.all_gather(norm_ff, "dp", axis=0, tiled=True),
            lax.all_gather(ff_gate, "dp", axis=0, tiled=True),
            lax.all_gather(ff_up, "dp", axis=0, tiled=True),
            lax.all_gather(ff_down, "dp", axis=0, tiled=True),
        )
        (
            gain_self,
            query_self,
            key_self,
            value_self,
            output_self,
            bias_whole,
            gain_cross,
            query_cross,
            key_cross,
            value_cross,
            output_cross,
            gain_ff,
            gate_weight,
            up_weight,
            down_weight,
        ) = gathered
        gain_self = gain_self.astype(jnp.float32)
        gain_cross = gain_cross.astype(jnp.float32)
        gain_ff = gain_ff.astype(jnp.float32)
        table = lax.dot_general(
            bias_whole.astype(jnp.float32), onehot, (((0,), (1,)), ((), ())), precision=HIGH
        )
        lengths = target_lengths[micro_step]
        spans = memory_lengths[micro_step]
        valid = (places[None, :] < lengths[:, None]).astype(jnp.float32).reshape(-1, 1)
        hidden = layer_input[micro_step].reshape(-1, model_width).astype(jnp.float32)
        normed_self = rms_norm(hidden, gain_self).astype(jnp.bfloat16)
        queries = (
            project(normed_self, query_self)
            .astype(jnp.bfloat16)
            .reshape(batch_rows, local_tokens, -1)
        )
        keys = (
            project(normed_self, key_self)
            .astype(jnp.bfloat16)
            .reshape(batch_rows, local_tokens, -1)
        )
        values = (
            project(normed_self, value_self)
            .astype(jnp.bfloat16)
            .reshape(batch_rows, local_tokens, -1)
        )
        encoded = memory[micro_step].reshape(-1, model_width)
        memory_keys = (
            project(encoded, key_cross).astype(jnp.bfloat16).reshape(batch_rows, memory_tokens, -1)
        )
        memory_values = (
            project(encoded, value_cross)
            .astype(jnp.bfloat16)
            .reshape(batch_rows, memory_tokens, -1)
        )
        head_queries, head_keys, head_values, far_keys, far_values = (
            lax.all_to_all(queries, "seq", split_axis=2, concat_axis=1, tiled=True),
            lax.all_to_all(keys, "seq", split_axis=2, concat_axis=1, tiled=True),
            lax.all_to_all(values, "seq", split_axis=2, concat_axis=1, tiled=True),
            lax.all_to_all(memory_keys, "seq", split_axis=2, concat_axis=1, tiled=True),
            lax.all_to_all(memory_values, "seq", split_axis=2, concat_axis=1, tiled=True),
        )
        self_queries = split_heads(head_queries, group)
        self_keys = split_shared(head_keys)
        self_values = split_shared(head_values)
        far_keys = split_shared(far_keys)
        far_values = split_shared(far_values)
        attended, self_sums = jax.vmap(self_forward, in_axes=(0, 0, 0, 0, None))(
            self_queries, self_keys, self_values, lengths, table
        )
        context = to_tokens(attended.reshape(batch_rows, TGT, -1)).reshape(
            batch_rows * local_tokens, -1
        )
        first = hidden + project(context, output_self)
        normed_cross = rms_norm(first, gain_cross).astype(jnp.bfloat16)
        cross_queries = (
            project(normed_cross, query_cross)
            .astype(jnp.bfloat16)
            .reshape(batch_rows, local_tokens, -1)
        )
        cross_heads = split_heads(
            lax.all_to_all(cross_queries, "seq", split_axis=2, concat_axis=1, tiled=True), group
        )
        cross_attended, cross_sums = jax.vmap(cross_forward)(
            cross_heads, far_keys, far_values, spans
        )
        cross_context = to_tokens(cross_attended.reshape(batch_rows, TGT, -1)).reshape(
            batch_rows * local_tokens, -1
        )
        second = first + project(cross_context, output_cross)
        normed_ff = rms_norm(second, gain_ff).astype(jnp.bfloat16)
        gate = project(normed_ff, gate_weight)
        upward = project(normed_ff, up_weight)
        middle = gated(gate, upward).astype(jnp.bfloat16)
        third = second + project(middle, down_weight)
        outputs.append(
            (third * valid).astype(jnp.bfloat16).reshape(batch_rows, local_tokens, model_width)
        )
        upstream = cotangent[micro_step].reshape(-1, model_width).astype(jnp.float32) * valid
        down_grad = upstream.astype(jnp.bfloat16)
        totals[14] = totals[14] + weight_grad(middle, down_grad)
        _, pullback = jax.vjp(gated, gate, upward)
        gate_grad, upward_grad = pullback(project_back(down_grad, down_weight))
        gate_grad = gate_grad.astype(jnp.bfloat16)
        upward_grad = upward_grad.astype(jnp.bfloat16)
        totals[12] = totals[12] + weight_grad(normed_ff, gate_grad)
        totals[13] = totals[13] + weight_grad(normed_ff, upward_grad)
        _, pullback = jax.vjp(rms_norm, second, gain_ff)
        second_grad, gain_grad = pullback(
            project_back(gate_grad, gate_weight) + project_back(upward_grad, up_weight)
        )
        totals[11] = totals[11] + gain_grad
        second_grad = second_grad + upstream
        cross_grad = second_grad.astype(jnp.bfloat16)
        totals[10] = totals[10] + weight_grad(cross_context, cross_grad)
        context_grad = (
            project_back(cross_grad, output_cross)
            .astype(jnp.bfloat16)
            .reshape(batch_rows, local_tokens, -1)
        )
        cross_query_grad, far_key_grad, far_value_grad, _ = jax.vmap(cross_backward)(
            cross_heads,
            far_keys,
            far_values,
            cross_sums,
            split_heads(to_heads(context_grad), group),
            spans,
        )
        query_back, key_back, value_back = (
            lax.all_to_all(
                shortened(cross_query_grad.reshape(batch_rows, TGT, -1)),
                "seq",
                split_axis=1,
                concat_axis=2,
                tiled=True,
            ),
            lax.all_to_all(
                shortened(far_key_grad.reshape(batch_rows, MEM, -1)),
                "seq",
                split_axis=1,
                concat_axis=2,
                tiled=True,
            ),
            lax.all_to_all(
                shortened(far_value_grad.reshape(batch_rows, MEM, -1)),
                "seq",
                split_axis=1,
                concat_axis=2,
                tiled=True,
            ),
        )
        query_back = query_back.reshape(batch_rows * local_tokens, -1)
        key_back = key_back.reshape(batch_rows * memory_tokens, -1)
        value_back = value_back.reshape(batch_rows * memory_tokens, -1)
        totals[7] = totals[7] + weight_grad(normed_cross, query_back)
        totals[8] = totals[8] + weight_grad(encoded, key_back)
        totals[9] = totals[9] + weight_grad(encoded, value_back)
        memory_grads.append(
            (project_back(key_back, key_cross) + project_back(value_back, value_cross)).reshape(
                batch_rows, memory_tokens, model_width
            )
        )
        _, pullback = jax.vjp(rms_norm, first, gain_cross)
        first_grad, gain_grad = pullback(project_back(query_back, query_cross))
        totals[6] = totals[6] + gain_grad
        first_grad = first_grad + second_grad
        self_grad = first_grad.astype(jnp.bfloat16)
        totals[4] = totals[4] + weight_grad(context, self_grad)
        context_grad = (
            project_back(self_grad, output_self)
            .astype(jnp.bfloat16)
            .reshape(batch_rows, local_tokens, -1)
        )
        query_grad, key_grad, value_grad, bias_grad = jax.vmap(
            self_backward, in_axes=(0, 0, 0, 0, 0, 0, None)
        )(
            self_queries,
            self_keys,
            self_values,
            self_sums,
            split_heads(to_heads(context_grad), group),
            lengths,
            table,
        )
        diagonal = diagonal + jnp.sum(bias_grad, axis=0)
        query_back, key_back, value_back = (
            lax.all_to_all(
                shortened(query_grad.reshape(batch_rows, TGT, -1)),
                "seq",
                split_axis=1,
                concat_axis=2,
                tiled=True,
            ),
            lax.all_to_all(
                shortened(key_grad.reshape(batch_rows, TGT, -1)),
                "seq",
                split_axis=1,
                concat_axis=2,
                tiled=True,
            ),
            lax.all_to_all(
                shortened(value_grad.reshape(batch_rows, TGT, -1)),
                "seq",
                split_axis=1,
                concat_axis=2,
                tiled=True,
            ),
        )
        query_back = query_back.reshape(batch_rows * local_tokens, -1)
        key_back = key_back.reshape(batch_rows * local_tokens, -1)
        value_back = value_back.reshape(batch_rows * local_tokens, -1)
        totals[1] = totals[1] + weight_grad(normed_self, query_back)
        totals[2] = totals[2] + weight_grad(normed_self, key_back)
        totals[3] = totals[3] + weight_grad(normed_self, value_back)
        _, pullback = jax.vjp(rms_norm, hidden, gain_self)
        hidden_grad, gain_grad = pullback(
            project_back(query_back, query_self)
            + project_back(key_back, key_self)
            + project_back(value_back, value_self)
        )
        totals[0] = totals[0] + gain_grad
        input_grads.append(
            (hidden_grad + first_grad).reshape(batch_rows, local_tokens, model_width)
        )
    totals[5] = lax.dot_general(
        onehot, diagonal.reshape(-1, TGT), (((0,), (1,)), ((), ())), precision=HIGH
    )
    reduced = (
        lax.psum_scatter(totals[0], ("dp", "seq"), scatter_dimension=0, tiled=True),
        lax.psum_scatter(totals[1], ("dp", "seq"), scatter_dimension=0, tiled=True),
        lax.psum_scatter(totals[2], ("dp", "seq"), scatter_dimension=0, tiled=True),
        lax.psum_scatter(totals[3], ("dp", "seq"), scatter_dimension=0, tiled=True),
        lax.psum_scatter(totals[4], ("dp", "seq"), scatter_dimension=0, tiled=True),
        lax.psum_scatter(totals[6], ("dp", "seq"), scatter_dimension=0, tiled=True),
        lax.psum_scatter(totals[7], ("dp", "seq"), scatter_dimension=0, tiled=True),
        lax.psum_scatter(totals[8], ("dp", "seq"), scatter_dimension=0, tiled=True),
        lax.psum_scatter(totals[9], ("dp", "seq"), scatter_dimension=0, tiled=True),
        lax.psum_scatter(totals[10], ("dp", "seq"), scatter_dimension=0, tiled=True),
        lax.psum_scatter(totals[11], ("dp", "seq"), scatter_dimension=0, tiled=True),
        lax.psum_scatter(totals[12], ("dp", "seq"), scatter_dimension=0, tiled=True),
        lax.psum_scatter(totals[13], ("dp", "seq"), scatter_dimension=0, tiled=True),
        lax.psum_scatter(totals[14], ("dp", "seq"), scatter_dimension=0, tiled=True),
    )
    bias_share = lax.psum_scatter(totals[5], "dp", scatter_dimension=0, tiled=True)
    return (
        jnp.stack(outputs),
        jnp.stack(input_grads),
        jnp.stack(memory_grads),
        reduced[0],
        reduced[1],
        reduced[2],
        reduced[3],
        reduced[4],
        bias_share,
        reduced[5],
        reduced[6],
        reduced[7],
        reduced[8],
        reduced[9],
        reduced[10],
        reduced[11],
        reduced[12],
        reduced[13],
    )


def row_pieces(full):
    blocks = full.reshape(full.shape[0], -1, QB)
    return jnp.concatenate([blocks[:, 1:], blocks[:, :-1]], axis=2)


def seed_rows(vectors):
    return jnp.stack([jnp.roll(vectors, r, axis=-1) for r in range(8)], axis=-2)


def spread(seed):
    rows = 8
    tile = seed
    while rows < QB:
        tile = jnp.concatenate([tile, pltpu.roll(tile, rows, 1)], axis=0)
        rows *= 2
    return tile[:, :QB]


def fold(tile):
    width = 2 * QB
    tile = jnp.concatenate([tile, jnp.zeros_like(tile)], axis=1)
    rows = QB
    while rows > 8:
        rows //= 2
        tile = tile[:rows] + pltpu.roll(tile[rows:], width - rows, 1)
    return tile


def nt(left, right):
    return lax.dot_general(left, right, (((1,), (1,)), ((), ())), preferred_element_type=jnp.float32)


def tn(left, right):
    return lax.dot_general(left, right, (((0,), (0,)), ((), ())), preferred_element_type=jnp.float32)


def nn(left, right):
    return lax.dot_general(left, right, (((1,), (0,)), ((), ())), preferred_element_type=jnp.float32)


def inverse_rms(value):
    return lax.rsqrt(jnp.mean(value * value, axis=-1, keepdims=True) + EPS)


def pick(array, index, axis=0):
    return lax.dynamic_index_in_dim(array, index, axis, keepdims=False)


MESH = pl.DeviceIdType.MESH


class Spot:
    def __init__(self, depth):
        self.depth = depth
        place = lax.axis_index("dp")
        self.corner = lax.axis_index("seq")
        self.z, self.core = place // 2, place % 2
        self.y, self.x = self.corner // 2, self.corner % 2

    def at(self, z=None, core=None, y=None, x=None):
        z = self.z if z is None else z
        core = self.core if core is None else core
        y = self.y if y is None else y
        x = self.x if x is None else x
        return (z * 2 + core, y * 2 + x)

    def beside(self):
        return self.at(x=1 - self.x)

    def below(self):
        return self.at(y=1 - self.y)

    def sibling(self):
        return self.at(core=1 - self.core)

    def greet(self):
        barrier = pltpu.get_barrier_semaphore()
        others = [
            self.at(None, self.core ^ (i >> 2), self.y ^ (i >> 1 & 1), self.x ^ (i & 1)) for i in range(1, 8)
        ]
        for step in range(1, self.depth):
            for flip in range(2):
                others.append(self.at((self.z + step) % self.depth, self.core ^ flip))
        for other in others:
            pl.semaphore_signal(barrier, inc=1, device_id=other, device_id_type=MESH)
        pl.semaphore_wait(barrier, len(others))


class Wires:
    def __init__(self, sends, arrivals, moves):
        self.sends, self.arrivals, self.moves = sends, arrivals, moves
        self.count = 0
        self.moved = 0
        self.open = []

    def take(self, number):
        first = self.count
        self.count += number
        return first

    def send(self, source, target, device, index, landing=None):
        landing = index if landing is None else landing
        copy = pltpu.make_async_remote_copy(
            src_ref=source,
            dst_ref=target,
            send_sem=self.sends.at[index],
            recv_sem=self.arrivals.at[landing],
            device_id=device,
            device_id_type=MESH,
        )
        copy.start()
        self.open.append(copy)
        return copy

    def arrive(self, target, device, index):
        pltpu.make_async_remote_copy(
            src_ref=target,
            dst_ref=target,
            send_sem=self.sends.at[0],
            recv_sem=self.arrivals.at[index],
            device_id=device,
            device_id_type=MESH,
        ).wait_recv()

    def move(self, source, target):
        copy = pltpu.make_async_copy(source, target, self.moves.at[self.moved])
        self.moved += 1
        copy.start()
        return copy

    def close(self):
        for copy in self.open:
            copy.wait_send()
        self.open = []


def collect_tokens(spot, wires, parcel, whole):
    away = wires.take(4)
    over = wires.take(4)
    local = wires.moved
    wires.moved += 1
    for index in range(4):
        half, micro = spot.y ^ (index >> 1), spot.x ^ (index & 1)
        home = (half == spot.core) & (micro == spot.y) & (spot.core == spot.x)
        source = parcel.at[micro, half]
        target = whole.at[spot.corner, half]
        copy = pltpu.make_async_remote_copy(
            src_ref=source,
            dst_ref=target,
            send_sem=wires.sends.at[away + index],
            recv_sem=wires.arrivals.at[away + index],
            device_id=spot.at(core=half, y=micro, x=spot.core),
            device_id_type=MESH,
        )
        here = pltpu.make_async_copy(source, target, wires.moves.at[local])

        @pl.when(jnp.logical_not(home))
        def _():
            copy.start()

        @pl.when(home)
        def _():
            here.start()

    yield
    for index in range(4):
        block = 2 * (spot.core ^ (index >> 1)) + (spot.y ^ (index & 1))
        home = (spot.x == spot.core) & (block == spot.corner)
        piece = whole.at[block, spot.core]
        here = pltpu.make_async_copy(piece, piece, wires.moves.at[local])
        landed = pltpu.make_async_remote_copy(
            src_ref=piece,
            dst_ref=piece,
            send_sem=wires.sends.at[away + index],
            recv_sem=wires.arrivals.at[away + index],
            device_id=spot.sibling(),
            device_id_type=MESH,
        )

        @pl.when(jnp.logical_not(home))
        def _():
            landed.wait_recv()

        @pl.when(home)
        def _():
            here.wait()

        wires.send(piece, piece, spot.sibling(), over + index)
    yield
    for index in range(4):
        block = 2 * ((1 - spot.core) ^ (index >> 1)) + (spot.y ^ (index & 1))
        wires.arrive(whole.at[block, 1 - spot.core], spot.sibling(), over + index)
    for index in range(4):
        half, micro = spot.y ^ (index >> 1), spot.x ^ (index & 1)
        home = (half == spot.core) & (micro == spot.y) & (spot.core == spot.x)
        source = parcel.at[micro, half]

        @pl.when(jnp.logical_not(home))
        def _():
            pltpu.make_async_remote_copy(
                src_ref=source,
                dst_ref=source,
                send_sem=wires.sends.at[away + index],
                recv_sem=wires.arrivals.at[away + index],
                device_id=spot.sibling(),
                device_id_type=MESH,
            ).wait_send()

    yield


def deliver_tokens(spot, wires, pieces, homes):
    away = wires.take(4)
    local = wires.moved
    wires.moved += 1

    def parts():
        for index in range(4):
            block = 2 * (spot.core ^ (index >> 1)) + (spot.y ^ (index & 1))
            home = (spot.x == spot.core) & (block == spot.corner)
            source = pieces.at[block]
            target = homes.at[spot.y, spot.core]
            remote = pltpu.make_async_remote_copy(
                src_ref=source,
                dst_ref=target,
                send_sem=wires.sends.at[away + index],
                recv_sem=wires.arrivals.at[away + index],
                device_id=spot.at(core=spot.x, y=block // 2, x=block % 2),
                device_id_type=MESH,
            )
            yield home, remote, pltpu.make_async_copy(source, target, wires.moves.at[local])

    for home, remote, here in parts():
        pl.when(jnp.logical_not(home))(remote.start)
        pl.when(home)(here.start)
    yield
    for index in range(4):
        half, micro = spot.y ^ (index >> 1), spot.x ^ (index & 1)
        home = (half == spot.core) & (micro == spot.y) & (spot.core == spot.x)
        piece = homes.at[micro, half]
        landed = pltpu.make_async_remote_copy(
            src_ref=piece,
            dst_ref=piece,
            send_sem=wires.sends.at[away + index],
            recv_sem=wires.arrivals.at[away + index],
            device_id=spot.sibling(),
            device_id_type=MESH,
        )
        here = pltpu.make_async_copy(piece, piece, wires.moves.at[local])
        pl.when(jnp.logical_not(home))(landed.wait_recv)
        pl.when(home)(here.wait)
    for home, remote, here in parts():
        pl.when(jnp.logical_not(home))(remote.wait_send)
    yield


def gather_small(spot, wires, block, whole):
    own = wires.move(block, whole.at[spot.z, spot.core, spot.corner])
    first = wires.take(spot.depth + 3)
    for step in range(1, spot.depth):
        target = whole.at[spot.z, spot.core, spot.corner]
        wires.send(block, target, spot.at(z=(spot.z + step) % spot.depth), first + step)
    yield
    own.wait()
    for step in range(1, spot.depth):
        z = (spot.z - step + spot.depth) % spot.depth
        wires.arrive(whole.at[z, spot.core, spot.corner], spot.sibling(), first + step)
    column = whole.at[:, spot.core, spot.corner]
    wires.send(column, column, spot.beside(), first)
    wires.send(column, column, spot.below(), first + spot.depth)
    wires.send(column, column, spot.at(y=1 - spot.y, x=1 - spot.x), first + spot.depth + 1)
    yield
    for flip, index in ((1, first), (2, first + spot.depth), (3, first + spot.depth + 1)):
        wires.arrive(whole.at[:, spot.core, spot.corner ^ flip], spot.sibling(), index)
    plane = whole.at[:, spot.core]
    wires.send(plane, plane, spot.sibling(), first + spot.depth + 2)
    yield
    wires.arrive(whole.at[:, 1 - spot.core], spot.sibling(), first + spot.depth + 2)
    yield


def gather_columns(spot, wires, pack, whole):
    depth, me = spot.depth, spot.corner
    ahead = wires.take(2 * depth)
    flat = wires.take(4 * depth)
    own = wires.move(pack.at[spot.core], whole.at[spot.z, spot.core])
    for step in range(1, depth):
        for flip in range(2):
            wires.send(
                pack.at[spot.core ^ flip, me],
                whole.at[spot.z, spot.core, me],
                spot.at((spot.z + step) % depth, spot.core ^ flip),
                ahead + 2 * step + flip,
            )
    wires.send(pack.at[1 - spot.core], whole.at[spot.z, spot.core], spot.sibling(), ahead)
    yield
    for step in range(1, depth):
        z = (spot.z - step + depth) % depth
        for flip in range(2):
            wires.arrive(whole.at[z, spot.core ^ flip, me], spot.sibling(), ahead + 2 * step + flip)
        quarter = whole.at[z, :, me]
        wires.send(quarter, quarter, spot.beside(), flat + 4 * step)
        wires.send(quarter, quarter, spot.below(), flat + 4 * step + 1)
    yield
    for step in range(1, depth):
        z = (spot.z - step + depth) % depth
        wires.arrive(whole.at[z, :, me ^ 1], spot.sibling(), flat + 4 * step)
        piece = whole.at[z, 0, me ^ 1]
        wires.send(piece, piece, spot.below(), flat + 4 * step + 2)
        wires.arrive(whole.at[z, :, me ^ 2], spot.sibling(), flat + 4 * step + 1)
        piece = whole.at[z, 1, me ^ 2]
        wires.send(piece, piece, spot.beside(), flat + 4 * step + 3)
    yield
    own.wait()
    wires.arrive(whole.at[spot.z, 1 - spot.core], spot.sibling(), ahead)
    for step in range(1, depth):
        z = (spot.z - step + depth) % depth
        wires.arrive(whole.at[z, 0, me ^ 3], spot.sibling(), flat + 4 * step + 2)
        wires.arrive(whole.at[z, 1, me ^ 3], spot.sibling(), flat + 4 * step + 3)
    yield


def gather_rows(spot, wires, pack, whole):
    depth, me = spot.depth, spot.corner
    ahead = wires.take(depth)
    flat = wires.take(4 * depth)
    middle = pack.shape[-1] // 2

    def part(z, corner, side):
        if pack.shape[0] == 2:
            return whole.at[side, z, corner]
        return whole.at[0, z, corner, :, pl.ds(side * middle, middle)]

    own = wires.move(pack, whole.at[:, spot.z])
    for step in range(1, depth):
        wires.send(
            pack.at[:, me], whole.at[:, spot.z, me], spot.at((spot.z + step) % depth), ahead + step
        )
    yield
    for step in range(1, depth):
        z = (spot.z - step + depth) % depth
        quarter = whole.at[:, z, me]
        wires.arrive(quarter, spot.sibling(), ahead + step)
        wires.send(quarter, quarter, spot.beside(), flat + 4 * step)
        wires.send(quarter, quarter, spot.below(), flat + 4 * step + 1)
    yield
    for step in range(1, depth):
        z = (spot.z - step + depth) % depth
        wires.arrive(whole.at[:, z, me ^ 1], spot.sibling(), flat + 4 * step)
        piece = part(z, me ^ 1, 0)
        wires.send(piece, piece, spot.below(), flat + 4 * step + 2)
        wires.arrive(whole.at[:, z, me ^ 2], spot.sibling(), flat + 4 * step + 1)
        piece = part(z, me ^ 2, 1)
        wires.send(piece, piece, spot.beside(), flat + 4 * step + 3)
    yield
    own.wait()
    for step in range(1, depth):
        z = (spot.z - step + depth) % depth
        wires.arrive(part(z, me ^ 3, 0), spot.sibling(), flat + 4 * step + 2)
        wires.arrive(part(z, me ^ 3, 1), spot.sibling(), flat + 4 * step + 3)
    yield


def reach_columns(spot, wires, pack, near):
    depth, me = spot.depth, spot.corner
    ahead = wires.take(2 * depth)
    own = wires.move(pack.at[spot.core, me], near.at[spot.z, spot.core])
    for step in range(depth):
        for flip in range(2):
            if step or flip:
                wires.send(
                    pack.at[spot.core ^ flip, me],
                    near.at[spot.z, spot.core],
                    spot.at((spot.z + step) % depth, spot.core ^ flip),
                    ahead + 2 * step + flip,
                )
    yield
    own.wait()
    for step in range(depth):
        z = (spot.z - step + depth) % depth
        for flip in range(2):
            if step or flip:
                wires.arrive(near.at[z, spot.core ^ flip], spot.sibling(), ahead + 2 * step + flip)
    yield


def reach_rows(spot, wires, pack, near):
    depth, me = spot.depth, spot.corner
    ahead = wires.take(depth)
    own = wires.move(pack.at[0, me], near.at[spot.z])
    for step in range(1, depth):
        wires.send(pack.at[0, me], near.at[spot.z], spot.at((spot.z + step) % depth), ahead + step)
    yield
    own.wait()
    for step in range(1, depth):
        z = (spot.z - step + depth) % depth
        wires.arrive(near.at[z], spot.sibling(), ahead + step)
    yield


def share_plane(spot, wires, near, whole, parts):
    me = spot.corner
    flat = wires.take(4)
    own = wires.move(near, whole(me))
    wires.send(near, whole(me), spot.beside(), flat)
    wires.send(near, whole(me), spot.below(), flat + 1)
    yield
    wires.arrive(whole(me ^ 1), spot.sibling(), flat)
    piece = parts(whole(me ^ 1), 0)
    wires.send(piece, piece, spot.below(), flat + 2)
    wires.arrive(whole(me ^ 2), spot.sibling(), flat + 1)
    piece = parts(whole(me ^ 2), 1)
    wires.send(piece, piece, spot.beside(), flat + 3)
    yield
    own.wait()
    wires.arrive(parts(whole(me ^ 3), 0), spot.sibling(), flat + 2)
    wires.arrive(parts(whole(me ^ 3), 1), spot.sibling(), flat + 3)
    yield


def scatter_buffers(depth, lanes, rows, width):
    half = depth // 2
    return [
        pltpu.VMEM((half, lanes, 2, rows, width), jnp.bfloat16),
        pltpu.VMEM((half, lanes, 2, rows, width), jnp.bfloat16),
        pltpu.VMEM((half, lanes, 2, rows, width), jnp.bfloat16),
        pltpu.VMEM((half, lanes, 2, rows, width), jnp.bfloat16),
        pltpu.VMEM((half, lanes, rows, width), jnp.bfloat16),
        pltpu.VMEM((half, lanes, rows, width), jnp.bfloat16),
        pltpu.VMEM((depth, lanes, rows, width), jnp.bfloat16),
        pltpu.VMEM((depth, lanes, rows, width), jnp.bfloat16),
        pltpu.VMEM((rows, width), jnp.bfloat16),
    ]


def scatter_sums(spot, wires, grads, buffers, total, got, resident=False):
    depth, half = spot.depth, spot.depth // 2
    lanes = grads.shape[1]
    places = [(z, a, s) for z in range(half) for a in range(lanes) for s in range(2)]
    if resident:
        low_in, high_in, low_last, high_last, column, column_in, passing = buffers
        low, high = low_in, high_in
    else:
        low, high, low_in, high_in, low_last, high_last, column, column_in, passing = buffers
    first = wires.take(4)
    away = wires.take(depth)
    mine = []
    if not resident:
        mine = [
            wires.move(grads.at[pl.ds(0, half), :, :, spot.x], low),
            wires.move(grads.at[pl.ds(half, half), :, spot.y], high),
        ]
    wires.send(grads.at[pl.ds(0, half), :, :, 1 - spot.x], low_in, spot.beside(), first)
    wires.send(grads.at[pl.ds(half, half), :, 1 - spot.y], high_in, spot.below(), first + 1)
    yield
    for copy in mine:
        copy.wait()

    def join(target, other, index):
        target[index] = (target[index].astype(jnp.float32) + other.astype(jnp.float32)).astype(jnp.bfloat16)

    wires.arrive(low_in, spot.beside(), first)
    for z, a, s in places:
        join(low, grads[z, a, s, spot.x] if resident else low_in[z, a, s], (z, a, s))
    wires.send(low.at[:, :, 1 - spot.y], low_last, spot.below(), first + 2)
    wires.arrive(high_in, spot.below(), first + 1)
    for z, a, s in places:
        join(high, grads[half + z, a, spot.y, s] if resident else high_in[z, a, s], (z, a, s))
    wires.send(high.at[:, :, 1 - spot.x], high_last, spot.beside(), first + 3)
    yield
    wires.arrive(low_last, spot.below(), first + 2)
    wires.arrive(high_last, spot.beside(), first + 3)
    for z in range(half):
        for a in range(lanes):
            column[z, a] = (
                low[z, a, spot.y].astype(jnp.float32) + low_last[z, a].astype(jnp.float32)
            ).astype(jnp.bfloat16)
            column[half + z, a] = (
                high[z, a, spot.x].astype(jnp.float32) + high_last[z, a].astype(jnp.float32)
            ).astype(jnp.bfloat16)
    for step in range(1, depth):
        z = (spot.z + step) % depth
        wires.send(column.at[z], column_in.at[step], spot.at(z), away + step)
    yield
    for step in range(1, depth):
        wires.arrive(column_in.at[step], spot.sibling(), away + step)

    def added(lane):
        result = column[spot.z, lane].astype(jnp.float32)
        for step in range(1, depth):
            result = result + column_in[step, lane].astype(jnp.float32)
        return result

    if lanes == 1:
        total[...] = added(0)
    else:
        passing[...] = added(1 - spot.core).astype(jnp.bfloat16)
        wires.send(passing, got, spot.sibling(), away)
        total[...] = added(spot.core)
    yield
    if lanes == 2:
        wires.arrive(got, spot.sibling(), away)
    yield


def total_small(spot, wires, terms, work, total):
    first = wires.take(3 + spot.depth)
    work[0] = terms[...]
    wires.send(work.at[0], work.at[1], spot.sibling(), first)
    yield
    wires.arrive(work.at[1], spot.sibling(), first)
    work[2] = work[0] + work[1]
    wires.send(work.at[2], work.at[3], spot.beside(), first + 1)
    yield
    wires.arrive(work.at[3], spot.sibling(), first + 1)
    work[4] = work[2] + work[3]
    wires.send(work.at[4], work.at[5], spot.below(), first + 2)
    yield
    wires.arrive(work.at[5], spot.sibling(), first + 2)
    work[6] = work[4] + work[5]
    for step in range(1, spot.depth):
        target = work.at[6 + step]
        wires.send(work.at[6], target, spot.at((spot.z + step) % spot.depth), first + 2 + step)
    yield
    result = work[6]
    for step in range(1, spot.depth):
        wires.arrive(work.at[6 + step], spot.sibling(), first + 2 + step)
        result = result + work[6 + step]
    total[...] = result
    yield


def wire_scratch(number, moves):
    return [
        pltpu.SemaphoreType.DMA((number,)),
        pltpu.SemaphoreType.DMA((number,)),
        pltpu.SemaphoreType.DMA((moves,)),
    ]


def spread_row(vector):
    tile = pltpu.roll(jnp.broadcast_to(vector, (8, 2 * QB)), 0, 1, stride=1, stride_axis=0)
    return spread(tile)


def attend_block(query, keys, values, keep, bias):
    scores = nt(query, keys) + keep
    if bias is not None:
        scores = scores + bias
    peak = jnp.max(scores, axis=1, keepdims=True)
    weights = jnp.exp(scores - peak)
    total = jnp.sum(weights, axis=1, keepdims=True)
    return nn(weights.astype(jnp.bfloat16), values) / total, peak + jnp.log(total)


def pair_rows(block, kv):
    both = block[:, 2 * kv * HEAD_DIM : 2 * (kv + 1) * HEAD_DIM]
    return jnp.concatenate([both[:, :HEAD_DIM], both[:, HEAD_DIM:]], axis=0)


def normed(value, gain):
    return (value * inverse_rms(value) * gain).astype(jnp.bfloat16)


def pack_heads(pack, weights, start):
    size = sum(w.shape[1] for w in weights) // 8
    for place in range(8):
        units = [w.shape[1] // 8 for w in weights]
        pieces = [w[:, place * u : (place + 1) * u] for w, u in zip(weights, units)]
        piece = pieces[0] if len(pieces) == 1 else jnp.concatenate(pieces, axis=1)
        lanes = slice(start + place // 2 * size, start + (place // 2 + 1) * size)
        pack[place % 2, :, :, lanes] = piece.reshape(4, -1, size)


def pack_hidden(pack, weights, first, last):
    size = 16 * (last - first)
    for order, weight in enumerate(weights):
        unit = weight.shape[1] // 8
        quarter = unit // 4
        for side in range(2):
            pieces = [
                weight[:, place * unit + q * quarter + first : place * unit + q * quarter + last]
                for place in range(side, 8, 2)
                for q in range(4)
            ]
            row = jnp.concatenate(pieces, axis=1)
            pack[side, :, :, order * size : (order + 1) * size] = row.reshape(4, -1, size).astype(pack.dtype)


def forward_layer_kernel(depth, cuts, *refs):
    (
        x, t, m, s, p3, p5, p7, codes, holes, sq, sk, sv, ck, cv, cq, wg, wu,
        o_wx, wt, o_wm, ws, o_w1, o_w2, o_w3, w4, w5,
        o_a1, o_qkv, o_ctx, lse, o_x1, o_a2, o_qc, o_ckv, o_ctxc, lsec, o_x2, o_a3, gains, keeps, keepc, bent,
        down_s, down_c, n6, n7, p8,
        p1, p2, p4, p6, bias, own, got, own2, got2, wx, wm, w1, w2, w3, a1, qkv, ctx, x1, a2, qc, ckv, ctxc, x2, a3, *sems
    ) = refs
    leaving = []
    pack_heads(p1, [sq, sk, sv], 0)
    pack_heads(p2, [ck, cv], 0)
    pack_heads(p2, [cq], ck.shape[1])

    def leave(*pairs):
        leaving.extend(wires.move(source, target) for source, target in pairs)

    f32, bf16 = jnp.float32, jnp.bfloat16
    spot = Spot(depth)
    wires = Wires(*sems)
    blocks = 4
    kvs = 4
    inner = 2 * kvs * HEAD_DIM

    def rows(block):
        return slice(block * QB, (block + 1) * QB)

    spot.greet()
    tokens = collect_tokens(spot, wires, x, wx)
    small = gather_small(spot, wires, s, ws)
    first = gather_columns(spot, wires, p1, w1)
    memory = collect_tokens(spot, wires, m, wm)
    second = gather_columns(spot, wires, p2, w2)
    outs = gather_rows(spot, wires, p3, w3)
    wide = gather_columns(spot, wires, p4, w4)
    down = gather_rows(spot, wires, p5, w5)
    top = collect_tokens(spot, wires, t, wt)
    wide_next = reach_columns(spot, wires, p6, n6)
    down_next = reach_rows(spot, wires, p7, n7)
    over = wires.take(2 * blocks)

    def advance(*programs):
        for program in programs:
            next(program)

    advance(small, first, small, tokens)
    pack_hidden(p4, [wg[...], wu[...]], 0, cuts[0])
    pack_hidden(p6, [wg[...], wu[...]], cuts[0], cuts[1])
    pack_hidden(p8, [wg[...], wu[...]], cuts[1], cuts[2])
    advance(small, small)

    def line(row):
        return jnp.concatenate([ws[z, c, 0, row : row + 1, :] for z in range(depth) for c in range(2)], axis=1)

    for row in range(3):
        gains[row : row + 1, :] = line(row)
    counts = ws[spot.z, spot.x, 0, 3:4, :]
    length = jnp.where(spot.y == 0, counts[:, 0:1], counts[:, 1:2])
    span = jnp.where(spot.y == 0, counts[:, 2:3], counts[:, 3:4])
    places = lax.broadcasted_iota(jnp.int32, (1, blocks * QB), 1).astype(f32)
    keeps[...] = jnp.where(places < length, 0.0, NEG)
    keepc[...] = jnp.where(places[:, : keepc.shape[1]] < span, 0.0, NEG)
    places = lax.broadcasted_iota(jnp.int32, (blocks * QB, 1), 0).astype(f32)
    down_s[...] = jnp.where(places < length, 0.0, NEG)
    down_c[...] = jnp.where(places[: down_c.shape[0]] < span, 0.0, NEG)
    table = jnp.concatenate(
        [
            ws[z, c, 0, 4:8, :] + ws[z, c, 1, 4:8, :] + ws[z, c, 2, 4:8, :] + ws[z, c, 3, 4:8, :]
            for z in range(depth)
            for c in range(2)
        ],
        axis=0,
    )
    table = jnp.where(spot.core == 0, table[:, :64], table[:, 64:]).astype(bf16)
    vectors = tn(table, codes[...])[:8] + holes[...]
    bent[...] = vectors[:, 4 * 2 * QB :]
    for kv in range(kvs):
        for member in range(2):
            for offset in range(4):
                head = 2 * kv + member
                bias[kv, member * QB : (member + 1) * QB, (3 - offset) * QB : (4 - offset) * QB] = spread_row(
                    vectors[head : head + 1, offset * 2 * QB : (offset + 1) * 2 * QB]
                ).astype(bf16)

    advance(first, outs, second, tokens, tokens)
    for block in range(blocks):
        a1[rows(block), :] = normed(wx[block].reshape(QB, -1).astype(f32), gains[0:1, :])
    advance(first, memory, first)
    leave((wx, o_wx), (w1, o_w1), (a1, o_a1))

    def attend_rows(block, queries, keys, stop, keep, mixed, sums, causal):
        for kv in range(kvs):
            base = 2 * kv * HEAD_DIM
            query = queries[rows(block), base : base + 2 * HEAD_DIM]
            shape = None
            if causal:
                base = 4 * kv * HEAD_DIM
                query = queries[rows(block), base : base + 2 * HEAD_DIM]
                base += 2 * HEAD_DIM
                shape = bias[kv, :, (3 - block) * QB : (3 - block) * QB + stop]
            out, level = attend_block(
                pair_rows(query, 0),
                keys[:stop, base : base + HEAD_DIM],
                keys[:stop, base + HEAD_DIM : base + 2 * HEAD_DIM],
                keep[:, :stop],
                shape,
            )
            mixed[rows(block), 2 * kv * HEAD_DIM : 2 * (kv + 1) * HEAD_DIM] = jnp.concatenate(
                [out[:QB], out[QB:]], axis=1
            ).astype(bf16)
            level = jnp.broadcast_to(level, (2 * QB, 128)).T
            sums[2 * kv : 2 * kv + 1, rows(block)] = level[:1, :QB]
            sums[2 * kv + 1 : 2 * kv + 2, rows(block)] = level[:1, QB:]

    weight = w1[...].reshape(-1, w1.shape[-1])
    for block in range(blocks):
        qkv[rows(block), :] = nn(a1[rows(block), :], weight).astype(bf16)
        attend_rows(block, qkv, qkv, (block + 1) * QB, keeps, ctx, lse, True)
        if block == 1:
            advance(outs, wide, down, second, memory)
        if block == 2:
            advance(outs)
    advance(outs, second, wide, down, wide_next, down_next)

    def pass_on(block, mine, theirs, value, weight, index):
        mine[rows(block), :] = nn(value[rows(block), :], weight).astype(bf16)
        wires.send(mine.at[rows(block)], theirs.at[rows(block)], spot.sibling(), over + index + block)

    def joined(block, mine, theirs, index):
        wires.arrive(theirs.at[rows(block)], spot.sibling(), over + index + block)
        return mine[rows(block), :].astype(f32) + theirs[rows(block), :].astype(f32)

    weight = w3[0].reshape(-1, w3.shape[-1])
    for block in range(blocks):
        pass_on(block, own, got, ctx, weight, 0)
    advance(memory, second, wide, down, top)
    leave((wm, o_wm), (w2, o_w2), (w3, o_w3), (qkv, o_qkv), (ctx, o_ctx))
    weight = w2[...].reshape(-1, w2.shape[-1])
    ckv[...] = nn(wm[...].reshape(-1, wm.shape[-1]), weight[:, :inner]).astype(bf16)
    for block in range(blocks):
        value = wx[block].reshape(QB, -1).astype(f32) + joined(block, own, got, 0)
        x1[rows(block), :] = value
        a2[rows(block), :] = normed(value, gains[1:2, :])
        qc[rows(block), :] = nn(a2[rows(block), :], weight[:, inner:]).astype(bf16)
    leave((x1, o_x1), (a2, o_a2), (qc, o_qc), (ckv, o_ckv))
    weight = w3[1].reshape(-1, w3.shape[-1])
    for block in range(blocks):
        attend_rows(block, qc, ckv, ckv.shape[0], keepc, ctxc, lsec, False)
        pass_on(block, own2, got2, ctxc, weight, blocks)
        if block == 0:
            advance(wide, down)
        if block == 2:
            advance(top)
    for block in range(blocks):
        value = x1[rows(block), :] + joined(block, own2, got2, blocks)
        x2[rows(block), :] = value
        a3[rows(block), :] = normed(value, gains[2:3, :])
        leave(
            (x2.at[rows(block)], o_x2.at[rows(block)]),
            (a3.at[rows(block)], o_a3.at[rows(block)]),
            (ctxc.at[rows(block)], o_ctxc.at[rows(block)]),
        )
    advance(wide_next, down_next, top)
    for program in (tokens, small, first, memory, second, outs, wide, down, top, wide_next, down_next):
        assert next(program, None) is None
    for copy in leaving:
        copy.wait()
    wires.close()


def forward_layer(depth, cuts, x, t, m, small, p3, p5, p7, codes, holes, *weights):
    bf16, f32 = jnp.bfloat16, jnp.float32
    shape = jax.ShapeDtypeStruct

    def whole_columns(pack):
        return shape((depth, 2) + pack.shape[1:], bf16)

    def whole_rows(pack):
        return shape((pack.shape[0], depth) + pack.shape[1:], bf16)

    def whole_tokens(parcel):
        return shape((4, 2) + parcel.shape[2:], bf16)

    rows = p3.shape[2]
    p1 = p2 = shape((2, 4, rows, weights[0].shape[1]), bf16)
    p4, p6, p8 = (
        shape((2, 4, rows, 32 * (stop - start)), bf16) for start, stop in zip((0,) + cuts[:2], cuts)
    )
    width = x.shape[-1]
    tokens = 8 * x.shape[2]
    span = 8 * m.shape[2]
    inner = p3.shape[0] * p3.shape[1] * p3.shape[2] * depth // 2
    heads = inner // HEAD_DIM
    hbm = pl.BlockSpec(memory_space=pl.ANY)
    vmem = pl.BlockSpec(memory_space=pltpu.VMEM)
    outs = [
        (whole_tokens(x), hbm),
        (whole_tokens(t), hbm),
        (whole_tokens(m), hbm),
        (shape((depth, 2, 4, 8, 128), f32), vmem),
        (whole_columns(p1), hbm),
        (whole_columns(p2), hbm),
        (whole_rows(p3), hbm),
        (whole_columns(p4), hbm),
        (whole_rows(p5), hbm),
        (shape((tokens, width), bf16), hbm),
        (shape((tokens, 2 * inner), bf16), hbm),
        (shape((tokens, inner), bf16), hbm),
        (shape((heads, tokens), f32), vmem),
        (shape((tokens, width), f32), hbm),
        (shape((tokens, width), bf16), hbm),
        (shape((tokens, inner), bf16), hbm),
        (shape((span, inner), bf16), hbm),
        (shape((tokens, inner), bf16), hbm),
        (shape((heads, tokens), f32), vmem),
        (shape((tokens, width), f32), hbm),
        (shape((tokens, width), bf16), hbm),
        (shape((8, width), f32), vmem),
        (shape((1, tokens), f32), vmem),
        (shape((1, span), f32), vmem),
        (shape((heads, 8 * QB), f32), vmem),
        (shape((tokens, 1), f32), vmem),
        (shape((span, 1), f32), vmem),
        (shape((depth, 2) + p6.shape[2:], bf16), hbm),
        (shape((depth,) + p7.shape[2:], bf16), hbm),
        (p8, vmem),
    ]
    packs = [pltpu.VMEM(pack.shape, bf16) for pack in (p1, p2, p4, p6)]
    swap = pltpu.VMEM((tokens, width), bf16)
    return pl.pallas_call(
        functools.partial(forward_layer_kernel, depth, cuts),
        in_specs=[hbm] * 7 + [vmem] * 10,
        out_specs=[spec for _, spec in outs],
        out_shape=[kind for kind, _ in outs],
        scratch_shapes=packs
        + [pltpu.VMEM((heads // 2, 2 * QB, 4 * QB), bf16), swap, swap, swap, swap]
        + [pltpu.VMEM(outs[i][0].shape, outs[i][0].dtype) for i in (0, 2, 4, 5, 6, 9, 10, 11, 13, 14, 15, 16, 17, 19, 20)]
        + wire_scratch(35 + 33 * depth, 40),
        compiler_params=pltpu.CompilerParams(
            collective_id=0, has_side_effects=True, vmem_limit_bytes=60 * 2**20
        ),
        cost_estimate=pl.CostEstimate(
            flops=16 * 10**9, bytes_accessed=128 * 2**20, transcendentals=10**7
        ),
    )(x, t, m, small, p3, p5, p7, codes, holes, *weights)


def pipeline(programs, ahead=2, stages=5):
    count = len(programs)
    for turn in range(count + stages):
        if turn == 0:
            for program in programs[:ahead]:
                next(program)
            yield
        for stage in range(stages - 1, 0, -1):
            index = turn - (stage - 1)
            if 0 <= index < count:
                next(programs[index])
        if turn + ahead < count:
            next(programs[turn + ahead])
        yield


def backward_tile(keys, values, query, grads, keep, bias, level, delta):
    scores = nt(keys, query) + keep
    if bias is not None:
        scores = scores + bias
    probs = jnp.exp(scores - level)
    return probs, probs * (nt(values, grads) - delta)


def row_sums(upstream, mixed):
    inner = (upstream.astype(jnp.float32) * mixed.astype(jnp.float32)).T
    return jnp.concatenate(
        [
            jnp.sum(inner[:HEAD_DIM], axis=0, keepdims=True),
            jnp.sum(inner[HEAD_DIM:], axis=0, keepdims=True),
        ],
        axis=1,
    )


def cross_backward_kernel(depth, *refs):
    g_early, g_down, g_gate, g_up, x2, x1, t_out, *far = refs[:17]
    (
        lsec, keep, gains,
        r_early, r_down, r_gate, r_up, q_gate, q_up, o_cout, o_cq, o_ckv, half, do_s, g_out, o_mem, terms, h_out,
        *rest
    ) = refs[17:]
    take = lambda n: [rest.pop(0) for _ in range(n)]
    near = take(10)
    u, top, qc, ckv, ctxc, a2, mem, w2, w3, ctx = near
    g_cout, g_cq, g_ckv = take(3)
    stage, e2, eb, do_c, dqc, dkv, dk_sum, dv_sum, got, own_c, got_c, own_m, got_m = take(13)
    buffers = [take(9) for _ in range(4)]
    f32, bf16 = jnp.float32, jnp.bfloat16
    spot = Spot(depth)
    wires = Wires(*rest)
    blocks = kvs = 4
    inner = 2 * kvs * HEAD_DIM

    def rows(block):
        return slice(block * QB, (block + 1) * QB)

    coming = [wires.move(source, target) for source, target in zip(far, near)]
    spot.greet()
    over = wires.take(2 * blocks + 4)
    for block in range(blocks):
        wires.send(far[0].at[rows(block)], got.at[rows(block)], spot.sibling(), over + block)
    home = deliver_tokens(spot, wires, t_out, h_out)
    programs = [
        scatter_sums(spot, wires, g_down, buffers[0], r_down, None),
        scatter_sums(spot, wires, g_gate, buffers[1], r_gate, q_gate),
        scatter_sums(spot, wires, g_up, buffers[2], r_up, q_up),
        scatter_sums(spot, wires, g_early, buffers[3], r_early, None),
    ]
    links = pipeline(programs)
    next(links)
    next(home)

    loads = {}

    def fetch(source, block, slot):
        loads[slot] = wires.move(source.at[rows(block)], stage.at[slot])

    def norm_back(block, slot, gain, upstream):
        loads[slot].wait()
        value = stage[slot]
        inverse = inverse_rms(value)
        scaled = upstream * gain
        mean = jnp.mean(value * scaled, axis=-1, keepdims=True)
        change = inverse * scaled - value * (inverse * inverse * inverse) * mean
        return change, jnp.sum(upstream * value * inverse, axis=0, keepdims=True)

    fetch(x2, 0, 0)
    for copy in coming:
        copy.wait()
    gain_terms = jnp.zeros((1, e2.shape[1]), f32)
    for block in range(blocks):
        if block + 1 < blocks:
            fetch(x2, block + 1, (block + 1) % 2)
        else:
            fetch(x1, 0, 0)
        wires.arrive(got.at[rows(block)], spot.sibling(), over + block)
        change, term = norm_back(
            block, block % 2, gains[2:3, :], u[rows(block), :].astype(f32) + got[rows(block), :].astype(f32)
        )
        gain_terms = gain_terms + term
        value = top[rows(block), :].astype(f32) + change
        e2[rows(block), :] = value
        eb[rows(block), :] = value.astype(bf16)
        do_c[rows(block), :] = nt(value.astype(bf16), w3[1].reshape(inner, -1)).astype(bf16)
    terms[0:1, :] = 0.5 * gain_terms
    next(links)

    span = ckv.shape[0]
    for kv in range(kvs):
        both = slice(2 * kv * HEAD_DIM, 2 * (kv + 1) * HEAD_DIM)
        base = 2 * kv * HEAD_DIM
        dk_sum[...] = jnp.zeros_like(dk_sum)
        dv_sum[...] = jnp.zeros_like(dv_sum)
        for block in range(blocks):
            query = pair_rows(qc[rows(block), :], kv)
            grads = pair_rows(do_c[rows(block), :], kv)
            delta = row_sums(do_c[rows(block), both], ctxc[rows(block), both])
            level = jnp.concatenate(
                [lsec[2 * kv : 2 * kv + 1, rows(block)], lsec[2 * kv + 1 : 2 * kv + 2, rows(block)]], axis=1
            )
            dq = jnp.zeros((2 * QB, HEAD_DIM), f32)
            for part in range(span // QB):
                keys = ckv[rows(part), base : base + HEAD_DIM]
                values = ckv[rows(part), base + HEAD_DIM : base + 2 * HEAD_DIM]
                probs, dscores = backward_tile(keys, values, query, grads, keep[rows(part)], None, level, delta)
                dscores = dscores.astype(bf16)
                dv_sum[rows(part)] += nn(probs.astype(bf16), grads)
                dk_sum[rows(part)] += nn(dscores, query)
                dq += tn(dscores, keys)
            dqc[rows(block), both] = jnp.concatenate([dq[:QB], dq[QB:]], axis=1).astype(bf16)
        dkv[:, base : base + HEAD_DIM] = dk_sum[...].astype(bf16)
        dkv[:, base + HEAD_DIM : base + 2 * HEAD_DIM] = dv_sum[...].astype(bf16)
        if kv:
            next(links)
        if kv == 3:
            next(home)

    weight = w2[...].reshape(-1, w2.shape[-1])
    for block in range(blocks):
        own_c[rows(block), :] = nt(dqc[rows(block), :], weight[:, inner:]).astype(bf16)
        wires.send(own_c.at[rows(block)], got_c.at[rows(block)], spot.sibling(), over + blocks + block)
    own_m[...] = nt(dkv[...], weight[:, :inner]).astype(bf16).reshape(own_m.shape)
    wires.send(own_m.at[:, 1 - spot.core], got_m, spot.sibling(), over + 2 * blocks)
    for block in range(blocks):
        g_cq[block] = tn(a2[:, rows(block)], dqc[...]).reshape(g_cq.shape[1:]).astype(bf16)
    next(links)
    for block in range(blocks):
        g_ckv[block] = tn(mem[:, rows(block)], dkv[...]).reshape(g_ckv.shape[1:]).astype(bf16)
    next(links)
    for block in range(2):
        g_cout[2 * block : 2 * block + 2] = (
            tn(ctxc[:, rows(block)], eb[...]).reshape((2,) + g_cout.shape[1:]).astype(bf16)
        )
    leaving = [wires.move(*pair) for pair in ((g_cq, o_cq), (g_ckv, o_ckv), (g_cout, o_cout))]
    gain_terms = jnp.zeros((1, e2.shape[1]), f32)
    for block in range(blocks):
        if block + 1 < blocks:
            fetch(x1, block + 1, (block + 1) % 2)
        wires.arrive(got_c.at[rows(block)], spot.sibling(), over + blocks + block)
        change, term = norm_back(
            block,
            block % 2,
            gains[1:2, :],
            own_c[rows(block), :].astype(f32) + got_c[rows(block), :].astype(f32),
        )
        gain_terms = gain_terms + term
        value = e2[rows(block), :] + change
        e2[rows(block), :] = value
        half[block] = e2[pl.ds(pl.multiple_of(block * QB + spot.core * (QB // 2), QB // 2), QB // 2), :]
        eb[rows(block), :] = value.astype(bf16)
        do_s[rows(block), :] = nt(value.astype(bf16), w3[0].reshape(inner, -1)).astype(bf16)
    terms[1:2, :] = 0.5 * gain_terms
    next(links)
    for block in range(inner // QB):
        g_out[rows(block), :] = tn(ctx[:, rows(block)], eb[...]).astype(bf16)
    wires.arrive(got_m, spot.sibling(), over + 2 * blocks)
    o_mem[...] = (own_m[:, spot.core].astype(f32) + got_m[...].astype(f32)).astype(bf16)
    for _ in links:
        pass
    for program in [home]:
        for _ in program:
            pass
    for copy in leaving:
        copy.wait()
    wires.close()


def cross_part(depth, *operands):
    bf16, f32 = jnp.bfloat16, jnp.float32
    shape = jax.ShapeDtypeStruct
    hbm = pl.BlockSpec(memory_space=pl.ANY)
    vmem = pl.BlockSpec(memory_space=pltpu.VMEM)
    g_early, g_down, g_gate, g_up, x2, _, t_out, _, _, _, ckv = operands[:11]
    far = operands[7:17]
    tokens, width = x2.shape
    span, inner = ckv.shape
    own = tokens // 8
    rows = g_gate.shape[4]
    outs = [
        (shape(g_early.shape[4:], f32), vmem),
        (shape(g_down.shape[4:], f32), vmem),
        (shape(g_gate.shape[4:], f32), vmem),
        (shape(g_up.shape[4:], f32), vmem),
        (shape(g_gate.shape[4:], bf16), vmem),
        (shape(g_up.shape[4:], bf16), vmem),
        (shape((depth, 1, 2, 2, rows, width), bf16), hbm),
        (shape((depth, 2, 2, 2, rows, inner), bf16), hbm),
        (shape((depth, 2, 2, 2, rows, inner), bf16), hbm),
        (shape((4, own, width), f32), vmem),
        (shape((tokens, inner), bf16), vmem),
        (shape((inner, width), bf16), vmem),
        (shape((4, span // 8, width), bf16), vmem),
        (shape((8, width), f32), vmem),
        (shape((2, 2) + t_out.shape[1:], bf16), hbm),
    ]
    scratch = [pltpu.VMEM(array.shape, bf16) for array in far]
    scratch += [pltpu.VMEM(outs[i][0].shape, bf16) for i in (6, 7, 8)]
    scratch += [
        pltpu.VMEM((2, QB, width), f32),
        pltpu.VMEM((tokens, width), f32),
        pltpu.VMEM((tokens, width), bf16),
        pltpu.VMEM((tokens, inner), bf16),
        pltpu.VMEM((tokens, inner), bf16),
        pltpu.VMEM((span, inner), bf16),
        pltpu.VMEM((span, HEAD_DIM), f32),
        pltpu.VMEM((span, HEAD_DIM), f32),
        pltpu.VMEM((tokens, width), bf16),
        pltpu.VMEM((tokens, width), bf16),
        pltpu.VMEM((tokens, width), bf16),
        pltpu.VMEM((4, 2, span // 8, width), bf16),
        pltpu.VMEM((4, span // 8, width), bf16),
    ]
    for grads in (g_down, g_gate, g_up, g_early):
        scratch += scatter_buffers(depth, grads.shape[1], *grads.shape[4:])
    number = 16 + 4 * (4 + depth)
    return pl.pallas_call(
        functools.partial(cross_backward_kernel, depth),
        in_specs=[hbm] * 17 + [vmem] * 3,
        out_specs=[spec for _, spec in outs],
        out_shape=[kind for kind, _ in outs],
        scratch_shapes=scratch + wire_scratch(number, 48),
        compiler_params=pltpu.CompilerParams(
            collective_id=1, has_side_effects=True, vmem_limit_bytes=60 * 2**20
        ),
        cost_estimate=pl.CostEstimate(
            flops=16 * 10**9, bytes_accessed=128 * 2**20, transcendentals=10**7
        ),
    )(*operands)


def sides(core, own, got):
    got = got.astype(jnp.float32)
    return jnp.where(core == 0, own, got), jnp.where(core == 0, got, own)


def spread_hidden(core, owns, gots):
    pairs = [sides(core, own[...], got[...]) for own, got in zip(owns, gots)]
    sizes = [own.shape[1] // 16 for own in owns]
    return jnp.concatenate(
        [
            pair[place % 2][:, (place // 2 * 4 + q) * size : (place // 2 * 4 + q + 1) * size]
            for place in range(8)
            for q in range(4)
            for pair, size in zip(pairs, sizes)
        ],
        axis=1,
    )


def spread_heads(core, own, got, targets, units):
    even, odd = sides(core, own[...], got[...])
    step = even.shape[1] // 4
    for group in range(4):
        start = group * step
        for target, unit in zip(targets, units):
            lanes = slice(start, start + unit)
            target[:, 2 * group * unit : 2 * (group + 1) * unit] = jnp.concatenate(
                [even[:, lanes], odd[:, lanes]], axis=1
            )
            start += unit


def self_backward_kernel(depth, *refs):
    (
        g_cout, g_cq, g_ckv, g_out, t_mem, f_do, f_qkv, f_ctx, f_a1, f_x, f_half, f_w1, lse, keep, bent, gains,
        terms, codes,
        rg0, rg1, rg2, ru0, ru1, ru2, qg0, qg1, qg2, qu0, qu1, qu2, rd0, rd1, rd2,
        r_cout, r_out, h_mem, h_in, packed, d_q, d_k, d_v, d_cq, d_ck, d_cv, d_gate, d_up, d_down,
        *rest
    ) = refs
    take = lambda n: [rest.pop(0) for _ in range(n)]
    bias, sums, dk_sum, dv_sum, dqkv, grad, mine, theirs, pieces, line, small, work = take(12)
    near = take(7)
    do_s, qkv, ctx, a1, x, half, w1 = near
    r_cq, r_ckv, r_qkv, q_cq, q_ckv, q_qkv = take(6)
    buffers = [take(9) for _ in range(4)]
    resident = [take(7) for _ in range(4)]
    f32, bf16 = jnp.float32, jnp.bfloat16
    spot = Spot(depth)
    wires = Wires(*rest)
    blocks = kvs = 4
    inner = 2 * kvs * HEAD_DIM

    def rows(block):
        return slice(block * QB, (block + 1) * QB)

    far = (f_do, f_qkv, f_ctx, f_a1, f_x, f_half, f_w1)
    coming = [wires.move(source, target) for source, target in zip(far, near)]
    spot.greet()
    over = wires.take(blocks)
    homes = [deliver_tokens(spot, wires, t_mem, h_mem)]
    early = pipeline(
        [
            scatter_sums(spot, wires, g_cout, buffers[0], r_cout, None),
            scatter_sums(spot, wires, g_cq, buffers[1], r_cq, q_cq),
            scatter_sums(spot, wires, g_ckv, buffers[2], r_ckv, q_ckv),
            scatter_sums(spot, wires, g_out, buffers[3], r_out, None),
        ]
    )
    late = []
    for kv in range(kvs):
        lanes = pl.ds(kv * QB, QB)
        late.append(
            scatter_sums(
                spot, wires, grad.at[kv], resident[kv], r_qkv.at[:, lanes], q_qkv.at[:, lanes], True
            )
        )
    next(early)
    for program in homes:
        next(program)
    d_gate[...] = spread_hidden(spot.core, (rg0, rg1, rg2), (qg0, qg1, qg2))
    d_up[...] = spread_hidden(spot.core, (ru0, ru1, ru2), (qu0, qu1, qu2))
    low = 0
    for piece in (rd0, rd1, rd2):
        d_down[low : low + piece.shape[0], :] = piece[...]
        low += piece.shape[0]
    for copy in coming:
        copy.wait()
    for kv in range(kvs):
        base = kv * 4 * HEAD_DIM
        both = slice(2 * kv * HEAD_DIM, 2 * (kv + 1) * HEAD_DIM)
        dk_sum[...] = jnp.zeros_like(dk_sum)
        dv_sum[...] = jnp.zeros_like(dv_sum)
        sums[...] = jnp.zeros_like(sums)
        for member in range(2):
            for offset in range(4):
                head = 2 * kv + member
                bias[offset, :, member * QB : (member + 1) * QB] = spread_row(
                    bent[head : head + 1, offset * 2 * QB : (offset + 1) * 2 * QB]
                )
        for block in range(blocks):
            query = pair_rows(qkv[rows(block), base : base + 2 * HEAD_DIM], 0)
            grads = pair_rows(do_s[rows(block), :], kv)
            delta = row_sums(do_s[rows(block), both], ctx[rows(block), both])
            level = jnp.concatenate(
                [lse[2 * kv : 2 * kv + 1, rows(block)], lse[2 * kv + 1 : 2 * kv + 2, rows(block)]], axis=1
            )
            dq = jnp.zeros((2 * QB, HEAD_DIM), f32)
            for part in range(block + 1):
                keys = qkv[rows(part), base + 2 * HEAD_DIM : base + 3 * HEAD_DIM]
                values = qkv[rows(part), base + 3 * HEAD_DIM : base + 4 * HEAD_DIM]
                probs, dscores = backward_tile(
                    keys, values, query, grads, keep[rows(part)], bias[block - part], level, delta
                )
                sums[block - part] += dscores
                dscores = dscores.astype(bf16)
                dv_sum[rows(part)] += nn(probs.astype(bf16), grads)
                dk_sum[rows(part)] += nn(dscores, query)
                dq += tn(dscores, keys)
            dqkv[rows(block), base : base + 2 * HEAD_DIM] = jnp.concatenate(
                [dq[:QB], dq[QB:]], axis=1
            ).astype(bf16)
            if block % 2 or kv == 0 and block:
                next(early, None)
            for earlier in range(kv):
                if block == 2:
                    next(late[earlier], None)
        dqkv[:, base + 2 * HEAD_DIM : base + 3 * HEAD_DIM] = dk_sum[...].astype(bf16)
        dqkv[:, base + 3 * HEAD_DIM : base + 4 * HEAD_DIM] = dv_sum[...].astype(bf16)
        for member in range(2):
            for offset in range(4):
                tile = fold(sums[offset, :, member * QB : (member + 1) * QB])
                row = tile[0:1]
                for r in range(1, 8):
                    row = row + pltpu.roll(tile[r : r + 1], 2 * QB - r, 1)
                head = 2 * kv + member
                line[head : head + 1, (offset + 1) * QB : (offset + 2) * QB] = row[:, :QB]
                if offset > 0:
                    line[head : head + 1, offset * QB : (offset + 1) * QB] += row[:, QB:]
        chunk = dqkv[:, base : base + 4 * HEAD_DIM]
        for block in range(blocks):
            grad[kv, block] = tn(a1[:, rows(block)], chunk).astype(bf16).reshape(grad.shape[2:])
        next(late[kv])
        if kv == 1:
            for program in homes:
                next(program)
    weight = w1[...].reshape(-1, w1.shape[-1])
    size = QB // 2

    def half_rows(block, core):
        return pl.ds(pl.multiple_of(block * QB + core * size, size), size)

    for block in range(blocks):
        mine[block] = nt(dqkv[half_rows(block, 1 - spot.core), :], weight).astype(bf16)
        wires.send(mine.at[block], theirs.at[block], spot.sibling(), over + block)
    for program in late:
        next(program, None)
    gain_terms = jnp.zeros((1, x.shape[-1]), f32)
    for block in range(blocks):
        upstream = nt(dqkv[half_rows(block, spot.core), :], weight).astype(bf16).astype(f32)
        wires.arrive(theirs.at[block], spot.sibling(), over + block)
        upstream = upstream + theirs[block].astype(f32)
        value = x[block, spot.core].astype(f32)
        inverse = inverse_rms(value)
        scaled = upstream * gains[0:1, :]
        mean = jnp.mean(value * scaled, axis=-1, keepdims=True)
        change = inverse * scaled - value * (inverse * inverse * inverse) * mean
        gain_terms = gain_terms + jnp.sum(upstream * value * inverse, axis=0, keepdims=True)
        pieces[block] = (half[block] + change).astype(bf16)
    homing = deliver_tokens(spot, wires, pieces, h_in)
    next(homing)
    shares = nt_exact(line[:, QB:], codes[...])
    small[...] = jnp.zeros_like(small)
    for r in range(8):
        lanes = slice(r * 128, (r + 1) * 128)
        small[r : r + 1, :] = terms[0:1, lanes]
        small[8 + r : 9 + r, :] = terms[1:2, lanes]
        small[16 + r : 17 + r, :] = gain_terms[:, lanes]
    zero = jnp.zeros_like(shares)
    small[24:32, :BUCKETS] = jnp.where(spot.core == 0, shares, zero)
    small[24:32, BUCKETS : 2 * BUCKETS] = jnp.where(spot.core == 1, shares, zero)
    summing = total_small(spot, wires, small, work, packed)
    next(summing)
    for _ in range(4):
        next(summing, None)
        for program in late:
            next(program, None)
    for program in late + homes + [homing, summing]:
        for _ in program:
            pass
    for _ in early:
        pass
    spread_heads(spot.core, r_qkv, q_qkv, (d_q, d_k, d_v), (2 * HEAD_DIM, HEAD_DIM, HEAD_DIM))
    spread_heads(spot.core, r_ckv, q_ckv, (d_ck, d_cv), (HEAD_DIM, HEAD_DIM))
    spread_heads(spot.core, r_cq, q_cq, (d_cq,), (2 * HEAD_DIM,))
    wires.close()


def nt_exact(left, right):
    return lax.dot_general(
        left, right, (((1,), (1,)), ((), ())), precision=HIGH, preferred_element_type=jnp.float32
    )


def self_part(depth, *operands):
    bf16, f32 = jnp.bfloat16, jnp.float32
    shape = jax.ShapeDtypeStruct
    hbm = pl.BlockSpec(memory_space=pl.ANY)
    vmem = pl.BlockSpec(memory_space=pltpu.VMEM)
    _, g_cq, _, g_out, t_mem, do_s = operands[:6]
    tokens, inner = do_s.shape
    width = g_out.shape[-1]
    rows = g_out.shape[4]
    own = tokens // 8
    hidden = 2 * sum(tile.shape[1] for tile in operands[18:21])
    outs = [
        (shape((rows, width), f32), vmem),
        (shape((rows, width), f32), vmem),
        (shape((2, 2) + t_mem.shape[1:], bf16), hbm),
        (shape((2, 2, own, width), bf16), hbm),
        (shape((32, 128), f32), vmem),
    ]
    for size in (2 * inner, inner, inner, 2 * inner, inner, inner, hidden, hidden):
        outs.append((shape((rows, size), f32), vmem))
    outs.append((shape((sum(piece.shape[0] for piece in operands[-3:]), width), f32), vmem))
    scratch = [
        pltpu.VMEM((4, QB, 2 * QB), f32),
        pltpu.VMEM((4, QB, 2 * QB), f32),
        pltpu.VMEM((tokens, HEAD_DIM), f32),
        pltpu.VMEM((tokens, HEAD_DIM), f32),
        pltpu.VMEM((tokens, 2 * inner), bf16),
        pltpu.VMEM((4, depth, 2, 2, 2, rows, QB), bf16),
        pltpu.VMEM((4, own, width), bf16),
        pltpu.VMEM((4, own, width), bf16),
        pltpu.VMEM((4, own, width), bf16),
        pltpu.VMEM((8, 5 * QB), f32),
        pltpu.VMEM((32, 128), f32),
        pltpu.VMEM((6 + depth, 32, 128), f32),
    ]
    scratch += [pltpu.VMEM(array.shape, array.dtype) for array in operands[5:12]]
    for kind in (f32, bf16):
        scratch += [pltpu.VMEM((rows, size), kind) for size in (inner, inner, 2 * inner)]
    for lanes, size in ((1, width), (2, inner), (2, inner), (1, width)):
        scratch += scatter_buffers(depth, lanes, rows, size)
    for _ in range(4):
        scratch += scatter_buffers(depth, 2, rows, QB)[2:]
    return pl.pallas_call(
        functools.partial(self_backward_kernel, depth),
        in_specs=[hbm] * 12 + [vmem] * 21,
        out_specs=[spec for _, spec in outs],
        out_shape=[kind for kind, _ in outs],
        scratch_shapes=scratch + wire_scratch(4 + 8 + 3 + depth + 8 * (4 + depth), 20),
        compiler_params=pltpu.CompilerParams(
            collective_id=2, has_side_effects=True, vmem_limit_bytes=60 * 2**20
        ),
        cost_estimate=pl.CostEstimate(
            flops=16 * 10**9, bytes_accessed=128 * 2**20, transcendentals=10**7
        ),
    )(*operands)


def feed_forward_kernel(depth, tiles, *refs):
    (
        a3_far, wt_far, valid, x2, gu0_far, d0_far, gu1p, d1p, gu2p, d2p,
        o_top, o_u, pieces, g_gate2, g_up2, g_down2, g5,
        r_gate0, r_up0, r_down0, r_gate1, r_up1, q_gate0, q_up0, q_gate1, q_up1,
        *rest
    ) = refs
    take = lambda n: [rest.pop(0) for _ in range(n)]
    gu1, d1, gu2, d2, mid, dgate, dup, g0, g1, g2, g3, g4, mine, theirs, second = take(15)
    a3, wt, gu0, d0, low_top, u = take(6)
    buffers = [take(7) for _ in range(5)]
    f32, bf16 = jnp.float32, jnp.bfloat16
    spot = Spot(depth)
    wires = Wires(*rest)
    blocks = 4
    starts = [sum(tiles[:i]) for i in range(3)]
    coming = [
        wires.move(source, target)
        for source, target in ((wt_far, wt), (a3_far, a3), (gu0_far, gu0), (d0_far, d0))
    ]

    def rows(block):
        return slice(block * QB, (block + 1) * QB)

    spot.greet()
    over = wires.take(blocks)
    middle = d1.shape[-1] // 2
    wide1 = share_plane(
        spot, wires, gu1p, lambda corner: gu1.at[:, :, corner], lambda view, side: view.at[:, side]
    )
    down1 = share_plane(
        spot,
        wires,
        d1p,
        lambda corner: d1.at[0, :, corner],
        lambda view, side: view.at[:, :, pl.ds(side * middle, middle)],
    )
    wide2 = gather_columns(spot, wires, gu2p, gu2)
    down2 = gather_rows(spot, wires, d2p, d2)
    sums = [
        scatter_sums(spot, wires, grads, scratch, total, got, True)
        for grads, scratch, total, got in (
            (g0, buffers[0], r_gate0, q_gate0),
            (g1, buffers[1], r_up0, q_up0),
            (g2, buffers[2], r_down0, None),
            (g3, buffers[3], r_gate1, q_gate1),
            (g4, buffers[4], r_up1, q_up1),
        )
    ]

    def advance(*programs):
        for program in programs:
            next(program, None)

    advance(wide1, down1, wide2, down2)
    halves = [
        wires.move(
            x2.at[pl.ds(pl.multiple_of(block * QB + spot.core * (QB // 2), QB // 2), QB // 2)], second.at[block]
        )
        for block in range(blocks)
    ]
    for copy in coming:
        copy.wait()
    for block in range(blocks):
        value = wt[block].reshape(QB, -1).astype(f32) * valid[rows(block)]
        low_top[rows(block), :] = value.astype(bf16)
    coming = [wires.move(low_top, o_top)]
    wides = [gu0, gu1, gu2]
    downs = [d0, d1, d2]

    def wide_weight(tile, part):
        both = wides[tile]
        lanes = pl.ds(part * tiles[tile], tiles[tile])
        return both[:, :, :, :, lanes].reshape(-1, tiles[tile])

    def down_weight(tile):
        weight = downs[tile][0]
        if weight.shape[2] % 16:
            return weight.astype(f32).reshape(tiles[tile], -1).astype(bf16)
        return weight.reshape(tiles[tile], -1)

    def hidden(tile, block):
        lanes = slice(starts[tile], starts[tile] + tiles[tile])
        left = a3[rows(block), :]
        gate = nn(left, wide_weight(tile, 0))
        upward = nn(left, wide_weight(tile, 1))
        back = nt(low_top[rows(block), :], down_weight(tile))
        bend = jnp.tanh(GELU_SCALE * (gate + GELU_CUBE * gate * gate * gate))
        share = 0.5 * (1.0 + bend)
        active = gate * share
        slope = share + 0.5 * gate * (1.0 - bend * bend) * (
            GELU_SCALE * (1.0 + 3.0 * GELU_CUBE * gate * gate)
        )
        mid[rows(block), lanes] = (active * upward).astype(bf16)
        dgate[rows(block), lanes] = (back * upward * slope).astype(bf16)
        dup[rows(block), lanes] = (back * active).astype(bf16)

    def wide_grads(tile, source, target):
        lanes = slice(starts[tile], starts[tile] + tiles[tile])
        right = source[:, lanes]
        for block in range(blocks):
            target[block] = tn(a3[:, rows(block)], right).reshape(target.shape[1:]).astype(bf16)

    def down_grads(tile, target):
        lanes = slice(starts[tile], starts[tile] + tiles[tile])
        target[...] = tn(mid[:, lanes], low_top[...]).reshape(target.shape).astype(bf16)

    hidden(0, 0)
    hidden(0, 1)
    hidden(0, 2)
    hidden(0, 3)
    wide_grads(0, dgate, g0)
    advance(sums[0])
    wide_grads(0, dup, g1)
    advance(wide1, down1, wide2, down2)
    down_grads(0, g2)
    advance(wide1, down1, sums[1])
    for block in range(blocks):
        hidden(1, block)
        if block == 1:
            advance(sums[0], wide2, down2, sums[2])
    advance(sums[1])
    wide_grads(1, dgate, g3)
    advance(sums[0], wide2, down2, sums[3])
    wide_grads(1, dup, g4)
    advance(sums[2], sums[1])
    down_grads(1, g5)
    advance(sums[0], sums[4])
    for block in range(blocks):
        hidden(2, block)
        if block == 1:
            advance(sums[3], sums[2])
        if block == 3:
            advance(sums[1], sums[0])
    wide_grads(2, dgate, g_gate2)
    wide_grads(2, dup, g_up2)
    advance(sums[4], sums[3], sums[2])
    down_grads(2, g_down2)

    def half_rows(block, core):
        return pl.ds(pl.multiple_of(block * QB + core * (QB // 2), QB // 2), QB // 2)

    def contribution(block, core):
        total = None
        for tile in range(3):
            lanes = slice(starts[tile], starts[tile] + tiles[tile])
            term = nn(mid[half_rows(block, core), lanes], down_weight(tile))
            total = term if total is None else total + term
        return total.astype(bf16)

    for block in range(blocks):
        mine[block] = contribution(block, 1 - spot.core)
        wires.send(mine.at[block], theirs.at[block], spot.sibling(), over + block)
    for block in range(blocks):
        total = None
        for tile in range(3):
            lanes = slice(starts[tile], starts[tile] + tiles[tile])
            term = nt(dgate[rows(block), lanes], wide_weight(tile, 0))
            term = term + nt(dup[rows(block), lanes], wide_weight(tile, 1))
            total = term if total is None else total + term
        u[rows(block), :] = total.astype(bf16)
        coming.append(wires.move(u.at[rows(block)], o_u.at[rows(block)]))
        if block == 1:
            advance(sums[4], sums[3])
    advance(sums[4])
    for block in range(blocks):
        value = contribution(block, spot.core).astype(f32)
        wires.arrive(theirs.at[block], spot.sibling(), over + block)
        value = value + theirs[block].astype(f32)
        halves[block].wait()
        pieces[block] = ((second[block] + value) * valid[half_rows(block, spot.core), :]).astype(bf16)
    for program in sums + [wide1, down1, wide2, down2]:
        for _ in program:
            pass
    for copy in coming:
        copy.wait()
    wires.close()


def feed_forward(depth, tiles, *operands):
    bf16, f32 = jnp.bfloat16, jnp.float32
    shape = jax.ShapeDtypeStruct
    hbm = pl.BlockSpec(memory_space=pl.ANY)
    vmem = pl.BlockSpec(memory_space=pltpu.VMEM)
    a3, _, _, _, gu0, d0, gu1p, d1p, gu2p, d2p = operands
    tokens, width = a3.shape
    hidden_width = sum(tiles)
    rows = [d1p.shape[1], d1p.shape[1], d2p.shape[2]]
    own = tokens // 8
    wide = gu2p.shape[2]

    def wide_grad(tile):
        return (depth, 2, 2, 2, wide, tiles[tile])

    def down_grad(tile):
        return (depth, 1, 2, 2, rows[tile], width)

    outs = [
        (shape((tokens, width), bf16), hbm),
        (shape((tokens, width), bf16), hbm),
        (shape((4, own, width), bf16), vmem),
        (shape(wide_grad(2), bf16), vmem),
        (shape(wide_grad(2), bf16), vmem),
        (shape(down_grad(2), bf16), vmem),
        (shape(down_grad(1), bf16), vmem),
    ]
    for tile in range(2):
        outs += [(shape((wide, tiles[tile]), f32), vmem)] * 2
        if tile == 0:
            outs.append((shape((rows[tile], width), f32), vmem))
    for tile in range(2):
        outs += [(shape((wide, tiles[tile]), bf16), vmem)] * 2
    scratch = [
        pltpu.VMEM(gu0.shape, bf16),
        pltpu.VMEM(d0.shape, bf16),
        pltpu.VMEM((depth, 2) + gu2p.shape[1:], bf16),
        pltpu.VMEM((1, depth) + d2p.shape[1:], bf16),
    ]
    scratch += [pltpu.VMEM((tokens, hidden_width), bf16)] * 3
    for tile in range(2):
        scratch += [pltpu.VMEM(wide_grad(tile), bf16)] * 2
        if tile == 0:
            scratch.append(pltpu.VMEM(down_grad(tile), bf16))
    scratch += [
        pltpu.VMEM((4, own, width), bf16),
        pltpu.VMEM((4, own, width), bf16),
        pltpu.VMEM((4, own, width), f32),
        pltpu.VMEM((tokens, width), bf16),
        pltpu.VMEM((4, 2, own, width), bf16),
        pltpu.VMEM(gu0.shape, bf16),
        pltpu.VMEM(d0.shape, bf16),
        pltpu.VMEM((tokens, width), bf16),
        pltpu.VMEM((tokens, width), bf16),
    ]
    for tile in range(2):
        for _ in range(2):
            scratch += scatter_buffers(depth, 2, wide, tiles[tile])[2:]
        if tile == 0:
            scratch += scatter_buffers(depth, 1, rows[tile], width)[2:]
    return pl.pallas_call(
        functools.partial(feed_forward_kernel, depth, tiles),
        in_specs=[hbm, hbm, vmem] + [hbm] * 7,
        out_specs=[spec for _, spec in outs],
        out_shape=[kind for kind, _ in outs],
        scratch_shapes=scratch + wire_scratch(4 + 22 * depth + 6 * (4 + depth), 24),
        compiler_params=pltpu.CompilerParams(
            collective_id=3, has_side_effects=True, vmem_limit_bytes=60 * 2**20
        ),
        cost_estimate=pl.CostEstimate(
            flops=27 * 10**9, bytes_accessed=64 * 2**20, transcendentals=10**7
        ),
    )(*operands)


def per_chip(
    layer_input,
    memory,
    target_lengths,
    memory_lengths,
    buckets,
    norm_self,
    self_q,
    self_k,
    self_v,
    self_out,
    rel_bias,
    norm_cross,
    cross_q,
    cross_k,
    cross_v,
    cross_out,
    norm_ff,
    ff_gate,
    ff_up,
    ff_down,
    cotangent,
):
    bf16, f32 = jnp.bfloat16, jnp.float32
    depth = lax.axis_size("dp") // 2
    spot = Spot(depth)
    core = spot.core
    width = layer_input.shape[3]
    local = layer_input.shape[2]
    near = memory.shape[2]
    shard = norm_self.shape[0]

    cuts = [(0, 32), (32, 64), (64, ff_down.shape[0] // 4)]
    tiles = tuple(16 * (stop - start) for start, stop in cuts)
    down_packs = [ff_down.reshape(4, -1, width)[None, :, start:stop] for start, stop in cuts]

    heads = jnp.arange(4)
    spots = (heads // 2) * 64 + 2 * spot.corner + heads % 2
    placed = jnp.sum(
        jnp.where(jnp.arange(128)[None, None, :] == spots[None, :, None], rel_bias[:, :, None].astype(f32), 0.0),
        axis=1,
    )
    lengths = jnp.concatenate([target_lengths, memory_lengths]).reshape(1, 4).astype(f32)
    small = jnp.concatenate(
        [
            jnp.stack([norm_self, norm_cross, norm_ff]).astype(f32),
            jnp.pad(lengths, ((0, 0), (0, 124))),
            placed,
        ]
    )
    padded = jnp.concatenate([jnp.full((1, QB), -1, jnp.int32), buckets[None, :]], axis=1)
    vectors = row_pieces(padded)
    vectors = jnp.concatenate([jnp.roll(vectors[..., ::-1], 1, axis=-1), vectors], axis=1).reshape(1, -1)
    codes = (vectors == jnp.arange(BUCKETS, dtype=jnp.int32)[:, None]).astype(bf16)
    holes = jnp.where(vectors < 0, NEG, 0.0).astype(f32)
    onehot = (buckets[:, None] == jnp.arange(BUCKETS, dtype=jnp.int32)[None, :]).astype(f32)
    (
        inputs, upstream, encoded, _, w_qkv, w_cross, w_outs, w_gu, w_down,
        normed_self, qkv, context, self_sums, first, normed_cross, cross_queries, far_kv, cross_context,
        cross_sums, second, normed_ff, gains, _, _, bent, keep_self, keep_cross, near_wide, near_down, wide_pack,
    ) = forward_layer(
        depth,
        tuple(stop for _, stop in cuts),
        layer_input.reshape(2, 2, local // 2, width),
        cotangent.reshape(2, 2, local // 2, width),
        memory.reshape(2, 2, near // 2, width),
        small,
        jnp.stack([self_out, cross_out]).reshape(2, 4, -1, width),
        down_packs[0],
        down_packs[1],
        codes,
        holes,
        self_q,
        self_k,
        self_v,
        cross_k,
        cross_v,
        cross_q,
        ff_gate,
        ff_up,
    )
    encoded = encoded.reshape(-1, width)
    valid = (keep_self == 0).astype(f32)
    (
        top_low, changed, output, g_gate, g_up, g_down, g_early,
        r_gate0, r_up0, r_down0, r_gate1, r_up1, q_gate0, q_up0, q_gate1, q_up1,
    ) = feed_forward(
        depth, tiles, normed_ff, upstream, valid, second, w_gu, w_down,
        near_wide, near_down, wide_pack, down_packs[2],
    )

    (
        r_down1, r_down2, r_gate2, r_up2, q_gate2, q_up2, g_cout, g_cq, g_ckv, half, self_up, g_out, memory_grad, terms,
        output,
    ) = cross_part(
        depth, g_early, g_down, g_gate, g_up, second, first, output, changed, top_low, cross_queries, far_kv, cross_context,
        normed_cross, encoded, w_cross, w_outs, context, cross_sums, keep_cross, gains,
    )
    (
        r_cout, r_out, memory_grad, input_grad, packed, d_q, d_k, d_v, d_cq, d_ck, d_cv, d_gate, d_up, d_down,
    ) = self_part(
        depth, g_cout, g_cq, g_ckv, g_out.reshape(depth, 1, 2, 2, -1, width), memory_grad, self_up, qkv, context,
        normed_self, inputs, half, w_qkv, self_sums, keep_self, bent, gains, terms, onehot.T,
        r_gate0, r_gate1, r_gate2, r_up0, r_up1, r_up2, q_gate0, q_gate1, q_gate2, q_up0, q_up1, q_up2,
        r_down0, r_down1, r_down2,
    )
    bias_grad = packed[24:, :64].reshape(4, 2, 2, BUCKETS)
    bias_grad = jnp.transpose(bias_grad, (3, 0, 2, 1)).reshape(BUCKETS, HEADS)
    packed = packed[:24].reshape(3, width)
    mine = lax.axis_index("dp") * 4 + spot.corner
    piece = width // (depth * 8)
    n_ff, n_cross, n_self = (lax.dynamic_slice_in_dim(packed[i], mine * piece, piece) for i in range(3))
    bias_grad = lax.dynamic_slice(
        bias_grad, (lax.axis_index("dp") * rel_bias.shape[0], spot.corner * rel_bias.shape[1]), rel_bias.shape
    )

    return (
        output.reshape(layer_input.shape),
        input_grad.astype(f32).reshape(layer_input.shape),
        memory_grad.astype(f32).reshape(memory.shape),
        n_self,
        d_q,
        d_k,
        d_v,
        r_out,
        bias_grad,
        n_cross,
        d_cq,
        d_ck,
        d_cv,
        r_cout,
        n_ff,
        d_gate,
        d_up,
        d_down,
    )


def solution(mesh):
    placed = (
        P(None, "dp", "seq", None),
        P(None, "dp", "seq", None),
        P(None, "dp"),
        P(None, "dp"),
        P(),
        P("dp"),
        P("dp", None),
        P("dp", None),
        P("dp", None),
        P("dp", None),
        P("dp", "seq"),
        P("dp"),
        P("dp", None),
        P("dp", None),
        P("dp", None),
        P("dp", None),
        P("dp"),
        P("dp", None),
        P("dp", None),
        P("dp", None),
        P(None, "dp", "seq", None),
    )
    chips = mesh.shape["seq"] == 4 and mesh.shape["dp"] == HEADS // 2
    return jax.shard_map(
        per_chip if chips else per_device,
        mesh=mesh,
        in_specs=placed,
        out_specs=(
            P(None, "dp", "seq", None),
            P(None, "dp", "seq", None),
            P(None, "dp", "seq", None),
            P(("dp", "seq")),
            P(("dp", "seq"), None),
            P(("dp", "seq"), None),
            P(("dp", "seq"), None),
            P(("dp", "seq"), None),
            P("dp", "seq"),
            P(("dp", "seq")),
            P(("dp", "seq"), None),
            P(("dp", "seq"), None),
            P(("dp", "seq"), None),
            P(("dp", "seq"), None),
            P(("dp", "seq")),
            P(("dp", "seq"), None),
            P(("dp", "seq"), None),
            P(("dp", "seq"), None),
        ),
        check_vma=False,
    )
```

```python
import functools

import jax
import jax.numpy as jnp
from jax import lax
from jax.experimental import pallas as pl
from jax.experimental.pallas import tpu as pltpu
from jax.sharding import PartitionSpec as P

HEADS = 16
HEAD_DIM = 64
BUCKETS = 32
KV_HEADS = 8
TGT = 1024
MEM = 512
QB = 256
GELU_SCALE = 0.7978845608
GELU_CUBE = 0.044715


EPS = 1e-06
NEG = -1e30
HIGH = lax.Precision.HIGHEST


def shortened(shard):
    return jax.tree.map(lambda a: a.astype(jnp.bfloat16) if a.dtype == jnp.float32 else a, shard)


def rms_norm(value, gain):
    return value * lax.rsqrt(jnp.mean(value * value, axis=-1, keepdims=True) + EPS) * gain


def gated(gate, upward):
    return jax.nn.gelu(gate, approximate=True) * upward


def project(left, right):
    return jnp.dot(left, right, preferred_element_type=jnp.float32)


def project_back(grad, weight):
    return lax.dot_general(
        grad, weight, (((1,), (1,)), ((), ())), preferred_element_type=jnp.float32
    )


def weight_grad(left, right):
    return lax.dot_general(
        left, right, (((0,), (0,)), ((), ())), preferred_element_type=jnp.float32
    )


def split_heads(values, group):
    return values.reshape(values.shape[:2] + (-1, group, HEAD_DIM))


def split_shared(values):
    return values.reshape(values.shape[:2] + (-1, HEAD_DIM))


def causal_masks(table, length, group):

    def masks(start, block):
        stop = start + block
        rows = start + jnp.arange(block, dtype=jnp.int32)
        columns = jnp.arange(stop, dtype=jnp.int32)
        distance = rows[:, None] - columns[None, :]
        keep = (distance >= 0) & (columns[None, :] < length)
        extra = jnp.take(table, jnp.maximum(distance, 0), axis=1)
        return (extra.reshape((-1, group, block, stop)), keep, stop)

    return masks


def memory_masks(length, width):

    def masks(start, block):
        keep = jnp.broadcast_to(
            jnp.arange(width, dtype=jnp.int32)[None, :] < length, (block, width)
        )
        return (None, keep, width)

    return masks


def diagonal_sums(grads, block, stop):
    leading = grads.shape[:2]
    flipped = jnp.pad(grads[..., ::-1], ((0, 0), (0, 0), (0, 0), (0, block)))
    skewed = flipped.reshape(leading + (block * (stop + block),))[..., : block * (stop + block - 1)]
    skewed = skewed.reshape(leading + (block, stop + block - 1))
    return jnp.sum(skewed, axis=2)[..., block - 1 :]


def attend_forward(queries, keys, values, masks):
    block = min(512, queries.shape[0])
    outputs = []
    totals = []
    for index in range(queries.shape[0] // block):
        start = index * block
        extra, keep, stop = masks(start, block)
        rows = queries[start : start + block]
        scores = jnp.einsum("rkgd,skd->kgrs", rows, keys[:stop], preferred_element_type=jnp.float32)
        if extra is not None:
            scores = scores + extra
        scores = jnp.where(keep, scores, NEG)
        peak = jnp.max(scores, axis=-1, keepdims=True)
        weights = jnp.where(keep, jnp.exp(scores - peak), 0.0)
        total = jnp.sum(weights, axis=-1, keepdims=True)
        probs = (weights / total).astype(jnp.bfloat16)
        mixed = jnp.einsum(
            "kgrs,skd->rkgd", probs, values[:stop], preferred_element_type=jnp.float32
        )
        outputs.append(mixed.astype(jnp.bfloat16))
        totals.append(peak + jnp.log(total))
    return (jnp.concatenate(outputs, 0), jnp.concatenate(totals, 2))


def attend_backward(queries, keys, values, sums, grads, masks):
    block = min(512, queries.shape[0])
    key_grads = jnp.zeros(keys.shape, jnp.float32)
    value_grads = jnp.zeros(values.shape, jnp.float32)
    diagonal = jnp.zeros(sums.shape[:3], jnp.float32)
    query_grads = []
    for index in range(queries.shape[0] // block):
        start = index * block
        extra, keep, stop = masks(start, block)
        rows = queries[start : start + block]
        grad_rows = grads[start : start + block]
        scores = jnp.einsum("rkgd,skd->kgrs", rows, keys[:stop], preferred_element_type=jnp.float32)
        if extra is not None:
            scores = scores + extra
        scores = jnp.where(keep, scores, NEG)
        probs = jnp.where(keep, jnp.exp(scores - sums[:, :, start : start + block]), 0.0)
        value_grads = value_grads.at[:stop].add(
            jnp.einsum(
                "kgrs,rkgd->skd",
                probs.astype(jnp.bfloat16),
                grad_rows,
                preferred_element_type=jnp.float32,
            )
        )
        dprobs = jnp.einsum(
            "rkgd,skd->kgrs", grad_rows, values[:stop], preferred_element_type=jnp.float32
        )
        delta = jnp.sum(probs * dprobs, axis=-1, keepdims=True)
        dscores = (probs * (dprobs - delta)).astype(jnp.bfloat16)
        query_grads.append(
            jnp.einsum(
                "kgrs,skd->rkgd", dscores, keys[:stop], preferred_element_type=jnp.float32
            ).astype(jnp.bfloat16)
        )
        key_grads = key_grads.at[:stop].add(
            jnp.einsum("kgrs,rkgd->skd", dscores, rows, preferred_element_type=jnp.float32)
        )
        if extra is not None:
            diagonal = diagonal.at[:, :, :stop].add(
                diagonal_sums(dscores.astype(jnp.float32), block, stop)
            )
    return (
        jnp.concatenate(query_grads, 0),
        key_grads.astype(jnp.bfloat16),
        value_grads.astype(jnp.bfloat16),
        diagonal,
    )


def self_forward(queries, keys, values, length, table):
    return attend_forward(queries, keys, values, causal_masks(table, length, queries.shape[2]))


def self_backward(queries, keys, values, sums, grads, length, table):
    return attend_backward(
        queries, keys, values, sums, grads, causal_masks(table, length, queries.shape[2])
    )


def cross_forward(queries, keys, values, length):
    return attend_forward(queries, keys, values, memory_masks(length, keys.shape[0]))


def cross_backward(queries, keys, values, sums, grads, length):
    return attend_backward(queries, keys, values, sums, grads, memory_masks(length, keys.shape[0]))


def to_tokens(values):
    return lax.all_to_all(shortened(values), "seq", split_axis=1, concat_axis=2, tiled=True).astype(
        values.dtype
    )


def to_heads(grads):
    return lax.all_to_all(grads, "seq", split_axis=2, concat_axis=1, tiled=True)


def per_device(
    layer_input,
    memory,
    target_lengths,
    memory_lengths,
    buckets,
    norm_self,
    self_q,
    self_k,
    self_v,
    self_out,
    rel_bias,
    norm_cross,
    cross_q,
    cross_k,
    cross_v,
    cross_out,
    norm_ff,
    ff_gate,
    ff_up,
    ff_down,
    cotangent,
):
    micro_count, batch_rows, local_tokens, model_width = layer_input.shape
    memory_tokens = memory.shape[2]
    group = HEADS // KV_HEADS
    replicas = lax.axis_size("dp")
    shards = (
        norm_self,
        self_q,
        self_k,
        self_v,
        self_out,
        rel_bias,
        norm_cross,
        cross_q,
        cross_k,
        cross_v,
        cross_out,
        norm_ff,
        ff_gate,
        ff_up,
        ff_down,
    )
    totals = [
        jnp.zeros((piece.shape[0] * replicas,) + piece.shape[1:], jnp.float32) for piece in shards
    ]
    onehot = (buckets[:, None] == jnp.arange(BUCKETS, dtype=jnp.int32)[None, :]).astype(jnp.float32)
    places = lax.axis_index("seq") * local_tokens + jnp.arange(local_tokens, dtype=jnp.int32)
    diagonal = jnp.zeros((rel_bias.shape[1] // group, group, TGT), jnp.float32)
    outputs = []
    input_grads = []
    memory_grads = []
    for micro_step in range(micro_count):
        gathered = (
            lax.all_gather(norm_self, "dp", axis=0, tiled=True),
            lax.all_gather(self_q, "dp", axis=0, tiled=True),
            lax.all_gather(self_k, "dp", axis=0, tiled=True),
            lax.all_gather(self_v, "dp", axis=0, tiled=True),
            lax.all_gather(self_out, "dp", axis=0, tiled=True),
            lax.all_gather(rel_bias, "dp", axis=0, tiled=True),
            lax.all_gather(norm_cross, "dp", axis=0, tiled=True),
            lax.all_gather(cross_q, "dp", axis=0, tiled=True),
            lax.all_gather(cross_k, "dp", axis=0, tiled=True),
            lax.all_gather(cross_v, "dp", axis=0, tiled=True),
            lax.all_gather(cross_out, "dp", axis=0, tiled=True),
            lax.all_gather(norm_ff, "dp", axis=0, tiled=True),
            lax.all_gather(ff_gate, "dp", axis=0, tiled=True),
            lax.all_gather(ff_up, "dp", axis=0, tiled=True),
            lax.all_gather(ff_down, "dp", axis=0, tiled=True),
        )
        (
            gain_self,
            query_self,
            key_self,
            value_self,
            output_self,
            bias_whole,
            gain_cross,
            query_cross,
            key_cross,
            value_cross,
            output_cross,
            gain_ff,
            gate_weight,
            up_weight,
            down_weight,
        ) = gathered
        gain_self = gain_self.astype(jnp.float32)
        gain_cross = gain_cross.astype(jnp.float32)
        gain_ff = gain_ff.astype(jnp.float32)
        table = lax.dot_general(
            bias_whole.astype(jnp.float32), onehot, (((0,), (1,)), ((), ())), precision=HIGH
        )
        lengths = target_lengths[micro_step]
        spans = memory_lengths[micro_step]
        valid = (places[None, :] < lengths[:, None]).astype(jnp.float32).reshape(-1, 1)
        hidden = layer_input[micro_step].reshape(-1, model_width).astype(jnp.float32)
        normed_self = rms_norm(hidden, gain_self).astype(jnp.bfloat16)
        queries = (
            project(normed_self, query_self)
            .astype(jnp.bfloat16)
            .reshape(batch_rows, local_tokens, -1)
        )
        keys = (
            project(normed_self, key_self)
            .astype(jnp.bfloat16)
            .reshape(batch_rows, local_tokens, -1)
        )
        values = (
            project(normed_self, value_self)
            .astype(jnp.bfloat16)
            .reshape(batch_rows, local_tokens, -1)
        )
        encoded = memory[micro_step].reshape(-1, model_width)
        memory_keys = (
            project(encoded, key_cross).astype(jnp.bfloat16).reshape(batch_rows, memory_tokens, -1)
        )
        memory_values = (
            project(encoded, value_cross)
            .astype(jnp.bfloat16)
            .reshape(batch_rows, memory_tokens, -1)
        )
        head_queries, head_keys, head_values, far_keys, far_values = (
            lax.all_to_all(queries, "seq", split_axis=2, concat_axis=1, tiled=True),
            lax.all_to_all(keys, "seq", split_axis=2, concat_axis=1, tiled=True),
            lax.all_to_all(values, "seq", split_axis=2, concat_axis=1, tiled=True),
            lax.all_to_all(memory_keys, "seq", split_axis=2, concat_axis=1, tiled=True),
            lax.all_to_all(memory_values, "seq", split_axis=2, concat_axis=1, tiled=True),
        )
        self_queries = split_heads(head_queries, group)
        self_keys = split_shared(head_keys)
        self_values = split_shared(head_values)
        far_keys = split_shared(far_keys)
        far_values = split_shared(far_values)
        attended, self_sums = jax.vmap(self_forward, in_axes=(0, 0, 0, 0, None))(
            self_queries, self_keys, self_values, lengths, table
        )
        context = to_tokens(attended.reshape(batch_rows, TGT, -1)).reshape(
            batch_rows * local_tokens, -1
        )
        first = hidden + project(context, output_self)
        normed_cross = rms_norm(first, gain_cross).astype(jnp.bfloat16)
        cross_queries = (
            project(normed_cross, query_cross)
            .astype(jnp.bfloat16)
            .reshape(batch_rows, local_tokens, -1)
        )
        cross_heads = split_heads(
            lax.all_to_all(cross_queries, "seq", split_axis=2, concat_axis=1, tiled=True), group
        )
        cross_attended, cross_sums = jax.vmap(cross_forward)(
            cross_heads, far_keys, far_values, spans
        )
        cross_context = to_tokens(cross_attended.reshape(batch_rows, TGT, -1)).reshape(
            batch_rows * local_tokens, -1
        )
        second = first + project(cross_context, output_cross)
        normed_ff = rms_norm(second, gain_ff).astype(jnp.bfloat16)
        gate = project(normed_ff, gate_weight)
        upward = project(normed_ff, up_weight)
        middle = gated(gate, upward).astype(jnp.bfloat16)
        third = second + project(middle, down_weight)
        outputs.append(
            (third * valid).astype(jnp.bfloat16).reshape(batch_rows, local_tokens, model_width)
        )
        upstream = cotangent[micro_step].reshape(-1, model_width).astype(jnp.float32) * valid
        down_grad = upstream.astype(jnp.bfloat16)
        totals[14] = totals[14] + weight_grad(middle, down_grad)
        _, pullback = jax.vjp(gated, gate, upward)
        gate_grad, upward_grad = pullback(project_back(down_grad, down_weight))
        gate_grad = gate_grad.astype(jnp.bfloat16)
        upward_grad = upward_grad.astype(jnp.bfloat16)
        totals[12] = totals[12] + weight_grad(normed_ff, gate_grad)
        totals[13] = totals[13] + weight_grad(normed_ff, upward_grad)
        _, pullback = jax.vjp(rms_norm, second, gain_ff)
        second_grad, gain_grad = pullback(
            project_back(gate_grad, gate_weight) + project_back(upward_grad, up_weight)
        )
        totals[11] = totals[11] + gain_grad
        second_grad = second_grad + upstream
        cross_grad = second_grad.astype(jnp.bfloat16)
        totals[10] = totals[10] + weight_grad(cross_context, cross_grad)
        context_grad = (
            project_back(cross_grad, output_cross)
            .astype(jnp.bfloat16)
            .reshape(batch_rows, local_tokens, -1)
        )
        cross_query_grad, far_key_grad, far_value_grad, _ = jax.vmap(cross_backward)(
            cross_heads,
            far_keys,
            far_values,
            cross_sums,
            split_heads(to_heads(context_grad), group),
            spans,
        )
        query_back, key_back, value_back = (
            lax.all_to_all(
                shortened(cross_query_grad.reshape(batch_rows, TGT, -1)),
                "seq",
                split_axis=1,
                concat_axis=2,
                tiled=True,
            ),
            lax.all_to_all(
                shortened(far_key_grad.reshape(batch_rows, MEM, -1)),
                "seq",
                split_axis=1,
                concat_axis=2,
                tiled=True,
            ),
            lax.all_to_all(
                shortened(far_value_grad.reshape(batch_rows, MEM, -1)),
                "seq",
                split_axis=1,
                concat_axis=2,
                tiled=True,
            ),
        )
        query_back = query_back.reshape(batch_rows * local_tokens, -1)
        key_back = key_back.reshape(batch_rows * memory_tokens, -1)
        value_back = value_back.reshape(batch_rows * memory_tokens, -1)
        totals[7] = totals[7] + weight_grad(normed_cross, query_back)
        totals[8] = totals[8] + weight_grad(encoded, key_back)
        totals[9] = totals[9] + weight_grad(encoded, value_back)
        memory_grads.append(
            (project_back(key_back, key_cross) + project_back(value_back, value_cross)).reshape(
                batch_rows, memory_tokens, model_width
            )
        )
        _, pullback = jax.vjp(rms_norm, first, gain_cross)
        first_grad, gain_grad = pullback(project_back(query_back, query_cross))
        totals[6] = totals[6] + gain_grad
        first_grad = first_grad + second_grad
        self_grad = first_grad.astype(jnp.bfloat16)
        totals[4] = totals[4] + weight_grad(context, self_grad)
        context_grad = (
            project_back(self_grad, output_self)
            .astype(jnp.bfloat16)
            .reshape(batch_rows, local_tokens, -1)
        )
        query_grad, key_grad, value_grad, bias_grad = jax.vmap(
            self_backward, in_axes=(0, 0, 0, 0, 0, 0, None)
        )(
            self_queries,
            self_keys,
            self_values,
            self_sums,
            split_heads(to_heads(context_grad), group),
            lengths,
            table,
        )
        diagonal = diagonal + jnp.sum(bias_grad, axis=0)
        query_back, key_back, value_back = (
            lax.all_to_all(
                shortened(query_grad.reshape(batch_rows, TGT, -1)),
                "seq",
                split_axis=1,
                concat_axis=2,
                tiled=True,
            ),
            lax.all_to_all(
                shortened(key_grad.reshape(batch_rows, TGT, -1)),
                "seq",
                split_axis=1,
                concat_axis=2,
                tiled=True,
            ),
            lax.all_to_all(
                shortened(value_grad.reshape(batch_rows, TGT, -1)),
                "seq",
                split_axis=1,
                concat_axis=2,
                tiled=True,
            ),
        )
        query_back = query_back.reshape(batch_rows * local_tokens, -1)
        key_back = key_back.reshape(batch_rows * local_tokens, -1)
        value_back = value_back.reshape(batch_rows * local_tokens, -1)
        totals[1] = totals[1] + weight_grad(normed_self, query_back)
        totals[2] = totals[2] + weight_grad(normed_self, key_back)
        totals[3] = totals[3] + weight_grad(normed_self, value_back)
        _, pullback = jax.vjp(rms_norm, hidden, gain_self)
        hidden_grad, gain_grad = pullback(
            project_back(query_back, query_self)
            + project_back(key_back, key_self)
            + project_back(value_back, value_self)
        )
        totals[0] = totals[0] + gain_grad
        input_grads.append(
            (hidden_grad + first_grad).reshape(batch_rows, local_tokens, model_width)
        )
    totals[5] = lax.dot_general(
        onehot, diagonal.reshape(-1, TGT), (((0,), (1,)), ((), ())), precision=HIGH
    )
    reduced = (
        lax.psum_scatter(totals[0], ("dp", "seq"), scatter_dimension=0, tiled=True),
        lax.psum_scatter(totals[1], ("dp", "seq"), scatter_dimension=0, tiled=True),
        lax.psum_scatter(totals[2], ("dp", "seq"), scatter_dimension=0, tiled=True),
        lax.psum_scatter(totals[3], ("dp", "seq"), scatter_dimension=0, tiled=True),
        lax.psum_scatter(totals[4], ("dp", "seq"), scatter_dimension=0, tiled=True),
        lax.psum_scatter(totals[6], ("dp", "seq"), scatter_dimension=0, tiled=True),
        lax.psum_scatter(totals[7], ("dp", "seq"), scatter_dimension=0, tiled=True),
        lax.psum_scatter(totals[8], ("dp", "seq"), scatter_dimension=0, tiled=True),
        lax.psum_scatter(totals[9], ("dp", "seq"), scatter_dimension=0, tiled=True),
        lax.psum_scatter(totals[10], ("dp", "seq"), scatter_dimension=0, tiled=True),
        lax.psum_scatter(totals[11], ("dp", "seq"), scatter_dimension=0, tiled=True),
        lax.psum_scatter(totals[12], ("dp", "seq"), scatter_dimension=0, tiled=True),
        lax.psum_scatter(totals[13], ("dp", "seq"), scatter_dimension=0, tiled=True),
        lax.psum_scatter(totals[14], ("dp", "seq"), scatter_dimension=0, tiled=True),
    )
    bias_share = lax.psum_scatter(totals[5], "dp", scatter_dimension=0, tiled=True)
    return (
        jnp.stack(outputs),
        jnp.stack(input_grads),
        jnp.stack(memory_grads),
        reduced[0],
        reduced[1],
        reduced[2],
        reduced[3],
        reduced[4],
        bias_share,
        reduced[5],
        reduced[6],
        reduced[7],
        reduced[8],
        reduced[9],
        reduced[10],
        reduced[11],
        reduced[12],
        reduced[13],
    )


def row_pieces(full):
    blocks = full.reshape(full.shape[0], -1, QB)
    return jnp.concatenate([blocks[:, 1:], blocks[:, :-1]], axis=2)


def seed_rows(vectors):
    return jnp.stack([jnp.roll(vectors, r, axis=-1) for r in range(8)], axis=-2)


def spread(seed):
    rows = 8
    tile = seed
    while rows < QB:
        tile = jnp.concatenate([tile, pltpu.roll(tile, rows, 1)], axis=0)
        rows *= 2
    return tile[:, :QB]


def fold(tile):
    width = 2 * QB
    tile = jnp.concatenate([tile, jnp.zeros_like(tile)], axis=1)
    rows = QB
    while rows > 8:
        rows //= 2
        tile = tile[:rows] + pltpu.roll(tile[rows:], width - rows, 1)
    return tile


def nt(left, right):
    return lax.dot_general(left, right, (((1,), (1,)), ((), ())), preferred_element_type=jnp.float32)


def tn(left, right):
    return lax.dot_general(left, right, (((0,), (0,)), ((), ())), preferred_element_type=jnp.float32)


def nn(left, right):
    return lax.dot_general(left, right, (((1,), (0,)), ((), ())), preferred_element_type=jnp.float32)


def inverse_rms(value):
    return lax.rsqrt(jnp.mean(value * value, axis=-1, keepdims=True) + EPS)


def pick(array, index, axis=0):
    return lax.dynamic_index_in_dim(array, index, axis, keepdims=False)


MESH = pl.DeviceIdType.MESH


class Spot:
    def __init__(self, depth):
        self.depth = depth
        place = lax.axis_index("dp")
        self.corner = lax.axis_index("seq")
        self.z, self.core = place // 2, place % 2
        self.y, self.x = self.corner // 2, self.corner % 2

    def at(self, z=None, core=None, y=None, x=None):
        z = self.z if z is None else z
        core = self.core if core is None else core
        y = self.y if y is None else y
        x = self.x if x is None else x
        return (z * 2 + core, y * 2 + x)

    def beside(self):
        return self.at(x=1 - self.x)

    def below(self):
        return self.at(y=1 - self.y)

    def sibling(self):
        return self.at(core=1 - self.core)

    def greet(self):
        barrier = pltpu.get_barrier_semaphore()
        others = [
            self.at(None, self.core ^ (i >> 2), self.y ^ (i >> 1 & 1), self.x ^ (i & 1)) for i in range(1, 8)
        ]
        for step in range(1, self.depth):
            for flip in range(2):
                others.append(self.at((self.z + step) % self.depth, self.core ^ flip))
        for other in others:
            pl.semaphore_signal(barrier, inc=1, device_id=other, device_id_type=MESH)
        pl.semaphore_wait(barrier, len(others))


class Wires:
    def __init__(self, sends, arrivals, moves):
        self.sends, self.arrivals, self.moves = sends, arrivals, moves
        self.count = 0
        self.moved = 0
        self.open = []

    def take(self, number):
        first = self.count
        self.count += number
        return first

    def send(self, source, target, device, index, landing=None):
        landing = index if landing is None else landing
        copy = pltpu.make_async_remote_copy(
            src_ref=source,
            dst_ref=target,
            send_sem=self.sends.at[index],
            recv_sem=self.arrivals.at[landing],
            device_id=device,
            device_id_type=MESH,
        )
        copy.start()
        self.open.append(copy)
        return copy

    def arrive(self, target, device, index):
        pltpu.make_async_remote_copy(
            src_ref=target,
            dst_ref=target,
            send_sem=self.sends.at[0],
            recv_sem=self.arrivals.at[index],
            device_id=device,
            device_id_type=MESH,
        ).wait_recv()

    def move(self, source, target):
        copy = pltpu.make_async_copy(source, target, self.moves.at[self.moved])
        self.moved += 1
        copy.start()
        return copy

    def close(self):
        for copy in self.open:
            copy.wait_send()
        self.open = []


def collect_tokens(spot, wires, parcel, whole):
    away = wires.take(4)
    over = wires.take(4)
    local = wires.moved
    wires.moved += 1
    for index in range(4):
        half, micro = spot.y ^ (index >> 1), spot.x ^ (index & 1)
        home = (half == spot.core) & (micro == spot.y) & (spot.core == spot.x)
        source = parcel.at[micro, half]
        target = whole.at[spot.corner, half]
        copy = pltpu.make_async_remote_copy(
            src_ref=source,
            dst_ref=target,
            send_sem=wires.sends.at[away + index],
            recv_sem=wires.arrivals.at[away + index],
            device_id=spot.at(core=half, y=micro, x=spot.core),
            device_id_type=MESH,
        )
        here = pltpu.make_async_copy(source, target, wires.moves.at[local])

        @pl.when(jnp.logical_not(home))
        def _():
            copy.start()

        @pl.when(home)
        def _():
            here.start()

    yield
    for index in range(4):
        block = 2 * (spot.core ^ (index >> 1)) + (spot.y ^ (index & 1))
        home = (spot.x == spot.core) & (block == spot.corner)
        piece = whole.at[block, spot.core]
        here = pltpu.make_async_copy(piece, piece, wires.moves.at[local])
        landed = pltpu.make_async_remote_copy(
            src_ref=piece,
            dst_ref=piece,
            send_sem=wires.sends.at[away + index],
            recv_sem=wires.arrivals.at[away + index],
            device_id=spot.sibling(),
            device_id_type=MESH,
        )

        @pl.when(jnp.logical_not(home))
        def _():
            landed.wait_recv()

        @pl.when(home)
        def _():
            here.wait()

        wires.send(piece, piece, spot.sibling(), over + index)
    yield
    for index in range(4):
        block = 2 * ((1 - spot.core) ^ (index >> 1)) + (spot.y ^ (index & 1))
        wires.arrive(whole.at[block, 1 - spot.core], spot.sibling(), over + index)
    for index in range(4):
        half, micro = spot.y ^ (index >> 1), spot.x ^ (index & 1)
        home = (half == spot.core) & (micro == spot.y) & (spot.core == spot.x)
        source = parcel.at[micro, half]

        @pl.when(jnp.logical_not(home))
        def _():
            pltpu.make_async_remote_copy(
                src_ref=source,
                dst_ref=source,
                send_sem=wires.sends.at[away + index],
                recv_sem=wires.arrivals.at[away + index],
                device_id=spot.sibling(),
                device_id_type=MESH,
            ).wait_send()

    yield


def deliver_tokens(spot, wires, pieces, homes):
    away = wires.take(4)
    local = wires.moved
    wires.moved += 1

    def parts():
        for index in range(4):
            block = 2 * (spot.core ^ (index >> 1)) + (spot.y ^ (index & 1))
            home = (spot.x == spot.core) & (block == spot.corner)
            source = pieces.at[block]
            target = homes.at[spot.y, spot.core]
            remote = pltpu.make_async_remote_copy(
                src_ref=source,
                dst_ref=target,
                send_sem=wires.sends.at[away + index],
                recv_sem=wires.arrivals.at[away + index],
                device_id=spot.at(core=spot.x, y=block // 2, x=block % 2),
                device_id_type=MESH,
            )
            yield home, remote, pltpu.make_async_copy(source, target, wires.moves.at[local])

    for home, remote, here in parts():
        pl.when(jnp.logical_not(home))(remote.start)
        pl.when(home)(here.start)
    yield
    for index in range(4):
        half, micro = spot.y ^ (index >> 1), spot.x ^ (index & 1)
        home = (half == spot.core) & (micro == spot.y) & (spot.core == spot.x)
        piece = homes.at[micro, half]
        landed = pltpu.make_async_remote_copy(
            src_ref=piece,
            dst_ref=piece,
            send_sem=wires.sends.at[away + index],
            recv_sem=wires.arrivals.at[away + index],
            device_id=spot.sibling(),
            device_id_type=MESH,
        )
        here = pltpu.make_async_copy(piece, piece, wires.moves.at[local])
        pl.when(jnp.logical_not(home))(landed.wait_recv)
        pl.when(home)(here.wait)
    for home, remote, here in parts():
        pl.when(jnp.logical_not(home))(remote.wait_send)
    yield


def gather_small(spot, wires, block, whole):
    own = wires.move(block, whole.at[spot.z, spot.core, spot.corner])
    first = wires.take(spot.depth + 3)
    for step in range(1, spot.depth):
        target = whole.at[spot.z, spot.core, spot.corner]
        wires.send(block, target, spot.at(z=(spot.z + step) % spot.depth), first + step)
    yield
    own.wait()
    for step in range(1, spot.depth):
        z = (spot.z - step + spot.depth) % spot.depth
        wires.arrive(whole.at[z, spot.core, spot.corner], spot.sibling(), first + step)
    column = whole.at[:, spot.core, spot.corner]
    wires.send(column, column, spot.beside(), first)
    wires.send(column, column, spot.below(), first + spot.depth)
    wires.send(column, column, spot.at(y=1 - spot.y, x=1 - spot.x), first + spot.depth + 1)
    yield
    for flip, index in ((1, first), (2, first + spot.depth), (3, first + spot.depth + 1)):
        wires.arrive(whole.at[:, spot.core, spot.corner ^ flip], spot.sibling(), index)
    plane = whole.at[:, spot.core]
    wires.send(plane, plane, spot.sibling(), first + spot.depth + 2)
    yield
    wires.arrive(whole.at[:, 1 - spot.core], spot.sibling(), first + spot.depth + 2)
    yield


def gather_columns(spot, wires, pack, whole):
    depth, me = spot.depth, spot.corner
    ahead = wires.take(2 * depth)
    flat = wires.take(4 * depth)
    own = wires.move(pack.at[spot.core], whole.at[spot.z, spot.core])
    for step in range(1, depth):
        for flip in range(2):
            wires.send(
                pack.at[spot.core ^ flip, me],
                whole.at[spot.z, spot.core, me],
                spot.at((spot.z + step) % depth, spot.core ^ flip),
                ahead + 2 * step + flip,
            )
    wires.send(pack.at[1 - spot.core], whole.at[spot.z, spot.core], spot.sibling(), ahead)
    yield
    for step in range(1, depth):
        z = (spot.z - step + depth) % depth
        for flip in range(2):
            wires.arrive(whole.at[z, spot.core ^ flip, me], spot.sibling(), ahead + 2 * step + flip)
        quarter = whole.at[z, :, me]
        wires.send(quarter, quarter, spot.beside(), flat + 4 * step)
        wires.send(quarter, quarter, spot.below(), flat + 4 * step + 1)
    yield
    for step in range(1, depth):
        z = (spot.z - step + depth) % depth
        wires.arrive(whole.at[z, :, me ^ 1], spot.sibling(), flat + 4 * step)
        piece = whole.at[z, 0, me ^ 1]
        wires.send(piece, piece, spot.below(), flat + 4 * step + 2)
        wires.arrive(whole.at[z, :, me ^ 2], spot.sibling(), flat + 4 * step + 1)
        piece = whole.at[z, 1, me ^ 2]
        wires.send(piece, piece, spot.beside(), flat + 4 * step + 3)
    yield
    own.wait()
    wires.arrive(whole.at[spot.z, 1 - spot.core], spot.sibling(), ahead)
    for step in range(1, depth):
        z = (spot.z - step + depth) % depth
        wires.arrive(whole.at[z, 0, me ^ 3], spot.sibling(), flat + 4 * step + 2)
        wires.arrive(whole.at[z, 1, me ^ 3], spot.sibling(), flat + 4 * step + 3)
    yield


def gather_rows(spot, wires, pack, whole):
    depth, me = spot.depth, spot.corner
    ahead = wires.take(depth)
    flat = wires.take(4 * depth)
    middle = pack.shape[-1] // 2

    def part(z, corner, side):
        if pack.shape[0] == 2:
            return whole.at[side, z, corner]
        return whole.at[0, z, corner, :, pl.ds(side * middle, middle)]

    own = wires.move(pack, whole.at[:, spot.z])
    for step in range(1, depth):
        wires.send(
            pack.at[:, me], whole.at[:, spot.z, me], spot.at((spot.z + step) % depth), ahead + step
        )
    yield
    for step in range(1, depth):
        z = (spot.z - step + depth) % depth
        quarter = whole.at[:, z, me]
        wires.arrive(quarter, spot.sibling(), ahead + step)
        wires.send(quarter, quarter, spot.beside(), flat + 4 * step)
        wires.send(quarter, quarter, spot.below(), flat + 4 * step + 1)
    yield
    for step in range(1, depth):
        z = (spot.z - step + depth) % depth
        wires.arrive(whole.at[:, z, me ^ 1], spot.sibling(), flat + 4 * step)
        piece = part(z, me ^ 1, 0)
        wires.send(piece, piece, spot.below(), flat + 4 * step + 2)
        wires.arrive(whole.at[:, z, me ^ 2], spot.sibling(), flat + 4 * step + 1)
        piece = part(z, me ^ 2, 1)
        wires.send(piece, piece, spot.beside(), flat + 4 * step + 3)
    yield
    own.wait()
    for step in range(1, depth):
        z = (spot.z - step + depth) % depth
        wires.arrive(part(z, me ^ 3, 0), spot.sibling(), flat + 4 * step + 2)
        wires.arrive(part(z, me ^ 3, 1), spot.sibling(), flat + 4 * step + 3)
    yield


def reach_columns(spot, wires, pack, near):
    depth, me = spot.depth, spot.corner
    ahead = wires.take(2 * depth)
    own = wires.move(pack.at[spot.core, me], near.at[spot.z, spot.core])
    for step in range(depth):
        for flip in range(2):
            if step or flip:
                wires.send(
                    pack.at[spot.core ^ flip, me],
                    near.at[spot.z, spot.core],
                    spot.at((spot.z + step) % depth, spot.core ^ flip),
                    ahead + 2 * step + flip,
                )
    yield
    own.wait()
    for step in range(depth):
        z = (spot.z - step + depth) % depth
        for flip in range(2):
            if step or flip:
                wires.arrive(near.at[z, spot.core ^ flip], spot.sibling(), ahead + 2 * step + flip)
    yield


def reach_rows(spot, wires, pack, near):
    depth, me = spot.depth, spot.corner
    ahead = wires.take(depth)
    own = wires.move(pack.at[0, me], near.at[spot.z])
    for step in range(1, depth):
        wires.send(pack.at[0, me], near.at[spot.z], spot.at((spot.z + step) % depth), ahead + step)
    yield
    own.wait()
    for step in range(1, depth):
        z = (spot.z - step + depth) % depth
        wires.arrive(near.at[z], spot.sibling(), ahead + step)
    yield


def share_plane(spot, wires, near, whole, parts):
    me = spot.corner
    flat = wires.take(4)
    own = wires.move(near, whole(me))
    wires.send(near, whole(me), spot.beside(), flat)
    wires.send(near, whole(me), spot.below(), flat + 1)
    yield
    wires.arrive(whole(me ^ 1), spot.sibling(), flat)
    piece = parts(whole(me ^ 1), 0)
    wires.send(piece, piece, spot.below(), flat + 2)
    wires.arrive(whole(me ^ 2), spot.sibling(), flat + 1)
    piece = parts(whole(me ^ 2), 1)
    wires.send(piece, piece, spot.beside(), flat + 3)
    yield
    own.wait()
    wires.arrive(parts(whole(me ^ 3), 0), spot.sibling(), flat + 2)
    wires.arrive(parts(whole(me ^ 3), 1), spot.sibling(), flat + 3)
    yield


def scatter_buffers(depth, lanes, rows, width):
    half = depth // 2
    return [
        pltpu.VMEM((half, lanes, 2, rows, width), jnp.bfloat16),
        pltpu.VMEM((half, lanes, 2, rows, width), jnp.bfloat16),
        pltpu.VMEM((half, lanes, 2, rows, width), jnp.bfloat16),
        pltpu.VMEM((half, lanes, 2, rows, width), jnp.bfloat16),
        pltpu.VMEM((half, lanes, rows, width), jnp.bfloat16),
        pltpu.VMEM((half, lanes, rows, width), jnp.bfloat16),
        pltpu.VMEM((depth, lanes, rows, width), jnp.bfloat16),
        pltpu.VMEM((depth, lanes, rows, width), jnp.bfloat16),
        pltpu.VMEM((rows, width), jnp.bfloat16),
    ]


def scatter_sums(spot, wires, grads, buffers, total, got, resident=False):
    depth, half = spot.depth, spot.depth // 2
    lanes = grads.shape[1]
    places = [(z, a, s) for z in range(half) for a in range(lanes) for s in range(2)]
    if resident:
        low_in, high_in, low_last, high_last, column, column_in, passing = buffers
        low, high = low_in, high_in
    else:
        low, high, low_in, high_in, low_last, high_last, column, column_in, passing = buffers
    first = wires.take(4)
    away = wires.take(depth)
    mine = []
    if not resident:
        mine = [
            wires.move(grads.at[pl.ds(0, half), :, :, spot.x], low),
            wires.move(grads.at[pl.ds(half, half), :, spot.y], high),
        ]
    wires.send(grads.at[pl.ds(0, half), :, :, 1 - spot.x], low_in, spot.beside(), first)
    wires.send(grads.at[pl.ds(half, half), :, 1 - spot.y], high_in, spot.below(), first + 1)
    yield
    for copy in mine:
        copy.wait()

    def join(target, other, index):
        target[index] = (target[index].astype(jnp.float32) + other.astype(jnp.float32)).astype(jnp.bfloat16)

    wires.arrive(low_in, spot.beside(), first)
    for z, a, s in places:
        join(low, grads[z, a, s, spot.x] if resident else low_in[z, a, s], (z, a, s))
    wires.send(low.at[:, :, 1 - spot.y], low_last, spot.below(), first + 2)
    wires.arrive(high_in, spot.below(), first + 1)
    for z, a, s in places:
        join(high, grads[half + z, a, spot.y, s] if resident else high_in[z, a, s], (z, a, s))
    wires.send(high.at[:, :, 1 - spot.x], high_last, spot.beside(), first + 3)
    yield
    wires.arrive(low_last, spot.below(), first + 2)
    wires.arrive(high_last, spot.beside(), first + 3)
    for z in range(half):
        for a in range(lanes):
            column[z, a] = (
                low[z, a, spot.y].astype(jnp.float32) + low_last[z, a].astype(jnp.float32)
            ).astype(jnp.bfloat16)
            column[half + z, a] = (
                high[z, a, spot.x].astype(jnp.float32) + high_last[z, a].astype(jnp.float32)
            ).astype(jnp.bfloat16)
    for step in range(1, depth):
        z = (spot.z + step) % depth
        wires.send(column.at[z], column_in.at[step], spot.at(z), away + step)
    yield
    for step in range(1, depth):
        wires.arrive(column_in.at[step], spot.sibling(), away + step)

    def added(lane):
        result = column[spot.z, lane].astype(jnp.float32)
        for step in range(1, depth):
            result = result + column_in[step, lane].astype(jnp.float32)
        return result

    if lanes == 1:
        total[...] = added(0)
    else:
        passing[...] = added(1 - spot.core).astype(jnp.bfloat16)
        wires.send(passing, got, spot.sibling(), away)
        total[...] = added(spot.core)
    yield
    if lanes == 2:
        wires.arrive(got, spot.sibling(), away)
    yield


def total_small(spot, wires, terms, work, total):
    first = wires.take(3 + spot.depth)
    work[0] = terms[...]
    wires.send(work.at[0], work.at[1], spot.sibling(), first)
    yield
    wires.arrive(work.at[1], spot.sibling(), first)
    work[2] = work[0] + work[1]
    wires.send(work.at[2], work.at[3], spot.beside(), first + 1)
    yield
    wires.arrive(work.at[3], spot.sibling(), first + 1)
    work[4] = work[2] + work[3]
    wires.send(work.at[4], work.at[5], spot.below(), first + 2)
    yield
    wires.arrive(work.at[5], spot.sibling(), first + 2)
    work[6] = work[4] + work[5]
    for step in range(1, spot.depth):
        target = work.at[6 + step]
        wires.send(work.at[6], target, spot.at((spot.z + step) % spot.depth), first + 2 + step)
    yield
    result = work[6]
    for step in range(1, spot.depth):
        wires.arrive(work.at[6 + step], spot.sibling(), first + 2 + step)
        result = result + work[6 + step]
    total[...] = result
    yield


def wire_scratch(number, moves):
    return [
        pltpu.SemaphoreType.DMA((number,)),
        pltpu.SemaphoreType.DMA((number,)),
        pltpu.SemaphoreType.DMA((moves,)),
    ]


def spread_row(vector):
    tile = pltpu.roll(jnp.broadcast_to(vector, (8, 2 * QB)), 0, 1, stride=1, stride_axis=0)
    return spread(tile)


def attend_block(query, keys, values, keep, bias):
    scores = nt(query, keys) + keep
    if bias is not None:
        scores = scores + bias
    peak = jnp.max(scores, axis=1, keepdims=True)
    weights = jnp.exp(scores - peak)
    total = jnp.sum(weights, axis=1, keepdims=True)
    return nn(weights.astype(jnp.bfloat16), values) / total, peak + jnp.log(total)


def pair_rows(block, kv):
    both = block[:, 2 * kv * HEAD_DIM : 2 * (kv + 1) * HEAD_DIM]
    return jnp.concatenate([both[:, :HEAD_DIM], both[:, HEAD_DIM:]], axis=0)


def normed(value, gain):
    return (value * inverse_rms(value) * gain).astype(jnp.bfloat16)


def pack_heads(pack, weights, start):
    size = sum(w.shape[1] for w in weights) // 8
    for place in range(8):
        units = [w.shape[1] // 8 for w in weights]
        pieces = [w[:, place * u : (place + 1) * u] for w, u in zip(weights, units)]
        piece = pieces[0] if len(pieces) == 1 else jnp.concatenate(pieces, axis=1)
        lanes = slice(start + place // 2 * size, start + (place // 2 + 1) * size)
        pack[place % 2, :, :, lanes] = piece.reshape(4, -1, size)


def pack_hidden(pack, weights, first, last):
    size = 16 * (last - first)
    for order, weight in enumerate(weights):
        unit = weight.shape[1] // 8
        quarter = unit // 4
        for side in range(2):
            pieces = [
                weight[:, place * unit + q * quarter + first : place * unit + q * quarter + last]
                for place in range(side, 8, 2)
                for q in range(4)
            ]
            row = jnp.concatenate(pieces, axis=1)
            pack[side, :, :, order * size : (order + 1) * size] = row.reshape(4, -1, size).astype(pack.dtype)


def forward_layer_kernel(depth, cuts, *refs):
    (
        x, t, m, s, p3, p5, p7, codes, holes, sq, sk, sv, ck, cv, cq, wg, wu,
        o_wx, wt, o_wm, ws, o_w1, o_w2, o_w3, w4, w5,
        o_a1, o_qkv, o_ctx, lse, o_x1, o_a2, o_qc, o_ckv, o_ctxc, lsec, o_x2, o_a3, gains, keeps, keepc, bent,
        down_s, down_c, n6, n7, p8,
        p1, p2, p4, p6, bias, own, got, own2, got2, wx, wm, w1, w2, w3, a1, qkv, ctx, x1, a2, qc, ckv, ctxc, x2, a3, *sems
    ) = refs
    leaving = []
    pack_heads(p1, [sq, sk, sv], 0)
    pack_heads(p2, [ck, cv], 0)
    pack_heads(p2, [cq], ck.shape[1])

    def leave(*pairs):
        leaving.extend(wires.move(source, target) for source, target in pairs)

    f32, bf16 = jnp.float32, jnp.bfloat16
    spot = Spot(depth)
    wires = Wires(*sems)
    blocks = 4
    kvs = 4
    inner = 2 * kvs * HEAD_DIM

    def rows(block):
        return slice(block * QB, (block + 1) * QB)

    spot.greet()
    tokens = collect_tokens(spot, wires, x, wx)
    small = gather_small(spot, wires, s, ws)
    first = gather_columns(spot, wires, p1, w1)
    memory = collect_tokens(spot, wires, m, wm)
    second = gather_columns(spot, wires, p2, w2)
    outs = gather_rows(spot, wires, p3, w3)
    wide = gather_columns(spot, wires, p4, w4)
    down = gather_rows(spot, wires, p5, w5)
    top = collect_tokens(spot, wires, t, wt)
    wide_next = reach_columns(spot, wires, p6, n6)
    down_next = reach_rows(spot, wires, p7, n7)
    over = wires.take(2 * blocks)

    def advance(*programs):
        for program in programs:
            next(program)

    advance(small, first, small, tokens)
    pack_hidden(p4, [wg[...], wu[...]], 0, cuts[0])
    pack_hidden(p6, [wg[...], wu[...]], cuts[0], cuts[1])
    pack_hidden(p8, [wg[...], wu[...]], cuts[1], cuts[2])
    advance(small, small)

    def line(row):
        return jnp.concatenate([ws[z, c, 0, row : row + 1, :] for z in range(depth) for c in range(2)], axis=1)

    for row in range(3):
        gains[row : row + 1, :] = line(row)
    counts = ws[spot.z, spot.x, 0, 3:4, :]
    length = jnp.where(spot.y == 0, counts[:, 0:1], counts[:, 1:2])
    span = jnp.where(spot.y == 0, counts[:, 2:3], counts[:, 3:4])
    places = lax.broadcasted_iota(jnp.int32, (1, blocks * QB), 1).astype(f32)
    keeps[...] = jnp.where(places < length, 0.0, NEG)
    keepc[...] = jnp.where(places[:, : keepc.shape[1]] < span, 0.0, NEG)
    places = lax.broadcasted_iota(jnp.int32, (blocks * QB, 1), 0).astype(f32)
    down_s[...] = jnp.where(places < length, 0.0, NEG)
    down_c[...] = jnp.where(places[: down_c.shape[0]] < span, 0.0, NEG)
    table = jnp.concatenate(
        [
            ws[z, c, 0, 4:8, :] + ws[z, c, 1, 4:8, :] + ws[z, c, 2, 4:8, :] + ws[z, c, 3, 4:8, :]
            for z in range(depth)
            for c in range(2)
        ],
        axis=0,
    )
    table = jnp.where(spot.core == 0, table[:, :64], table[:, 64:]).astype(bf16)
    vectors = tn(table, codes[...])[:8] + holes[...]
    bent[...] = vectors[:, 4 * 2 * QB :]
    for kv in range(kvs):
        for member in range(2):
            for offset in range(4):
                head = 2 * kv + member
                bias[kv, member * QB : (member + 1) * QB, (3 - offset) * QB : (4 - offset) * QB] = spread_row(
                    vectors[head : head + 1, offset * 2 * QB : (offset + 1) * 2 * QB]
                ).astype(bf16)

    advance(first, outs, second, tokens, tokens)
    for block in range(blocks):
        a1[rows(block), :] = normed(wx[block].reshape(QB, -1).astype(f32), gains[0:1, :])
    advance(first, memory, first)
    leave((wx, o_wx), (w1, o_w1), (a1, o_a1))

    def attend_rows(block, queries, keys, stop, keep, mixed, sums, causal):
        for kv in range(kvs):
            base = 2 * kv * HEAD_DIM
            query = queries[rows(block), base : base + 2 * HEAD_DIM]
            shape = None
            if causal:
                base = 4 * kv * HEAD_DIM
                query = queries[rows(block), base : base + 2 * HEAD_DIM]
                base += 2 * HEAD_DIM
                shape = bias[kv, :, (3 - block) * QB : (3 - block) * QB + stop]
            out, level = attend_block(
                pair_rows(query, 0),
                keys[:stop, base : base + HEAD_DIM],
                keys[:stop, base + HEAD_DIM : base + 2 * HEAD_DIM],
                keep[:, :stop],
                shape,
            )
            mixed[rows(block), 2 * kv * HEAD_DIM : 2 * (kv + 1) * HEAD_DIM] = jnp.concatenate(
                [out[:QB], out[QB:]], axis=1
            ).astype(bf16)
            level = jnp.broadcast_to(level, (2 * QB, 128)).T
            sums[2 * kv : 2 * kv + 1, rows(block)] = level[:1, :QB]
            sums[2 * kv + 1 : 2 * kv + 2, rows(block)] = level[:1, QB:]

    weight = w1[...].reshape(-1, w1.shape[-1])
    for block in range(blocks):
        qkv[rows(block), :] = nn(a1[rows(block), :], weight).astype(bf16)
        attend_rows(block, qkv, qkv, (block + 1) * QB, keeps, ctx, lse, True)
        if block == 1:
            advance(outs, wide, down, second, memory)
        if block == 2:
            advance(outs)
    advance(outs, second, wide, down, wide_next, down_next)

    def pass_on(block, mine, theirs, value, weight, index):
        mine[rows(block), :] = nn(value[rows(block), :], weight).astype(bf16)
        wires.send(mine.at[rows(block)], theirs.at[rows(block)], spot.sibling(), over + index + block)

    def joined(block, mine, theirs, index):
        wires.arrive(theirs.at[rows(block)], spot.sibling(), over + index + block)
        return mine[rows(block), :].astype(f32) + theirs[rows(block), :].astype(f32)

    weight = w3[0].reshape(-1, w3.shape[-1])
    for block in range(blocks):
        pass_on(block, own, got, ctx, weight, 0)
    advance(memory, second, wide, down, top)
    leave((wm, o_wm), (w2, o_w2), (w3, o_w3), (qkv, o_qkv), (ctx, o_ctx))
    weight = w2[...].reshape(-1, w2.shape[-1])
    ckv[...] = nn(wm[...].reshape(-1, wm.shape[-1]), weight[:, :inner]).astype(bf16)
    for block in range(blocks):
        value = wx[block].reshape(QB, -1).astype(f32) + joined(block, own, got, 0)
        x1[rows(block), :] = value
        a2[rows(block), :] = normed(value, gains[1:2, :])
        qc[rows(block), :] = nn(a2[rows(block), :], weight[:, inner:]).astype(bf16)
    leave((x1, o_x1), (a2, o_a2), (qc, o_qc), (ckv, o_ckv))
    weight = w3[1].reshape(-1, w3.shape[-1])
    for block in range(blocks):
        attend_rows(block, qc, ckv, ckv.shape[0], keepc, ctxc, lsec, False)
        pass_on(block, own2, got2, ctxc, weight, blocks)
        if block == 0:
            advance(wide, down)
        if block == 2:
            advance(top)
    for block in range(blocks):
        value = x1[rows(block), :] + joined(block, own2, got2, blocks)
        x2[rows(block), :] = value
        a3[rows(block), :] = normed(value, gains[2:3, :])
        leave(
            (x2.at[rows(block)], o_x2.at[rows(block)]),
            (a3.at[rows(block)], o_a3.at[rows(block)]),
            (ctxc.at[rows(block)], o_ctxc.at[rows(block)]),
        )
    advance(wide_next, down_next, top)
    for program in (tokens, small, first, memory, second, outs, wide, down, top, wide_next, down_next):
        assert next(program, None) is None
    for copy in leaving:
        copy.wait()
    wires.close()


def forward_layer(depth, cuts, x, t, m, small, p3, p5, p7, codes, holes, *weights):
    bf16, f32 = jnp.bfloat16, jnp.float32
    shape = jax.ShapeDtypeStruct

    def whole_columns(pack):
        return shape((depth, 2) + pack.shape[1:], bf16)

    def whole_rows(pack):
        return shape((pack.shape[0], depth) + pack.shape[1:], bf16)

    def whole_tokens(parcel):
        return shape((4, 2) + parcel.shape[2:], bf16)

    rows = p3.shape[2]
    p1 = p2 = shape((2, 4, rows, weights[0].shape[1]), bf16)
    p4, p6, p8 = (
        shape((2, 4, rows, 32 * (stop - start)), bf16) for start, stop in zip((0,) + cuts[:2], cuts)
    )
    width = x.shape[-1]
    tokens = 8 * x.shape[2]
    span = 8 * m.shape[2]
    inner = p3.shape[0] * p3.shape[1] * p3.shape[2] * depth // 2
    heads = inner // HEAD_DIM
    hbm = pl.BlockSpec(memory_space=pl.ANY)
    vmem = pl.BlockSpec(memory_space=pltpu.VMEM)
    outs = [
        (whole_tokens(x), hbm),
        (whole_tokens(t), hbm),
        (whole_tokens(m), hbm),
        (shape((depth, 2, 4, 8, 128), f32), vmem),
        (whole_columns(p1), hbm),
        (whole_columns(p2), hbm),
        (whole_rows(p3), hbm),
        (whole_columns(p4), hbm),
        (whole_rows(p5), hbm),
        (shape((tokens, width), bf16), hbm),
        (shape((tokens, 2 * inner), bf16), hbm),
        (shape((tokens, inner), bf16), hbm),
        (shape((heads, tokens), f32), vmem),
        (shape((tokens, width), f32), hbm),
        (shape((tokens, width), bf16), hbm),
        (shape((tokens, inner), bf16), hbm),
        (shape((span, inner), bf16), hbm),
        (shape((tokens, inner), bf16), hbm),
        (shape((heads, tokens), f32), vmem),
        (shape((tokens, width), f32), hbm),
        (shape((tokens, width), bf16), hbm),
        (shape((8, width), f32), vmem),
        (shape((1, tokens), f32), vmem),
        (shape((1, span), f32), vmem),
        (shape((heads, 8 * QB), f32), vmem),
        (shape((tokens, 1), f32), vmem),
        (shape((span, 1), f32), vmem),
        (shape((depth, 2) + p6.shape[2:], bf16), hbm),
        (shape((depth,) + p7.shape[2:], bf16), hbm),
        (p8, vmem),
    ]
    packs = [pltpu.VMEM(pack.shape, bf16) for pack in (p1, p2, p4, p6)]
    swap = pltpu.VMEM((tokens, width), bf16)
    return pl.pallas_call(
        functools.partial(forward_layer_kernel, depth, cuts),
        in_specs=[hbm] * 7 + [vmem] * 10,
        out_specs=[spec for _, spec in outs],
        out_shape=[kind for kind, _ in outs],
        scratch_shapes=packs
        + [pltpu.VMEM((heads // 2, 2 * QB, 4 * QB), bf16), swap, swap, swap, swap]
        + [pltpu.VMEM(outs[i][0].shape, outs[i][0].dtype) for i in (0, 2, 4, 5, 6, 9, 10, 11, 13, 14, 15, 16, 17, 19, 20)]
        + wire_scratch(35 + 33 * depth, 40),
        compiler_params=pltpu.CompilerParams(
            collective_id=0, has_side_effects=True, vmem_limit_bytes=60 * 2**20
        ),
        cost_estimate=pl.CostEstimate(
            flops=16 * 10**9, bytes_accessed=128 * 2**20, transcendentals=10**7
        ),
    )(x, t, m, small, p3, p5, p7, codes, holes, *weights)


def pipeline(programs, ahead=2, stages=5):
    count = len(programs)
    for turn in range(count + stages):
        if turn == 0:
            for program in programs[:ahead]:
                next(program)
            yield
        for stage in range(stages - 1, 0, -1):
            index = turn - (stage - 1)
            if 0 <= index < count:
                next(programs[index])
        if turn + ahead < count:
            next(programs[turn + ahead])
        yield


def backward_tile(keys, values, query, grads, keep, bias, level, delta):
    scores = nt(keys, query) + keep
    if bias is not None:
        scores = scores + bias
    probs = jnp.exp(scores - level)
    return probs, probs * (nt(values, grads) - delta)


def row_sums(upstream, mixed):
    inner = (upstream.astype(jnp.float32) * mixed.astype(jnp.float32)).T
    return jnp.concatenate(
        [
            jnp.sum(inner[:HEAD_DIM], axis=0, keepdims=True),
            jnp.sum(inner[HEAD_DIM:], axis=0, keepdims=True),
        ],
        axis=1,
    )


def cross_backward_kernel(depth, *refs):
    g_early, g_down, g_gate, g_up, x2, x1, t_out, *far = refs[:17]
    (
        lsec, keep, gains,
        r_early, r_down, r_gate, r_up, q_gate, q_up, o_cout, o_cq, o_ckv, half, do_s, g_out, o_mem, terms, h_out,
        *rest
    ) = refs[17:]
    take = lambda n: [rest.pop(0) for _ in range(n)]
    near = take(10)
    u, top, qc, ckv, ctxc, a2, mem, w2, w3, ctx = near
    g_cout, g_cq, g_ckv = take(3)
    stage, e2, eb, do_c, dqc, dkv, dk_sum, dv_sum, got, own_c, got_c, own_m, got_m = take(13)
    buffers = [take(9) for _ in range(4)]
    f32, bf16 = jnp.float32, jnp.bfloat16
    spot = Spot(depth)
    wires = Wires(*rest)
    blocks = kvs = 4
    inner = 2 * kvs * HEAD_DIM

    def rows(block):
        return slice(block * QB, (block + 1) * QB)

    coming = [wires.move(source, target) for source, target in zip(far, near)]
    spot.greet()
    over = wires.take(2 * blocks + 4)
    for block in range(blocks):
        wires.send(far[0].at[rows(block)], got.at[rows(block)], spot.sibling(), over + block)
    home = deliver_tokens(spot, wires, t_out, h_out)
    programs = [
        scatter_sums(spot, wires, g_down, buffers[0], r_down, None),
        scatter_sums(spot, wires, g_gate, buffers[1], r_gate, q_gate),
        scatter_sums(spot, wires, g_up, buffers[2], r_up, q_up),
        scatter_sums(spot, wires, g_early, buffers[3], r_early, None),
    ]
    links = pipeline(programs)
    next(links)
    next(home)

    loads = {}

    def fetch(source, block, slot):
        loads[slot] = wires.move(source.at[rows(block)], stage.at[slot])

    def norm_back(block, slot, gain, upstream):
        loads[slot].wait()
        value = stage[slot]
        inverse = inverse_rms(value)
        scaled = upstream * gain
        mean = jnp.mean(value * scaled, axis=-1, keepdims=True)
        change = inverse * scaled - value * (inverse * inverse * inverse) * mean
        return change, jnp.sum(upstream * value * inverse, axis=0, keepdims=True)

    fetch(x2, 0, 0)
    for copy in coming:
        copy.wait()
    gain_terms = jnp.zeros((1, e2.shape[1]), f32)
    for block in range(blocks):
        if block + 1 < blocks:
            fetch(x2, block + 1, (block + 1) % 2)
        else:
            fetch(x1, 0, 0)
        wires.arrive(got.at[rows(block)], spot.sibling(), over + block)
        change, term = norm_back(
            block, block % 2, gains[2:3, :], u[rows(block), :].astype(f32) + got[rows(block), :].astype(f32)
        )
        gain_terms = gain_terms + term
        value = top[rows(block), :].astype(f32) + change
        e2[rows(block), :] = value
        eb[rows(block), :] = value.astype(bf16)
        do_c[rows(block), :] = nt(value.astype(bf16), w3[1].reshape(inner, -1)).astype(bf16)
    terms[0:1, :] = 0.5 * gain_terms
    next(links)

    span = ckv.shape[0]
    for kv in range(kvs):
        both = slice(2 * kv * HEAD_DIM, 2 * (kv + 1) * HEAD_DIM)
        base = 2 * kv * HEAD_DIM
        dk_sum[...] = jnp.zeros_like(dk_sum)
        dv_sum[...] = jnp.zeros_like(dv_sum)
        for block in range(blocks):
            query = pair_rows(qc[rows(block), :], kv)
            grads = pair_rows(do_c[rows(block), :], kv)
            delta = row_sums(do_c[rows(block), both], ctxc[rows(block), both])
            level = jnp.concatenate(
                [lsec[2 * kv : 2 * kv + 1, rows(block)], lsec[2 * kv + 1 : 2 * kv + 2, rows(block)]], axis=1
            )
            dq = jnp.zeros((2 * QB, HEAD_DIM), f32)
            for part in range(span // QB):
                keys = ckv[rows(part), base : base + HEAD_DIM]
                values = ckv[rows(part), base + HEAD_DIM : base + 2 * HEAD_DIM]
                probs, dscores = backward_tile(keys, values, query, grads, keep[rows(part)], None, level, delta)
                dscores = dscores.astype(bf16)
                dv_sum[rows(part)] += nn(probs.astype(bf16), grads)
                dk_sum[rows(part)] += nn(dscores, query)
                dq += tn(dscores, keys)
            dqc[rows(block), both] = jnp.concatenate([dq[:QB], dq[QB:]], axis=1).astype(bf16)
        dkv[:, base : base + HEAD_DIM] = dk_sum[...].astype(bf16)
        dkv[:, base + HEAD_DIM : base + 2 * HEAD_DIM] = dv_sum[...].astype(bf16)
        if kv:
            next(links)
        if kv == 3:
            next(home)

    weight = w2[...].reshape(-1, w2.shape[-1])
    for block in range(blocks):
        own_c[rows(block), :] = nt(dqc[rows(block), :], weight[:, inner:]).astype(bf16)
        wires.send(own_c.at[rows(block)], got_c.at[rows(block)], spot.sibling(), over + blocks + block)
    own_m[...] = nt(dkv[...], weight[:, :inner]).astype(bf16).reshape(own_m.shape)
    wires.send(own_m.at[:, 1 - spot.core], got_m, spot.sibling(), over + 2 * blocks)
    for block in range(blocks):
        g_cq[block] = tn(a2[:, rows(block)], dqc[...]).reshape(g_cq.shape[1:]).astype(bf16)
    next(links)
    for block in range(blocks):
        g_ckv[block] = tn(mem[:, rows(block)], dkv[...]).reshape(g_ckv.shape[1:]).astype(bf16)
    next(links)
    for block in range(2):
        g_cout[2 * block : 2 * block + 2] = (
            tn(ctxc[:, rows(block)], eb[...]).reshape((2,) + g_cout.shape[1:]).astype(bf16)
        )
    leaving = [wires.move(*pair) for pair in ((g_cq, o_cq), (g_ckv, o_ckv), (g_cout, o_cout))]
    gain_terms = jnp.zeros((1, e2.shape[1]), f32)
    for block in range(blocks):
        if block + 1 < blocks:
            fetch(x1, block + 1, (block + 1) % 2)
        wires.arrive(got_c.at[rows(block)], spot.sibling(), over + blocks + block)
        change, term = norm_back(
            block,
            block % 2,
            gains[1:2, :],
            own_c[rows(block), :].astype(f32) + got_c[rows(block), :].astype(f32),
        )
        gain_terms = gain_terms + term
        value = e2[rows(block), :] + change
        e2[rows(block), :] = value
        half[block] = e2[pl.ds(pl.multiple_of(block * QB + spot.core * (QB // 2), QB // 2), QB // 2), :]
        eb[rows(block), :] = value.astype(bf16)
        do_s[rows(block), :] = nt(value.astype(bf16), w3[0].reshape(inner, -1)).astype(bf16)
    terms[1:2, :] = 0.5 * gain_terms
    next(links)
    for block in range(inner // QB):
        g_out[rows(block), :] = tn(ctx[:, rows(block)], eb[...]).astype(bf16)
    wires.arrive(got_m, spot.sibling(), over + 2 * blocks)
    o_mem[...] = (own_m[:, spot.core].astype(f32) + got_m[...].astype(f32)).astype(bf16)
    for _ in links:
        pass
    for program in [home]:
        for _ in program:
            pass
    for copy in leaving:
        copy.wait()
    wires.close()


def cross_part(depth, *operands):
    bf16, f32 = jnp.bfloat16, jnp.float32
    shape = jax.ShapeDtypeStruct
    hbm = pl.BlockSpec(memory_space=pl.ANY)
    vmem = pl.BlockSpec(memory_space=pltpu.VMEM)
    g_early, g_down, g_gate, g_up, x2, _, t_out, _, _, _, ckv = operands[:11]
    far = operands[7:17]
    tokens, width = x2.shape
    span, inner = ckv.shape
    own = tokens // 8
    rows = g_gate.shape[4]
    outs = [
        (shape(g_early.shape[4:], f32), vmem),
        (shape(g_down.shape[4:], f32), vmem),
        (shape(g_gate.shape[4:], f32), vmem),
        (shape(g_up.shape[4:], f32), vmem),
        (shape(g_gate.shape[4:], bf16), vmem),
        (shape(g_up.shape[4:], bf16), vmem),
        (shape((depth, 1, 2, 2, rows, width), bf16), hbm),
        (shape((depth, 2, 2, 2, rows, inner), bf16), hbm),
        (shape((depth, 2, 2, 2, rows, inner), bf16), hbm),
        (shape((4, own, width), f32), vmem),
        (shape((tokens, inner), bf16), vmem),
        (shape((inner, width), bf16), vmem),
        (shape((4, span // 8, width), bf16), vmem),
        (shape((8, width), f32), vmem),
        (shape((2, 2) + t_out.shape[1:], bf16), hbm),
    ]
    scratch = [pltpu.VMEM(array.shape, bf16) for array in far]
    scratch += [pltpu.VMEM(outs[i][0].shape, bf16) for i in (6, 7, 8)]
    scratch += [
        pltpu.VMEM((2, QB, width), f32),
        pltpu.VMEM((tokens, width), f32),
        pltpu.VMEM((tokens, width), bf16),
        pltpu.VMEM((tokens, inner), bf16),
        pltpu.VMEM((tokens, inner), bf16),
        pltpu.VMEM((span, inner), bf16),
        pltpu.VMEM((span, HEAD_DIM), f32),
        pltpu.VMEM((span, HEAD_DIM), f32),
        pltpu.VMEM((tokens, width), bf16),
        pltpu.VMEM((tokens, width), bf16),
        pltpu.VMEM((tokens, width), bf16),
        pltpu.VMEM((4, 2, span // 8, width), bf16),
        pltpu.VMEM((4, span // 8, width), bf16),
    ]
    for grads in (g_down, g_gate, g_up, g_early):
        scratch += scatter_buffers(depth, grads.shape[1], *grads.shape[4:])
    number = 16 + 4 * (4 + depth)
    return pl.pallas_call(
        functools.partial(cross_backward_kernel, depth),
        in_specs=[hbm] * 17 + [vmem] * 3,
        out_specs=[spec for _, spec in outs],
        out_shape=[kind for kind, _ in outs],
        scratch_shapes=scratch + wire_scratch(number, 48),
        compiler_params=pltpu.CompilerParams(
            collective_id=1, has_side_effects=True, vmem_limit_bytes=60 * 2**20
        ),
        cost_estimate=pl.CostEstimate(
            flops=16 * 10**9, bytes_accessed=128 * 2**20, transcendentals=10**7
        ),
    )(*operands)


def sides(core, own, got):
    got = got.astype(jnp.float32)
    return jnp.where(core == 0, own, got), jnp.where(core == 0, got, own)


def spread_hidden(core, owns, gots):
    pairs = [sides(core, own[...], got[...]) for own, got in zip(owns, gots)]
    sizes = [own.shape[1] // 16 for own in owns]
    return jnp.concatenate(
        [
            pair[place % 2][:, (place // 2 * 4 + q) * size : (place // 2 * 4 + q + 1) * size]
            for place in range(8)
            for q in range(4)
            for pair, size in zip(pairs, sizes)
        ],
        axis=1,
    )


def spread_heads(core, own, got, targets, units):
    even, odd = sides(core, own[...], got[...])
    step = even.shape[1] // 4
    for group in range(4):
        start = group * step
        for target, unit in zip(targets, units):
            lanes = slice(start, start + unit)
            target[:, 2 * group * unit : 2 * (group + 1) * unit] = jnp.concatenate(
                [even[:, lanes], odd[:, lanes]], axis=1
            )
            start += unit


def self_backward_kernel(depth, *refs):
    (
        g_cout, g_cq, g_ckv, g_out, t_mem, f_do, f_qkv, f_ctx, f_a1, f_x, f_half, f_w1, lse, keep, bent, gains,
        terms, codes,
        r_cout, r_out, h_mem, h_in, packed, r_cq, r_ckv, r_qkv, q_cq, q_ckv, q_qkv,
        *rest
    ) = refs
    take = lambda n: [rest.pop(0) for _ in range(n)]
    bias, sums, dk_sum, dv_sum, dqkv, grad, mine, theirs, pieces, line, small, work = take(12)
    near = take(7)
    do_s, qkv, ctx, a1, x, half, w1 = near
    buffers = [take(9) for _ in range(4)]
    resident = [take(7) for _ in range(4)]
    f32, bf16 = jnp.float32, jnp.bfloat16
    spot = Spot(depth)
    wires = Wires(*rest)
    blocks = kvs = 4
    inner = 2 * kvs * HEAD_DIM

    def rows(block):
        return slice(block * QB, (block + 1) * QB)

    far = (f_do, f_qkv, f_ctx, f_a1, f_x, f_half, f_w1)
    coming = [wires.move(source, target) for source, target in zip(far, near)]
    spot.greet()
    over = wires.take(blocks)
    homes = [deliver_tokens(spot, wires, t_mem, h_mem)]
    early = pipeline(
        [
            scatter_sums(spot, wires, g_cout, buffers[0], r_cout, None),
            scatter_sums(spot, wires, g_cq, buffers[1], r_cq, q_cq),
            scatter_sums(spot, wires, g_ckv, buffers[2], r_ckv, q_ckv),
            scatter_sums(spot, wires, g_out, buffers[3], r_out, None),
        ]
    )
    late = []
    for kv in range(kvs):
        lanes = pl.ds(kv * QB, QB)
        late.append(
            scatter_sums(
                spot, wires, grad.at[kv], resident[kv], r_qkv.at[:, lanes], q_qkv.at[:, lanes], True
            )
        )
    next(early)
    for program in homes:
        next(program)
    for copy in coming:
        copy.wait()
    for kv in range(kvs):
        base = kv * 4 * HEAD_DIM
        both = slice(2 * kv * HEAD_DIM, 2 * (kv + 1) * HEAD_DIM)
        dk_sum[...] = jnp.zeros_like(dk_sum)
        dv_sum[...] = jnp.zeros_like(dv_sum)
        sums[...] = jnp.zeros_like(sums)
        for member in range(2):
            for offset in range(4):
                head = 2 * kv + member
                bias[offset, :, member * QB : (member + 1) * QB] = spread_row(
                    bent[head : head + 1, offset * 2 * QB : (offset + 1) * 2 * QB]
                )
        for block in range(blocks):
            query = pair_rows(qkv[rows(block), base : base + 2 * HEAD_DIM], 0)
            grads = pair_rows(do_s[rows(block), :], kv)
            delta = row_sums(do_s[rows(block), both], ctx[rows(block), both])
            level = jnp.concatenate(
                [lse[2 * kv : 2 * kv + 1, rows(block)], lse[2 * kv + 1 : 2 * kv + 2, rows(block)]], axis=1
            )
            dq = jnp.zeros((2 * QB, HEAD_DIM), f32)
            for part in range(block + 1):
                keys = qkv[rows(part), base + 2 * HEAD_DIM : base + 3 * HEAD_DIM]
                values = qkv[rows(part), base + 3 * HEAD_DIM : base + 4 * HEAD_DIM]
                probs, dscores = backward_tile(
                    keys, values, query, grads, keep[rows(part)], bias[block - part], level, delta
                )
                sums[block - part] += dscores
                dscores = dscores.astype(bf16)
                dv_sum[rows(part)] += nn(probs.astype(bf16), grads)
                dk_sum[rows(part)] += nn(dscores, query)
                dq += tn(dscores, keys)
            dqkv[rows(block), base : base + 2 * HEAD_DIM] = jnp.concatenate(
                [dq[:QB], dq[QB:]], axis=1
            ).astype(bf16)
            if block % 2 or kv == 0 and block:
                next(early, None)
            for earlier in range(kv):
                if block == 2:
                    next(late[earlier], None)
        dqkv[:, base + 2 * HEAD_DIM : base + 3 * HEAD_DIM] = dk_sum[...].astype(bf16)
        dqkv[:, base + 3 * HEAD_DIM : base + 4 * HEAD_DIM] = dv_sum[...].astype(bf16)
        for member in range(2):
            for offset in range(4):
                tile = fold(sums[offset, :, member * QB : (member + 1) * QB])
                row = tile[0:1]
                for r in range(1, 8):
                    row = row + pltpu.roll(tile[r : r + 1], 2 * QB - r, 1)
                head = 2 * kv + member
                line[head : head + 1, (offset + 1) * QB : (offset + 2) * QB] = row[:, :QB]
                if offset > 0:
                    line[head : head + 1, offset * QB : (offset + 1) * QB] += row[:, QB:]
        chunk = dqkv[:, base : base + 4 * HEAD_DIM]
        for block in range(blocks):
            grad[kv, block] = tn(a1[:, rows(block)], chunk).astype(bf16).reshape(grad.shape[2:])
        next(late[kv])
        if kv == 1:
            for program in homes:
                next(program)
    weight = w1[...].reshape(-1, w1.shape[-1])
    size = QB // 2

    def half_rows(block, core):
        return pl.ds(pl.multiple_of(block * QB + core * size, size), size)

    for block in range(blocks):
        mine[block] = nt(dqkv[half_rows(block, 1 - spot.core), :], weight).astype(bf16)
        wires.send(mine.at[block], theirs.at[block], spot.sibling(), over + block)
    for program in late:
        next(program, None)
    gain_terms = jnp.zeros((1, x.shape[-1]), f32)
    for block in range(blocks):
        upstream = nt(dqkv[half_rows(block, spot.core), :], weight).astype(bf16).astype(f32)
        wires.arrive(theirs.at[block], spot.sibling(), over + block)
        upstream = upstream + theirs[block].astype(f32)
        value = x[block, spot.core].astype(f32)
        inverse = inverse_rms(value)
        scaled = upstream * gains[0:1, :]
        mean = jnp.mean(value * scaled, axis=-1, keepdims=True)
        change = inverse * scaled - value * (inverse * inverse * inverse) * mean
        gain_terms = gain_terms + jnp.sum(upstream * value * inverse, axis=0, keepdims=True)
        pieces[block] = (half[block] + change).astype(bf16)
    homing = deliver_tokens(spot, wires, pieces, h_in)
    next(homing)
    shares = nt_exact(line[:, QB:], codes[...])
    small[...] = jnp.zeros_like(small)
    for r in range(8):
        lanes = slice(r * 128, (r + 1) * 128)
        small[r : r + 1, :] = terms[0:1, lanes]
        small[8 + r : 9 + r, :] = terms[1:2, lanes]
        small[16 + r : 17 + r, :] = gain_terms[:, lanes]
    zero = jnp.zeros_like(shares)
    small[24:32, :BUCKETS] = jnp.where(spot.core == 0, shares, zero)
    small[24:32, BUCKETS : 2 * BUCKETS] = jnp.where(spot.core == 1, shares, zero)
    summing = total_small(spot, wires, small, work, packed)
    next(summing)
    for _ in range(4):
        next(summing, None)
        for program in late:
            next(program, None)
    for program in late + homes + [homing, summing]:
        for _ in program:
            pass
    for _ in early:
        pass
    wires.close()


def nt_exact(left, right):
    return lax.dot_general(
        left, right, (((1,), (1,)), ((), ())), precision=HIGH, preferred_element_type=jnp.float32
    )


def self_part(depth, *operands):
    bf16, f32 = jnp.bfloat16, jnp.float32
    shape = jax.ShapeDtypeStruct
    hbm = pl.BlockSpec(memory_space=pl.ANY)
    vmem = pl.BlockSpec(memory_space=pltpu.VMEM)
    _, g_cq, _, g_out, t_mem, do_s = operands[:6]
    tokens, inner = do_s.shape
    width = g_out.shape[-1]
    rows = g_out.shape[4]
    own = tokens // 8
    outs = [
        (shape((rows, width), f32), vmem),
        (shape((rows, width), f32), vmem),
        (shape((2, 2) + t_mem.shape[1:], bf16), hbm),
        (shape((2, 2, own, width), bf16), hbm),
        (shape((32, 128), f32), vmem),
    ]
    for kind in (f32, bf16):
        outs += [(shape((rows, size), kind), vmem) for size in (inner, inner, 2 * inner)]
    scratch = [
        pltpu.VMEM((4, QB, 2 * QB), f32),
        pltpu.VMEM((4, QB, 2 * QB), f32),
        pltpu.VMEM((tokens, HEAD_DIM), f32),
        pltpu.VMEM((tokens, HEAD_DIM), f32),
        pltpu.VMEM((tokens, 2 * inner), bf16),
        pltpu.VMEM((4, depth, 2, 2, 2, rows, QB), bf16),
        pltpu.VMEM((4, own, width), bf16),
        pltpu.VMEM((4, own, width), bf16),
        pltpu.VMEM((4, own, width), bf16),
        pltpu.VMEM((8, 5 * QB), f32),
        pltpu.VMEM((32, 128), f32),
        pltpu.VMEM((6 + depth, 32, 128), f32),
    ]
    scratch += [pltpu.VMEM(array.shape, array.dtype) for array in operands[5:12]]
    for lanes, size in ((1, width), (2, inner), (2, inner), (1, width)):
        scratch += scatter_buffers(depth, lanes, rows, size)
    for _ in range(4):
        scratch += scatter_buffers(depth, 2, rows, QB)[2:]
    return pl.pallas_call(
        functools.partial(self_backward_kernel, depth),
        in_specs=[hbm] * 12 + [vmem] * 6,
        out_specs=[spec for _, spec in outs],
        out_shape=[kind for kind, _ in outs],
        scratch_shapes=scratch + wire_scratch(4 + 8 + 3 + depth + 8 * (4 + depth), 20),
        compiler_params=pltpu.CompilerParams(
            collective_id=2, has_side_effects=True, vmem_limit_bytes=60 * 2**20
        ),
        cost_estimate=pl.CostEstimate(
            flops=16 * 10**9, bytes_accessed=128 * 2**20, transcendentals=10**7
        ),
    )(*operands)


def finish_kernel(
    t_in, t_mem, t_out, packed, c_out, c_cout, r_cq, r_ckv, r_qkv, q_cq, q_ckv, q_qkv,
    rg0, rg1, rg2, ru0, ru1, ru2, qg0, qg1, qg2, qu0, qu1, qu2, rd0, rd1, rd2,
    d_in, d_mem, d_out, n_self, n_cross, n_ff, d_self, d_cross, d_q, d_k, d_v, d_cq, d_ck, d_cv, d_gate, d_up,
    d_down,
):
    core = lax.axis_index("dp") % 2
    d_in[...] = t_in[...].astype(jnp.float32)
    d_mem[...] = t_mem[...].astype(jnp.float32)
    d_out[...] = t_out[...]
    mine = lax.axis_index("dp") * 4 + lax.axis_index("seq")
    size = n_self.shape[1]
    per = 128 // size
    for index, target in ((2, n_self), (1, n_cross), (0, n_ff)):
        line = packed[pl.ds(8 * index + mine // per, 1), :]
        value = line[:, :size]
        for place in range(1, per):
            value = jnp.where(mine % per == place, line[:, place * size : (place + 1) * size], value)
        target[...] = value
    d_self[...] = c_out[...]
    d_cross[...] = c_cout[...]
    d_gate[...] = spread_hidden(core, (rg0, rg1, rg2), (qg0, qg1, qg2))
    d_up[...] = spread_hidden(core, (ru0, ru1, ru2), (qu0, qu1, qu2))
    low = 0
    for piece in (rd0, rd1, rd2):
        d_down[low : low + piece.shape[0], :] = piece[...]
        low += piece.shape[0]
    spread_heads(core, r_qkv, q_qkv, (d_q, d_k, d_v), (2 * HEAD_DIM, HEAD_DIM, HEAD_DIM))
    spread_heads(core, r_ckv, q_ckv, (d_ck, d_cv), (HEAD_DIM, HEAD_DIM))
    spread_heads(core, r_cq, q_cq, (d_cq,), (2 * HEAD_DIM,))


def finish(piece, *operands):
    f32 = jnp.float32
    shape = jax.ShapeDtypeStruct
    t_in, t_mem, t_out = operands[:3]
    rows, width = operands[4].shape
    inner = operands[6].shape[1]
    hidden = 2 * sum(tile.shape[1] for tile in operands[12:15])
    outs = [shape(t_in.shape, f32), shape(t_mem.shape, f32), shape(t_out.shape, t_out.dtype)]
    outs += [shape((1, piece), f32)] * 3 + [shape((rows, width), f32)] * 2
    for size in (2 * inner, inner, inner, 2 * inner, inner, inner, hidden, hidden):
        outs.append(shape((rows, size), f32))
    outs.append(shape((sum(down.shape[0] for down in operands[-3:]), width), f32))
    vmem = pl.BlockSpec(memory_space=pltpu.VMEM)
    return pl.pallas_call(
        finish_kernel,
        in_specs=[vmem] * len(operands),
        out_specs=[vmem] * len(outs),
        out_shape=outs,
        compiler_params=pltpu.CompilerParams(vmem_limit_bytes=60 * 2**20),
        cost_estimate=pl.CostEstimate(flops=0, bytes_accessed=16 * 2**20, transcendentals=0),
    )(*operands)


def feed_forward_kernel(depth, tiles, *refs):
    (
        a3_far, wt_far, keep, x2, gu0_far, d0_far, gu1p, d1p, gu2p, d2p,
        o_top, o_u, pieces, g_gate2, g_up2, g_down2, g5,
        r_gate0, r_up0, r_down0, r_gate1, r_up1, q_gate0, q_up0, q_gate1, q_up1,
        *rest
    ) = refs
    take = lambda n: [rest.pop(0) for _ in range(n)]
    gu1, d1, gu2, d2, mid, dgate, dup, g0, g1, g2, g3, g4, mine, theirs, second = take(15)
    a3, wt, gu0, d0, low_top, u = take(6)
    buffers = [take(7) for _ in range(5)]
    f32, bf16 = jnp.float32, jnp.bfloat16
    spot = Spot(depth)
    wires = Wires(*rest)
    blocks = 4
    starts = [sum(tiles[:i]) for i in range(3)]
    coming = [
        wires.move(source, target)
        for source, target in ((wt_far, wt), (a3_far, a3), (gu0_far, gu0), (d0_far, d0))
    ]

    def rows(block):
        return slice(block * QB, (block + 1) * QB)

    spot.greet()
    over = wires.take(blocks)
    middle = d1.shape[-1] // 2
    wide1 = share_plane(
        spot, wires, gu1p, lambda corner: gu1.at[:, :, corner], lambda view, side: view.at[:, side]
    )
    down1 = share_plane(
        spot,
        wires,
        d1p,
        lambda corner: d1.at[0, :, corner],
        lambda view, side: view.at[:, :, pl.ds(side * middle, middle)],
    )
    wide2 = gather_columns(spot, wires, gu2p, gu2)
    down2 = gather_rows(spot, wires, d2p, d2)
    sums = [
        scatter_sums(spot, wires, grads, scratch, total, got, True)
        for grads, scratch, total, got in (
            (g0, buffers[0], r_gate0, q_gate0),
            (g1, buffers[1], r_up0, q_up0),
            (g2, buffers[2], r_down0, None),
            (g3, buffers[3], r_gate1, q_gate1),
            (g4, buffers[4], r_up1, q_up1),
        )
    ]

    def advance(*programs):
        for program in programs:
            next(program, None)

    advance(wide1, down1, wide2, down2)
    halves = [
        wires.move(
            x2.at[pl.ds(pl.multiple_of(block * QB + spot.core * (QB // 2), QB // 2), QB // 2)], second.at[block]
        )
        for block in range(blocks)
    ]
    for copy in coming:
        copy.wait()
    for block in range(blocks):
        value = wt[block].reshape(QB, -1).astype(f32) * (keep[rows(block)] == 0.0).astype(f32)
        low_top[rows(block), :] = value.astype(bf16)
    coming = [wires.move(low_top, o_top)]
    wides = [gu0, gu1, gu2]
    downs = [d0, d1, d2]

    def wide_weight(tile, part):
        both = wides[tile]
        lanes = pl.ds(part * tiles[tile], tiles[tile])
        return both[:, :, :, :, lanes].reshape(-1, tiles[tile])

    def down_weight(tile):
        weight = downs[tile][0]
        if weight.shape[2] % 16:
            return weight.astype(f32).reshape(tiles[tile], -1).astype(bf16)
        return weight.reshape(tiles[tile], -1)

    def hidden(tile, block):
        lanes = slice(starts[tile], starts[tile] + tiles[tile])
        left = a3[rows(block), :]
        gate = nn(left, wide_weight(tile, 0))
        upward = nn(left, wide_weight(tile, 1))
        back = nt(low_top[rows(block), :], down_weight(tile))
        bend = jnp.tanh(GELU_SCALE * (gate + GELU_CUBE * gate * gate * gate))
        share = 0.5 * (1.0 + bend)
        active = gate * share
        slope = share + 0.5 * gate * (1.0 - bend * bend) * (
            GELU_SCALE * (1.0 + 3.0 * GELU_CUBE * gate * gate)
        )
        mid[rows(block), lanes] = (active * upward).astype(bf16)
        dgate[rows(block), lanes] = (back * upward * slope).astype(bf16)
        dup[rows(block), lanes] = (back * active).astype(bf16)

    def wide_grads(tile, source, target):
        lanes = slice(starts[tile], starts[tile] + tiles[tile])
        right = source[:, lanes]
        for block in range(blocks):
            target[block] = tn(a3[:, rows(block)], right).reshape(target.shape[1:]).astype(bf16)

    def down_grads(tile, target):
        lanes = slice(starts[tile], starts[tile] + tiles[tile])
        target[...] = tn(mid[:, lanes], low_top[...]).reshape(target.shape).astype(bf16)

    hidden(0, 0)
    hidden(0, 1)
    hidden(0, 2)
    hidden(0, 3)
    wide_grads(0, dgate, g0)
    advance(sums[0])
    wide_grads(0, dup, g1)
    advance(wide1, down1, wide2, down2)
    down_grads(0, g2)
    advance(wide1, down1, sums[1])
    for block in range(blocks):
        hidden(1, block)
        if block == 1:
            advance(sums[0], wide2, down2, sums[2])
    advance(sums[1])
    wide_grads(1, dgate, g3)
    advance(sums[0], wide2, down2, sums[3])
    wide_grads(1, dup, g4)
    advance(sums[2], sums[1])
    down_grads(1, g5)
    advance(sums[0], sums[4])
    for block in range(blocks):
        hidden(2, block)
        if block == 1:
            advance(sums[3], sums[2])
        if block == 3:
            advance(sums[1], sums[0])
    wide_grads(2, dgate, g_gate2)
    wide_grads(2, dup, g_up2)
    advance(sums[4], sums[3], sums[2])
    down_grads(2, g_down2)

    def half_rows(block, core):
        return pl.ds(pl.multiple_of(block * QB + core * (QB // 2), QB // 2), QB // 2)

    def contribution(block, core):
        total = None
        for tile in range(3):
            lanes = slice(starts[tile], starts[tile] + tiles[tile])
            term = nn(mid[half_rows(block, core), lanes], down_weight(tile))
            total = term if total is None else total + term
        return total.astype(bf16)

    for block in range(blocks):
        mine[block] = contribution(block, 1 - spot.core)
        wires.send(mine.at[block], theirs.at[block], spot.sibling(), over + block)
    for block in range(blocks):
        total = None
        for tile in range(3):
            lanes = slice(starts[tile], starts[tile] + tiles[tile])
            term = nt(dgate[rows(block), lanes], wide_weight(tile, 0))
            term = term + nt(dup[rows(block), lanes], wide_weight(tile, 1))
            total = term if total is None else total + term
        u[rows(block), :] = total.astype(bf16)
        coming.append(wires.move(u.at[rows(block)], o_u.at[rows(block)]))
        if block == 1:
            advance(sums[4], sums[3])
    advance(sums[4])
    for block in range(blocks):
        value = contribution(block, spot.core).astype(f32)
        wires.arrive(theirs.at[block], spot.sibling(), over + block)
        value = value + theirs[block].astype(f32)
        halves[block].wait()
        kept = (keep[half_rows(block, spot.core), :] == 0.0).astype(f32)
        pieces[block] = ((second[block] + value) * kept).astype(bf16)
    for program in sums + [wide1, down1, wide2, down2]:
        for _ in program:
            pass
    for copy in coming:
        copy.wait()
    wires.close()


def feed_forward(depth, tiles, *operands):
    bf16, f32 = jnp.bfloat16, jnp.float32
    shape = jax.ShapeDtypeStruct
    hbm = pl.BlockSpec(memory_space=pl.ANY)
    vmem = pl.BlockSpec(memory_space=pltpu.VMEM)
    a3, _, _, _, gu0, d0, gu1p, d1p, gu2p, d2p = operands
    tokens, width = a3.shape
    hidden_width = sum(tiles)
    rows = [d1p.shape[1], d1p.shape[1], d2p.shape[2]]
    own = tokens // 8
    wide = gu2p.shape[2]

    def wide_grad(tile):
        return (depth, 2, 2, 2, wide, tiles[tile])

    def down_grad(tile):
        return (depth, 1, 2, 2, rows[tile], width)

    outs = [
        (shape((tokens, width), bf16), hbm),
        (shape((tokens, width), bf16), hbm),
        (shape((4, own, width), bf16), vmem),
        (shape(wide_grad(2), bf16), vmem),
        (shape(wide_grad(2), bf16), vmem),
        (shape(down_grad(2), bf16), vmem),
        (shape(down_grad(1), bf16), vmem),
    ]
    for tile in range(2):
        outs += [(shape((wide, tiles[tile]), f32), vmem)] * 2
        if tile == 0:
            outs.append((shape((rows[tile], width), f32), vmem))
    for tile in range(2):
        outs += [(shape((wide, tiles[tile]), bf16), vmem)] * 2
    scratch = [
        pltpu.VMEM(gu0.shape, bf16),
        pltpu.VMEM(d0.shape, bf16),
        pltpu.VMEM((depth, 2) + gu2p.shape[1:], bf16),
        pltpu.VMEM((1, depth) + d2p.shape[1:], bf16),
    ]
    scratch += [pltpu.VMEM((tokens, hidden_width), bf16)] * 3
    for tile in range(2):
        scratch += [pltpu.VMEM(wide_grad(tile), bf16)] * 2
        if tile == 0:
            scratch.append(pltpu.VMEM(down_grad(tile), bf16))
    scratch += [
        pltpu.VMEM((4, own, width), bf16),
        pltpu.VMEM((4, own, width), bf16),
        pltpu.VMEM((4, own, width), f32),
        pltpu.VMEM((tokens, width), bf16),
        pltpu.VMEM((4, 2, own, width), bf16),
        pltpu.VMEM(gu0.shape, bf16),
        pltpu.VMEM(d0.shape, bf16),
        pltpu.VMEM((tokens, width), bf16),
        pltpu.VMEM((tokens, width), bf16),
    ]
    for tile in range(2):
        for _ in range(2):
            scratch += scatter_buffers(depth, 2, wide, tiles[tile])[2:]
        if tile == 0:
            scratch += scatter_buffers(depth, 1, rows[tile], width)[2:]
    return pl.pallas_call(
        functools.partial(feed_forward_kernel, depth, tiles),
        in_specs=[hbm, hbm, vmem] + [hbm] * 7,
        out_specs=[spec for _, spec in outs],
        out_shape=[kind for kind, _ in outs],
        scratch_shapes=scratch + wire_scratch(4 + 22 * depth + 6 * (4 + depth), 24),
        compiler_params=pltpu.CompilerParams(
            collective_id=3, has_side_effects=True, vmem_limit_bytes=60 * 2**20
        ),
        cost_estimate=pl.CostEstimate(
            flops=27 * 10**9, bytes_accessed=64 * 2**20, transcendentals=10**7
        ),
    )(*operands)


def per_chip(
    layer_input,
    memory,
    target_lengths,
    memory_lengths,
    buckets,
    norm_self,
    self_q,
    self_k,
    self_v,
    self_out,
    rel_bias,
    norm_cross,
    cross_q,
    cross_k,
    cross_v,
    cross_out,
    norm_ff,
    ff_gate,
    ff_up,
    ff_down,
    cotangent,
):
    bf16, f32 = jnp.bfloat16, jnp.float32
    depth = lax.axis_size("dp") // 2
    spot = Spot(depth)
    core = spot.core
    width = layer_input.shape[3]
    local = layer_input.shape[2]
    near = memory.shape[2]
    shard = norm_self.shape[0]

    cuts = [(0, 32), (32, 64), (64, ff_down.shape[0] // 4)]
    tiles = tuple(16 * (stop - start) for start, stop in cuts)
    down_packs = [ff_down.reshape(4, -1, width)[None, :, start:stop] for start, stop in cuts]

    heads = jnp.arange(4)
    spots = (heads // 2) * 64 + 2 * spot.corner + heads % 2
    placed = jnp.sum(
        jnp.where(jnp.arange(128)[None, None, :] == spots[None, :, None], rel_bias[:, :, None].astype(f32), 0.0),
        axis=1,
    )
    lengths = jnp.concatenate([target_lengths, memory_lengths]).reshape(1, 4).astype(f32)
    small = jnp.concatenate(
        [
            jnp.stack([norm_self, norm_cross, norm_ff]).astype(f32),
            jnp.pad(lengths, ((0, 0), (0, 124))),
            placed,
        ]
    )
    padded = jnp.concatenate([jnp.full((1, QB), -1, jnp.int32), buckets[None, :]], axis=1)
    vectors = row_pieces(padded)
    vectors = jnp.concatenate([jnp.roll(vectors[..., ::-1], 1, axis=-1), vectors], axis=1).reshape(1, -1)
    codes = (vectors == jnp.arange(BUCKETS, dtype=jnp.int32)[:, None]).astype(bf16)
    holes = jnp.where(vectors < 0, NEG, 0.0).astype(f32)
    onehot = (buckets[:, None] == jnp.arange(BUCKETS, dtype=jnp.int32)[None, :]).astype(f32)
    (
        inputs, upstream, encoded, _, w_qkv, w_cross, w_outs, w_gu, w_down,
        normed_self, qkv, context, self_sums, first, normed_cross, cross_queries, far_kv, cross_context,
        cross_sums, second, normed_ff, gains, _, _, bent, keep_self, keep_cross, near_wide, near_down, wide_pack,
    ) = forward_layer(
        depth,
        tuple(stop for _, stop in cuts),
        layer_input.reshape(2, 2, local // 2, width),
        cotangent.reshape(2, 2, local // 2, width),
        memory.reshape(2, 2, near // 2, width),
        small,
        jnp.stack([self_out, cross_out]).reshape(2, 4, -1, width),
        down_packs[0],
        down_packs[1],
        codes,
        holes,
        self_q,
        self_k,
        self_v,
        cross_k,
        cross_v,
        cross_q,
        ff_gate,
        ff_up,
    )
    encoded = encoded.reshape(-1, width)
    (
        top_low, changed, output, g_gate, g_up, g_down, g_early,
        r_gate0, r_up0, r_down0, r_gate1, r_up1, q_gate0, q_up0, q_gate1, q_up1,
    ) = feed_forward(
        depth, tiles, normed_ff, upstream, keep_self, second, w_gu, w_down,
        near_wide, near_down, wide_pack, down_packs[2],
    )

    (
        r_down1, r_down2, r_gate2, r_up2, q_gate2, q_up2, g_cout, g_cq, g_ckv, half, self_up, g_out, memory_grad, terms,
        output,
    ) = cross_part(
        depth, g_early, g_down, g_gate, g_up, second, first, output, changed, top_low, cross_queries, far_kv, cross_context,
        normed_cross, encoded, w_cross, w_outs, context, cross_sums, keep_cross, gains,
    )
    r_cout, r_out, memory_grad, input_grad, packed, r_cq, r_ckv, r_qkv, q_cq, q_ckv, q_qkv = self_part(
        depth, g_cout, g_cq, g_ckv, g_out.reshape(depth, 1, 2, 2, -1, width), memory_grad, self_up, qkv, context,
        normed_self, inputs, half, w_qkv, self_sums, keep_self, bent, gains, terms, onehot.T,
    )
    (
        input_grad, memory_grad, output, n_self, n_cross, n_ff, r_out, r_cout, d_q, d_k, d_v, d_cq, d_ck, d_cv,
        d_gate, d_up, d_down,
    ) = finish(
        width // (depth * 8),
        input_grad, memory_grad, output, packed, r_out, r_cout, r_cq, r_ckv, r_qkv, q_cq, q_ckv, q_qkv,
        r_gate0, r_gate1, r_gate2, r_up0, r_up1, r_up2, q_gate0, q_gate1, q_gate2, q_up0, q_up1, q_up2,
        r_down0, r_down1, r_down2,
    )
    bias_grad = packed[24:, :64].reshape(4, 2, 2, BUCKETS)
    bias_grad = jnp.transpose(bias_grad, (3, 0, 2, 1)).reshape(BUCKETS, HEADS)
    bias_grad = lax.dynamic_slice(
        bias_grad, (lax.axis_index("dp") * rel_bias.shape[0], spot.corner * rel_bias.shape[1]), rel_bias.shape
    )

    return (
        output.reshape(layer_input.shape),
        input_grad.reshape(layer_input.shape),
        memory_grad.reshape(memory.shape),
        n_self.reshape(-1),
        d_q,
        d_k,
        d_v,
        r_out,
        bias_grad,
        n_cross.reshape(-1),
        d_cq,
        d_ck,
        d_cv,
        r_cout,
        n_ff.reshape(-1),
        d_gate,
        d_up,
        d_down,
    )


def solution(mesh):
    placed = (
        P(None, "dp", "seq", None),
        P(None, "dp", "seq", None),
        P(None, "dp"),
        P(None, "dp"),
        P(),
        P("dp"),
        P("dp", None),
        P("dp", None),
        P("dp", None),
        P("dp", None),
        P("dp", "seq"),
        P("dp"),
        P("dp", None),
        P("dp", None),
        P("dp", None),
        P("dp", None),
        P("dp"),
        P("dp", None),
        P("dp", None),
        P("dp", None),
        P(None, "dp", "seq", None),
    )
    chips = mesh.shape["seq"] == 4 and mesh.shape["dp"] == HEADS // 2
    return jax.shard_map(
        per_chip if chips else per_device,
        mesh=mesh,
        in_specs=placed,
        out_specs=(
            P(None, "dp", "seq", None),
            P(None, "dp", "seq", None),
            P(None, "dp", "seq", None),
            P(("dp", "seq")),
            P(("dp", "seq"), None),
            P(("dp", "seq"), None),
            P(("dp", "seq"), None),
            P(("dp", "seq"), None),
            P("dp", "seq"),
            P(("dp", "seq")),
            P(("dp", "seq"), None),
            P(("dp", "seq"), None),
            P(("dp", "seq"), None),
            P(("dp", "seq"), None),
            P(("dp", "seq")),
            P(("dp", "seq"), None),
            P(("dp", "seq"), None),
            P(("dp", "seq"), None),
        ),
        check_vma=False,
    )
```

```python
import functools

import jax
import jax.numpy as jnp
from jax import lax
from jax.experimental import pallas as pl
from jax.experimental.pallas import tpu as pltpu
from jax.sharding import PartitionSpec as P

HEADS = 16
HEAD_DIM = 64
BUCKETS = 32
KV_HEADS = 8
TGT = 1024
MEM = 512
QB = 256
GELU_SCALE = 0.7978845608
GELU_CUBE = 0.044715


EPS = 1e-06
NEG = -1e30
HIGH = lax.Precision.HIGHEST


def shortened(shard):
    return jax.tree.map(lambda a: a.astype(jnp.bfloat16) if a.dtype == jnp.float32 else a, shard)


def rms_norm(value, gain):
    return value * lax.rsqrt(jnp.mean(value * value, axis=-1, keepdims=True) + EPS) * gain


def gated(gate, upward):
    return jax.nn.gelu(gate, approximate=True) * upward


def project(left, right):
    return jnp.dot(left, right, preferred_element_type=jnp.float32)


def project_back(grad, weight):
    return lax.dot_general(
        grad, weight, (((1,), (1,)), ((), ())), preferred_element_type=jnp.float32
    )


def weight_grad(left, right):
    return lax.dot_general(
        left, right, (((0,), (0,)), ((), ())), preferred_element_type=jnp.float32
    )


def split_heads(values, group):
    return values.reshape(values.shape[:2] + (-1, group, HEAD_DIM))


def split_shared(values):
    return values.reshape(values.shape[:2] + (-1, HEAD_DIM))


def causal_masks(table, length, group):

    def masks(start, block):
        stop = start + block
        rows = start + jnp.arange(block, dtype=jnp.int32)
        columns = jnp.arange(stop, dtype=jnp.int32)
        distance = rows[:, None] - columns[None, :]
        keep = (distance >= 0) & (columns[None, :] < length)
        extra = jnp.take(table, jnp.maximum(distance, 0), axis=1)
        return (extra.reshape((-1, group, block, stop)), keep, stop)

    return masks


def memory_masks(length, width):

    def masks(start, block):
        keep = jnp.broadcast_to(
            jnp.arange(width, dtype=jnp.int32)[None, :] < length, (block, width)
        )
        return (None, keep, width)

    return masks


def diagonal_sums(grads, block, stop):
    leading = grads.shape[:2]
    flipped = jnp.pad(grads[..., ::-1], ((0, 0), (0, 0), (0, 0), (0, block)))
    skewed = flipped.reshape(leading + (block * (stop + block),))[..., : block * (stop + block - 1)]
    skewed = skewed.reshape(leading + (block, stop + block - 1))
    return jnp.sum(skewed, axis=2)[..., block - 1 :]


def attend_forward(queries, keys, values, masks):
    block = min(512, queries.shape[0])
    outputs = []
    totals = []
    for index in range(queries.shape[0] // block):
        start = index * block
        extra, keep, stop = masks(start, block)
        rows = queries[start : start + block]
        scores = jnp.einsum("rkgd,skd->kgrs", rows, keys[:stop], preferred_element_type=jnp.float32)
        if extra is not None:
            scores = scores + extra
        scores = jnp.where(keep, scores, NEG)
        peak = jnp.max(scores, axis=-1, keepdims=True)
        weights = jnp.where(keep, jnp.exp(scores - peak), 0.0)
        total = jnp.sum(weights, axis=-1, keepdims=True)
        probs = (weights / total).astype(jnp.bfloat16)
        mixed = jnp.einsum(
            "kgrs,skd->rkgd", probs, values[:stop], preferred_element_type=jnp.float32
        )
        outputs.append(mixed.astype(jnp.bfloat16))
        totals.append(peak + jnp.log(total))
    return (jnp.concatenate(outputs, 0), jnp.concatenate(totals, 2))


def attend_backward(queries, keys, values, sums, grads, masks):
    block = min(512, queries.shape[0])
    key_grads = jnp.zeros(keys.shape, jnp.float32)
    value_grads = jnp.zeros(values.shape, jnp.float32)
    diagonal = jnp.zeros(sums.shape[:3], jnp.float32)
    query_grads = []
    for index in range(queries.shape[0] // block):
        start = index * block
        extra, keep, stop = masks(start, block)
        rows = queries[start : start + block]
        grad_rows = grads[start : start + block]
        scores = jnp.einsum("rkgd,skd->kgrs", rows, keys[:stop], preferred_element_type=jnp.float32)
        if extra is not None:
            scores = scores + extra
        scores = jnp.where(keep, scores, NEG)
        probs = jnp.where(keep, jnp.exp(scores - sums[:, :, start : start + block]), 0.0)
        value_grads = value_grads.at[:stop].add(
            jnp.einsum(
                "kgrs,rkgd->skd",
                probs.astype(jnp.bfloat16),
                grad_rows,
                preferred_element_type=jnp.float32,
            )
        )
        dprobs = jnp.einsum(
            "rkgd,skd->kgrs", grad_rows, values[:stop], preferred_element_type=jnp.float32
        )
        delta = jnp.sum(probs * dprobs, axis=-1, keepdims=True)
        dscores = (probs * (dprobs - delta)).astype(jnp.bfloat16)
        query_grads.append(
            jnp.einsum(
                "kgrs,skd->rkgd", dscores, keys[:stop], preferred_element_type=jnp.float32
            ).astype(jnp.bfloat16)
        )
        key_grads = key_grads.at[:stop].add(
            jnp.einsum("kgrs,rkgd->skd", dscores, rows, preferred_element_type=jnp.float32)
        )
        if extra is not None:
            diagonal = diagonal.at[:, :, :stop].add(
                diagonal_sums(dscores.astype(jnp.float32), block, stop)
            )
    return (
        jnp.concatenate(query_grads, 0),
        key_grads.astype(jnp.bfloat16),
        value_grads.astype(jnp.bfloat16),
        diagonal,
    )


def self_forward(queries, keys, values, length, table):
    return attend_forward(queries, keys, values, causal_masks(table, length, queries.shape[2]))


def self_backward(queries, keys, values, sums, grads, length, table):
    return attend_backward(
        queries, keys, values, sums, grads, causal_masks(table, length, queries.shape[2])
    )


def cross_forward(queries, keys, values, length):
    return attend_forward(queries, keys, values, memory_masks(length, keys.shape[0]))


def cross_backward(queries, keys, values, sums, grads, length):
    return attend_backward(queries, keys, values, sums, grads, memory_masks(length, keys.shape[0]))


def to_tokens(values):
    return lax.all_to_all(shortened(values), "seq", split_axis=1, concat_axis=2, tiled=True).astype(
        values.dtype
    )


def to_heads(grads):
    return lax.all_to_all(grads, "seq", split_axis=2, concat_axis=1, tiled=True)


def per_device(
    layer_input,
    memory,
    target_lengths,
    memory_lengths,
    buckets,
    norm_self,
    self_q,
    self_k,
    self_v,
    self_out,
    rel_bias,
    norm_cross,
    cross_q,
    cross_k,
    cross_v,
    cross_out,
    norm_ff,
    ff_gate,
    ff_up,
    ff_down,
    cotangent,
):
    micro_count, batch_rows, local_tokens, model_width = layer_input.shape
    memory_tokens = memory.shape[2]
    group = HEADS // KV_HEADS
    replicas = lax.axis_size("dp")
    shards = (
        norm_self,
        self_q,
        self_k,
        self_v,
        self_out,
        rel_bias,
        norm_cross,
        cross_q,
        cross_k,
        cross_v,
        cross_out,
        norm_ff,
        ff_gate,
        ff_up,
        ff_down,
    )
    totals = [
        jnp.zeros((piece.shape[0] * replicas,) + piece.shape[1:], jnp.float32) for piece in shards
    ]
    onehot = (buckets[:, None] == jnp.arange(BUCKETS, dtype=jnp.int32)[None, :]).astype(jnp.float32)
    places = lax.axis_index("seq") * local_tokens + jnp.arange(local_tokens, dtype=jnp.int32)
    diagonal = jnp.zeros((rel_bias.shape[1] // group, group, TGT), jnp.float32)
    outputs = []
    input_grads = []
    memory_grads = []
    for micro_step in range(micro_count):
        gathered = (
            lax.all_gather(norm_self, "dp", axis=0, tiled=True),
            lax.all_gather(self_q, "dp", axis=0, tiled=True),
            lax.all_gather(self_k, "dp", axis=0, tiled=True),
            lax.all_gather(self_v, "dp", axis=0, tiled=True),
            lax.all_gather(self_out, "dp", axis=0, tiled=True),
            lax.all_gather(rel_bias, "dp", axis=0, tiled=True),
            lax.all_gather(norm_cross, "dp", axis=0, tiled=True),
            lax.all_gather(cross_q, "dp", axis=0, tiled=True),
            lax.all_gather(cross_k, "dp", axis=0, tiled=True),
            lax.all_gather(cross_v, "dp", axis=0, tiled=True),
            lax.all_gather(cross_out, "dp", axis=0, tiled=True),
            lax.all_gather(norm_ff, "dp", axis=0, tiled=True),
            lax.all_gather(ff_gate, "dp", axis=0, tiled=True),
            lax.all_gather(ff_up, "dp", axis=0, tiled=True),
            lax.all_gather(ff_down, "dp", axis=0, tiled=True),
        )
        (
            gain_self,
            query_self,
            key_self,
            value_self,
            output_self,
            bias_whole,
            gain_cross,
            query_cross,
            key_cross,
            value_cross,
            output_cross,
            gain_ff,
            gate_weight,
            up_weight,
            down_weight,
        ) = gathered
        gain_self = gain_self.astype(jnp.float32)
        gain_cross = gain_cross.astype(jnp.float32)
        gain_ff = gain_ff.astype(jnp.float32)
        table = lax.dot_general(
            bias_whole.astype(jnp.float32), onehot, (((0,), (1,)), ((), ())), precision=HIGH
        )
        lengths = target_lengths[micro_step]
        spans = memory_lengths[micro_step]
        valid = (places[None, :] < lengths[:, None]).astype(jnp.float32).reshape(-1, 1)
        hidden = layer_input[micro_step].reshape(-1, model_width).astype(jnp.float32)
        normed_self = rms_norm(hidden, gain_self).astype(jnp.bfloat16)
        queries = (
            project(normed_self, query_self)
            .astype(jnp.bfloat16)
            .reshape(batch_rows, local_tokens, -1)
        )
        keys = (
            project(normed_self, key_self)
            .astype(jnp.bfloat16)
            .reshape(batch_rows, local_tokens, -1)
        )
        values = (
            project(normed_self, value_self)
            .astype(jnp.bfloat16)
            .reshape(batch_rows, local_tokens, -1)
        )
        encoded = memory[micro_step].reshape(-1, model_width)
        memory_keys = (
            project(encoded, key_cross).astype(jnp.bfloat16).reshape(batch_rows, memory_tokens, -1)
        )
        memory_values = (
            project(encoded, value_cross)
            .astype(jnp.bfloat16)
            .reshape(batch_rows, memory_tokens, -1)
        )
        head_queries, head_keys, head_values, far_keys, far_values = (
            lax.all_to_all(queries, "seq", split_axis=2, concat_axis=1, tiled=True),
            lax.all_to_all(keys, "seq", split_axis=2, concat_axis=1, tiled=True),
            lax.all_to_all(values, "seq", split_axis=2, concat_axis=1, tiled=True),
            lax.all_to_all(memory_keys, "seq", split_axis=2, concat_axis=1, tiled=True),
            lax.all_to_all(memory_values, "seq", split_axis=2, concat_axis=1, tiled=True),
        )
        self_queries = split_heads(head_queries, group)
        self_keys = split_shared(head_keys)
        self_values = split_shared(head_values)
        far_keys = split_shared(far_keys)
        far_values = split_shared(far_values)
        attended, self_sums = jax.vmap(self_forward, in_axes=(0, 0, 0, 0, None))(
            self_queries, self_keys, self_values, lengths, table
        )
        context = to_tokens(attended.reshape(batch_rows, TGT, -1)).reshape(
            batch_rows * local_tokens, -1
        )
        first = hidden + project(context, output_self)
        normed_cross = rms_norm(first, gain_cross).astype(jnp.bfloat16)
        cross_queries = (
            project(normed_cross, query_cross)
            .astype(jnp.bfloat16)
            .reshape(batch_rows, local_tokens, -1)
        )
        cross_heads = split_heads(
            lax.all_to_all(cross_queries, "seq", split_axis=2, concat_axis=1, tiled=True), group
        )
        cross_attended, cross_sums = jax.vmap(cross_forward)(
            cross_heads, far_keys, far_values, spans
        )
        cross_context = to_tokens(cross_attended.reshape(batch_rows, TGT, -1)).reshape(
            batch_rows * local_tokens, -1
        )
        second = first + project(cross_context, output_cross)
        normed_ff = rms_norm(second, gain_ff).astype(jnp.bfloat16)
        gate = project(normed_ff, gate_weight)
        upward = project(normed_ff, up_weight)
        middle = gated(gate, upward).astype(jnp.bfloat16)
        third = second + project(middle, down_weight)
        outputs.append(
            (third * valid).astype(jnp.bfloat16).reshape(batch_rows, local_tokens, model_width)
        )
        upstream = cotangent[micro_step].reshape(-1, model_width).astype(jnp.float32) * valid
        down_grad = upstream.astype(jnp.bfloat16)
        totals[14] = totals[14] + weight_grad(middle, down_grad)
        _, pullback = jax.vjp(gated, gate, upward)
        gate_grad, upward_grad = pullback(project_back(down_grad, down_weight))
        gate_grad = gate_grad.astype(jnp.bfloat16)
        upward_grad = upward_grad.astype(jnp.bfloat16)
        totals[12] = totals[12] + weight_grad(normed_ff, gate_grad)
        totals[13] = totals[13] + weight_grad(normed_ff, upward_grad)
        _, pullback = jax.vjp(rms_norm, second, gain_ff)
        second_grad, gain_grad = pullback(
            project_back(gate_grad, gate_weight) + project_back(upward_grad, up_weight)
        )
        totals[11] = totals[11] + gain_grad
        second_grad = second_grad + upstream
        cross_grad = second_grad.astype(jnp.bfloat16)
        totals[10] = totals[10] + weight_grad(cross_context, cross_grad)
        context_grad = (
            project_back(cross_grad, output_cross)
            .astype(jnp.bfloat16)
            .reshape(batch_rows, local_tokens, -1)
        )
        cross_query_grad, far_key_grad, far_value_grad, _ = jax.vmap(cross_backward)(
            cross_heads,
            far_keys,
            far_values,
            cross_sums,
            split_heads(to_heads(context_grad), group),
            spans,
        )
        query_back, key_back, value_back = (
            lax.all_to_all(
                shortened(cross_query_grad.reshape(batch_rows, TGT, -1)),
                "seq",
                split_axis=1,
                concat_axis=2,
                tiled=True,
            ),
            lax.all_to_all(
                shortened(far_key_grad.reshape(batch_rows, MEM, -1)),
                "seq",
                split_axis=1,
                concat_axis=2,
                tiled=True,
            ),
            lax.all_to_all(
                shortened(far_value_grad.reshape(batch_rows, MEM, -1)),
                "seq",
                split_axis=1,
                concat_axis=2,
                tiled=True,
            ),
        )
        query_back = query_back.reshape(batch_rows * local_tokens, -1)
        key_back = key_back.reshape(batch_rows * memory_tokens, -1)
        value_back = value_back.reshape(batch_rows * memory_tokens, -1)
        totals[7] = totals[7] + weight_grad(normed_cross, query_back)
        totals[8] = totals[8] + weight_grad(encoded, key_back)
        totals[9] = totals[9] + weight_grad(encoded, value_back)
        memory_grads.append(
            (project_back(key_back, key_cross) + project_back(value_back, value_cross)).reshape(
                batch_rows, memory_tokens, model_width
            )
        )
        _, pullback = jax.vjp(rms_norm, first, gain_cross)
        first_grad, gain_grad = pullback(project_back(query_back, query_cross))
        totals[6] = totals[6] + gain_grad
        first_grad = first_grad + second_grad
        self_grad = first_grad.astype(jnp.bfloat16)
        totals[4] = totals[4] + weight_grad(context, self_grad)
        context_grad = (
            project_back(self_grad, output_self)
            .astype(jnp.bfloat16)
            .reshape(batch_rows, local_tokens, -1)
        )
        query_grad, key_grad, value_grad, bias_grad = jax.vmap(
            self_backward, in_axes=(0, 0, 0, 0, 0, 0, None)
        )(
            self_queries,
            self_keys,
            self_values,
            self_sums,
            split_heads(to_heads(context_grad), group),
            lengths,
            table,
        )
        diagonal = diagonal + jnp.sum(bias_grad, axis=0)
        query_back, key_back, value_back = (
            lax.all_to_all(
                shortened(query_grad.reshape(batch_rows, TGT, -1)),
                "seq",
                split_axis=1,
                concat_axis=2,
                tiled=True,
            ),
            lax.all_to_all(
                shortened(key_grad.reshape(batch_rows, TGT, -1)),
                "seq",
                split_axis=1,
                concat_axis=2,
                tiled=True,
            ),
            lax.all_to_all(
                shortened(value_grad.reshape(batch_rows, TGT, -1)),
                "seq",
                split_axis=1,
                concat_axis=2,
                tiled=True,
            ),
        )
        query_back = query_back.reshape(batch_rows * local_tokens, -1)
        key_back = key_back.reshape(batch_rows * local_tokens, -1)
        value_back = value_back.reshape(batch_rows * local_tokens, -1)
        totals[1] = totals[1] + weight_grad(normed_self, query_back)
        totals[2] = totals[2] + weight_grad(normed_self, key_back)
        totals[3] = totals[3] + weight_grad(normed_self, value_back)
        _, pullback = jax.vjp(rms_norm, hidden, gain_self)
        hidden_grad, gain_grad = pullback(
            project_back(query_back, query_self)
            + project_back(key_back, key_self)
            + project_back(value_back, value_self)
        )
        totals[0] = totals[0] + gain_grad
        input_grads.append(
            (hidden_grad + first_grad).reshape(batch_rows, local_tokens, model_width)
        )
    totals[5] = lax.dot_general(
        onehot, diagonal.reshape(-1, TGT), (((0,), (1,)), ((), ())), precision=HIGH
    )
    reduced = (
        lax.psum_scatter(totals[0], ("dp", "seq"), scatter_dimension=0, tiled=True),
        lax.psum_scatter(totals[1], ("dp", "seq"), scatter_dimension=0, tiled=True),
        lax.psum_scatter(totals[2], ("dp", "seq"), scatter_dimension=0, tiled=True),
        lax.psum_scatter(totals[3], ("dp", "seq"), scatter_dimension=0, tiled=True),
        lax.psum_scatter(totals[4], ("dp", "seq"), scatter_dimension=0, tiled=True),
        lax.psum_scatter(totals[6], ("dp", "seq"), scatter_dimension=0, tiled=True),
        lax.psum_scatter(totals[7], ("dp", "seq"), scatter_dimension=0, tiled=True),
        lax.psum_scatter(totals[8], ("dp", "seq"), scatter_dimension=0, tiled=True),
        lax.psum_scatter(totals[9], ("dp", "seq"), scatter_dimension=0, tiled=True),
        lax.psum_scatter(totals[10], ("dp", "seq"), scatter_dimension=0, tiled=True),
        lax.psum_scatter(totals[11], ("dp", "seq"), scatter_dimension=0, tiled=True),
        lax.psum_scatter(totals[12], ("dp", "seq"), scatter_dimension=0, tiled=True),
        lax.psum_scatter(totals[13], ("dp", "seq"), scatter_dimension=0, tiled=True),
        lax.psum_scatter(totals[14], ("dp", "seq"), scatter_dimension=0, tiled=True),
    )
    bias_share = lax.psum_scatter(totals[5], "dp", scatter_dimension=0, tiled=True)
    return (
        jnp.stack(outputs),
        jnp.stack(input_grads),
        jnp.stack(memory_grads),
        reduced[0],
        reduced[1],
        reduced[2],
        reduced[3],
        reduced[4],
        bias_share,
        reduced[5],
        reduced[6],
        reduced[7],
        reduced[8],
        reduced[9],
        reduced[10],
        reduced[11],
        reduced[12],
        reduced[13],
    )


def row_pieces(full):
    blocks = full.reshape(full.shape[0], -1, QB)
    return jnp.concatenate([blocks[:, 1:], blocks[:, :-1]], axis=2)


def seed_rows(vectors):
    return jnp.stack([jnp.roll(vectors, r, axis=-1) for r in range(8)], axis=-2)


def spread(seed):
    rows = 8
    tile = seed
    while rows < QB:
        tile = jnp.concatenate([tile, pltpu.roll(tile, rows, 1)], axis=0)
        rows *= 2
    return tile[:, :QB]


def fold(tile):
    width = 2 * QB
    tile = jnp.concatenate([tile, jnp.zeros_like(tile)], axis=1)
    rows = QB
    while rows > 8:
        rows //= 2
        tile = tile[:rows] + pltpu.roll(tile[rows:], width - rows, 1)
    return tile


def nt(left, right):
    return lax.dot_general(left, right, (((1,), (1,)), ((), ())), preferred_element_type=jnp.float32)


def tn(left, right):
    return lax.dot_general(left, right, (((0,), (0,)), ((), ())), preferred_element_type=jnp.float32)


def nn(left, right):
    return lax.dot_general(left, right, (((1,), (0,)), ((), ())), preferred_element_type=jnp.float32)


def inverse_rms(value):
    return lax.rsqrt(jnp.mean(value * value, axis=-1, keepdims=True) + EPS)


def pick(array, index, axis=0):
    return lax.dynamic_index_in_dim(array, index, axis, keepdims=False)


MESH = pl.DeviceIdType.MESH


class Spot:
    def __init__(self, depth):
        self.depth = depth
        place = lax.axis_index("dp")
        self.corner = lax.axis_index("seq")
        self.z, self.core = place // 2, place % 2
        self.y, self.x = self.corner // 2, self.corner % 2

    def at(self, z=None, core=None, y=None, x=None):
        z = self.z if z is None else z
        core = self.core if core is None else core
        y = self.y if y is None else y
        x = self.x if x is None else x
        return (z * 2 + core, y * 2 + x)

    def beside(self):
        return self.at(x=1 - self.x)

    def below(self):
        return self.at(y=1 - self.y)

    def sibling(self):
        return self.at(core=1 - self.core)

    def greet(self):
        barrier = pltpu.get_barrier_semaphore()
        others = [
            self.at(None, self.core ^ (i >> 2), self.y ^ (i >> 1 & 1), self.x ^ (i & 1)) for i in range(1, 8)
        ]
        for step in range(1, self.depth):
            for flip in range(2):
                others.append(self.at((self.z + step) % self.depth, self.core ^ flip))
        for other in others:
            pl.semaphore_signal(barrier, inc=1, device_id=other, device_id_type=MESH)
        pl.semaphore_wait(barrier, len(others))


class Wires:
    def __init__(self, sends, arrivals, moves):
        self.sends, self.arrivals, self.moves = sends, arrivals, moves
        self.count = 0
        self.moved = 0
        self.open = []

    def take(self, number):
        first = self.count
        self.count += number
        return first

    def send(self, source, target, device, index, landing=None):
        landing = index if landing is None else landing
        copy = pltpu.make_async_remote_copy(
            src_ref=source,
            dst_ref=target,
            send_sem=self.sends.at[index],
            recv_sem=self.arrivals.at[landing],
            device_id=device,
            device_id_type=MESH,
        )
        copy.start()
        self.open.append(copy)
        return copy

    def arrive(self, target, device, index):
        pltpu.make_async_remote_copy(
            src_ref=target,
            dst_ref=target,
            send_sem=self.sends.at[0],
            recv_sem=self.arrivals.at[index],
            device_id=device,
            device_id_type=MESH,
        ).wait_recv()

    def move(self, source, target):
        copy = pltpu.make_async_copy(source, target, self.moves.at[self.moved])
        self.moved += 1
        copy.start()
        return copy

    def close(self):
        for copy in self.open:
            copy.wait_send()
        self.open = []


def collect_tokens(spot, wires, parcel, whole):
    away = wires.take(4)
    over = wires.take(4)
    local = wires.moved
    wires.moved += 1
    for index in range(4):
        half, micro = spot.y ^ (index >> 1), spot.x ^ (index & 1)
        home = (half == spot.core) & (micro == spot.y) & (spot.core == spot.x)
        source = parcel.at[micro, half]
        target = whole.at[spot.corner, half]
        copy = pltpu.make_async_remote_copy(
            src_ref=source,
            dst_ref=target,
            send_sem=wires.sends.at[away + index],
            recv_sem=wires.arrivals.at[away + index],
            device_id=spot.at(core=half, y=micro, x=spot.core),
            device_id_type=MESH,
        )
        here = pltpu.make_async_copy(source, target, wires.moves.at[local])

        @pl.when(jnp.logical_not(home))
        def _():
            copy.start()

        @pl.when(home)
        def _():
            here.start()

    yield
    for index in range(4):
        block = 2 * (spot.core ^ (index >> 1)) + (spot.y ^ (index & 1))
        home = (spot.x == spot.core) & (block == spot.corner)
        piece = whole.at[block, spot.core]
        here = pltpu.make_async_copy(piece, piece, wires.moves.at[local])
        landed = pltpu.make_async_remote_copy(
            src_ref=piece,
            dst_ref=piece,
            send_sem=wires.sends.at[away + index],
            recv_sem=wires.arrivals.at[away + index],
            device_id=spot.sibling(),
            device_id_type=MESH,
        )

        @pl.when(jnp.logical_not(home))
        def _():
            landed.wait_recv()

        @pl.when(home)
        def _():
            here.wait()

        wires.send(piece, piece, spot.sibling(), over + index)
    yield
    for index in range(4):
        block = 2 * ((1 - spot.core) ^ (index >> 1)) + (spot.y ^ (index & 1))
        wires.arrive(whole.at[block, 1 - spot.core], spot.sibling(), over + index)
    for index in range(4):
        half, micro = spot.y ^ (index >> 1), spot.x ^ (index & 1)
        home = (half == spot.core) & (micro == spot.y) & (spot.core == spot.x)
        source = parcel.at[micro, half]

        @pl.when(jnp.logical_not(home))
        def _():
            pltpu.make_async_remote_copy(
                src_ref=source,
                dst_ref=source,
                send_sem=wires.sends.at[away + index],
                recv_sem=wires.arrivals.at[away + index],
                device_id=spot.sibling(),
                device_id_type=MESH,
            ).wait_send()

    yield


def deliver_tokens(spot, wires, pieces, homes):
    away = wires.take(4)
    local = wires.moved
    wires.moved += 1

    def parts():
        for index in range(4):
            block = 2 * (spot.core ^ (index >> 1)) + (spot.y ^ (index & 1))
            home = (spot.x == spot.core) & (block == spot.corner)
            source = pieces.at[block]
            target = homes.at[spot.y, spot.core]
            remote = pltpu.make_async_remote_copy(
                src_ref=source,
                dst_ref=target,
                send_sem=wires.sends.at[away + index],
                recv_sem=wires.arrivals.at[away + index],
                device_id=spot.at(core=spot.x, y=block // 2, x=block % 2),
                device_id_type=MESH,
            )
            yield home, remote, pltpu.make_async_copy(source, target, wires.moves.at[local])

    for home, remote, here in parts():
        pl.when(jnp.logical_not(home))(remote.start)
        pl.when(home)(here.start)
    yield
    for index in range(4):
        half, micro = spot.y ^ (index >> 1), spot.x ^ (index & 1)
        home = (half == spot.core) & (micro == spot.y) & (spot.core == spot.x)
        piece = homes.at[micro, half]
        landed = pltpu.make_async_remote_copy(
            src_ref=piece,
            dst_ref=piece,
            send_sem=wires.sends.at[away + index],
            recv_sem=wires.arrivals.at[away + index],
            device_id=spot.sibling(),
            device_id_type=MESH,
        )
        here = pltpu.make_async_copy(piece, piece, wires.moves.at[local])
        pl.when(jnp.logical_not(home))(landed.wait_recv)
        pl.when(home)(here.wait)
    for home, remote, here in parts():
        pl.when(jnp.logical_not(home))(remote.wait_send)
    yield


def gather_small(spot, wires, block, whole):
    own = wires.move(block, whole.at[spot.z, spot.core, spot.corner])
    first = wires.take(spot.depth + 3)
    for step in range(1, spot.depth):
        target = whole.at[spot.z, spot.core, spot.corner]
        wires.send(block, target, spot.at(z=(spot.z + step) % spot.depth), first + step)
    yield
    own.wait()
    for step in range(1, spot.depth):
        z = (spot.z - step + spot.depth) % spot.depth
        wires.arrive(whole.at[z, spot.core, spot.corner], spot.sibling(), first + step)
    column = whole.at[:, spot.core, spot.corner]
    wires.send(column, column, spot.beside(), first)
    wires.send(column, column, spot.below(), first + spot.depth)
    wires.send(column, column, spot.at(y=1 - spot.y, x=1 - spot.x), first + spot.depth + 1)
    yield
    for flip, index in ((1, first), (2, first + spot.depth), (3, first + spot.depth + 1)):
        wires.arrive(whole.at[:, spot.core, spot.corner ^ flip], spot.sibling(), index)
    plane = whole.at[:, spot.core]
    wires.send(plane, plane, spot.sibling(), first + spot.depth + 2)
    yield
    wires.arrive(whole.at[:, 1 - spot.core], spot.sibling(), first + spot.depth + 2)
    yield


def gather_columns(spot, wires, pack, whole):
    depth, me = spot.depth, spot.corner
    ahead = wires.take(2 * depth)
    flat = wires.take(4 * depth)
    own = wires.move(pack.at[spot.core], whole.at[spot.z, spot.core])
    for step in range(1, depth):
        for flip in range(2):
            wires.send(
                pack.at[spot.core ^ flip, me],
                whole.at[spot.z, spot.core, me],
                spot.at((spot.z + step) % depth, spot.core ^ flip),
                ahead + 2 * step + flip,
            )
    wires.send(pack.at[1 - spot.core], whole.at[spot.z, spot.core], spot.sibling(), ahead)
    yield
    for step in range(1, depth):
        z = (spot.z - step + depth) % depth
        for flip in range(2):
            wires.arrive(whole.at[z, spot.core ^ flip, me], spot.sibling(), ahead + 2 * step + flip)
        quarter = whole.at[z, :, me]
        wires.send(quarter, quarter, spot.beside(), flat + 4 * step)
        wires.send(quarter, quarter, spot.below(), flat + 4 * step + 1)
    yield
    for step in range(1, depth):
        z = (spot.z - step + depth) % depth
        wires.arrive(whole.at[z, :, me ^ 1], spot.sibling(), flat + 4 * step)
        piece = whole.at[z, 0, me ^ 1]
        wires.send(piece, piece, spot.below(), flat + 4 * step + 2)
        wires.arrive(whole.at[z, :, me ^ 2], spot.sibling(), flat + 4 * step + 1)
        piece = whole.at[z, 1, me ^ 2]
        wires.send(piece, piece, spot.beside(), flat + 4 * step + 3)
    yield
    own.wait()
    wires.arrive(whole.at[spot.z, 1 - spot.core], spot.sibling(), ahead)
    for step in range(1, depth):
        z = (spot.z - step + depth) % depth
        wires.arrive(whole.at[z, 0, me ^ 3], spot.sibling(), flat + 4 * step + 2)
        wires.arrive(whole.at[z, 1, me ^ 3], spot.sibling(), flat + 4 * step + 3)
    yield


def gather_rows(spot, wires, pack, whole):
    depth, me = spot.depth, spot.corner
    ahead = wires.take(depth)
    flat = wires.take(4 * depth)
    middle = pack.shape[-1] // 2

    def part(z, corner, side):
        if pack.shape[0] == 2:
            return whole.at[side, z, corner]
        return whole.at[0, z, corner, :, pl.ds(side * middle, middle)]

    own = wires.move(pack, whole.at[:, spot.z])
    for step in range(1, depth):
        wires.send(
            pack.at[:, me], whole.at[:, spot.z, me], spot.at((spot.z + step) % depth), ahead + step
        )
    yield
    for step in range(1, depth):
        z = (spot.z - step + depth) % depth
        quarter = whole.at[:, z, me]
        wires.arrive(quarter, spot.sibling(), ahead + step)
        wires.send(quarter, quarter, spot.beside(), flat + 4 * step)
        wires.send(quarter, quarter, spot.below(), flat + 4 * step + 1)
    yield
    for step in range(1, depth):
        z = (spot.z - step + depth) % depth
        wires.arrive(whole.at[:, z, me ^ 1], spot.sibling(), flat + 4 * step)
        piece = part(z, me ^ 1, 0)
        wires.send(piece, piece, spot.below(), flat + 4 * step + 2)
        wires.arrive(whole.at[:, z, me ^ 2], spot.sibling(), flat + 4 * step + 1)
        piece = part(z, me ^ 2, 1)
        wires.send(piece, piece, spot.beside(), flat + 4 * step + 3)
    yield
    own.wait()
    for step in range(1, depth):
        z = (spot.z - step + depth) % depth
        wires.arrive(part(z, me ^ 3, 0), spot.sibling(), flat + 4 * step + 2)
        wires.arrive(part(z, me ^ 3, 1), spot.sibling(), flat + 4 * step + 3)
    yield


def reach_columns(spot, wires, pack, near):
    depth, me = spot.depth, spot.corner
    ahead = wires.take(2 * depth)
    own = wires.move(pack.at[spot.core, me], near.at[spot.z, spot.core])
    for step in range(depth):
        for flip in range(2):
            if step or flip:
                wires.send(
                    pack.at[spot.core ^ flip, me],
                    near.at[spot.z, spot.core],
                    spot.at((spot.z + step) % depth, spot.core ^ flip),
                    ahead + 2 * step + flip,
                )
    yield
    own.wait()
    for step in range(depth):
        z = (spot.z - step + depth) % depth
        for flip in range(2):
            if step or flip:
                wires.arrive(near.at[z, spot.core ^ flip], spot.sibling(), ahead + 2 * step + flip)
    yield


def reach_rows(spot, wires, pack, near):
    depth, me = spot.depth, spot.corner
    ahead = wires.take(depth)
    own = wires.move(pack.at[0, me], near.at[spot.z])
    for step in range(1, depth):
        wires.send(pack.at[0, me], near.at[spot.z], spot.at((spot.z + step) % depth), ahead + step)
    yield
    own.wait()
    for step in range(1, depth):
        z = (spot.z - step + depth) % depth
        wires.arrive(near.at[z], spot.sibling(), ahead + step)
    yield


def share_plane(spot, wires, near, whole, parts):
    me = spot.corner
    flat = wires.take(4)
    own = wires.move(near, whole(me))
    wires.send(near, whole(me), spot.beside(), flat)
    wires.send(near, whole(me), spot.below(), flat + 1)
    yield
    wires.arrive(whole(me ^ 1), spot.sibling(), flat)
    piece = parts(whole(me ^ 1), 0)
    wires.send(piece, piece, spot.below(), flat + 2)
    wires.arrive(whole(me ^ 2), spot.sibling(), flat + 1)
    piece = parts(whole(me ^ 2), 1)
    wires.send(piece, piece, spot.beside(), flat + 3)
    yield
    own.wait()
    wires.arrive(parts(whole(me ^ 3), 0), spot.sibling(), flat + 2)
    wires.arrive(parts(whole(me ^ 3), 1), spot.sibling(), flat + 3)
    yield


def scatter_buffers(depth, lanes, rows, width):
    half = depth // 2
    return [
        pltpu.VMEM((half, lanes, 2, rows, width), jnp.bfloat16),
        pltpu.VMEM((half, lanes, 2, rows, width), jnp.bfloat16),
        pltpu.VMEM((half, lanes, 2, rows, width), jnp.bfloat16),
        pltpu.VMEM((half, lanes, 2, rows, width), jnp.bfloat16),
        pltpu.VMEM((half, lanes, rows, width), jnp.bfloat16),
        pltpu.VMEM((half, lanes, rows, width), jnp.bfloat16),
        pltpu.VMEM((depth, lanes, rows, width), jnp.bfloat16),
        pltpu.VMEM((depth, lanes, rows, width), jnp.bfloat16),
        pltpu.VMEM((rows, width), jnp.bfloat16),
    ]


def scatter_sums(spot, wires, grads, buffers, total, got, resident=False):
    depth, half = spot.depth, spot.depth // 2
    lanes = grads.shape[1]
    places = [(z, a, s) for z in range(half) for a in range(lanes) for s in range(2)]
    if resident:
        low_in, high_in, low_last, high_last, column, column_in, passing = buffers
        low, high = low_in, high_in
    else:
        low, high, low_in, high_in, low_last, high_last, column, column_in, passing = buffers
    first = wires.take(4)
    away = wires.take(depth)
    mine = []
    if not resident:
        mine = [
            wires.move(grads.at[pl.ds(0, half), :, :, spot.x], low),
            wires.move(grads.at[pl.ds(half, half), :, spot.y], high),
        ]
    wires.send(grads.at[pl.ds(0, half), :, :, 1 - spot.x], low_in, spot.beside(), first)
    wires.send(grads.at[pl.ds(half, half), :, 1 - spot.y], high_in, spot.below(), first + 1)
    yield
    for copy in mine:
        copy.wait()

    def join(target, other, index):
        target[index] = (target[index].astype(jnp.float32) + other.astype(jnp.float32)).astype(jnp.bfloat16)

    wires.arrive(low_in, spot.beside(), first)
    for z, a, s in places:
        join(low, grads[z, a, s, spot.x] if resident else low_in[z, a, s], (z, a, s))
    wires.send(low.at[:, :, 1 - spot.y], low_last, spot.below(), first + 2)
    wires.arrive(high_in, spot.below(), first + 1)
    for z, a, s in places:
        join(high, grads[half + z, a, spot.y, s] if resident else high_in[z, a, s], (z, a, s))
    wires.send(high.at[:, :, 1 - spot.x], high_last, spot.beside(), first + 3)
    yield
    wires.arrive(low_last, spot.below(), first + 2)
    wires.arrive(high_last, spot.beside(), first + 3)
    for z in range(half):
        for a in range(lanes):
            column[z, a] = (
                low[z, a, spot.y].astype(jnp.float32) + low_last[z, a].astype(jnp.float32)
            ).astype(jnp.bfloat16)
            column[half + z, a] = (
                high[z, a, spot.x].astype(jnp.float32) + high_last[z, a].astype(jnp.float32)
            ).astype(jnp.bfloat16)
    for step in range(1, depth):
        z = (spot.z + step) % depth
        wires.send(column.at[z], column_in.at[step], spot.at(z), away + step)
    yield
    for step in range(1, depth):
        wires.arrive(column_in.at[step], spot.sibling(), away + step)

    def added(lane):
        result = column[spot.z, lane].astype(jnp.float32)
        for step in range(1, depth):
            result = result + column_in[step, lane].astype(jnp.float32)
        return result

    if lanes == 1:
        total[...] = added(0)
    else:
        passing[...] = added(1 - spot.core).astype(jnp.bfloat16)
        wires.send(passing, got, spot.sibling(), away)
        total[...] = added(spot.core)
    yield
    if lanes == 2:
        wires.arrive(got, spot.sibling(), away)
    yield


def total_small(spot, wires, terms, work, total):
    first = wires.take(3 + spot.depth)
    work[0] = terms[...]
    wires.send(work.at[0], work.at[1], spot.sibling(), first)
    yield
    wires.arrive(work.at[1], spot.sibling(), first)
    work[2] = work[0] + work[1]
    wires.send(work.at[2], work.at[3], spot.beside(), first + 1)
    yield
    wires.arrive(work.at[3], spot.sibling(), first + 1)
    work[4] = work[2] + work[3]
    wires.send(work.at[4], work.at[5], spot.below(), first + 2)
    yield
    wires.arrive(work.at[5], spot.sibling(), first + 2)
    work[6] = work[4] + work[5]
    for step in range(1, spot.depth):
        target = work.at[6 + step]
        wires.send(work.at[6], target, spot.at((spot.z + step) % spot.depth), first + 2 + step)
    yield
    result = work[6]
    for step in range(1, spot.depth):
        wires.arrive(work.at[6 + step], spot.sibling(), first + 2 + step)
        result = result + work[6 + step]
    total[...] = result
    yield


def wire_scratch(number, moves):
    return [
        pltpu.SemaphoreType.DMA((number,)),
        pltpu.SemaphoreType.DMA((number,)),
        pltpu.SemaphoreType.DMA((moves,)),
    ]


def spread_row(vector):
    tile = pltpu.roll(jnp.broadcast_to(vector, (8, 2 * QB)), 0, 1, stride=1, stride_axis=0)
    return spread(tile)


def attend_block(query, keys, values, keep, bias):
    scores = nt(query, keys) + keep
    if bias is not None:
        scores = scores + bias
    peak = jnp.max(scores, axis=1, keepdims=True)
    weights = jnp.exp(scores - peak)
    total = jnp.sum(weights, axis=1, keepdims=True)
    return nn(weights.astype(jnp.bfloat16), values) / total, peak + jnp.log(total)


def pair_rows(block, kv):
    both = block[:, 2 * kv * HEAD_DIM : 2 * (kv + 1) * HEAD_DIM]
    return jnp.concatenate([both[:, :HEAD_DIM], both[:, HEAD_DIM:]], axis=0)


def normed(value, gain):
    return (value * inverse_rms(value) * gain).astype(jnp.bfloat16)


def pack_heads(pack, weights, start):
    size = sum(w.shape[1] for w in weights) // 8
    for place in range(8):
        units = [w.shape[1] // 8 for w in weights]
        pieces = [w[:, place * u : (place + 1) * u] for w, u in zip(weights, units)]
        piece = pieces[0] if len(pieces) == 1 else jnp.concatenate(pieces, axis=1)
        lanes = slice(start + place // 2 * size, start + (place // 2 + 1) * size)
        pack[place % 2, :, :, lanes] = piece.reshape(4, -1, size)


def pack_hidden(pack, weights, first, last):
    size = 16 * (last - first)
    for order, weight in enumerate(weights):
        unit = weight.shape[1] // 8
        quarter = unit // 4
        for side in range(2):
            pieces = [
                weight[:, place * unit + q * quarter + first : place * unit + q * quarter + last]
                for place in range(side, 8, 2)
                for q in range(4)
            ]
            row = jnp.concatenate(pieces, axis=1)
            pack[side, :, :, order * size : (order + 1) * size] = row.reshape(4, -1, size).astype(pack.dtype)


def forward_layer_kernel(depth, cuts, *refs):
    (
        x, t, m, s, codes, holes, sq, sk, sv, ck, cv, cq, wg, wu, so, co, wd,
        o_wx, wt, o_wm, ws, o_w1, o_w2, o_w3, w4, w5,
        o_a1, o_qkv, o_ctx, lse, o_x1, o_a2, o_qc, o_ckv, o_ctxc, lsec, o_x2, o_a3, gains, keeps, keepc, bent,
        down_s, down_c, n6, n7, p8, p9,
        p1, p2, p4, p6, p3, p5, p7, bias, own, got, got2, wx, wm, w1, w2, w3, a1, qkv, ctx, x1, a2, qc, ckv, ctxc, x2, a3, *sems
    ) = refs
    leaving = []
    p3[0] = so[...].reshape(p3.shape[1:])
    p3[1] = co[...].reshape(p3.shape[1:])
    p5[0] = wd[:, : cuts[0]]
    p7[0] = wd[:, cuts[0] : cuts[1]]
    p9[0] = wd[:, cuts[1] : cuts[2]]
    pack_heads(p1, [sq, sk, sv], 0)
    pack_heads(p2, [ck, cv], 0)
    pack_heads(p2, [cq], ck.shape[1])

    def leave(*pairs):
        leaving.extend(wires.move(source, target) for source, target in pairs)

    f32, bf16 = jnp.float32, jnp.bfloat16
    spot = Spot(depth)
    wires = Wires(*sems)
    blocks = 4
    kvs = 4
    inner = 2 * kvs * HEAD_DIM

    def rows(block):
        return slice(block * QB, (block + 1) * QB)

    spot.greet()
    tokens = collect_tokens(spot, wires, x, wx)
    small = gather_small(spot, wires, s, ws)
    first = gather_columns(spot, wires, p1, w1)
    memory = collect_tokens(spot, wires, m, wm)
    second = gather_columns(spot, wires, p2, w2)
    outs = gather_rows(spot, wires, p3, w3)
    wide = gather_columns(spot, wires, p4, w4)
    down = gather_rows(spot, wires, p5, w5)
    top = collect_tokens(spot, wires, t, wt)
    wide_next = reach_columns(spot, wires, p6, n6)
    down_next = reach_rows(spot, wires, p7, n7)
    over = wires.take(2 * blocks)

    def advance(*programs):
        for program in programs:
            next(program)

    advance(small, first, small, tokens)
    pack_hidden(p4, [wg[...], wu[...]], 0, cuts[0])
    pack_hidden(p6, [wg[...], wu[...]], cuts[0], cuts[1])
    pack_hidden(p8, [wg[...], wu[...]], cuts[1], cuts[2])
    advance(small, small)

    def line(row):
        return jnp.concatenate([ws[z, c, 0, row : row + 1, :] for z in range(depth) for c in range(2)], axis=1)

    for row in range(3):
        gains[row : row + 1, :] = line(row)
    counts = ws[spot.z, spot.x, 0, 3:4, :]
    length = jnp.where(spot.y == 0, counts[:, 0:1], counts[:, 1:2])
    span = jnp.where(spot.y == 0, counts[:, 2:3], counts[:, 3:4])
    places = lax.broadcasted_iota(jnp.int32, (1, blocks * QB), 1).astype(f32)
    keeps[...] = jnp.where(places < length, 0.0, NEG)
    keepc[...] = jnp.where(places[:, : keepc.shape[1]] < span, 0.0, NEG)
    places = lax.broadcasted_iota(jnp.int32, (blocks * QB, 1), 0).astype(f32)
    down_s[...] = jnp.where(places < length, 0.0, NEG)
    down_c[...] = jnp.where(places[: down_c.shape[0]] < span, 0.0, NEG)
    table = jnp.concatenate(
        [
            ws[z, c, 0, 4:8, :] + ws[z, c, 1, 4:8, :] + ws[z, c, 2, 4:8, :] + ws[z, c, 3, 4:8, :]
            for z in range(depth)
            for c in range(2)
        ],
        axis=0,
    )
    table = jnp.where(spot.core == 0, table[:, :64], table[:, 64:]).astype(bf16)
    vectors = tn(table, codes[...])[:8] + holes[...]
    bent[...] = vectors[:, 4 * 2 * QB :]
    for kv in range(kvs):
        for member in range(2):
            for offset in range(4):
                head = 2 * kv + member
                bias[kv, member * QB : (member + 1) * QB, (3 - offset) * QB : (4 - offset) * QB] = spread_row(
                    vectors[head : head + 1, offset * 2 * QB : (offset + 1) * 2 * QB]
                ).astype(bf16)

    advance(first, outs, second, tokens, tokens)
    for block in range(blocks):
        a1[rows(block), :] = normed(wx[block].reshape(QB, -1).astype(f32), gains[0:1, :])
    advance(first, memory, first)
    leave((wx, o_wx), (w1, o_w1), (a1, o_a1))

    def attend_rows(block, queries, keys, stop, keep, mixed, sums, causal):
        for kv in range(kvs):
            base = 2 * kv * HEAD_DIM
            query = queries[rows(block), base : base + 2 * HEAD_DIM]
            shape = None
            if causal:
                base = 4 * kv * HEAD_DIM
                query = queries[rows(block), base : base + 2 * HEAD_DIM]
                base += 2 * HEAD_DIM
                shape = bias[kv, :, (3 - block) * QB : (3 - block) * QB + stop]
            out, level = attend_block(
                pair_rows(query, 0),
                keys[:stop, base : base + HEAD_DIM],
                keys[:stop, base + HEAD_DIM : base + 2 * HEAD_DIM],
                keep[:, :stop],
                shape,
            )
            mixed[rows(block), 2 * kv * HEAD_DIM : 2 * (kv + 1) * HEAD_DIM] = jnp.concatenate(
                [out[:QB], out[QB:]], axis=1
            ).astype(bf16)
            level = jnp.broadcast_to(level, (2 * QB, 128)).T
            sums[2 * kv : 2 * kv + 1, rows(block)] = level[:1, :QB]
            sums[2 * kv + 1 : 2 * kv + 2, rows(block)] = level[:1, QB:]

    weight = w1[...].reshape(-1, w1.shape[-1])
    for block in range(blocks):
        qkv[rows(block), :] = nn(a1[rows(block), :], weight).astype(bf16)
        attend_rows(block, qkv, qkv, (block + 1) * QB, keeps, ctx, lse, True)
        if block == 1:
            advance(outs, wide, down, second, memory)
        if block == 2:
            advance(outs)
    advance(outs, second, wide, down, wide_next, down_next)

    sent = {}

    def pass_on(block, mine, theirs, value, weight, index):
        if block in sent:
            sent[block].wait_send()
            wires.open = [copy for copy in wires.open if copy is not sent[block]]
        mine[rows(block), :] = nn(value[rows(block), :], weight).astype(bf16)
        sent[block] = wires.send(
            mine.at[rows(block)], theirs.at[rows(block)], spot.sibling(), over + index + block
        )

    def joined(block, mine, theirs, index):
        wires.arrive(theirs.at[rows(block)], spot.sibling(), over + index + block)
        return mine[rows(block), :].astype(f32) + theirs[rows(block), :].astype(f32)

    weight = w3[0].reshape(-1, w3.shape[-1])
    for block in range(blocks):
        pass_on(block, own, got, ctx, weight, 0)
    advance(memory, second, wide, down, top)
    leave((wm, o_wm), (w2, o_w2), (w3, o_w3), (qkv, o_qkv), (ctx, o_ctx))
    weight = w2[...].reshape(-1, w2.shape[-1])
    ckv[...] = nn(wm[...].reshape(-1, wm.shape[-1]), weight[:, :inner]).astype(bf16)
    for block in range(blocks):
        value = wx[block].reshape(QB, -1).astype(f32) + joined(block, own, got, 0)
        x1[rows(block), :] = value
        a2[rows(block), :] = normed(value, gains[1:2, :])
        qc[rows(block), :] = nn(a2[rows(block), :], weight[:, inner:]).astype(bf16)
    leave((x1, o_x1), (a2, o_a2), (qc, o_qc), (ckv, o_ckv))
    weight = w3[1].reshape(-1, w3.shape[-1])
    for block in range(blocks):
        attend_rows(block, qc, ckv, ckv.shape[0], keepc, ctxc, lsec, False)
        pass_on(block, own, got2, ctxc, weight, blocks)
        if block == 0:
            advance(wide, down)
        if block == 2:
            advance(top)
    for block in range(blocks):
        value = x1[rows(block), :] + joined(block, own, got2, blocks)
        x2[rows(block), :] = value
        a3[rows(block), :] = normed(value, gains[2:3, :])
        leave(
            (x2.at[rows(block)], o_x2.at[rows(block)]),
            (a3.at[rows(block)], o_a3.at[rows(block)]),
            (ctxc.at[rows(block)], o_ctxc.at[rows(block)]),
        )
    advance(wide_next, down_next, top)
    for program in (tokens, small, first, memory, second, outs, wide, down, top, wide_next, down_next):
        assert next(program, None) is None
    for copy in leaving:
        copy.wait()
    wires.close()


def forward_layer(depth, cuts, x, t, m, small, codes, holes, *weights):
    bf16, f32 = jnp.bfloat16, jnp.float32
    shape = jax.ShapeDtypeStruct

    def whole_columns(pack):
        return shape((depth, 2) + pack.shape[1:], bf16)

    def whole_rows(pack):
        return shape((pack.shape[0], depth) + pack.shape[1:], bf16)

    def whole_tokens(parcel):
        return shape((4, 2) + parcel.shape[2:], bf16)

    rows = weights[0].shape[0] // 4
    p3 = shape((2, 4) + (rows, weights[8].shape[1]), bf16)
    p5, p7, p9 = (
        shape((1, 4, stop - start, weights[10].shape[2]), bf16) for start, stop in zip((0,) + cuts[:2], cuts)
    )
    p1 = p2 = shape((2, 4, rows, weights[0].shape[1]), bf16)
    p4, p6, p8 = (
        shape((2, 4, rows, 32 * (stop - start)), bf16) for start, stop in zip((0,) + cuts[:2], cuts)
    )
    width = x.shape[-1]
    tokens = 8 * x.shape[2]
    span = 8 * m.shape[2]
    inner = p3.shape[0] * p3.shape[1] * p3.shape[2] * depth // 2
    heads = inner // HEAD_DIM
    hbm = pl.BlockSpec(memory_space=pl.ANY)
    vmem = pl.BlockSpec(memory_space=pltpu.VMEM)
    outs = [
        (whole_tokens(x), hbm),
        (whole_tokens(t), hbm),
        (whole_tokens(m), hbm),
        (shape((depth, 2, 4, 8, 128), f32), vmem),
        (whole_columns(p1), hbm),
        (whole_columns(p2), hbm),
        (whole_rows(p3), hbm),
        (whole_columns(p4), hbm),
        (whole_rows(p5), hbm),
        (shape((tokens, width), bf16), hbm),
        (shape((tokens, 2 * inner), bf16), hbm),
        (shape((tokens, inner), bf16), hbm),
        (shape((heads, tokens), f32), vmem),
        (shape((tokens, width), f32), hbm),
        (shape((tokens, width), bf16), hbm),
        (shape((tokens, inner), bf16), hbm),
        (shape((span, inner), bf16), hbm),
        (shape((tokens, inner), bf16), hbm),
        (shape((heads, tokens), f32), vmem),
        (shape((tokens, width), f32), hbm),
        (shape((tokens, width), bf16), hbm),
        (shape((8, width), f32), vmem),
        (shape((1, tokens), f32), vmem),
        (shape((1, span), f32), vmem),
        (shape((heads, 8 * QB), f32), vmem),
        (shape((tokens, 1), f32), vmem),
        (shape((span, 1), f32), vmem),
        (shape((depth, 2) + p6.shape[2:], bf16), hbm),
        (shape((depth,) + p7.shape[2:], bf16), hbm),
        (p8, vmem),
        (p9, vmem),
    ]
    packs = [pltpu.VMEM(pack.shape, bf16) for pack in (p1, p2, p4, p6, p3, p5, p7)]
    swap = pltpu.VMEM((tokens, width), bf16)
    return pl.pallas_call(
        functools.partial(forward_layer_kernel, depth, cuts),
        in_specs=[hbm] * 4 + [vmem] * 13,
        out_specs=[spec for _, spec in outs],
        out_shape=[kind for kind, _ in outs],
        scratch_shapes=packs
        + [pltpu.VMEM((heads // 2, 2 * QB, 4 * QB), bf16), swap, swap, swap]
        + [pltpu.VMEM(outs[i][0].shape, outs[i][0].dtype) for i in (0, 2, 4, 5, 6, 9, 10, 11, 13, 14, 15, 16, 17, 19, 20)]
        + wire_scratch(35 + 33 * depth, 40),
        compiler_params=pltpu.CompilerParams(
            collective_id=0, has_side_effects=True, vmem_limit_bytes=60 * 2**20
        ),
        cost_estimate=pl.CostEstimate(
            flops=16 * 10**9, bytes_accessed=128 * 2**20, transcendentals=10**7
        ),
    )(x, t, m, small, codes, holes, *weights)


def pipeline(programs, ahead=2, stages=5):
    count = len(programs)
    for turn in range(count + stages):
        if turn == 0:
            for program in programs[:ahead]:
                next(program)
            yield
        for stage in range(stages - 1, 0, -1):
            index = turn - (stage - 1)
            if 0 <= index < count:
                next(programs[index])
        if turn + ahead < count:
            next(programs[turn + ahead])
        yield


def backward_tile(keys, values, query, grads, keep, bias, level, delta):
    scores = nt(keys, query) + keep
    if bias is not None:
        scores = scores + bias
    probs = jnp.exp(scores - level)
    return probs, probs * (nt(values, grads) - delta)


def row_sums(upstream, mixed):
    inner = (upstream.astype(jnp.float32) * mixed.astype(jnp.float32)).T
    return jnp.concatenate(
        [
            jnp.sum(inner[:HEAD_DIM], axis=0, keepdims=True),
            jnp.sum(inner[HEAD_DIM:], axis=0, keepdims=True),
        ],
        axis=1,
    )


def cross_backward_kernel(depth, *refs):
    g_early, g_down, g_gate, g_up, x2, x1, t_out, *far = refs[:17]
    (
        lsec, keep, gains,
        r_early, r_down, r_gate, r_up, q_gate, q_up, o_cout, o_cq, o_ckv, half, do_s, g_out, o_mem, terms, h_out,
        *rest
    ) = refs[17:]
    take = lambda n: [rest.pop(0) for _ in range(n)]
    near = take(10)
    u, top, qc, ckv, ctxc, a2, mem, w2, w3, ctx = near
    g_cout, g_cq, g_ckv = take(3)
    stage, e2, eb, do_c, dqc, dkv, dk_sum, dv_sum, got, own_c, got_c, own_m, got_m = take(13)
    buffers = [take(9) for _ in range(4)]
    f32, bf16 = jnp.float32, jnp.bfloat16
    spot = Spot(depth)
    wires = Wires(*rest)
    blocks = kvs = 4
    inner = 2 * kvs * HEAD_DIM

    def rows(block):
        return slice(block * QB, (block + 1) * QB)

    coming = [wires.move(source, target) for source, target in zip(far, near)]
    spot.greet()
    over = wires.take(2 * blocks + 4)
    for block in range(blocks):
        wires.send(far[0].at[rows(block)], got.at[rows(block)], spot.sibling(), over + block)
    home = deliver_tokens(spot, wires, t_out, h_out)
    programs = [
        scatter_sums(spot, wires, g_down, buffers[0], r_down, None),
        scatter_sums(spot, wires, g_gate, buffers[1], r_gate, q_gate),
        scatter_sums(spot, wires, g_up, buffers[2], r_up, q_up),
        scatter_sums(spot, wires, g_early, buffers[3], r_early, None),
    ]
    links = pipeline(programs)
    next(links)
    next(home)

    loads = {}

    def fetch(source, block, slot):
        loads[slot] = wires.move(source.at[rows(block)], stage.at[slot])

    def norm_back(block, slot, gain, upstream):
        loads[slot].wait()
        value = stage[slot]
        inverse = inverse_rms(value)
        scaled = upstream * gain
        mean = jnp.mean(value * scaled, axis=-1, keepdims=True)
        change = inverse * scaled - value * (inverse * inverse * inverse) * mean
        return change, jnp.sum(upstream * value * inverse, axis=0, keepdims=True)

    fetch(x2, 0, 0)
    for copy in coming:
        copy.wait()
    gain_terms = jnp.zeros((1, e2.shape[1]), f32)
    for block in range(blocks):
        if block + 1 < blocks:
            fetch(x2, block + 1, (block + 1) % 2)
        else:
            fetch(x1, 0, 0)
        wires.arrive(got.at[rows(block)], spot.sibling(), over + block)
        change, term = norm_back(
            block, block % 2, gains[2:3, :], u[rows(block), :].astype(f32) + got[rows(block), :].astype(f32)
        )
        gain_terms = gain_terms + term
        value = top[rows(block), :].astype(f32) + change
        e2[rows(block), :] = value
        eb[rows(block), :] = value.astype(bf16)
        do_c[rows(block), :] = nt(value.astype(bf16), w3[1].reshape(inner, -1)).astype(bf16)
    terms[0:1, :] = 0.5 * gain_terms
    next(links)

    span = ckv.shape[0]
    for kv in range(kvs):
        both = slice(2 * kv * HEAD_DIM, 2 * (kv + 1) * HEAD_DIM)
        base = 2 * kv * HEAD_DIM
        dk_sum[...] = jnp.zeros_like(dk_sum)
        dv_sum[...] = jnp.zeros_like(dv_sum)
        for block in range(blocks):
            query = pair_rows(qc[rows(block), :], kv)
            grads = pair_rows(do_c[rows(block), :], kv)
            delta = row_sums(do_c[rows(block), both], ctxc[rows(block), both])
            level = jnp.concatenate(
                [lsec[2 * kv : 2 * kv + 1, rows(block)], lsec[2 * kv + 1 : 2 * kv + 2, rows(block)]], axis=1
            )
            dq = jnp.zeros((2 * QB, HEAD_DIM), f32)
            for part in range(span // QB):
                keys = ckv[rows(part), base : base + HEAD_DIM]
                values = ckv[rows(part), base + HEAD_DIM : base + 2 * HEAD_DIM]
                probs, dscores = backward_tile(keys, values, query, grads, keep[rows(part)], None, level, delta)
                dscores = dscores.astype(bf16)
                dv_sum[rows(part)] += nn(probs.astype(bf16), grads)
                dk_sum[rows(part)] += nn(dscores, query)
                dq += tn(dscores, keys)
            dqc[rows(block), both] = jnp.concatenate([dq[:QB], dq[QB:]], axis=1).astype(bf16)
        dkv[:, base : base + HEAD_DIM] = dk_sum[...].astype(bf16)
        dkv[:, base + HEAD_DIM : base + 2 * HEAD_DIM] = dv_sum[...].astype(bf16)
        if kv:
            next(links)
        if kv == 3:
            next(home)

    weight = w2[...].reshape(-1, w2.shape[-1])
    for block in range(blocks):
        own_c[rows(block), :] = nt(dqc[rows(block), :], weight[:, inner:]).astype(bf16)
        wires.send(own_c.at[rows(block)], got_c.at[rows(block)], spot.sibling(), over + blocks + block)
    own_m[...] = nt(dkv[...], weight[:, :inner]).astype(bf16).reshape(own_m.shape)
    wires.send(own_m.at[:, 1 - spot.core], got_m, spot.sibling(), over + 2 * blocks)
    for block in range(blocks):
        g_cq[block] = tn(a2[:, rows(block)], dqc[...]).reshape(g_cq.shape[1:]).astype(bf16)
    next(links)
    for block in range(blocks):
        g_ckv[block] = tn(mem[:, rows(block)], dkv[...]).reshape(g_ckv.shape[1:]).astype(bf16)
    next(links)
    for block in range(2):
        g_cout[2 * block : 2 * block + 2] = (
            tn(ctxc[:, rows(block)], eb[...]).reshape((2,) + g_cout.shape[1:]).astype(bf16)
        )
    leaving = [wires.move(*pair) for pair in ((g_cq, o_cq), (g_ckv, o_ckv), (g_cout, o_cout))]
    gain_terms = jnp.zeros((1, e2.shape[1]), f32)
    for block in range(blocks):
        if block + 1 < blocks:
            fetch(x1, block + 1, (block + 1) % 2)
        wires.arrive(got_c.at[rows(block)], spot.sibling(), over + blocks + block)
        change, term = norm_back(
            block,
            block % 2,
            gains[1:2, :],
            own_c[rows(block), :].astype(f32) + got_c[rows(block), :].astype(f32),
        )
        gain_terms = gain_terms + term
        value = e2[rows(block), :] + change
        e2[rows(block), :] = value
        half[block] = e2[pl.ds(pl.multiple_of(block * QB + spot.core * (QB // 2), QB // 2), QB // 2), :]
        eb[rows(block), :] = value.astype(bf16)
        do_s[rows(block), :] = nt(value.astype(bf16), w3[0].reshape(inner, -1)).astype(bf16)
    terms[1:2, :] = 0.5 * gain_terms
    next(links)
    for block in range(inner // QB):
        g_out[rows(block), :] = tn(ctx[:, rows(block)], eb[...]).astype(bf16)
    wires.arrive(got_m, spot.sibling(), over + 2 * blocks)
    o_mem[...] = (own_m[:, spot.core].astype(f32) + got_m[...].astype(f32)).astype(bf16)
    for _ in links:
        pass
    for program in [home]:
        for _ in program:
            pass
    for copy in leaving:
        copy.wait()
    wires.close()


def cross_part(depth, *operands):
    bf16, f32 = jnp.bfloat16, jnp.float32
    shape = jax.ShapeDtypeStruct
    hbm = pl.BlockSpec(memory_space=pl.ANY)
    vmem = pl.BlockSpec(memory_space=pltpu.VMEM)
    g_early, g_down, g_gate, g_up, x2, _, t_out, _, _, _, ckv = operands[:11]
    far = operands[7:17]
    tokens, width = x2.shape
    span, inner = ckv.shape
    own = tokens // 8
    rows = g_gate.shape[4]
    outs = [
        (shape(g_early.shape[4:], f32), vmem),
        (shape(g_down.shape[4:], f32), vmem),
        (shape(g_gate.shape[4:], f32), vmem),
        (shape(g_up.shape[4:], f32), vmem),
        (shape(g_gate.shape[4:], bf16), vmem),
        (shape(g_up.shape[4:], bf16), vmem),
        (shape((depth, 1, 2, 2, rows, width), bf16), hbm),
        (shape((depth, 2, 2, 2, rows, inner), bf16), hbm),
        (shape((depth, 2, 2, 2, rows, inner), bf16), hbm),
        (shape((4, own, width), f32), vmem),
        (shape((tokens, inner), bf16), vmem),
        (shape((inner, width), bf16), vmem),
        (shape((4, span // 8, width), bf16), vmem),
        (shape((8, width), f32), vmem),
        (shape((2, 2) + t_out.shape[1:], bf16), hbm),
    ]
    scratch = [pltpu.VMEM(array.shape, bf16) for array in far]
    scratch += [pltpu.VMEM(outs[i][0].shape, bf16) for i in (6, 7, 8)]
    scratch += [
        pltpu.VMEM((2, QB, width), f32),
        pltpu.VMEM((tokens, width), f32),
        pltpu.VMEM((tokens, width), bf16),
        pltpu.VMEM((tokens, inner), bf16),
        pltpu.VMEM((tokens, inner), bf16),
        pltpu.VMEM((span, inner), bf16),
        pltpu.VMEM((span, HEAD_DIM), f32),
        pltpu.VMEM((span, HEAD_DIM), f32),
        pltpu.VMEM((tokens, width), bf16),
        pltpu.VMEM((tokens, width), bf16),
        pltpu.VMEM((tokens, width), bf16),
        pltpu.VMEM((4, 2, span // 8, width), bf16),
        pltpu.VMEM((4, span // 8, width), bf16),
    ]
    for grads in (g_down, g_gate, g_up, g_early):
        scratch += scatter_buffers(depth, grads.shape[1], *grads.shape[4:])
    number = 16 + 4 * (4 + depth)
    return pl.pallas_call(
        functools.partial(cross_backward_kernel, depth),
        in_specs=[hbm] * 17 + [vmem] * 3,
        out_specs=[spec for _, spec in outs],
        out_shape=[kind for kind, _ in outs],
        scratch_shapes=scratch + wire_scratch(number, 48),
        compiler_params=pltpu.CompilerParams(
            collective_id=1, has_side_effects=True, vmem_limit_bytes=60 * 2**20
        ),
        cost_estimate=pl.CostEstimate(
            flops=16 * 10**9, bytes_accessed=128 * 2**20, transcendentals=10**7
        ),
    )(*operands)


def sides(core, own, got):
    got = got.astype(jnp.float32)
    return jnp.where(core == 0, own, got), jnp.where(core == 0, got, own)


def spread_hidden(core, owns, gots):
    pairs = [sides(core, own[...], got[...]) for own, got in zip(owns, gots)]
    sizes = [own.shape[1] // 16 for own in owns]
    return jnp.concatenate(
        [
            pair[place % 2][:, (place // 2 * 4 + q) * size : (place // 2 * 4 + q + 1) * size]
            for place in range(8)
            for q in range(4)
            for pair, size in zip(pairs, sizes)
        ],
        axis=1,
    )


def spread_heads(core, own, got, targets, units):
    even, odd = sides(core, own[...], got[...])
    step = even.shape[1] // 4
    for group in range(4):
        start = group * step
        for target, unit in zip(targets, units):
            lanes = slice(start, start + unit)
            target[:, 2 * group * unit : 2 * (group + 1) * unit] = jnp.concatenate(
                [even[:, lanes], odd[:, lanes]], axis=1
            )
            start += unit


def self_backward_kernel(depth, *refs):
    (
        g_cout, g_cq, g_ckv, g_out, t_mem, f_do, f_qkv, f_ctx, f_a1, f_x, f_half, f_w1, lse, keep, bent, gains,
        terms, codes,
        r_cout, r_out, h_mem, h_in, packed, r_cq, r_ckv, r_qkv, q_cq, q_ckv, q_qkv,
        *rest
    ) = refs
    take = lambda n: [rest.pop(0) for _ in range(n)]
    bias, sums, dk_sum, dv_sum, dqkv, grad, mine, theirs, pieces, line, small, work = take(12)
    near = take(7)
    do_s, qkv, ctx, a1, x, half, w1 = near
    buffers = [take(9) for _ in range(4)]
    resident = [take(7) for _ in range(4)]
    f32, bf16 = jnp.float32, jnp.bfloat16
    spot = Spot(depth)
    wires = Wires(*rest)
    blocks = kvs = 4
    inner = 2 * kvs * HEAD_DIM

    def rows(block):
        return slice(block * QB, (block + 1) * QB)

    far = (f_do, f_qkv, f_ctx, f_a1, f_x, f_half, f_w1)
    coming = [wires.move(source, target) for source, target in zip(far, near)]
    spot.greet()
    over = wires.take(blocks)
    homes = [deliver_tokens(spot, wires, t_mem, h_mem)]
    early = pipeline(
        [
            scatter_sums(spot, wires, g_cout, buffers[0], r_cout, None),
            scatter_sums(spot, wires, g_cq, buffers[1], r_cq, q_cq),
            scatter_sums(spot, wires, g_ckv, buffers[2], r_ckv, q_ckv),
            scatter_sums(spot, wires, g_out, buffers[3], r_out, None),
        ]
    )
    late = []
    for kv in range(kvs):
        lanes = pl.ds(kv * QB, QB)
        late.append(
            scatter_sums(
                spot, wires, grad.at[kv], resident[kv], r_qkv.at[:, lanes], q_qkv.at[:, lanes], True
            )
        )
    next(early)
    for program in homes:
        next(program)
    for copy in coming:
        copy.wait()
    for kv in range(kvs):
        base = kv * 4 * HEAD_DIM
        both = slice(2 * kv * HEAD_DIM, 2 * (kv + 1) * HEAD_DIM)
        dk_sum[...] = jnp.zeros_like(dk_sum)
        dv_sum[...] = jnp.zeros_like(dv_sum)
        sums[...] = jnp.zeros_like(sums)
        for member in range(2):
            for offset in range(4):
                head = 2 * kv + member
                bias[offset, :, member * QB : (member + 1) * QB] = spread_row(
                    bent[head : head + 1, offset * 2 * QB : (offset + 1) * 2 * QB]
                )
        for block in range(blocks):
            query = pair_rows(qkv[rows(block), base : base + 2 * HEAD_DIM], 0)
            grads = pair_rows(do_s[rows(block), :], kv)
            delta = row_sums(do_s[rows(block), both], ctx[rows(block), both])
            level = jnp.concatenate(
                [lse[2 * kv : 2 * kv + 1, rows(block)], lse[2 * kv + 1 : 2 * kv + 2, rows(block)]], axis=1
            )
            dq = jnp.zeros((2 * QB, HEAD_DIM), f32)
            for part in range(block + 1):
                keys = qkv[rows(part), base + 2 * HEAD_DIM : base + 3 * HEAD_DIM]
                values = qkv[rows(part), base + 3 * HEAD_DIM : base + 4 * HEAD_DIM]
                probs, dscores = backward_tile(
                    keys, values, query, grads, keep[rows(part)], bias[block - part], level, delta
                )
                sums[block - part] += dscores
                dscores = dscores.astype(bf16)
                dv_sum[rows(part)] += nn(probs.astype(bf16), grads)
                dk_sum[rows(part)] += nn(dscores, query)
                dq += tn(dscores, keys)
            dqkv[rows(block), base : base + 2 * HEAD_DIM] = jnp.concatenate(
                [dq[:QB], dq[QB:]], axis=1
            ).astype(bf16)
            if block % 2 or kv == 0 and block:
                next(early, None)
            for earlier in range(kv):
                if block == 2:
                    next(late[earlier], None)
        dqkv[:, base + 2 * HEAD_DIM : base + 3 * HEAD_DIM] = dk_sum[...].astype(bf16)
        dqkv[:, base + 3 * HEAD_DIM : base + 4 * HEAD_DIM] = dv_sum[...].astype(bf16)
        for member in range(2):
            for offset in range(4):
                tile = fold(sums[offset, :, member * QB : (member + 1) * QB])
                row = tile[0:1]
                for r in range(1, 8):
                    row = row + pltpu.roll(tile[r : r + 1], 2 * QB - r, 1)
                head = 2 * kv + member
                line[head : head + 1, (offset + 1) * QB : (offset + 2) * QB] = row[:, :QB]
                if offset > 0:
                    line[head : head + 1, offset * QB : (offset + 1) * QB] += row[:, QB:]
        chunk = dqkv[:, base : base + 4 * HEAD_DIM]
        for block in range(blocks):
            grad[kv, block] = tn(a1[:, rows(block)], chunk).astype(bf16).reshape(grad.shape[2:])
        next(late[kv])
        if kv == 1:
            for program in homes:
                next(program)
    weight = w1[...].reshape(-1, w1.shape[-1])
    size = QB // 2

    def half_rows(block, core):
        return pl.ds(pl.multiple_of(block * QB + core * size, size), size)

    for block in range(blocks):
        mine[block] = nt(dqkv[half_rows(block, 1 - spot.core), :], weight).astype(bf16)
        wires.send(mine.at[block], theirs.at[block], spot.sibling(), over + block)
    for program in late:
        next(program, None)
    gain_terms = jnp.zeros((1, x.shape[-1]), f32)
    for block in range(blocks):
        upstream = nt(dqkv[half_rows(block, spot.core), :], weight).astype(bf16).astype(f32)
        wires.arrive(theirs.at[block], spot.sibling(), over + block)
        upstream = upstream + theirs[block].astype(f32)
        value = x[block, spot.core].astype(f32)
        inverse = inverse_rms(value)
        scaled = upstream * gains[0:1, :]
        mean = jnp.mean(value * scaled, axis=-1, keepdims=True)
        change = inverse * scaled - value * (inverse * inverse * inverse) * mean
        gain_terms = gain_terms + jnp.sum(upstream * value * inverse, axis=0, keepdims=True)
        pieces[block] = (half[block] + change).astype(bf16)
    homing = deliver_tokens(spot, wires, pieces, h_in)
    next(homing)
    shares = nt_exact(line[:, QB:], codes[...])
    small[...] = jnp.zeros_like(small)
    for r in range(8):
        lanes = slice(r * 128, (r + 1) * 128)
        small[r : r + 1, :] = terms[0:1, lanes]
        small[8 + r : 9 + r, :] = terms[1:2, lanes]
        small[16 + r : 17 + r, :] = gain_terms[:, lanes]
    zero = jnp.zeros_like(shares)
    small[24:32, :BUCKETS] = jnp.where(spot.core == 0, shares, zero)
    small[24:32, BUCKETS : 2 * BUCKETS] = jnp.where(spot.core == 1, shares, zero)
    summing = total_small(spot, wires, small, work, packed)
    next(summing)
    for _ in range(4):
        next(summing, None)
        for program in late:
            next(program, None)
    for program in late + homes + [homing, summing]:
        for _ in program:
            pass
    for _ in early:
        pass
    wires.close()


def nt_exact(left, right):
    return lax.dot_general(
        left, right, (((1,), (1,)), ((), ())), precision=HIGH, preferred_element_type=jnp.float32
    )


def self_part(depth, *operands):
    bf16, f32 = jnp.bfloat16, jnp.float32
    shape = jax.ShapeDtypeStruct
    hbm = pl.BlockSpec(memory_space=pl.ANY)
    vmem = pl.BlockSpec(memory_space=pltpu.VMEM)
    _, g_cq, _, g_out, t_mem, do_s = operands[:6]
    tokens, inner = do_s.shape
    width = g_out.shape[-1]
    rows = g_out.shape[4]
    own = tokens // 8
    outs = [
        (shape((rows, width), f32), vmem),
        (shape((rows, width), f32), vmem),
        (shape((2, 2) + t_mem.shape[1:], bf16), hbm),
        (shape((2, 2, own, width), bf16), hbm),
        (shape((32, 128), f32), vmem),
    ]
    for kind in (f32, bf16):
        outs += [(shape((rows, size), kind), vmem) for size in (inner, inner, 2 * inner)]
    scratch = [
        pltpu.VMEM((4, QB, 2 * QB), f32),
        pltpu.VMEM((4, QB, 2 * QB), f32),
        pltpu.VMEM((tokens, HEAD_DIM), f32),
        pltpu.VMEM((tokens, HEAD_DIM), f32),
        pltpu.VMEM((tokens, 2 * inner), bf16),
        pltpu.VMEM((4, depth, 2, 2, 2, rows, QB), bf16),
        pltpu.VMEM((4, own, width), bf16),
        pltpu.VMEM((4, own, width), bf16),
        pltpu.VMEM((4, own, width), bf16),
        pltpu.VMEM((8, 5 * QB), f32),
        pltpu.VMEM((32, 128), f32),
        pltpu.VMEM((6 + depth, 32, 128), f32),
    ]
    scratch += [pltpu.VMEM(array.shape, array.dtype) for array in operands[5:12]]
    for lanes, size in ((1, width), (2, inner), (2, inner), (1, width)):
        scratch += scatter_buffers(depth, lanes, rows, size)
    for _ in range(4):
        scratch += scatter_buffers(depth, 2, rows, QB)[2:]
    return pl.pallas_call(
        functools.partial(self_backward_kernel, depth),
        in_specs=[hbm] * 12 + [vmem] * 6,
        out_specs=[spec for _, spec in outs],
        out_shape=[kind for kind, _ in outs],
        scratch_shapes=scratch + wire_scratch(4 + 8 + 3 + depth + 8 * (4 + depth), 20),
        compiler_params=pltpu.CompilerParams(
            collective_id=2, has_side_effects=True, vmem_limit_bytes=60 * 2**20
        ),
        cost_estimate=pl.CostEstimate(
            flops=16 * 10**9, bytes_accessed=128 * 2**20, transcendentals=10**7
        ),
    )(*operands)


def finish_kernel(
    t_in, t_mem, t_out, packed, c_out, c_cout, r_cq, r_ckv, r_qkv, q_cq, q_ckv, q_qkv,
    rg0, rg1, rg2, ru0, ru1, ru2, qg0, qg1, qg2, qu0, qu1, qu2, rd0, rd1, rd2,
    d_in, d_mem, d_out, n_self, n_cross, n_ff, d_self, d_cross, d_q, d_k, d_v, d_cq, d_ck, d_cv, d_gate, d_up,
    d_down,
):
    core = lax.axis_index("dp") % 2
    d_in[...] = t_in[...].astype(jnp.float32)
    d_mem[...] = t_mem[...].astype(jnp.float32)
    d_out[...] = t_out[...]
    mine = lax.axis_index("dp") * 4 + lax.axis_index("seq")
    size = n_self.shape[1]
    per = 128 // size
    for index, target in ((2, n_self), (1, n_cross), (0, n_ff)):
        line = packed[pl.ds(8 * index + mine // per, 1), :]
        value = line[:, :size]
        for place in range(1, per):
            value = jnp.where(mine % per == place, line[:, place * size : (place + 1) * size], value)
        target[...] = value
    d_self[...] = c_out[...]
    d_cross[...] = c_cout[...]
    d_gate[...] = spread_hidden(core, (rg0, rg1, rg2), (qg0, qg1, qg2))
    d_up[...] = spread_hidden(core, (ru0, ru1, ru2), (qu0, qu1, qu2))
    low = 0
    for piece in (rd0, rd1, rd2):
        d_down[low : low + piece.shape[0], :] = piece[...]
        low += piece.shape[0]
    spread_heads(core, r_qkv, q_qkv, (d_q, d_k, d_v), (2 * HEAD_DIM, HEAD_DIM, HEAD_DIM))
    spread_heads(core, r_ckv, q_ckv, (d_ck, d_cv), (HEAD_DIM, HEAD_DIM))
    spread_heads(core, r_cq, q_cq, (d_cq,), (2 * HEAD_DIM,))


def finish(piece, *operands):
    f32 = jnp.float32
    shape = jax.ShapeDtypeStruct
    t_in, t_mem, t_out = operands[:3]
    rows, width = operands[4].shape
    inner = operands[6].shape[1]
    hidden = 2 * sum(tile.shape[1] for tile in operands[12:15])
    outs = [shape(t_in.shape, f32), shape(t_mem.shape, f32), shape(t_out.shape, t_out.dtype)]
    outs += [shape((1, piece), f32)] * 3 + [shape((rows, width), f32)] * 2
    for size in (2 * inner, inner, inner, 2 * inner, inner, inner, hidden, hidden):
        outs.append(shape((rows, size), f32))
    outs.append(shape((sum(down.shape[0] for down in operands[-3:]), width), f32))
    vmem = pl.BlockSpec(memory_space=pltpu.VMEM)
    return pl.pallas_call(
        finish_kernel,
        in_specs=[vmem] * len(operands),
        out_specs=[vmem] * len(outs),
        out_shape=outs,
        compiler_params=pltpu.CompilerParams(vmem_limit_bytes=60 * 2**20),
        cost_estimate=pl.CostEstimate(flops=0, bytes_accessed=16 * 2**20, transcendentals=0),
    )(*operands)


def feed_forward_kernel(depth, tiles, *refs):
    (
        a3_far, wt_far, keep, x2, gu0_far, d0_far, gu1p, d1p, gu2p, d2p,
        o_top, o_u, pieces, g_gate2, g_up2, g_down2, g5,
        r_gate0, r_up0, r_down0, r_gate1, r_up1, q_gate0, q_up0, q_gate1, q_up1,
        *rest
    ) = refs
    take = lambda n: [rest.pop(0) for _ in range(n)]
    gu1, d1, gu2, d2, mid, dgate, dup, g0, g1, g2, g3, g4, mine, theirs, second = take(15)
    a3, wt, gu0, d0, low_top, u = take(6)
    buffers = [take(7) for _ in range(5)]
    f32, bf16 = jnp.float32, jnp.bfloat16
    spot = Spot(depth)
    wires = Wires(*rest)
    blocks = 4
    starts = [sum(tiles[:i]) for i in range(3)]
    coming = [
        wires.move(source, target)
        for source, target in ((wt_far, wt), (a3_far, a3), (gu0_far, gu0), (d0_far, d0))
    ]

    def rows(block):
        return slice(block * QB, (block + 1) * QB)

    spot.greet()
    over = wires.take(blocks)
    middle = d1.shape[-1] // 2
    wide1 = share_plane(
        spot, wires, gu1p, lambda corner: gu1.at[:, :, corner], lambda view, side: view.at[:, side]
    )
    down1 = share_plane(
        spot,
        wires,
        d1p,
        lambda corner: d1.at[0, :, corner],
        lambda view, side: view.at[:, :, pl.ds(side * middle, middle)],
    )
    wide2 = gather_columns(spot, wires, gu2p, gu2)
    down2 = gather_rows(spot, wires, d2p, d2)
    sums = [
        scatter_sums(spot, wires, grads, scratch, total, got, True)
        for grads, scratch, total, got in (
            (g0, buffers[0], r_gate0, q_gate0),
            (g1, buffers[1], r_up0, q_up0),
            (g2, buffers[2], r_down0, None),
            (g3, buffers[3], r_gate1, q_gate1),
            (g4, buffers[4], r_up1, q_up1),
        )
    ]

    def advance(*programs):
        for program in programs:
            next(program, None)

    advance(wide1, down1, wide2, down2)
    halves = [
        wires.move(
            x2.at[pl.ds(pl.multiple_of(block * QB + spot.core * (QB // 2), QB // 2), QB // 2)], second.at[block]
        )
        for block in range(blocks)
    ]
    for copy in coming:
        copy.wait()
    for block in range(blocks):
        value = wt[block].reshape(QB, -1).astype(f32) * (keep[rows(block)] == 0.0).astype(f32)
        low_top[rows(block), :] = value.astype(bf16)
    coming = [wires.move(low_top, o_top)]
    wides = [gu0, gu1, gu2]
    downs = [d0, d1, d2]

    def wide_weight(tile, part):
        both = wides[tile]
        lanes = pl.ds(part * tiles[tile], tiles[tile])
        return both[:, :, :, :, lanes].reshape(-1, tiles[tile])

    def down_weight(tile):
        weight = downs[tile][0]
        if weight.shape[2] % 16:
            return weight.astype(f32).reshape(tiles[tile], -1).astype(bf16)
        return weight.reshape(tiles[tile], -1)

    def hidden(tile, block):
        lanes = slice(starts[tile], starts[tile] + tiles[tile])
        left = a3[rows(block), :]
        gate = nn(left, wide_weight(tile, 0))
        upward = nn(left, wide_weight(tile, 1))
        back = nt(low_top[rows(block), :], down_weight(tile))
        bend = jnp.tanh(GELU_SCALE * (gate + GELU_CUBE * gate * gate * gate))
        share = 0.5 * (1.0 + bend)
        active = gate * share
        slope = share + 0.5 * gate * (1.0 - bend * bend) * (
            GELU_SCALE * (1.0 + 3.0 * GELU_CUBE * gate * gate)
        )
        mid[rows(block), lanes] = (active * upward).astype(bf16)
        dgate[rows(block), lanes] = (back * upward * slope).astype(bf16)
        dup[rows(block), lanes] = (back * active).astype(bf16)

    def wide_grads(tile, source, target):
        lanes = slice(starts[tile], starts[tile] + tiles[tile])
        right = source[:, lanes]
        for block in range(blocks):
            target[block] = tn(a3[:, rows(block)], right).reshape(target.shape[1:]).astype(bf16)

    def down_grads(tile, target):
        lanes = slice(starts[tile], starts[tile] + tiles[tile])
        target[...] = tn(mid[:, lanes], low_top[...]).reshape(target.shape).astype(bf16)

    hidden(0, 0)
    hidden(0, 1)
    hidden(0, 2)
    hidden(0, 3)
    wide_grads(0, dgate, g0)
    advance(sums[0])
    wide_grads(0, dup, g1)
    advance(wide1, down1, wide2, down2)
    down_grads(0, g2)
    advance(wide1, down1, sums[1])
    for block in range(blocks):
        hidden(1, block)
        if block == 1:
            advance(sums[0], wide2, down2, sums[2])
    advance(sums[1])
    wide_grads(1, dgate, g3)
    advance(sums[0], wide2, down2, sums[3])
    wide_grads(1, dup, g4)
    advance(sums[2], sums[1])
    down_grads(1, g5)
    advance(sums[0], sums[4])
    for block in range(blocks):
        hidden(2, block)
        if block == 1:
            advance(sums[3], sums[2])
        if block == 3:
            advance(sums[1], sums[0])
    wide_grads(2, dgate, g_gate2)
    wide_grads(2, dup, g_up2)
    advance(sums[4], sums[3], sums[2])
    down_grads(2, g_down2)

    def half_rows(block, core):
        return pl.ds(pl.multiple_of(block * QB + core * (QB // 2), QB // 2), QB // 2)

    def contribution(block, core):
        total = None
        for tile in range(3):
            lanes = slice(starts[tile], starts[tile] + tiles[tile])
            term = nn(mid[half_rows(block, core), lanes], down_weight(tile))
            total = term if total is None else total + term
        return total.astype(bf16)

    for block in range(blocks):
        mine[block] = contribution(block, 1 - spot.core)
        wires.send(mine.at[block], theirs.at[block], spot.sibling(), over + block)
    for block in range(blocks):
        total = None
        for tile in range(3):
            lanes = slice(starts[tile], starts[tile] + tiles[tile])
            term = nt(dgate[rows(block), lanes], wide_weight(tile, 0))
            term = term + nt(dup[rows(block), lanes], wide_weight(tile, 1))
            total = term if total is None else total + term
        u[rows(block), :] = total.astype(bf16)
        coming.append(wires.move(u.at[rows(block)], o_u.at[rows(block)]))
        if block == 1:
            advance(sums[4], sums[3])
    advance(sums[4])
    for block in range(blocks):
        value = contribution(block, spot.core).astype(f32)
        wires.arrive(theirs.at[block], spot.sibling(), over + block)
        value = value + theirs[block].astype(f32)
        halves[block].wait()
        kept = (keep[half_rows(block, spot.core), :] == 0.0).astype(f32)
        pieces[block] = ((second[block] + value) * kept).astype(bf16)
    for program in sums + [wide1, down1, wide2, down2]:
        for _ in program:
            pass
    for copy in coming:
        copy.wait()
    wires.close()


def feed_forward(depth, tiles, *operands):
    bf16, f32 = jnp.bfloat16, jnp.float32
    shape = jax.ShapeDtypeStruct
    hbm = pl.BlockSpec(memory_space=pl.ANY)
    vmem = pl.BlockSpec(memory_space=pltpu.VMEM)
    a3, _, _, _, gu0, d0, gu1p, d1p, gu2p, d2p = operands
    tokens, width = a3.shape
    hidden_width = sum(tiles)
    rows = [d1p.shape[1], d1p.shape[1], d2p.shape[2]]
    own = tokens // 8
    wide = gu2p.shape[2]

    def wide_grad(tile):
        return (depth, 2, 2, 2, wide, tiles[tile])

    def down_grad(tile):
        return (depth, 1, 2, 2, rows[tile], width)

    outs = [
        (shape((tokens, width), bf16), hbm),
        (shape((tokens, width), bf16), hbm),
        (shape((4, own, width), bf16), vmem),
        (shape(wide_grad(2), bf16), vmem),
        (shape(wide_grad(2), bf16), vmem),
        (shape(down_grad(2), bf16), vmem),
        (shape(down_grad(1), bf16), vmem),
    ]
    for tile in range(2):
        outs += [(shape((wide, tiles[tile]), f32), vmem)] * 2
        if tile == 0:
            outs.append((shape((rows[tile], width), f32), vmem))
    for tile in range(2):
        outs += [(shape((wide, tiles[tile]), bf16), vmem)] * 2
    scratch = [
        pltpu.VMEM(gu0.shape, bf16),
        pltpu.VMEM(d0.shape, bf16),
        pltpu.VMEM((depth, 2) + gu2p.shape[1:], bf16),
        pltpu.VMEM((1, depth) + d2p.shape[1:], bf16),
    ]
    scratch += [pltpu.VMEM((tokens, hidden_width), bf16)] * 3
    for tile in range(2):
        scratch += [pltpu.VMEM(wide_grad(tile), bf16)] * 2
        if tile == 0:
            scratch.append(pltpu.VMEM(down_grad(tile), bf16))
    scratch += [
        pltpu.VMEM((4, own, width), bf16),
        pltpu.VMEM((4, own, width), bf16),
        pltpu.VMEM((4, own, width), f32),
        pltpu.VMEM((tokens, width), bf16),
        pltpu.VMEM((4, 2, own, width), bf16),
        pltpu.VMEM(gu0.shape, bf16),
        pltpu.VMEM(d0.shape, bf16),
        pltpu.VMEM((tokens, width), bf16),
        pltpu.VMEM((tokens, width), bf16),
    ]
    for tile in range(2):
        for _ in range(2):
            scratch += scatter_buffers(depth, 2, wide, tiles[tile])[2:]
        if tile == 0:
            scratch += scatter_buffers(depth, 1, rows[tile], width)[2:]
    return pl.pallas_call(
        functools.partial(feed_forward_kernel, depth, tiles),
        in_specs=[hbm, hbm, vmem] + [hbm] * 7,
        out_specs=[spec for _, spec in outs],
        out_shape=[kind for kind, _ in outs],
        scratch_shapes=scratch + wire_scratch(4 + 22 * depth + 6 * (4 + depth), 24),
        compiler_params=pltpu.CompilerParams(
            collective_id=3, has_side_effects=True, vmem_limit_bytes=60 * 2**20
        ),
        cost_estimate=pl.CostEstimate(
            flops=27 * 10**9, bytes_accessed=64 * 2**20, transcendentals=10**7
        ),
    )(*operands)


def per_chip(
    layer_input,
    memory,
    target_lengths,
    memory_lengths,
    buckets,
    norm_self,
    self_q,
    self_k,
    self_v,
    self_out,
    rel_bias,
    norm_cross,
    cross_q,
    cross_k,
    cross_v,
    cross_out,
    norm_ff,
    ff_gate,
    ff_up,
    ff_down,
    cotangent,
):
    bf16, f32 = jnp.bfloat16, jnp.float32
    depth = lax.axis_size("dp") // 2
    spot = Spot(depth)
    core = spot.core
    width = layer_input.shape[3]
    local = layer_input.shape[2]
    near = memory.shape[2]
    shard = norm_self.shape[0]

    cuts = [(0, 32), (32, 64), (64, ff_down.shape[0] // 4)]
    tiles = tuple(16 * (stop - start) for start, stop in cuts)

    heads = jnp.arange(4)
    spots = (heads // 2) * 64 + 2 * spot.corner + heads % 2
    placed = jnp.sum(
        jnp.where(jnp.arange(128)[None, None, :] == spots[None, :, None], rel_bias[:, :, None].astype(f32), 0.0),
        axis=1,
    )
    lengths = jnp.concatenate([target_lengths, memory_lengths]).reshape(1, 4).astype(f32)
    small = jnp.concatenate(
        [
            jnp.stack([norm_self, norm_cross, norm_ff]).astype(f32),
            jnp.pad(lengths, ((0, 0), (0, 124))),
            placed,
        ]
    )
    padded = jnp.concatenate([jnp.full((1, QB), -1, jnp.int32), buckets[None, :]], axis=1)
    vectors = row_pieces(padded)
    vectors = jnp.concatenate([jnp.roll(vectors[..., ::-1], 1, axis=-1), vectors], axis=1).reshape(1, -1)
    codes = (vectors == jnp.arange(BUCKETS, dtype=jnp.int32)[:, None]).astype(bf16)
    holes = jnp.where(vectors < 0, NEG, 0.0).astype(f32)
    onehot = (buckets[:, None] == jnp.arange(BUCKETS, dtype=jnp.int32)[None, :]).astype(f32)
    (
        inputs, upstream, encoded, _, w_qkv, w_cross, w_outs, w_gu, w_down,
        normed_self, qkv, context, self_sums, first, normed_cross, cross_queries, far_kv, cross_context,
        cross_sums, second, normed_ff, gains, _, _, bent, keep_self, keep_cross, near_wide, near_down, wide_pack, down_pack,
    ) = forward_layer(
        depth,
        tuple(stop for _, stop in cuts),
        layer_input.reshape(2, 2, local // 2, width),
        cotangent.reshape(2, 2, local // 2, width),
        memory.reshape(2, 2, near // 2, width),
        small,
        codes,
        holes,
        self_q,
        self_k,
        self_v,
        cross_k,
        cross_v,
        cross_q,
        ff_gate,
        ff_up,
        self_out,
        cross_out,
        ff_down.reshape(4, -1, width),
    )
    encoded = encoded.reshape(-1, width)
    (
        top_low, changed, output, g_gate, g_up, g_down, g_early,
        r_gate0, r_up0, r_down0, r_gate1, r_up1, q_gate0, q_up0, q_gate1, q_up1,
    ) = feed_forward(
        depth, tiles, normed_ff, upstream, keep_self, second, w_gu, w_down,
        near_wide, near_down, wide_pack, down_pack,
    )

    (
        r_down1, r_down2, r_gate2, r_up2, q_gate2, q_up2, g_cout, g_cq, g_ckv, half, self_up, g_out, memory_grad, terms,
        output,
    ) = cross_part(
        depth, g_early, g_down, g_gate, g_up, second, first, output, changed, top_low, cross_queries, far_kv, cross_context,
        normed_cross, encoded, w_cross, w_outs, context, cross_sums, keep_cross, gains,
    )
    r_cout, r_out, memory_grad, input_grad, packed, r_cq, r_ckv, r_qkv, q_cq, q_ckv, q_qkv = self_part(
        depth, g_cout, g_cq, g_ckv, g_out.reshape(depth, 1, 2, 2, -1, width), memory_grad, self_up, qkv, context,
        normed_self, inputs, half, w_qkv, self_sums, keep_self, bent, gains, terms, onehot.T,
    )
    (
        input_grad, memory_grad, output, n_self, n_cross, n_ff, r_out, r_cout, d_q, d_k, d_v, d_cq, d_ck, d_cv,
        d_gate, d_up, d_down,
    ) = finish(
        width // (depth * 8),
        input_grad, memory_grad, output, packed, r_out, r_cout, r_cq, r_ckv, r_qkv, q_cq, q_ckv, q_qkv,
        r_gate0, r_gate1, r_gate2, r_up0, r_up1, r_up2, q_gate0, q_gate1, q_gate2, q_up0, q_up1, q_up2,
        r_down0, r_down1, r_down2,
    )
    bias_grad = packed[24:, :64].reshape(4, 2, 2, BUCKETS)
    bias_grad = jnp.transpose(bias_grad, (3, 0, 2, 1)).reshape(BUCKETS, HEADS)
    bias_grad = lax.dynamic_slice(
        bias_grad, (lax.axis_index("dp") * rel_bias.shape[0], spot.corner * rel_bias.shape[1]), rel_bias.shape
    )

    return (
        output.reshape(layer_input.shape),
        input_grad.reshape(layer_input.shape),
        memory_grad.reshape(memory.shape),
        n_self.reshape(-1),
        d_q,
        d_k,
        d_v,
        r_out,
        bias_grad,
        n_cross.reshape(-1),
        d_cq,
        d_ck,
        d_cv,
        r_cout,
        n_ff.reshape(-1),
        d_gate,
        d_up,
        d_down,
    )


def solution(mesh):
    placed = (
        P(None, "dp", "seq", None),
        P(None, "dp", "seq", None),
        P(None, "dp"),
        P(None, "dp"),
        P(),
        P("dp"),
        P("dp", None),
        P("dp", None),
        P("dp", None),
        P("dp", None),
        P("dp", "seq"),
        P("dp"),
        P("dp", None),
        P("dp", None),
        P("dp", None),
        P("dp", None),
        P("dp"),
        P("dp", None),
        P("dp", None),
        P("dp", None),
        P(None, "dp", "seq", None),
    )
    chips = mesh.shape["seq"] == 4 and mesh.shape["dp"] == HEADS // 2
    return jax.shard_map(
        per_chip if chips else per_device,
        mesh=mesh,
        in_specs=placed,
        out_specs=(
            P(None, "dp", "seq", None),
            P(None, "dp", "seq", None),
            P(None, "dp", "seq", None),
            P(("dp", "seq")),
            P(("dp", "seq"), None),
            P(("dp", "seq"), None),
            P(("dp", "seq"), None),
            P(("dp", "seq"), None),
            P("dp", "seq"),
            P(("dp", "seq")),
            P(("dp", "seq"), None),
            P(("dp", "seq"), None),
            P(("dp", "seq"), None),
            P(("dp", "seq"), None),
            P(("dp", "seq")),
            P(("dp", "seq"), None),
            P(("dp", "seq"), None),
            P(("dp", "seq"), None),
        ),
        check_vma=False,
    )
```
